32 devices in a mesh: ctx: 8 (over y, x, core), tp: 4 (over z).
Axes of the slice: x: 2, y: 2, z: 4, core: 2. Of those that a mesh axis runs over, the one named last changes fastest.
Arguments:
- tokens: bfloat16 [2048, 2048], P('ctx'), may hold values from -12 to 12
- feature_weight: bfloat16 [2048, 128], P(None, 'tp'), may hold values from -0.125 to 0.125
- window_weight: bfloat16 [2048, 1024], P(None, 'tp'), may hold values from -1 to 1
- value_weight: bfloat16 [2048, 512], P(None, 'tp'), may hold values from -0.125 to 0.125
- log_decay: float32 [2048, 4], P('ctx', 'tp'), may hold values from -1 to 0
- out_grad: bfloat16 [2048, 512], P('ctx', 'tp'), may hold values from -6 to 6
Outputs:
- attended: bfloat16 [2048, 512], P('ctx', 'tp')
- input_grad: bfloat16 [2048, 2048], P('ctx')
The draws below stay inside these ranges and needn't reach their ends.
All inputs are finite; a program needn't handle non-finite values.
Results may differ from the reference program's by a relative error of at most 0.012.
The reference program's roundings to bfloat16 on the way count: a program that leaves them out, or rounds other values in their place, can miss the bound.
Values may be sent and summed in bfloat16 or wider, within the bound.
No kernel may reach another device: no remote copies, remote signals or barrier semaphores. Data moves between devices by JAX's collectives and lax.ppermute only.
A program may use at most 64 MiB of HBM per device.

```python
import math
from functools import partial
import jax
import jax.numpy as jnp
from jax import lax

D = 2048
DH = 128
F = 16
WINDOW = 1024
ROWS = 256
ATTN_GROUPS = 4
PHI = 273
SEQ_SPAN = 2048


def draw_tokens(key, part):
    stochastic_seed_parts = jax.random.split(key, 2)
    offsets = jnp.clip(jax.random.normal(stochastic_seed_parts[1], (SEQ_SPAN // ROWS, D), jnp.float32), -3.0, 3.0) * 0.7
    shifted = jnp.repeat(offsets, ROWS, axis=0)
    basis = jnp.clip(jax.random.normal(stochastic_seed_parts[0], (SEQ_SPAN, D), jnp.float32), -4.0, 4.0)
    return (basis + shifted).astype(jnp.bfloat16)


def draw_window_weight(key, part):
    stochastic_seed_parts = jax.random.split(key, 2)
    scale = D ** (-0.5)
    query_part = jnp.clip(jax.random.normal(stochastic_seed_parts[0], (D, ATTN_GROUPS, 1, DH), jnp.float32), -6.0, 6.0)
    key_part = jnp.clip(jax.random.normal(stochastic_seed_parts[1], (D, ATTN_GROUPS, 1, DH), jnp.float32), -6.0, 6.0)
    joined = jnp.concatenate([query_part, key_part], axis=2) * scale
    return joined.reshape(D, 2 * DH * ATTN_GROUPS).astype(jnp.bfloat16)


def draw_log_decay(key, part):
    stochastic_seed_parts = jax.random.split(key, 6)
    portion = 0.5
    slow_heads = jax.random.uniform(stochastic_seed_parts[0], (1, ATTN_GROUPS), jnp.float32) < portion
    slow_rate = jax.random.uniform(stochastic_seed_parts[1], (1, ATTN_GROUPS), jnp.float32, 0.1, 0.5) * (math.log(10.0) / (1.25 * SEQ_SPAN))
    fast_rate = jax.random.uniform(stochastic_seed_parts[2], (1, ATTN_GROUPS), jnp.float32, 1.0 / 50.0, 1.0 / 30.0)
    chosen_speed = jnp.where(slow_heads, slow_rate, fast_rate)
    texture_jaggedness = jax.random.uniform(stochastic_seed_parts[3], (SEQ_SPAN, ATTN_GROUPS), jnp.float32, 0.5, 2.0)
    spike_occurrences = jax.random.uniform(stochastic_seed_parts[4], (SEQ_SPAN, ATTN_GROUPS), jnp.float32) < 3.0 / SEQ_SPAN
    objective_trace = jnp.log(jax.random.uniform(stochastic_seed_parts[5], (SEQ_SPAN, ATTN_GROUPS), jnp.float32, 0.6, 0.8))
    return -chosen_speed * texture_jaggedness + jnp.where(spike_occurrences, objective_trace, 0.0)


def shard_levels(rng, extent, shards, low, high):
    gain = 1.0
    for axis_at, shards_of in shards:
        draws = jax.random.uniform(jax.random.fold_in(jax.random.fold_in(rng, 6), axis_at), (shards_of,), jnp.float32, low / len(shards), high / len(shards))
        gain = gain * jnp.repeat(jnp.exp(draws), extent[axis_at] // shards_of).reshape((-1,) + (1,) * (len(extent) - 1 - axis_at))
    return gain


def normal_values(own_key, dims, spread, reach, cuts=(), kind=jnp.bfloat16):
    entries = spread * jax.random.normal(own_key, dims, jnp.float32)
    if cuts:
        entries = entries * shard_levels(own_key, dims, cuts, -0.22, 0.18)
    return jnp.clip(entries, -reach, reach).astype(kind)


def setup_inputs(seed: int = 0) -> dict:
    key_of = jax.random.split(jax.random.key(seed), 7)
    return {
        "tokens": draw_tokens(jax.random.fold_in(key_of[6], 71), 0),
        "feature_weight": normal_values(key_of[1], (D, 2 * F * ATTN_GROUPS), D ** -0.5, 0.125, ((1, 4),)),
        "window_weight": draw_window_weight(jax.random.fold_in(key_of[6], 71), 0),
        "value_weight": normal_values(key_of[3], (D, DH * ATTN_GROUPS), D ** -0.5, 0.125, ((1, 4),)),
        "log_decay": draw_log_decay(jax.random.fold_in(key_of[6], 71), 0),
        "out_grad": normal_values(key_of[5], (SEQ_SPAN, DH * ATTN_GROUPS), 1.0, 6.0, ((0, 8), (1, 4))),
    }


precise = lax.Precision.HIGHEST

def feature_map(vectors):
    row_count = vectors.shape[0]
    feat_width = vectors.shape[1]
    square = (vectors[:, :, None] * vectors[:, None, :]).reshape(row_count, feat_width * feat_width) * 0.5 ** 0.5
    return jnp.concatenate([square, vectors, jnp.ones((row_count, 1), jnp.float32)], axis=1)

def linear_part(query_feat, query_cum, query_pos, key_feat, key_cum, key_pos, value_rows, state_num, state_den):
    products = jnp.dot(query_feat, key_feat.T, precision=precise)
    kernel = 1.0 + products + 0.5 * products * products
    causal = key_pos[None, :] <= query_pos[:, None]
    decay_table = jnp.exp(jnp.where(causal, query_cum[:, None] - key_cum[None, :], -jnp.inf))
    weights = kernel * decay_table
    lifted = feature_map(query_feat)
    growth = jnp.exp(query_cum)
    numerator = jnp.dot(weights, value_rows, precision=precise) + growth[:, None] * jnp.dot(lifted, state_num, precision=precise)
    denominator = lax.optimization_barrier(jnp.sum(weights, axis=1)) + growth * jnp.dot(lifted, state_den, precision=precise)
    return numerator / denominator[:, None]

def window_part(queries, query_pos, key_rows, key_values, key_pos):
    scores = jnp.dot(queries, key_rows.T, precision=precise) * DH ** (-0.5)
    allowed = (key_pos[None, :] <= query_pos[:, None]) & (query_pos[:, None] - key_pos[None, :] < WINDOW) & (key_pos[None, :] >= 0)
    scores = jnp.where(allowed, scores, -jnp.inf)
    row_max = lax.optimization_barrier(jnp.max(scores, axis=1, keepdims=True))
    exponent = jnp.exp(scores - row_max)
    return jnp.dot(exponent, key_values, precision=precise) / lax.optimization_barrier(jnp.sum(exponent, axis=1, keepdims=True))

def head_forward(features, window, values, log_rates):
    feat_scale = F ** (-0.25)
    query_feat = features[:, :F] * feat_scale
    key_feat = features[:, F:] * feat_scale
    queries = window[:, :DH]
    pad_keys = jnp.concatenate([jnp.zeros((WINDOW, DH), jnp.float32), window[:, DH:]], axis=0)
    pad_values = jnp.concatenate([jnp.zeros((WINDOW, DH), jnp.float32), values], axis=0)
    local_pos = jnp.arange(ROWS, dtype=jnp.int32)
    window_pos = jnp.arange(WINDOW + ROWS, dtype=jnp.int32)

    def advance(states, block_index):
        state_num, state_den = states
        first_row = block_index * ROWS
        block_query = lax.dynamic_slice_in_dim(query_feat, first_row, ROWS, 0)
        block_key = lax.dynamic_slice_in_dim(key_feat, first_row, ROWS, 0)
        block_values = lax.dynamic_slice_in_dim(values, first_row, ROWS, 0)
        cumulative = jnp.cumsum(lax.dynamic_slice_in_dim(log_rates, first_row, ROWS, 0))
        linear = linear_part(block_query, cumulative, local_pos, block_key, cumulative, local_pos, block_values, state_num, state_den)
        windowed = window_part(lax.dynamic_slice_in_dim(queries, first_row, ROWS, 0), first_row + local_pos, lax.dynamic_slice_in_dim(pad_keys, first_row, WINDOW + ROWS, 0), lax.dynamic_slice_in_dim(pad_values, first_row, WINDOW + ROWS, 0), first_row - WINDOW + window_pos)
        tail_decay = jnp.exp(cumulative[-1] - cumulative)
        phi_keys = feature_map(block_key) * tail_decay[:, None]
        new_num = jnp.exp(cumulative[-1]) * state_num + jnp.dot(phi_keys.T, block_values, precision=precise)
        new_den = jnp.exp(cumulative[-1]) * state_den + lax.optimization_barrier(jnp.sum(phi_keys, axis=0))
        return ((new_num, new_den), linear + windowed)
    initial = (jnp.zeros((PHI, DH), jnp.float32), jnp.zeros((PHI,), jnp.float32))
    block_count = SEQ_SPAN // ROWS
    _, outputs = lax.scan(advance, initial, jnp.arange(block_count, dtype=jnp.int32))
    return outputs.reshape(SEQ_SPAN, DH)

def reference(tokens, feature_weight, window_weight, value_weight, log_decay, out_grad):
    features = jnp.dot(tokens, feature_weight, preferred_element_type=jnp.float32).astype(jnp.bfloat16)
    window = jnp.dot(tokens, window_weight, preferred_element_type=jnp.float32).astype(jnp.bfloat16)
    values = jnp.dot(tokens, value_weight, preferred_element_type=jnp.float32).astype(jnp.bfloat16)

    def per_head(head_index):
        feat_cols = lax.dynamic_slice_in_dim(features, head_index * (2 * F), 2 * F, 1).astype(jnp.float32)
        win_cols = lax.dynamic_slice_in_dim(window, head_index * (2 * DH), 2 * DH, 1).astype(jnp.float32)
        val_cols = lax.dynamic_slice_in_dim(values, head_index * DH, DH, 1).astype(jnp.float32)
        head_rates = lax.dynamic_slice_in_dim(log_decay, head_index, 1, 1)[:, 0]
        cotangent = lax.dynamic_slice_in_dim(out_grad, head_index * DH, DH, 1).astype(jnp.float32)
        result, pullback = jax.vjp(partial(head_forward, log_rates=head_rates), feat_cols, win_cols, val_cols)
        gradients = pullback(cotangent)
        return (result.astype(jnp.bfloat16), gradients[0].astype(jnp.bfloat16), gradients[1].astype(jnp.bfloat16), gradients[2].astype(jnp.bfloat16))
    head_out, grad_feat, grad_win, grad_val = lax.map(per_head, jnp.arange(ATTN_GROUPS, dtype=jnp.int32))
    attended = jnp.transpose(head_out, (1, 0, 2)).reshape(SEQ_SPAN, ATTN_GROUPS * DH)
    grad_feat = jnp.transpose(grad_feat, (1, 0, 2)).reshape(SEQ_SPAN, ATTN_GROUPS * 2 * F)
    grad_win = jnp.transpose(grad_win, (1, 0, 2)).reshape(SEQ_SPAN, ATTN_GROUPS * 2 * DH)
    grad_val = jnp.transpose(grad_val, (1, 0, 2)).reshape(SEQ_SPAN, ATTN_GROUPS * DH)
    input_grad = jnp.dot(grad_feat, feature_weight.T, preferred_element_type=jnp.float32) + jnp.dot(grad_win, window_weight.T, preferred_element_type=jnp.float32) + jnp.dot(grad_val, value_weight.T, preferred_element_type=jnp.float32)
    return (attended, input_grad.astype(jnp.bfloat16))
```

```python
from functools import partial

import jax
import jax.numpy as jnp
from jax import lax
from jax.experimental import pallas as pl
from jax.experimental.pallas import tpu as pltpu
from jax.sharding import Mesh
from jax.sharding import PartitionSpec as P

WINDOW = 1024
LANES = 128
MASKED = -1e30
CTX = ("chip", "core")
f32 = jnp.float32
bf16 = jnp.bfloat16


def nn(a, b):
    return lax.dot_general(a, b, (((1,), (0,)), ((), ())), preferred_element_type=f32)


def nt(a, b):
    return lax.dot_general(a, b, (((1,), (1,)), ((), ())), preferred_element_type=f32)


def wide(ref, at, start, count):
    view = ref if at is None else ref.at[at]
    return jnp.concatenate(
        [view[start : start + count, :], view[start + count : start + 2 * count, :]], axis=1
    )


def put_wide(ref, start, value):
    count = value.shape[0]
    for half in range(value.shape[1] // LANES):
        ref[start + half * count : start + (half + 1) * count, :] = value[
            :, half * LANES : (half + 1) * LANES
        ]


def cum_row(ref, at, start):
    view = ref if at is None else ref.at[at]
    tail = view[start : start + 16, :].astype(f32)
    first = tail[0:1] + tail[2:3] + tail[4:5]
    second = tail[1:2] + tail[3:4] + tail[5:6]
    return jnp.concatenate([first, second], axis=1)


def project_kernel(
    place_ref, tok_ref, fw_ref, ww_ref, vw_ref, ld_ref, do_ref,
    send_ref, own_ref, feat_ref, cum_ref, pack_ref,
):
    me, core = place_ref[0], place_ref[1]
    rows, dim = tok_ref.shape
    half = dim // 2
    dh = do_ref.shape[1]
    nf = fw_ref.shape[1] // 2
    count = send_ref.shape[0]
    tok = tok_ref[...]
    feat = nn(tok, fw_ref[...]).astype(bf16)
    window = nn(tok, ww_ref[...]).astype(bf16)
    values = nn(tok, vw_ref[...]).astype(bf16)
    feat_ref[...] = feat
    eye = (
        lax.broadcasted_iota(jnp.int32, (2 * nf, 2 * nf), 0)
        == lax.broadcasted_iota(jnp.int32, (2 * nf, 2 * nf), 1)
    ).astype(bf16)
    feat_t = nt(eye, feat).astype(bf16)
    at_row = lax.broadcasted_iota(jnp.int32, (rows, rows), 0)
    at_col = lax.broadcasted_iota(jnp.int32, (rows, rows), 1)
    ld = ld_ref[...]
    cum_r = jnp.sum(jnp.where(at_row <= at_col, ld, 0.0), axis=0, keepdims=True)
    ld_r = jnp.sum(jnp.where(at_row == at_col, ld, 0.0), axis=0, keepdims=True)
    cum_ref[...] = jnp.sum(jnp.where(at_col <= at_row, ld_r, 0.0), axis=1, keepdims=True)
    high = cum_r.astype(bf16)
    rest = cum_r - high.astype(f32)
    mid = rest.astype(bf16)
    low = (rest - mid.astype(f32)).astype(bf16)
    pieces = [high[:, :LANES], high[:, LANES:], mid[:, :LANES], mid[:, LANES:], low[:, :LANES], low[:, LANES:]]
    tail = jnp.concatenate(
        [p.astype(f32) for p in pieces] + [jnp.zeros((10, LANES), f32)], axis=0
    ).astype(bf16)
    feat_at = 2 * rows
    tail_at = feat_at + 2 * nf

    own_ref[0:rows, :] = window[:, dh:]
    own_ref[rows : 2 * rows, :] = values
    put_wide(own_ref, feat_at, feat_t[nf:, :])
    own_ref[tail_at : tail_at + 16, :] = tail

    def fill(j, carry):
        slot = send_ref.at[j]
        slot[tail_at : tail_at + 16, :] = tail

        @pl.when(j > me)
        def _():
            slot[0:rows, :] = window[:, dh:]
            slot[rows : 2 * rows, :] = values
            put_wide(slot, feat_at, feat_t[nf:, :])

        @pl.when(j <= me)
        def _():
            slot[0:rows, :] = window[:, :dh]
            slot[rows : 2 * rows, :] = do_ref[...]
            put_wide(slot, feat_at, feat_t[:nf, :])

        return carry

    lax.fori_loop(0, count, fill, 0)

    start = pl.multiple_of(core * half, half)
    pack_ref[0:half, :] = ww_ref[pl.ds(start, half), 0:dh]
    pack_ref[half : 2 * half, :] = ww_ref[pl.ds(start, half), dh : 2 * dh]
    pack_ref[2 * half : 3 * half, :] = vw_ref[pl.ds(start, half), :]
    fw_t = nt(eye, fw_ref[pl.ds(start, half), :]).astype(bf16)
    put_wide(pack_ref, 3 * half, fw_t)


def query_kernel(
    place_ref, recv_ref, own_ref, feat_ref, cum_ref,
    att_ref, stat_ref, dwq_ref, dqt_ref,
    p_ref,
):
    me = place_ref[0]
    rows, dh = att_ref.shape
    nf = feat_ref.shape[1] // 2
    back = WINDOW // rows
    feat_at = 2 * rows
    tail_at = feat_at + 2 * nf
    scale = dh ** (-0.5)
    feat_scale = nf ** (-0.5)
    wq = recv_ref[me, 0:rows, :]
    do = recv_ref[me, rows : 2 * rows, :]
    q = feat_ref[:, :nf]
    at_row = lax.broadcasted_iota(jnp.int32, (rows, rows), 0)
    at_col = lax.broadcasted_iota(jnp.int32, (rows, rows), 1)

    def keys(w):
        if w == back:
            return own_ref[0:rows, :]
        return recv_ref[jnp.maximum(me - back + w, 0), 0:rows, :]

    def vals(w):
        if w == back:
            return own_ref[rows : 2 * rows, :]
        return recv_ref[jnp.maximum(me - back + w, 0), rows : 2 * rows, :]

    top = jnp.full((rows, 1), MASKED, f32)
    for w in range(back + 1):
        s = nt(wq, keys(w)) * scale
        if w == back:
            ok = at_col <= at_row
        elif w == 0:
            ok = (at_col > at_row) & (me >= back)
        else:
            ok = (at_col >= 0) & (me >= back - w)
        s = jnp.where(ok, s, MASKED)
        p_ref[w] = s
        top = jnp.maximum(top, jnp.max(s, axis=1, keepdims=True))
    total = jnp.zeros((rows, 1), f32)
    out = jnp.zeros((rows, dh), f32)
    for w in range(back + 1):
        p = jnp.exp(p_ref[w] - top)
        p_ref[w] = p
        total += jnp.sum(p, axis=1, keepdims=True)
        out += nn(p.astype(bf16), vals(w))
    inv = 1.0 / total
    windowed = out * inv

    cum_c = cum_ref[...]
    growth = jnp.exp(cum_c)
    own_cum = cum_row(own_ref, None, tail_at)
    own_e = jnp.where(at_col <= at_row, jnp.exp(jnp.minimum(cum_c - own_cum, 0.0)), 0.0)

    def far_terms(j, between):
        cum = cum_row(recv_ref, j, tail_at)
        whole = cum[:, rows - 1 : rows]
        es = jnp.exp(between + whole - cum)
        x = nn(q, wide(recv_ref, j, feat_at, nf)) * feat_scale
        return es, x, between + whole

    def forward(step, carry):
        num, den, between = carry
        j = me - 1 - step
        es, x, between = far_terms(j, between)
        weight = (1.0 + x + 0.5 * x * x) * es
        den += jnp.sum(weight, axis=1, keepdims=True)
        num += nn(weight.astype(bf16), recv_ref[j, rows : 2 * rows, :])
        return num, den, between

    zero = jnp.zeros((1, 1), f32)
    num, den, _ = lax.fori_loop(
        0, me, forward, (jnp.zeros((rows, dh), f32), jnp.zeros((rows, 1), f32), zero)
    )
    own_x = nn(q, wide(own_ref, None, feat_at, nf)) * feat_scale
    weight = (1.0 + own_x + 0.5 * own_x * own_x) * own_e
    num = num * growth + nn(weight.astype(bf16), own_ref[rows : 2 * rows, :])
    den = den * growth + jnp.sum(weight, axis=1, keepdims=True)
    rden = 1.0 / den
    linear = num * rden
    att_ref[...] = (linear + windowed).astype(bf16)
    do_f = do.astype(f32)
    delta_w = jnp.sum(do_f * windowed, axis=1, keepdims=True)
    delta_l = jnp.sum(do_f * linear, axis=1, keepdims=True)
    lse = top + jnp.log(total)
    lane = lax.broadcasted_iota(jnp.int32, (rows, LANES), 1)
    sheet = jnp.where(lane == 0, lse, 0.0)
    sheet = jnp.where(lane == 1, delta_w, sheet)
    sheet = jnp.where(lane == 2, rden, sheet)
    sheet = jnp.where(lane == 3, delta_l, sheet)
    stat_ref[...] = jnp.transpose(sheet)[0:8, :]

    dwq = jnp.zeros((rows, dh), f32)
    for w in range(back + 1):
        dp = nt(do, vals(w))
        ds = (p_ref[w] * inv) * (dp - delta_w)
        dwq += nn(ds.astype(bf16), keys(w))
    dwq_ref[...] = (dwq * scale).astype(bf16)

    far_scale = growth * rden

    def backward(step, carry):
        dqt, between = carry
        j = me - 1 - step
        es, x, between = far_terms(j, between)
        dp = nt(do, recv_ref[j, rows : 2 * rows, :])
        dx = (dp - delta_l) * es * ((1.0 + x) * far_scale)
        dqt += nt(wide(recv_ref, j, feat_at, nf), dx.astype(bf16))
        return dqt, between

    dqt, _ = lax.fori_loop(0, me, backward, (jnp.zeros((nf, rows), f32), zero))
    dp = nt(do, own_ref[rows : 2 * rows, :])
    dx = (dp - delta_l) * own_e * ((1.0 + own_x) * rden)
    dqt += nt(wide(own_ref, None, feat_at, nf), dx.astype(bf16))
    dqt_ref[...] = (dqt * feat_scale).astype(bf16)


def key_kernel(
    place_ref, recv_ref, own_ref, feat_ref, cum_ref, stat_ref, dwq_ref, dqt_ref, grad_ref
):
    me = place_ref[0]
    count = recv_ref.shape[0]
    rows, dh = dwq_ref.shape
    nf = feat_ref.shape[1] // 2
    back = WINDOW // rows
    feat_at = 2 * rows
    tail_at = feat_at + 2 * nf
    scale = dh ** (-0.5)
    feat_scale = nf ** (-0.5)
    wk = own_ref[0:rows, :]
    v = own_ref[rows : 2 * rows, :]
    k = feat_ref[:, nf : 2 * nf]
    at_row = lax.broadcasted_iota(jnp.int32, (rows, rows), 0)
    at_col = lax.broadcasted_iota(jnp.int32, (rows, rows), 1)
    dwk = jnp.zeros((rows, dh), f32)
    dv = jnp.zeros((rows, dh), f32)
    for w in range(back + 1):
        j = jnp.minimum(me + w, count - 1)
        wq = recv_ref[j, 0:rows, :]
        do = recv_ref[j, rows : 2 * rows, :]
        if w == 0:
            ok = at_row <= at_col
        elif w == back:
            ok = (at_row > at_col) & (me + w < count)
        else:
            ok = (at_row >= 0) & (me + w < count)
        s = nt(wk, wq) * scale
        p = jnp.where(ok, jnp.exp(s - stat_ref[j, 0:1, :]), 0.0)
        ds = p * (nt(v, do) - stat_ref[j, 1:2, :])
        dv += nn(p.astype(bf16), do)
        dwk += nn(ds.astype(bf16), wq)

    cum_c = cum_ref[...]
    own_cum = cum_row(own_ref, None, tail_at)
    tail = jnp.exp(own_cum[:, rows - 1 : rows] - cum_c)

    def terms(j, e):
        qt = wide(recv_ref, j, feat_at, nf)
        do = recv_ref[j, rows : 2 * rows, :]
        x = nn(k, qt) * feat_scale
        weight = (1.0 + x + 0.5 * x * x) * e
        dx = (nt(v, do) - stat_ref[j, 3:4, :]) * e * (1.0 + x)
        return nn(weight.astype(bf16), do), nt(qt, dx.astype(bf16))

    own_e = jnp.where(at_row <= at_col, jnp.exp(jnp.minimum(own_cum - cum_c, 0.0)), 0.0)
    more_v, dkt = terms(me, own_e * stat_ref[me, 2:3, :])
    dv += more_v

    def far(j, carry):
        dv, dkt, between = carry
        cum = cum_row(recv_ref, j, tail_at)
        e = jnp.exp(between + cum) * stat_ref[j, 2:3, :] * tail
        more_v, more_k = terms(j, e)
        return dv + more_v, dkt + more_k, between + cum[:, rows - 1 : rows]

    dv, dkt, _ = lax.fori_loop(me + 1, count, far, (dv, dkt, jnp.zeros((1, 1), f32)))
    grad_ref[0:rows, :] = dwq_ref[...]
    grad_ref[rows : 2 * rows, :] = (dwk * scale).astype(bf16)
    grad_ref[2 * rows : 3 * rows, :] = dv.astype(bf16)
    dft = jnp.concatenate([dqt_ref[...], (dkt * feat_scale).astype(bf16)], axis=0)
    put_wide(grad_ref, 3 * rows, dft)


def merge_kernel(
    place_ref, grad_ref, mq_ref, mk_ref, mv_ref, mf_ref, oq_ref, ok_ref, ov_ref, of_ref,
    out_ref, cat_ref, feat_ref,
):
    heads = grad_ref.shape[0]
    rows = out_ref.shape[0]
    nf2 = mf_ref.shape[1] // (out_ref.shape[1] // LANES)
    step = pl.program_id(0)
    tiles = pl.num_programs(0) // 2

    @pl.when(step == 0)
    def _():
        for h in range(heads):
            for part in range(3):
                at = (3 * h + part) * LANES
                cat_ref[:, at : at + LANES] = grad_ref[h, part * rows : (part + 1) * rows, :]
        dft = jnp.concatenate([wide(grad_ref, h, 3 * rows, nf2) for h in range(heads)], axis=0)
        feat_ref[...] = jnp.transpose(dft.astype(f32)).astype(bf16)

    def product(q_ref, k_ref, v_ref, f_ref):
        weights = jnp.concatenate(
            [r[h] for h in range(heads) for r in (q_ref, k_ref, v_ref)], axis=1
        )
        feat_w = jnp.concatenate([wide(f_ref, h, 0, nf2) for h in range(heads)], axis=0)
        out = nt(cat_ref[...], weights) + nn(feat_ref[...], feat_w)
        out_ref[...] = out.astype(bf16)

    @pl.when(step < tiles)
    def _():
        product(mq_ref, mk_ref, mv_ref, mf_ref)

    @pl.when(step >= tiles)
    def _():
        product(oq_ref, ok_ref, ov_ref, of_ref)


VMEM = pl.BlockSpec(memory_space=pltpu.VMEM)
SMEM = pl.BlockSpec(memory_space=pltpu.SMEM)
params = pltpu.CompilerParams(vmem_limit_bytes=48 * 1024 * 1024)


def merge(place, grads, mine, other, dim):
    heads = grads.shape[0]
    rows = (grads.shape[1] * LANES) // (3 * LANES + 32)
    half = dim // 2
    tile = 256
    tiles = half // tile
    nf2 = (mine.shape[1] - 3 * half) * LANES // half
    frows = nf2 * tile // LANES

    def own_at(part):
        return lambda i, place: (0, part * tiles + jnp.minimum(i, tiles - 1), 0)

    def other_at(part):
        return lambda i, place: (0, part * tiles + jnp.maximum(i - tiles, 0), 0)

    first = 3 * half // frows
    big = (heads, tile, LANES)
    small = (heads, frows, LANES)
    specs = [pl.BlockSpec(grads.shape, lambda i, place: (0, 0, 0))]
    specs += [pl.BlockSpec(big, own_at(part)) for part in range(3)]
    specs += [pl.BlockSpec(small, lambda i, place: (0, first + jnp.minimum(i, tiles - 1), 0))]
    specs += [pl.BlockSpec(big, other_at(part)) for part in range(3)]
    specs += [pl.BlockSpec(small, lambda i, place: (0, first + jnp.maximum(i - tiles, 0), 0))]

    def out_at(i, place):
        core = place[1]
        return (0, jnp.where(i < tiles, core * tiles + i, (1 - core) * tiles + i - tiles))

    return pl.pallas_call(
        merge_kernel,
        out_shape=jax.ShapeDtypeStruct((rows, dim), bf16),
        grid_spec=pltpu.PrefetchScalarGridSpec(
            num_scalar_prefetch=1,
            grid=(2 * tiles,),
            in_specs=specs,
            out_specs=pl.BlockSpec((rows, tile), out_at),
            scratch_shapes=[
                pltpu.VMEM((rows, 3 * LANES * heads), bf16),
                pltpu.VMEM((rows, nf2 * heads), bf16),
            ],
        ),
        compiler_params=params,
        cost_estimate=pl.CostEstimate(
            flops=2 * rows * dim * heads * 416, bytes_accessed=heads * dim * 416 * 2, transcendentals=0
        ),
        name="head_sum",
    )(place, grads, mine, mine, mine, mine, other, other, other, other)


def per_device(tokens, feature_weight, window_weight, value_weight, log_decay, out_grad):
    rows, dim = tokens.shape
    nf2 = feature_weight.shape[1]
    nf = nf2 // 2
    dh = value_weight.shape[1]
    count = lax.axis_size(CTX)
    me = lax.axis_index(CTX)
    core = lax.axis_index("core")
    place = jnp.stack([me, core]).astype(jnp.int32)
    payload = 2 * rows + 2 * nf + 16
    pack = 3 * (dim // 2) + nf2 * (dim // 2) // LANES
    send, own, feat, cum, packed = pl.pallas_call(
        project_kernel,
        out_shape=(
            jax.ShapeDtypeStruct((count, payload, LANES), bf16),
            jax.ShapeDtypeStruct((payload, LANES), bf16),
            jax.ShapeDtypeStruct((rows, nf2), bf16),
            jax.ShapeDtypeStruct((rows, 1), f32),
            jax.ShapeDtypeStruct((pack, LANES), bf16),
        ),
        in_specs=[SMEM] + [VMEM] * 6,
        out_specs=[VMEM] * 5,
        compiler_params=params,
        cost_estimate=pl.CostEstimate(
            flops=2 * rows * dim * 416, bytes_accessed=4 * 1024 * 1024, transcendentals=0
        ),
        name="project",
    )(place, tokens, feature_weight, window_weight, value_weight, log_decay, out_grad)
    mine = lax.all_gather(packed, "tp")
    recv = lax.all_to_all(send, CTX, 0, 0, tiled=True)
    attended, stat, dwq, dqt = pl.pallas_call(
        query_kernel,
        out_shape=(
            jax.ShapeDtypeStruct((rows, dh), bf16),
            jax.ShapeDtypeStruct((8, rows), f32),
            jax.ShapeDtypeStruct((rows, dh), bf16),
            jax.ShapeDtypeStruct((nf, rows), bf16),
        ),
        in_specs=[SMEM] + [VMEM] * 4,
        out_specs=[VMEM] * 4,
        scratch_shapes=[pltpu.VMEM((WINDOW // rows + 1, rows, rows), f32)],
        compiler_params=params,
        cost_estimate=pl.CostEstimate(
            flops=10**9, bytes_accessed=2 * 1024 * 1024, transcendentals=10**6
        ),
        name="query_side",
    )(place, recv, own, feat, cum)
    stats = lax.all_gather(stat, CTX)
    grads = pl.pallas_call(
        key_kernel,
        out_shape=jax.ShapeDtypeStruct((3 * rows + nf2 * rows // LANES, LANES), bf16),
        in_specs=[SMEM] + [VMEM] * 7,
        out_specs=VMEM,
        compiler_params=params,
        cost_estimate=pl.CostEstimate(
            flops=10**9, bytes_accessed=2 * 1024 * 1024, transcendentals=10**6
        ),
        name="key_side",
    )(place, recv, own, feat, cum, stats, dwq, dqt)
    all_grads = lax.all_gather(grads, "tp")
    other = lax.ppermute(mine, "core", [(0, 1), (1, 0)])
    input_grad = merge(place, all_grads, mine, other, dim)
    return (attended, input_grad)


def solution(mesh):
    ctx, tp = mesh.devices.shape
    split = Mesh(mesh.devices.reshape(ctx // 2, 2, tp), ("chip", "core", "tp"))
    in_specs = (
        P(CTX, None),
        P(None, "tp"),
        P(None, "tp"),
        P(None, "tp"),
        P(CTX, "tp"),
        P(CTX, "tp"),
    )
    out_specs = (P(CTX, "tp"), P(CTX, None))
    return jax.shard_map(
        per_device, mesh=split, in_specs=in_specs, out_specs=out_specs, check_vma=False
    )
```

```python
import jax
import jax.numpy as jnp
from jax import lax
from jax.experimental import pallas as pl
from jax.experimental.pallas import tpu as pltpu
from jax.sharding import Mesh
from jax.sharding import PartitionSpec as P

WINDOW = 1024
LANES = 128
MASKED = -1e30
CTX = ("chip", "core")
CHUNKS = 4
f32 = jnp.float32
bf16 = jnp.bfloat16


def nn(a, b):
    return lax.dot_general(a, b, (((1,), (0,)), ((), ())), preferred_element_type=f32)


def nt(a, b):
    return lax.dot_general(a, b, (((1,), (1,)), ((), ())), preferred_element_type=f32)


def partner(me, d, count):
    assert count & (count - 1) == 0
    return jnp.bitwise_xor(me, d)


def wide(view, start, count):
    return jnp.concatenate(
        [view[start : start + count, :], view[start + count : start + 2 * count, :]], axis=1
    )


def put_wide(ref, start, value):
    count = value.shape[0]
    for half in range(value.shape[1] // LANES):
        ref[start + half * count : start + (half + 1) * count, :] = value[
            :, half * LANES : (half + 1) * LANES
        ]


def cum_row(view, start):
    tail = view[start : start + 16, :].astype(f32)
    first = tail[0:1] + tail[2:3] + tail[4:5]
    second = tail[1:2] + tail[3:4] + tail[5:6]
    return jnp.concatenate([first, second], axis=1)


def iotas(rows):
    return (
        lax.broadcasted_iota(jnp.int32, (rows, rows), 0),
        lax.broadcasted_iota(jnp.int32, (rows, rows), 1),
    )


def project_kernel(place_ref, tok_hbm, fw_hbm, ww_hbm, vw_hbm, ld_hbm, do_hbm, *rest):
    *sends, keys_ref, query_ref, feat_ref, cum_ref, pack_ref = rest[:-8]
    tok_ref, fw_ref, ww_ref, vw_ref, ld_ref, do_ref, sems, small = rest[-8:]
    me, piece = place_ref[0], place_ref[1]
    rows, dim = tok_ref.shape
    dh = do_ref.shape[1]
    nf = fw_ref.shape[0] // 2
    count = len(sends) + 1
    span = dim // CHUNKS
    copies = []
    for c in range(CHUNKS):
        part = pl.ds(c * span, span)
        copies.append([
            pltpu.make_async_copy(tok_hbm.at[:, part], tok_ref.at[:, part], sems.at[c, 0]),
            pltpu.make_async_copy(ww_hbm.at[part, :], ww_ref.at[part, :], sems.at[c, 1]),
            pltpu.make_async_copy(vw_hbm.at[part, :], vw_ref.at[part, :], sems.at[c, 2]),
            pltpu.make_async_copy(fw_hbm.at[:, part], fw_ref.at[:, part], sems.at[c, 3]),
        ])
    others = [
        pltpu.make_async_copy(ld_hbm, ld_ref, small.at[0]),
        pltpu.make_async_copy(do_hbm, do_ref, small.at[1]),
    ]
    for copy in copies[0] + others:
        copy.start()
    for group in copies[1:]:
        for copy in group:
            copy.start()
    for copy in others:
        copy.wait()
    at_row, at_col = iotas(rows)
    ld_r = ld_ref[...]
    ld_c = jnp.sum(jnp.where(at_row == at_col, ld_r, 0.0), axis=1, keepdims=True)
    cum_r = jnp.sum(jnp.where(at_row <= at_col, ld_c, 0.0), axis=0, keepdims=True)
    cum_ref[...] = jnp.sum(jnp.where(at_col <= at_row, ld_r, 0.0), axis=1, keepdims=True)
    high = cum_r.astype(bf16)
    left = cum_r - high.astype(f32)
    mid = left.astype(bf16)
    low = (left - mid.astype(f32)).astype(bf16)
    pieces = [t[:, h : h + LANES].astype(f32) for t in (high, mid, low) for h in range(0, rows, LANES)]
    tail = jnp.concatenate(pieces + [jnp.zeros((10, LANES), f32)], axis=0).astype(bf16)

    feat = jnp.zeros((rows, 2 * nf), f32)
    window = jnp.zeros((rows, 2 * dh), f32)
    values = jnp.zeros((rows, dh), f32)
    for c in range(CHUNKS):
        for copy in copies[c]:
            copy.wait()
        part = slice(c * span, (c + 1) * span)
        tok = tok_ref[:, part]
        feat += nt(tok, fw_ref[:, part])
        window += nn(tok, ww_ref[part, :])
        values += nn(tok, vw_ref[part, :])
    feat = feat.astype(bf16)
    window = window.astype(bf16)
    values = values.astype(bf16)
    feat_ref[...] = feat
    small_row, small_col = iotas(2 * nf)
    feat_t = nt((small_row == small_col).astype(bf16), feat).astype(bf16)
    feat_at = 2 * rows
    tail_at = feat_at + 2 * nf

    def put_keys(ref):
        ref[0:rows, :] = window[:, dh:]
        ref[rows : 2 * rows, :] = values
        put_wide(ref, feat_at, feat_t[nf:, :])
        ref[tail_at : tail_at + 16, :] = tail

    def put_query(ref):
        ref[0:rows, :] = window[:, :dh]
        ref[rows : 2 * rows, :] = do_ref[...]
        put_wide(ref, feat_at, feat_t[:nf, :])
        ref[tail_at : tail_at + 16, :] = tail

    put_keys(keys_ref)
    put_query(query_ref)
    for d in range(1, count):
        later = partner(me, d, count) > me
        ref = sends[d - 1]
        pl.when(later)(lambda ref=ref: put_keys(ref))
        pl.when(jnp.logical_not(later))(lambda ref=ref: put_query(ref))

    tile = pack_ref.shape[2]
    for p in range(pack_ref.shape[0]):
        at = pl.multiple_of((piece + p) * tile, tile)
        part = pl.ds(at, tile)
        pack_ref[p, 0 : 2 * dh, :] = jnp.transpose(ww_ref[part, :].astype(f32)).astype(bf16)
        pack_ref[p, 2 * dh : 3 * dh, :] = jnp.transpose(vw_ref[part, :].astype(f32)).astype(bf16)
        pack_ref[p, 3 * dh : 3 * dh + 2 * nf, :] = fw_ref[:, part]


def between(totals, low, high):
    at = lax.broadcasted_iota(jnp.int32, totals.shape, 0)
    return jnp.sum(jnp.where((at > low) & (at < high), totals, 0.0), axis=0, keepdims=True)


def over_partners(count, body, carry):
    if count <= 8:
        for d in range(1, count):
            carry = body(d, carry)
        return carry
    return lax.fori_loop(1, count, body, carry)


def query_kernel(count, place_ref, *rest):
    recvs = rest[: -10]
    (own_ref, query_ref, feat_ref, cum_ref, att_ref, stat_ref, sheet_ref, near_ref, p_ref,
     cums_ref) = rest[-10:]

    def recv(d):
        return recvs[d - 1] if len(recvs) > 1 else recvs[0].at[d - 1]

    me = place_ref[0]
    rows, dh = att_ref.shape
    nf = feat_ref.shape[1] // 2
    back = WINDOW // rows
    feat_at = 2 * rows
    tail_at = feat_at + 2 * nf
    scale = dh ** (-0.5)
    feat_scale = nf ** (-0.5)
    wq = query_ref[0:rows, :]
    do = query_ref[rows : 2 * rows, :]
    q = feat_ref[:, :nf]
    at_row, at_col = iotas(rows)
    own_cum = cum_row(own_ref, tail_at)
    cums_ref[pl.ds(me, 1), :] = own_cum
    near_ref[me] = own_ref[0 : 2 * rows, :]

    def gather(d, carry):
        j = partner(me, d, count)
        view = recv(d)
        near_ref[j] = view[0 : 2 * rows, :]
        cums_ref[pl.ds(j, 1), :] = cum_row(view, tail_at)
        return carry

    over_partners(count, gather, 0)

    def near(w):
        return near_ref.at[jnp.maximum(me - back + w, 0)]

    top = jnp.full((rows, LANES), MASKED, f32)
    for w in range(back + 1):
        keys = own_ref[0:rows, :] if w == back else near(w)[0:rows, :]
        s = nt(wq, keys) * scale
        if w == back:
            s = jnp.where(at_col <= at_row, s, MASKED)
        elif w == 0:
            s = jnp.where((at_col > at_row) & (me >= back), s, MASKED)
        else:
            s = jnp.where(me >= back - w, s, MASKED)
        p_ref[w] = s
        for h in range(0, rows, LANES):
            top = jnp.maximum(top, s[:, h : h + LANES])
    top = jnp.max(top, axis=1, keepdims=True)
    total = jnp.zeros((rows, LANES), f32)
    out = jnp.zeros((rows, dh), f32)
    for w in range(back + 1):
        p = jnp.exp(p_ref[w] - top)
        for h in range(0, rows, LANES):
            total += p[:, h : h + LANES]
        vals = own_ref[rows : 2 * rows, :] if w == back else near(w)[rows : 2 * rows, :]
        out += nn(p.astype(bf16), vals)
    total = jnp.sum(total, axis=1, keepdims=True)
    windowed = out * (1.0 / total)

    cum_c = cum_ref[...]
    growth = jnp.exp(cum_c)
    totals = cums_ref[:, rows - 1 : rows]

    def forward(d, carry):
        num, den = carry
        j = partner(me, d, count)
        view = recv(d)
        gap = between(totals, j - 1, me)
        es = jnp.where(j < me, jnp.exp(jnp.minimum(gap - cums_ref[pl.ds(j, 1), :], 0.0)), 0.0)
        x = nn(q, wide(view, feat_at, nf)) * feat_scale
        weight = (1.0 + x + 0.5 * x * x) * es
        for h in range(0, rows, LANES):
            den += weight[:, h : h + LANES]
        num += nn(weight.astype(bf16), view[rows : 2 * rows, :])
        return num, den

    num, den = over_partners(
        count, forward, (jnp.zeros((rows, dh), f32), jnp.zeros((rows, LANES), f32))
    )
    x = nn(q, wide(own_ref, feat_at, nf)) * feat_scale
    e = jnp.where(at_col <= at_row, jnp.exp(jnp.minimum(cum_c - own_cum, 0.0)), 0.0)
    weight = (1.0 + x + 0.5 * x * x) * e
    num = num * growth + nn(weight.astype(bf16), own_ref[rows : 2 * rows, :])
    den = den * growth
    for h in range(0, rows, LANES):
        den += weight[:, h : h + LANES]
    rden = 1.0 / jnp.sum(den, axis=1, keepdims=True)
    linear = num * rden
    att_ref[...] = (linear + windowed).astype(bf16)
    do_f = do.astype(f32)
    delta_w = jnp.sum(do_f * windowed, axis=1, keepdims=True)
    delta_l = jnp.sum(do_f * linear, axis=1, keepdims=True)
    lse = top + jnp.log(total)
    lane = lax.broadcasted_iota(jnp.int32, (rows, LANES), 1)
    sheet = jnp.where(lane == 0, lse, 0.0)
    sheet = jnp.where(lane == 1, delta_w, sheet)
    sheet = jnp.where(lane == 2, rden, sheet)
    sheet = jnp.where(lane == 3, delta_l, sheet)
    sheet = jnp.where(lane == 4, cum_c, sheet)
    sheet_ref[...] = sheet
    stat_ref[...] = jnp.transpose(sheet)[0:8, :]


def gradient_kernel(count, place_ref, *rest):
    recvs = rest[:-6]
    own_ref, query_ref, feat_ref, sheet_ref, stat_ref, grad_ref = rest[-6:]

    def recv(d):
        return recvs[d - 1] if len(recvs) > 1 else recvs[0].at[d - 1]

    me = place_ref[0]
    rows = feat_ref.shape[0]
    dh = LANES
    nf = feat_ref.shape[1] // 2
    feat_at = 2 * rows
    scale = dh ** (-0.5)
    feat_scale = nf ** (-0.5)
    at_row, at_col = iotas(rows)
    apart = at_row - at_col
    wq, wk = query_ref[0:rows, :], own_ref[0:rows, :]
    do, v = query_ref[rows : 2 * rows, :], own_ref[rows : 2 * rows, :]
    q, k = feat_ref[:, :nf], feat_ref[:, nf:]
    lse_c, dw_c = sheet_ref[:, 0:1], sheet_ref[:, 1:2]
    rden_c, dl_c, cum_c = sheet_ref[:, 2:3], sheet_ref[:, 3:4], sheet_ref[:, 4:5]
    totals = jnp.concatenate([stat_ref[j, 4:5, rows - 1 : rows] for j in range(count)], axis=0)
    own_cum = stat_ref[me, 4:5, :]
    growth_c = jnp.exp(cum_c) * rden_c
    tail_c = jnp.exp(own_cum[:, rows - 1 : rows] - cum_c)

    def pick(flag, a, b):
        return jnp.where(flag, a, b)

    s = nt(wq, wk) * scale
    causal = at_col <= at_row
    p = jnp.where(causal, jnp.exp(s - lse_c), 0.0)
    dp = nt(do, v)
    dwq = nn((p * (dp - dw_c)).astype(bf16), wk)
    x = nn(q, wide(own_ref, feat_at, nf)) * feat_scale
    e = jnp.where(causal, jnp.exp(jnp.minimum(cum_c - own_cum, 0.0)), 0.0) * rden_c
    dx = (dp - dl_c) * e * (1.0 + x)
    dqt = nt(wide(own_ref, feat_at, nf), dx.astype(bf16))

    s = nt(wk, wq) * scale
    causal = at_row <= at_col
    p = jnp.where(causal, jnp.exp(s - stat_ref[me, 0:1, :]), 0.0)
    dp = nt(v, do)
    dwk = nn((p * (dp - stat_ref[me, 1:2, :])).astype(bf16), wq)
    x = nn(k, wide(query_ref, feat_at, nf)) * feat_scale
    e = jnp.where(causal, jnp.exp(jnp.minimum(own_cum - cum_c, 0.0)), 0.0) * stat_ref[me, 2:3, :]
    dx = (dp - stat_ref[me, 3:4, :]) * e * (1.0 + x)
    dkt = nt(wide(query_ref, feat_at, nf), dx.astype(bf16))
    dv = nn((p + (1.0 + x + 0.5 * x * x) * e).astype(bf16), do)

    def step(d, carry):
        dwq, dqt, dwk, dkt, dv = carry
        j = partner(me, d, count)
        view = recv(d)
        mine = j < me
        sign = pick(mine, 1, -1)
        limit = WINDOW - jnp.abs(me - j) * rows
        rows_w = pick(mine, wq, wk)
        rows_v = pick(mine, do, v)
        rows_f = pick(mine, q, k)
        other_w = view[0:rows, :]
        other_v = view[rows : 2 * rows, :]
        other_f = wide(view, feat_at, nf)
        st = stat_ref[j]
        zero = jnp.zeros((1, rows), f32)
        cum = st[4:5, :]
        gap = between(totals, jnp.minimum(me, j), jnp.maximum(me, j))
        e_r = jnp.exp(jnp.minimum(gap + pick(mine, cum[:, rows - 1 : rows] - cum, cum), 0.0))
        e_r = e_r * pick(mine, 1.0, st[2:3, :])
        e_c = pick(mine, growth_c, tail_c)

        s = nt(rows_w, other_w) * scale
        p = jnp.exp(s - pick(mine, lse_c, 0.0) - pick(mine, zero, st[0:1, :]))
        p = jnp.where(apart * sign < limit, p, 0.0)
        dp = nt(rows_v, other_v)
        ds = p * (dp - pick(mine, dw_c, 0.0) - pick(mine, zero, st[1:2, :]))
        more_w = nn(ds.astype(bf16), other_w)
        x = nn(rows_f, other_f) * feat_scale
        e = e_r * e_c
        dx = (dp - pick(mine, dl_c, 0.0) - pick(mine, zero, st[3:4, :])) * e * (1.0 + x)
        more_f = nt(other_f, dx.astype(bf16))
        more_v = nn((p + (1.0 + x + 0.5 * x * x) * e).astype(bf16), other_v)
        dwq = dwq + pick(mine, more_w, 0.0)
        dwk = dwk + pick(mine, 0.0, more_w)
        dqt = dqt + pick(mine, more_f, 0.0)
        dkt = dkt + pick(mine, 0.0, more_f)
        dv = dv + pick(mine, 0.0, more_v)
        return dwq, dqt, dwk, dkt, dv

    dwq, dqt, dwk, dkt, dv = over_partners(count, step, (dwq, dqt, dwk, dkt, dv))
    grad_ref[0:rows, :] = (dwq * scale).astype(bf16)
    grad_ref[rows : 2 * rows, :] = (dwk * scale).astype(bf16)
    grad_ref[2 * rows : 3 * rows, :] = dv.astype(bf16)
    dft = (jnp.concatenate([dqt, dkt], axis=0) * feat_scale).astype(bf16)
    put_wide(grad_ref, 3 * rows, dft)


def merge_kernel(grad_ref, *rest):
    heads = grad_ref.shape[0]
    weights, out_ref, cat_ref, feat_ref = rest[:heads], rest[-3], rest[-2], rest[-1]
    rows = out_ref.shape[0]
    lanes = 3 * LANES
    nf2 = weights[0].shape[-2] - lanes

    @pl.when(pl.program_id(0) == 0)
    def _():
        for h in range(heads):
            for part in range(3):
                at = (3 * h + part) * LANES
                cat_ref[:, at : at + LANES] = grad_ref[h, part * rows : (part + 1) * rows, :]
        dft = jnp.concatenate([wide(grad_ref.at[h], 3 * rows, nf2) for h in range(heads)], axis=0)
        feat_ref[...] = jnp.transpose(dft.astype(f32)).astype(bf16)

    main = jnp.concatenate([w[0, 0, 0:lanes, :] for w in weights], axis=0)
    feats = jnp.concatenate([w[0, 0, lanes:, :] for w in weights], axis=0)
    out_ref[...] = (nn(cat_ref[...], main) + nn(feat_ref[...], feats)).astype(bf16)


VMEM = pl.BlockSpec(memory_space=pltpu.VMEM)
SMEM = pl.BlockSpec(memory_space=pltpu.SMEM)
ANY = pl.BlockSpec(memory_space=pl.ANY)
params = pltpu.CompilerParams(vmem_limit_bytes=48 * 1024 * 1024)


def cost(flops, nbytes, exps=0):
    return pl.CostEstimate(flops=flops, bytes_accessed=nbytes, transcendentals=exps)


def merge(grads, weights, by_head, rows, dim):
    heads = grads.shape[0]
    columns, tile = weights.shape[2:]
    pieces = dim // tile

    def at(h):
        return (lambda i: (h, i, 0, 0)) if by_head else (lambda i: (i, h, 0, 0))

    specs = [pl.BlockSpec(grads.shape, lambda i: (0, 0, 0))]
    specs += [pl.BlockSpec((1, 1, columns, tile), at(h)) for h in range(heads)]
    return pl.pallas_call(
        merge_kernel,
        out_shape=jax.ShapeDtypeStruct((rows, dim), bf16),
        grid=(pieces,),
        in_specs=specs,
        out_specs=pl.BlockSpec((rows, tile), lambda i: (0, i)),
        scratch_shapes=[
            pltpu.VMEM((rows, 3 * LANES * heads), bf16),
            pltpu.VMEM((rows, (columns - 3 * LANES) * heads), bf16),
        ],
        compiler_params=params,
        cost_estimate=cost(2 * rows * dim * heads * columns, heads * dim * columns * 2),
        name="head_sum",
    )(grads, *([weights] * heads))


def per_device(tokens, feature_weight, window_weight, value_weight, log_decay, out_grad):
    rows, dim = tokens.shape
    nf2 = feature_weight.shape[1]
    nf = nf2 // 2
    dh = value_weight.shape[1]
    columns = 3 * dh + nf2
    count = lax.axis_size(CTX)
    me = lax.axis_index(CTX)
    tile = 2 * LANES
    spread = count * tile == dim
    pieces = 1 if spread else dim // tile
    place = jnp.stack([me, me if spread else 0 * me]).astype(jnp.int32)
    payload = 2 * rows + 2 * nf + 16
    block = jax.ShapeDtypeStruct((payload, LANES), bf16)
    *sends, own, query, feat, cum, packed = pl.pallas_call(
        project_kernel,
        out_shape=[block] * (count + 1)
        + [
            jax.ShapeDtypeStruct((rows, nf2), bf16),
            jax.ShapeDtypeStruct((rows, 1), f32),
            jax.ShapeDtypeStruct((pieces, columns, tile), bf16),
        ],
        in_specs=[SMEM] + [ANY] * 6,
        out_specs=[VMEM] * (count + 4),
        scratch_shapes=[
            pltpu.VMEM((rows, dim), bf16),
            pltpu.VMEM((nf2, dim), bf16),
            pltpu.VMEM((dim, 2 * dh), bf16),
            pltpu.VMEM((dim, dh), bf16),
            pltpu.VMEM((1, rows), f32),
            pltpu.VMEM((rows, dh), bf16),
            pltpu.SemaphoreType.DMA((CHUNKS, 4)),
            pltpu.SemaphoreType.DMA((2,)),
        ],
        compiler_params=params,
        cost_estimate=cost(2 * rows * dim * columns, 4 * 1024 * 1024),
        name="project",
    )(place, tokens, feature_weight.T, window_weight, value_weight, log_decay.T, out_grad)
    if spread:
        weights = lax.all_gather(packed[0], CTX + ("tp",)).reshape(count, -1, columns, tile)
    else:
        weights = lax.all_gather(packed, "tp")

    recv = []
    for d in range(1, count):
        recv.append(lax.ppermute(sends[d - 1], CTX, [(i, i ^ d) for i in range(count)]))
    if count > 8:
        recv = [jnp.stack(recv)]

    attended, stat, sheet = pl.pallas_call(
        lambda *refs: query_kernel(count, *refs),
        out_shape=(
            jax.ShapeDtypeStruct((rows, dh), bf16),
            jax.ShapeDtypeStruct((8, rows), f32),
            jax.ShapeDtypeStruct((rows, LANES), f32),
        ),
        in_specs=[SMEM] + [VMEM] * (len(recv) + 4),
        out_specs=[VMEM] * 3,
        scratch_shapes=[
            pltpu.VMEM((count, 2 * rows, dh), bf16),
            pltpu.VMEM((WINDOW // rows + 1, rows, rows), f32),
            pltpu.VMEM((count, rows), f32),
        ],
        compiler_params=params,
        cost_estimate=cost(10**9, 2 * 1024 * 1024, 10**6),
        name="query_side",
    )(place, *recv, own, query, feat, cum)
    stats = lax.all_gather(stat, CTX)
    grads = pl.pallas_call(
        lambda *refs: gradient_kernel(count, *refs),
        out_shape=jax.ShapeDtypeStruct((3 * rows + nf2 * rows // LANES, LANES), bf16),
        in_specs=[SMEM] + [VMEM] * (len(recv) + 5),
        out_specs=VMEM,
        compiler_params=params,
        cost_estimate=cost(10**9, 2 * 1024 * 1024, 10**6),
        name="gradients",
    )(place, *recv, own, query, feat, sheet, stats)
    all_grads = lax.all_gather(grads, "tp")
    return (attended, merge(all_grads, weights, not spread, rows, dim))


def solution(mesh):
    ctx, tp = mesh.devices.shape
    split = Mesh(mesh.devices.reshape(ctx // 2, 2, tp), ("chip", "core", "tp"))
    in_specs = (
        P(CTX, None),
        P(None, "tp"),
        P(None, "tp"),
        P(None, "tp"),
        P(CTX, "tp"),
        P(CTX, "tp"),
    )
    out_specs = (P(CTX, "tp"), P(CTX, None))
    return jax.shard_map(
        per_device, mesh=split, in_specs=in_specs, out_specs=out_specs, check_vma=False
    )
```

```python
import jax
import jax.numpy as jnp
from jax import lax
from jax.experimental import pallas as pl
from jax.experimental.pallas import tpu as pltpu
from jax.sharding import Mesh
from jax.sharding import PartitionSpec as P

WINDOW = 1024
LANES = 128
MASKED = -1e30
CTX = ("chip", "core")
CHUNKS = 4
f32 = jnp.float32
bf16 = jnp.bfloat16


def nn(a, b):
    return lax.dot_general(a, b, (((1,), (0,)), ((), ())), preferred_element_type=f32)


def nt(a, b):
    return lax.dot_general(a, b, (((1,), (1,)), ((), ())), preferred_element_type=f32)


def partner(me, d, count):
    assert count & (count - 1) == 0
    return jnp.bitwise_xor(me, d)


def wide(view, start, count):
    return jnp.concatenate(
        [view[start : start + count, :], view[start + count : start + 2 * count, :]], axis=1
    )


def put_wide(ref, start, value):
    count = value.shape[0]
    for half in range(value.shape[1] // LANES):
        ref[start + half * count : start + (half + 1) * count, :] = value[
            :, half * LANES : (half + 1) * LANES
        ]


def cum_row(view, start):
    tail = view[start : start + 16, :].astype(f32)
    first = tail[0:1] + tail[2:3] + tail[4:5]
    second = tail[1:2] + tail[3:4] + tail[5:6]
    return jnp.concatenate([first, second], axis=1)


def iotas(rows):
    return (
        lax.broadcasted_iota(jnp.int32, (rows, rows), 0),
        lax.broadcasted_iota(jnp.int32, (rows, rows), 1),
    )


def project_kernel(place_ref, tok_hbm, fw_hbm, ww_hbm, vw_hbm, ld_hbm, do_hbm, *rest):
    *sends, keys_ref, query_ref, feat_ref, cum_ref = rest[:-8]
    tok_ref, fw_ref, ww_ref, vw_ref, ld_ref, do_ref, sems, small = rest[-8:]
    me = place_ref[0]
    rows, dim = tok_ref.shape
    dh = do_ref.shape[1]
    nf = fw_ref.shape[0] // 2
    span = dim // CHUNKS
    copies = []
    for c in range(CHUNKS):
        part = pl.ds(c * span, span)
        copies.append([
            pltpu.make_async_copy(tok_hbm.at[:, part], tok_ref.at[:, part], sems.at[c, 0]),
            pltpu.make_async_copy(ww_hbm.at[part, :], ww_ref.at[part, :], sems.at[c, 1]),
            pltpu.make_async_copy(vw_hbm.at[part, :], vw_ref.at[part, :], sems.at[c, 2]),
            pltpu.make_async_copy(fw_hbm.at[:, part], fw_ref.at[:, part], sems.at[c, 3]),
        ])
    others = [
        pltpu.make_async_copy(ld_hbm, ld_ref, small.at[0]),
        pltpu.make_async_copy(do_hbm, do_ref, small.at[1]),
    ]
    for copy in copies[0] + others:
        copy.start()
    for group in copies[1:]:
        for copy in group:
            copy.start()
    for copy in others:
        copy.wait()
    at_row, at_col = iotas(rows)
    ld_r = ld_ref[...]
    ld_c = jnp.sum(jnp.where(at_row == at_col, ld_r, 0.0), axis=1, keepdims=True)
    cum_r = jnp.sum(jnp.where(at_row <= at_col, ld_c, 0.0), axis=0, keepdims=True)
    cum_ref[...] = jnp.sum(jnp.where(at_col <= at_row, ld_r, 0.0), axis=1, keepdims=True)
    high = cum_r.astype(bf16)
    left = cum_r - high.astype(f32)
    mid = left.astype(bf16)
    low = (left - mid.astype(f32)).astype(bf16)
    pieces = [t[:, h : h + LANES].astype(f32) for t in (high, mid, low) for h in range(0, rows, LANES)]
    tail = jnp.concatenate(pieces + [jnp.zeros((10, LANES), f32)], axis=0).astype(bf16)

    feat = jnp.zeros((rows, 2 * nf), f32)
    window = jnp.zeros((rows, 2 * dh), f32)
    values = jnp.zeros((rows, dh), f32)
    for c in range(CHUNKS):
        for copy in copies[c]:
            copy.wait()
        part = slice(c * span, (c + 1) * span)
        tok = tok_ref[:, part]
        feat += nt(tok, fw_ref[:, part])
        window += nn(tok, ww_ref[part, :])
        values += nn(tok, vw_ref[part, :])
    feat = feat.astype(bf16)
    window = window.astype(bf16)
    values = values.astype(bf16)
    feat_ref[...] = feat
    small_row, small_col = iotas(2 * nf)
    feat_t = nt((small_row == small_col).astype(bf16), feat).astype(bf16)
    feat_at = 2 * rows
    tail_at = feat_at + 2 * nf

    def put_keys(ref):
        ref[0:rows, :] = window[:, dh:]
        ref[rows : 2 * rows, :] = values
        put_wide(ref, feat_at, feat_t[nf:, :])
        ref[tail_at : tail_at + 16, :] = tail

    def put_query(ref):
        ref[0:rows, :] = window[:, :dh]
        ref[rows : 2 * rows, :] = do_ref[...]
        put_wide(ref, feat_at, feat_t[:nf, :])
        ref[tail_at : tail_at + 16, :] = tail

    put_keys(keys_ref)
    put_query(query_ref)
    for at, ref in enumerate(sends):
        later = jnp.bitwise_xor(me, max(2 * at, 1)) > me
        pl.when(later)(lambda ref=ref: put_keys(ref))
        pl.when(jnp.logical_not(later))(lambda ref=ref: put_query(ref))


def pack_kernel(place_ref, ww_hbm, vw_hbm, fw_hbm, pack_ref, ww_ref, vw_ref, fw_ref, sems):
    pieces, height, tile = pack_ref.shape
    dh = vw_ref.shape[1]
    used = 3 * dh + fw_ref.shape[0]
    part = pl.ds(pl.multiple_of(place_ref[1] * tile, tile), pieces * tile)
    copies = [
        pltpu.make_async_copy(ww_hbm.at[part, :], ww_ref, sems.at[0]),
        pltpu.make_async_copy(vw_hbm.at[part, :], vw_ref, sems.at[1]),
        pltpu.make_async_copy(fw_hbm.at[:, part], fw_ref, sems.at[2]),
    ]
    for copy in copies:
        copy.start()
    for copy in copies:
        copy.wait()
    for p in range(pieces):
        at = slice(p * tile, (p + 1) * tile)
        pack_ref[p, 0 : 2 * dh, :] = jnp.transpose(ww_ref[at, :].astype(f32)).astype(bf16)
        pack_ref[p, 2 * dh : 3 * dh, :] = jnp.transpose(vw_ref[at, :].astype(f32)).astype(bf16)
        pack_ref[p, 3 * dh : used, :] = fw_ref[:, at]
        if height > used:
            pack_ref[p, used:, :] = jnp.zeros((height - used, tile), bf16)


def others_kernel(place_ref, pack_hbm, out_hbm, sems):
    head = place_ref[3]
    copies = [
        pltpu.make_async_copy(
            pack_hbm.at[jnp.bitwise_xor(head, t + 1), pl.ds(0, out_hbm.shape[1]), :],
            out_hbm.at[t],
            sems.at[t],
        )
        for t in range(out_hbm.shape[0])
    ]
    for copy in copies:
        copy.start()
    for copy in copies:
        copy.wait()


def between(totals, low, high):
    at = lax.broadcasted_iota(jnp.int32, totals.shape, 0)
    return jnp.sum(jnp.where((at > low) & (at < high), totals, 0.0), axis=0, keepdims=True)


def over_partners(count, body, carry):
    if count <= 8:
        for d in range(1, count):
            carry = body(d, carry)
        return carry
    return lax.fori_loop(1, count, body, carry)


def query_kernel(count, place_ref, *rest):
    recvs = rest[: -10]
    (own_ref, query_ref, feat_ref, cum_ref, att_ref, stat_ref, sheet_ref, near_ref, p_ref,
     cums_ref) = rest[-10:]

    def recv(d):
        return recvs[d - 1] if len(recvs) > 1 else recvs[0].at[d - 1]

    me = place_ref[0]
    rows, dh = att_ref.shape
    nf = feat_ref.shape[1] // 2
    back = WINDOW // rows
    feat_at = 2 * rows
    tail_at = feat_at + 2 * nf
    scale = dh ** (-0.5)
    feat_scale = nf ** (-0.5)
    wq = query_ref[0:rows, :]
    do = query_ref[rows : 2 * rows, :]
    q = feat_ref[:, :nf]
    at_row, at_col = iotas(rows)
    own_cum = cum_row(own_ref, tail_at)
    cums_ref[pl.ds(me, 1), :] = own_cum
    near_ref[me] = own_ref[0 : 2 * rows, :]

    def gather(d, carry):
        j = partner(me, d, count)
        view = recv(d)
        near_ref[j] = view[0 : 2 * rows, :]
        cums_ref[pl.ds(j, 1), :] = cum_row(view, tail_at)
        return carry

    over_partners(count, gather, 0)

    def near(w):
        return near_ref.at[jnp.maximum(me - back + w, 0)]

    top = jnp.full((rows, LANES), MASKED, f32)
    for w in range(back + 1):
        keys = own_ref[0:rows, :] if w == back else near(w)[0:rows, :]
        s = nt(wq, keys) * scale
        if w == back:
            s = jnp.where(at_col <= at_row, s, MASKED)
        elif w == 0:
            s = jnp.where((at_col > at_row) & (me >= back), s, MASKED)
        else:
            s = jnp.where(me >= back - w, s, MASKED)
        p_ref[w] = s
        for h in range(0, rows, LANES):
            top = jnp.maximum(top, s[:, h : h + LANES])
    top = jnp.max(top, axis=1, keepdims=True)
    total = jnp.zeros((rows, LANES), f32)
    out = jnp.zeros((rows, dh), f32)
    for w in range(back + 1):
        p = jnp.exp(p_ref[w] - top)
        for h in range(0, rows, LANES):
            total += p[:, h : h + LANES]
        vals = own_ref[rows : 2 * rows, :] if w == back else near(w)[rows : 2 * rows, :]
        out += nn(p.astype(bf16), vals)
    total = jnp.sum(total, axis=1, keepdims=True)
    windowed = out * (1.0 / total)

    cum_c = cum_ref[...]
    growth = jnp.exp(cum_c)
    totals = cums_ref[:, rows - 1 : rows]

    def forward(d, carry):
        num, den = carry
        j = partner(me, d, count)
        view = recv(d)
        gap = between(totals, j - 1, me)
        es = jnp.where(j < me, jnp.exp(jnp.minimum(gap - cums_ref[pl.ds(j, 1), :], 0.0)), 0.0)
        x = nn(q, wide(view, feat_at, nf)) * feat_scale
        weight = (1.0 + x + 0.5 * x * x) * es
        for h in range(0, rows, LANES):
            den += weight[:, h : h + LANES]
        num += nn(weight.astype(bf16), view[rows : 2 * rows, :])
        return num, den

    num, den = over_partners(
        count, forward, (jnp.zeros((rows, dh), f32), jnp.zeros((rows, LANES), f32))
    )
    x = nn(q, wide(own_ref, feat_at, nf)) * feat_scale
    e = jnp.where(at_col <= at_row, jnp.exp(jnp.minimum(cum_c - own_cum, 0.0)), 0.0)
    weight = (1.0 + x + 0.5 * x * x) * e
    num = num * growth + nn(weight.astype(bf16), own_ref[rows : 2 * rows, :])
    den = den * growth
    for h in range(0, rows, LANES):
        den += weight[:, h : h + LANES]
    rden = 1.0 / jnp.sum(den, axis=1, keepdims=True)
    linear = num * rden
    att_ref[...] = (linear + windowed).astype(bf16)
    do_f = do.astype(f32)
    delta_w = jnp.sum(do_f * windowed, axis=1, keepdims=True)
    delta_l = jnp.sum(do_f * linear, axis=1, keepdims=True)
    lse = top + jnp.log(total)
    lane = lax.broadcasted_iota(jnp.int32, (rows, LANES), 1)
    sheet = jnp.where(lane == 0, lse, 0.0)
    sheet = jnp.where(lane == 1, delta_w, sheet)
    sheet = jnp.where(lane == 2, rden, sheet)
    sheet = jnp.where(lane == 3, delta_l, sheet)
    sheet = jnp.where(lane == 4, cum_c, sheet)
    sheet_ref[...] = sheet
    stat_ref[...] = jnp.transpose(sheet)[0:8, :]


def gradient_kernel(count, place_ref, *rest):
    recvs = rest[:-6]
    own_ref, query_ref, feat_ref, sheet_ref, stat_ref, grad_ref = rest[-6:]

    def recv(d):
        return recvs[d - 1] if len(recvs) > 1 else recvs[0].at[d - 1]

    me = place_ref[0]
    rows = feat_ref.shape[0]
    dh = LANES
    nf = feat_ref.shape[1] // 2
    feat_at = 2 * rows
    scale = dh ** (-0.5)
    feat_scale = nf ** (-0.5)
    at_row, at_col = iotas(rows)
    apart = at_row - at_col
    wq, wk = query_ref[0:rows, :], own_ref[0:rows, :]
    do, v = query_ref[rows : 2 * rows, :], own_ref[rows : 2 * rows, :]
    q, k = feat_ref[:, :nf], feat_ref[:, nf:]
    lse_c, dw_c = sheet_ref[:, 0:1], sheet_ref[:, 1:2]
    rden_c, dl_c, cum_c = sheet_ref[:, 2:3], sheet_ref[:, 3:4], sheet_ref[:, 4:5]
    totals = jnp.concatenate([stat_ref[j, 4:5, rows - 1 : rows] for j in range(count)], axis=0)
    own_cum = stat_ref[me, 4:5, :]
    growth_c = jnp.exp(cum_c) * rden_c
    tail_c = jnp.exp(own_cum[:, rows - 1 : rows] - cum_c)

    def pick(flag, a, b):
        return jnp.where(flag, a, b)

    s = nt(wq, wk) * scale
    causal = at_col <= at_row
    p = jnp.where(causal, jnp.exp(s - lse_c), 0.0)
    dp = nt(do, v)
    dwq = nn((p * (dp - dw_c)).astype(bf16), wk)
    x = nn(q, wide(own_ref, feat_at, nf)) * feat_scale
    e = jnp.where(causal, jnp.exp(jnp.minimum(cum_c - own_cum, 0.0)), 0.0) * rden_c
    dx = (dp - dl_c) * e * (1.0 + x)
    dqt = nt(wide(own_ref, feat_at, nf), dx.astype(bf16))

    s = nt(wk, wq) * scale
    causal = at_row <= at_col
    p = jnp.where(causal, jnp.exp(s - stat_ref[me, 0:1, :]), 0.0)
    dp = nt(v, do)
    dwk = nn((p * (dp - stat_ref[me, 1:2, :])).astype(bf16), wq)
    x = nn(k, wide(query_ref, feat_at, nf)) * feat_scale
    e = jnp.where(causal, jnp.exp(jnp.minimum(own_cum - cum_c, 0.0)), 0.0) * stat_ref[me, 2:3, :]
    dx = (dp - stat_ref[me, 3:4, :]) * e * (1.0 + x)
    dkt = nt(wide(query_ref, feat_at, nf), dx.astype(bf16))
    dv = nn((p + (1.0 + x + 0.5 * x * x) * e).astype(bf16), do)

    def step(d, carry):
        dwq, dqt, dwk, dkt, dv = carry
        j = partner(me, d, count)
        view = recv(d)
        mine = j < me
        sign = pick(mine, 1, -1)
        limit = WINDOW - jnp.abs(me - j) * rows
        rows_w = pick(mine, wq, wk)
        rows_v = pick(mine, do, v)
        rows_f = pick(mine, q, k)
        other_w = view[0:rows, :]
        other_v = view[rows : 2 * rows, :]
        other_f = wide(view, feat_at, nf)
        st = stat_ref[j]
        zero = jnp.zeros((1, rows), f32)
        cum = st[4:5, :]
        gap = between(totals, jnp.minimum(me, j), jnp.maximum(me, j))
        e_r = jnp.exp(jnp.minimum(gap + pick(mine, cum[:, rows - 1 : rows] - cum, cum), 0.0))
        e_r = e_r * pick(mine, 1.0, st[2:3, :])
        e_c = pick(mine, growth_c, tail_c)

        s = nt(rows_w, other_w) * scale
        p = jnp.exp(s - pick(mine, lse_c, 0.0) - pick(mine, zero, st[0:1, :]))
        p = jnp.where(apart * sign < limit, p, 0.0)
        dp = nt(rows_v, other_v)
        ds = p * (dp - pick(mine, dw_c, 0.0) - pick(mine, zero, st[1:2, :]))
        more_w = nn(ds.astype(bf16), other_w)
        x = nn(rows_f, other_f) * feat_scale
        e = e_r * e_c
        dx = (dp - pick(mine, dl_c, 0.0) - pick(mine, zero, st[3:4, :])) * e * (1.0 + x)
        more_f = nt(other_f, dx.astype(bf16))
        more_v = nn((p + (1.0 + x + 0.5 * x * x) * e).astype(bf16), other_v)
        dwq = dwq + pick(mine, more_w, 0.0)
        dwk = dwk + pick(mine, 0.0, more_w)
        dqt = dqt + pick(mine, more_f, 0.0)
        dkt = dkt + pick(mine, 0.0, more_f)
        dv = dv + pick(mine, 0.0, more_v)
        return dwq, dqt, dwk, dkt, dv

    dwq, dqt, dwk, dkt, dv = over_partners(count, step, (dwq, dqt, dwk, dkt, dv))
    grad_ref[0:rows, :] = (dwq * scale).astype(bf16)
    grad_ref[rows : 2 * rows, :] = (dwk * scale).astype(bf16)
    grad_ref[2 * rows : 3 * rows, :] = dv.astype(bf16)
    dft = (jnp.concatenate([dqt, dkt], axis=0) * feat_scale).astype(bf16)
    put_wide(grad_ref, 3 * rows, dft)


def gather_rows(grad_ref, order, cat_ref, feat_ref):
    rows = cat_ref.shape[0]
    nf2 = feat_ref.shape[1] // len(order)
    for at, h in enumerate(order):
        for part in range(3):
            lane = (3 * at + part) * LANES
            cat_ref[:, lane : lane + LANES] = grad_ref[h, part * rows : (part + 1) * rows, :]
    dft = jnp.concatenate([wide(grad_ref.at[h], 3 * rows, nf2) for h in order], axis=0)
    feat_ref[...] = jnp.transpose(dft.astype(f32)).astype(bf16)


def merge_kernel(grad_ref, weight_ref, out_ref, cat_ref, feat_ref):
    heads, pieces = weight_ref.shape[:2]
    tile = weight_ref.shape[3]
    lanes = 3 * LANES

    @pl.when(pl.program_id(0) == 0)
    def _():
        gather_rows(grad_ref, range(heads), cat_ref, feat_ref)

    for p in range(pieces):
        main = jnp.concatenate([weight_ref[h, p, 0:lanes, :] for h in range(heads)], axis=0)
        feats = jnp.concatenate([weight_ref[h, p, lanes:, :] for h in range(heads)], axis=0)
        total = nn(cat_ref[...], main) + nn(feat_ref[...], feats)
        out_ref[:, p * tile : (p + 1) * tile] = total.astype(bf16)


def half_kernel(place_ref, grad_ref, weight_ref, ww_ref, vw_ref, fw_ref, *rest):
    out_ref, cat_ref, feat_ref = rest[-3:]
    head = place_ref[3]
    pieces, heads, _, tile = weight_ref.shape
    lanes = 3 * LANES

    @pl.when(pl.program_id(0) == 0)
    def _():
        order = [head] + [jnp.bitwise_xor(head, t + 1) for t in range(heads)]
        gather_rows(grad_ref, order, cat_ref, feat_ref)

    nf2 = fw_ref.shape[0]
    for p in range(pieces):
        at = slice(p * tile, (p + 1) * tile)
        main = jnp.concatenate([weight_ref[p, t, 0:lanes, :] for t in range(heads)], axis=0)
        feats = jnp.concatenate(
            [fw_ref[:, at]] + [weight_ref[p, t, lanes:, :] for t in range(heads)], axis=0
        )
        total = nn(cat_ref[:, lanes:], main) + nn(feat_ref[...], feats)
        total += nt(cat_ref[:, 0 : 2 * LANES], ww_ref[at, :])
        total += nt(cat_ref[:, 2 * LANES : lanes], vw_ref[at, :])
        out_ref[:, at] = total.astype(bf16)


VMEM = pl.BlockSpec(memory_space=pltpu.VMEM)
SMEM = pl.BlockSpec(memory_space=pltpu.SMEM)
ANY = pl.BlockSpec(memory_space=pl.ANY)
params = pltpu.CompilerParams(vmem_limit_bytes=48 * 1024 * 1024)
full = pltpu.CompilerParams(vmem_limit_bytes=60 * 1024 * 1024)


def cost(flops, nbytes, exps=0):
    return pl.CostEstimate(flops=flops, bytes_accessed=nbytes, transcendentals=exps)


def merge(grads, weights, rows, dim):
    heads, pieces, columns, tile = weights.shape
    return pl.pallas_call(
        merge_kernel,
        out_shape=jax.ShapeDtypeStruct((rows, dim), bf16),
        grid=(pieces,),
        in_specs=[
            pl.BlockSpec(grads.shape, lambda i: (0, 0, 0)),
            pl.BlockSpec((heads, 1, columns, tile), lambda i: (0, i, 0, 0)),
        ],
        out_specs=pl.BlockSpec((rows, tile), lambda i: (0, i)),
        scratch_shapes=[
            pltpu.VMEM((rows, 3 * LANES * heads), bf16),
            pltpu.VMEM((rows, (columns - 3 * LANES) * heads), bf16),
        ],
        compiler_params=params,
        cost_estimate=cost(2 * rows * dim * heads * columns, heads * dim * columns * 2),
        name="head_sum",
    )(grads, weights)


def merge_half(place, grads, weights, ww, vw, fw_t, own_half, before):
    pieces, others, columns, tile = weights.shape
    heads = others + 1
    dim = ww.shape[0]
    rows = grads.shape[1] * LANES // (3 * LANES + fw_t.shape[0])
    group = 2
    steps = pieces // group
    span = group * tile

    def at(i, place):
        core = place[2]
        return (core if own_half else 1 - core) * steps + i

    in_specs = [
        pl.BlockSpec(grads.shape, lambda i, place: (0, 0, 0)),
        pl.BlockSpec((group, others, columns, tile), lambda i, place: (i, 0, 0, 0)),
        pl.BlockSpec((span, ww.shape[1]), lambda i, place: (at(i, place), 0)),
        pl.BlockSpec((span, vw.shape[1]), lambda i, place: (at(i, place), 0)),
        pl.BlockSpec((fw_t.shape[0], span), lambda i, place: (0, at(i, place))),
    ]
    args = [place, grads, weights, ww, vw, fw_t]
    aliases = {}
    if before is not None:
        in_specs.append(ANY)
        aliases = {len(args): 0}
        args.append(before)
    return pl.pallas_call(
        half_kernel,
        out_shape=jax.ShapeDtypeStruct((rows, dim), bf16),
        grid_spec=pltpu.PrefetchScalarGridSpec(
            num_scalar_prefetch=1,
            grid=(steps,),
            in_specs=in_specs,
            out_specs=pl.BlockSpec((rows, span), lambda i, place: (0, at(i, place))),
            scratch_shapes=[
                pltpu.VMEM((rows, 3 * LANES * heads), bf16),
                pltpu.VMEM((rows, (columns - 3 * LANES) * heads), bf16),
            ],
        ),
        input_output_aliases=aliases,
        compiler_params=full,
        cost_estimate=cost(rows * dim * heads * columns, heads * dim * columns),
        name="half_sum",
    )(*args)


def per_device(tokens, feature_weight, window_weight, value_weight, log_decay, out_grad):
    rows, dim = tokens.shape
    nf2 = feature_weight.shape[1]
    nf = nf2 // 2
    dh = value_weight.shape[1]
    columns = 3 * dh + nf2
    chips, count = lax.axis_size("chip"), lax.axis_size(CTX)
    heads = lax.axis_size("tp")
    chip, core = lax.axis_index("chip"), lax.axis_index("core")
    me = lax.axis_index(CTX)
    tile = 2 * LANES
    spread = count * tile == dim and heads == 4
    pieces, height = (1, 4 * LANES) if spread else (dim // tile, columns)
    piece = core * chips + chip if spread else 0 * me
    place = jnp.stack([me, piece, core, lax.axis_index("tp")]).astype(jnp.int32)
    fw_t = feature_weight.T
    packed = pl.pallas_call(
        pack_kernel,
        out_shape=jax.ShapeDtypeStruct((pieces, height, tile), bf16),
        in_specs=[SMEM] + [ANY] * 3,
        out_specs=VMEM,
        scratch_shapes=[
            pltpu.VMEM((pieces * tile, 2 * dh), bf16),
            pltpu.VMEM((pieces * tile, dh), bf16),
            pltpu.VMEM((nf2, pieces * tile), bf16),
            pltpu.SemaphoreType.DMA((3,)),
        ],
        compiler_params=full,
        cost_estimate=cost(1, 2 * columns * tile * pieces * 2),
        name="pack",
    )(place, window_weight, value_weight, fw_t)
    weights = lax.all_gather(packed[0] if spread else packed, "tp")

    payload = 2 * rows + 2 * nf + 16
    block = jax.ShapeDtypeStruct((payload, LANES), bf16)
    *sends, own, query, feat, cum = pl.pallas_call(
        project_kernel,
        out_shape=[block] * (chips + 2)
        + [
            jax.ShapeDtypeStruct((rows, nf2), bf16),
            jax.ShapeDtypeStruct((rows, 1), f32),
        ],
        in_specs=[SMEM] + [ANY] * 6,
        out_specs=[VMEM] * (chips + 4),
        scratch_shapes=[
            pltpu.VMEM((rows, dim), bf16),
            pltpu.VMEM((nf2, dim), bf16),
            pltpu.VMEM((dim, 2 * dh), bf16),
            pltpu.VMEM((dim, dh), bf16),
            pltpu.VMEM((1, rows), f32),
            pltpu.VMEM((rows, dh), bf16),
            pltpu.SemaphoreType.DMA((CHUNKS, 4)),
            pltpu.SemaphoreType.DMA((2,)),
        ],
        compiler_params=full,
        cost_estimate=cost(2 * rows * dim * columns, 4 * 1024 * 1024),
        name="project",
    )(place, tokens, fw_t, window_weight, value_weight, log_decay.T, out_grad)

    swap = [(0, 1), (1, 0)]
    recv = {1: None}
    for d in range(1, chips):
        recv[2 * d] = lax.ppermute(sends[d], "chip", [(i, i ^ d) for i in range(chips)])
    recv[1] = lax.ppermute(sends[0], "core", swap)
    for d in range(1, chips):
        recv[2 * d + 1] = lax.ppermute(recv[2 * d], "core", swap)
    recv = [recv[d] for d in range(1, count)]
    if count > 8:
        recv = [jnp.stack(recv)]

    attended, stat, sheet = pl.pallas_call(
        lambda *refs: query_kernel(count, *refs),
        out_shape=(
            jax.ShapeDtypeStruct((rows, dh), bf16),
            jax.ShapeDtypeStruct((8, rows), f32),
            jax.ShapeDtypeStruct((rows, LANES), f32),
        ),
        in_specs=[SMEM] + [VMEM] * (len(recv) + 4),
        out_specs=[VMEM] * 3,
        scratch_shapes=[
            pltpu.VMEM((count, 2 * rows, dh), bf16),
            pltpu.VMEM((WINDOW // rows + 1, rows, rows), f32),
            pltpu.VMEM((count, rows), f32),
        ],
        compiler_params=params,
        cost_estimate=cost(10**9, 2 * 1024 * 1024, 10**6),
        name="query_side",
    )(place, *recv, own, query, feat, cum)
    if spread:
        weights, _ = lax.optimization_barrier((weights, stat))
        others = pl.pallas_call(
            others_kernel,
            out_shape=jax.ShapeDtypeStruct((heads - 1, columns, tile), bf16),
            in_specs=[SMEM, ANY],
            out_specs=ANY,
            scratch_shapes=[pltpu.SemaphoreType.DMA((heads - 1,))],
            compiler_params=full,
            cost_estimate=cost(1, heads * columns * tile * 4),
            name="others",
        )(place, weights)
        others, stat = lax.optimization_barrier((others, stat))
        weights = lax.all_gather(others, "chip")
    stats = lax.all_gather(stat, CTX)
    grads = pl.pallas_call(
        lambda *refs: gradient_kernel(count, *refs),
        out_shape=jax.ShapeDtypeStruct((3 * rows + nf2 * rows // LANES, LANES), bf16),
        in_specs=[SMEM] + [VMEM] * (len(recv) + 5),
        out_specs=VMEM,
        compiler_params=params,
        cost_estimate=cost(10**9, 2 * 1024 * 1024, 10**6),
        name="gradients",
    )(place, *recv, own, query, feat, sheet, stats)
    grads = lax.all_gather(grads, "tp")
    if not spread:
        return (attended, merge(grads, weights, rows, dim))
    weights, grads = lax.optimization_barrier((weights, grads))
    swapped = lax.ppermute(weights, "core", swap)
    total = merge_half(place, grads, weights, window_weight, value_weight, fw_t, True, None)
    total = merge_half(place, grads, swapped, window_weight, value_weight, fw_t, False, total)
    return (attended, total)


def solution(mesh):
    ctx, tp = mesh.devices.shape
    split = Mesh(mesh.devices.reshape(ctx // 2, 2, tp), ("chip", "core", "tp"))
    in_specs = (
        P(CTX, None),
        P(None, "tp"),
        P(None, "tp"),
        P(None, "tp"),
        P(CTX, "tp"),
        P(CTX, "tp"),
    )
    out_specs = (P(CTX, "tp"), P(CTX, None))
    return jax.shard_map(
        per_device, mesh=split, in_specs=in_specs, out_specs=out_specs, check_vma=False
    )
```

```python
import jax
import jax.numpy as jnp
from jax import lax
from jax.experimental import pallas as pl
from jax.experimental.pallas import tpu as pltpu
from jax.sharding import Mesh
from jax.sharding import PartitionSpec as P

WINDOW = 1024
LANES = 128
MASKED = -1e30
CTX = ("chip", "core")
CHUNKS = 4
f32 = jnp.float32
bf16 = jnp.bfloat16


def nn(a, b):
    return lax.dot_general(a, b, (((1,), (0,)), ((), ())), preferred_element_type=f32)


def nt(a, b):
    return lax.dot_general(a, b, (((1,), (1,)), ((), ())), preferred_element_type=f32)


def partner(me, d, count):
    assert count & (count - 1) == 0
    return jnp.bitwise_xor(me, d)


def wide(view, start, count):
    return jnp.concatenate(
        [view[start : start + count, :], view[start + count : start + 2 * count, :]], axis=1
    )


def put_wide(ref, start, value):
    count = value.shape[0]
    for half in range(value.shape[1] // LANES):
        ref[start + half * count : start + (half + 1) * count, :] = value[
            :, half * LANES : (half + 1) * LANES
        ]


def cum_row(view, start):
    tail = view[start : start + 16, :].astype(f32)
    first = tail[0:1] + tail[2:3] + tail[4:5]
    second = tail[1:2] + tail[3:4] + tail[5:6]
    return jnp.concatenate([first, second], axis=1)


def iotas(rows):
    return (
        lax.broadcasted_iota(jnp.int32, (rows, rows), 0),
        lax.broadcasted_iota(jnp.int32, (rows, rows), 1),
    )


def project_kernel(place_ref, tok_hbm, fw_hbm, ww_hbm, vw_hbm, ld_hbm, do_hbm, *rest):
    *sends, keys_ref, query_ref, feat_ref, cum_ref = rest[:-8]
    tok_ref, fw_ref, ww_ref, vw_ref, ld_ref, do_ref, sems, small = rest[-8:]
    me = place_ref[0]
    rows, dim = tok_ref.shape
    dh = do_ref.shape[1]
    nf = fw_ref.shape[0] // 2
    span = dim // CHUNKS
    copies = []
    for c in range(CHUNKS):
        part = pl.ds(c * span, span)
        copies.append([
            pltpu.make_async_copy(tok_hbm.at[:, part], tok_ref.at[:, part], sems.at[c, 0]),
            pltpu.make_async_copy(ww_hbm.at[part, :], ww_ref.at[part, :], sems.at[c, 1]),
            pltpu.make_async_copy(vw_hbm.at[part, :], vw_ref.at[part, :], sems.at[c, 2]),
            pltpu.make_async_copy(fw_hbm.at[:, part], fw_ref.at[:, part], sems.at[c, 3]),
        ])
    others = [
        pltpu.make_async_copy(ld_hbm, ld_ref, small.at[0]),
        pltpu.make_async_copy(do_hbm, do_ref, small.at[1]),
    ]
    for copy in copies[0] + others:
        copy.start()
    for group in copies[1:]:
        for copy in group:
            copy.start()
    for copy in others:
        copy.wait()
    at_row, at_col = iotas(rows)
    ld_r = ld_ref[...]
    ld_c = jnp.sum(jnp.where(at_row == at_col, ld_r, 0.0), axis=1, keepdims=True)
    cum_r = jnp.sum(jnp.where(at_row <= at_col, ld_c, 0.0), axis=0, keepdims=True)
    cum_ref[...] = jnp.sum(jnp.where(at_col <= at_row, ld_r, 0.0), axis=1, keepdims=True)
    high = cum_r.astype(bf16)
    left = cum_r - high.astype(f32)
    mid = left.astype(bf16)
    low = (left - mid.astype(f32)).astype(bf16)
    pieces = [t[:, h : h + LANES].astype(f32) for t in (high, mid, low) for h in range(0, rows, LANES)]
    tail = jnp.concatenate(pieces + [jnp.zeros((10, LANES), f32)], axis=0).astype(bf16)

    feat = jnp.zeros((rows, 2 * nf), f32)
    main = jnp.zeros((rows, 3 * dh), f32)
    for c in range(CHUNKS):
        for copy in copies[c]:
            copy.wait()
        part = slice(c * span, (c + 1) * span)
        tok = tok_ref[:, part]
        feat += nt(tok, fw_ref[:, part])
        main += nn(tok, jnp.concatenate([ww_ref[part, :], vw_ref[part, :]], axis=1))
    feat = feat.astype(bf16)
    window = main[:, : 2 * dh].astype(bf16)
    values = main[:, 2 * dh :].astype(bf16)
    feat_ref[...] = feat
    small_row, small_col = iotas(2 * nf)
    feat_t = nt((small_row == small_col).astype(bf16), feat).astype(bf16)
    feat_at = 2 * rows
    tail_at = feat_at + 2 * nf

    def put_keys(ref):
        ref[0:rows, :] = window[:, dh:]
        ref[rows : 2 * rows, :] = values
        put_wide(ref, feat_at, feat_t[nf:, :])
        ref[tail_at : tail_at + 16, :] = tail

    def put_query(ref):
        ref[0:rows, :] = window[:, :dh]
        ref[rows : 2 * rows, :] = do_ref[...]
        put_wide(ref, feat_at, feat_t[:nf, :])
        ref[tail_at : tail_at + 16, :] = tail

    put_keys(keys_ref)
    put_query(query_ref)
    for at, ref in enumerate(sends):
        later = jnp.bitwise_xor(me, max(2 * at, 1)) > me
        pl.when(later)(lambda ref=ref: put_keys(ref))
        pl.when(jnp.logical_not(later))(lambda ref=ref: put_query(ref))


def pack_kernel(place_ref, ww_hbm, vw_hbm, fw_hbm, pack_ref, ww_ref, vw_ref, fw_ref, sems):
    pieces, _, tile = pack_ref.shape
    dh = vw_ref.shape[1]
    used = 3 * dh + fw_ref.shape[0]
    part = pl.ds(pl.multiple_of(place_ref[1] * tile, tile), pieces * tile)
    copies = [
        pltpu.make_async_copy(ww_hbm.at[part, :], ww_ref, sems.at[0]),
        pltpu.make_async_copy(vw_hbm.at[part, :], vw_ref, sems.at[1]),
        pltpu.make_async_copy(fw_hbm.at[:, part], fw_ref, sems.at[2]),
    ]
    for copy in copies:
        copy.start()
    for copy in copies:
        copy.wait()
    for p in range(pieces):
        at = slice(p * tile, (p + 1) * tile)
        pack_ref[p, 0 : 2 * dh, :] = jnp.transpose(ww_ref[at, :].astype(f32)).astype(bf16)
        pack_ref[p, 2 * dh : 3 * dh, :] = jnp.transpose(vw_ref[at, :].astype(f32)).astype(bf16)
        pack_ref[p, 3 * dh : used, :] = fw_ref[:, at]


def between(totals, low, high):
    at = lax.broadcasted_iota(jnp.int32, totals.shape, 0)
    return jnp.sum(jnp.where((at > low) & (at < high), totals, 0.0), axis=0, keepdims=True)


def over_partners(count, body, carry):
    if count <= 8:
        for d in range(1, count):
            carry = body(d, carry)
        return carry
    return lax.fori_loop(1, count, body, carry)


def query_kernel(count, place_ref, *rest):
    recvs = rest[: -10]
    (own_ref, query_ref, feat_ref, cum_ref, att_ref, stat_ref, sheet_ref, near_ref, p_ref,
     cums_ref) = rest[-10:]

    def recv(d):
        return recvs[d - 1] if len(recvs) > 1 else recvs[0].at[d - 1]

    me = place_ref[0]
    rows, dh = att_ref.shape
    nf = feat_ref.shape[1] // 2
    back = WINDOW // rows
    feat_at = 2 * rows
    tail_at = feat_at + 2 * nf
    scale = dh ** (-0.5)
    feat_scale = nf ** (-0.5)
    wq = query_ref[0:rows, :]
    do = query_ref[rows : 2 * rows, :]
    q = feat_ref[:, :nf]
    at_row, at_col = iotas(rows)
    own_cum = cum_row(own_ref, tail_at)
    cums_ref[pl.ds(me, 1), :] = own_cum
    near_ref[me] = own_ref[0 : 2 * rows, :]

    def gather(d, carry):
        j = partner(me, d, count)
        view = recv(d)
        near_ref[j] = view[0 : 2 * rows, :]
        cums_ref[pl.ds(j, 1), :] = cum_row(view, tail_at)
        return carry

    over_partners(count, gather, 0)

    def near(w):
        return near_ref.at[jnp.maximum(me - back + w, 0)]

    top = jnp.full((rows, LANES), MASKED, f32)
    for w in range(back + 1):
        keys = own_ref[0:rows, :] if w == back else near(w)[0:rows, :]
        s = nt(wq, keys) * scale
        if w == back:
            s = jnp.where(at_col <= at_row, s, MASKED)
        elif w == 0:
            s = jnp.where((at_col > at_row) & (me >= back), s, MASKED)
        else:
            s = jnp.where(me >= back - w, s, MASKED)
        p_ref[w] = s
        for h in range(0, rows, LANES):
            top = jnp.maximum(top, s[:, h : h + LANES])
    top = jnp.max(top, axis=1, keepdims=True)
    total = jnp.zeros((rows, LANES), f32)
    out = jnp.zeros((rows, dh), f32)
    for w in range(back + 1):
        p = jnp.exp(p_ref[w] - top)
        for h in range(0, rows, LANES):
            total += p[:, h : h + LANES]
        vals = own_ref[rows : 2 * rows, :] if w == back else near(w)[rows : 2 * rows, :]
        out += nn(p.astype(bf16), vals)
    total = jnp.sum(total, axis=1, keepdims=True)
    windowed = out * (1.0 / total)

    cum_c = cum_ref[...]
    growth = jnp.exp(cum_c)
    totals = cums_ref[:, rows - 1 : rows]

    def forward(d, carry):
        num, den = carry
        j = partner(me, d, count)
        view = recv(d)
        gap = between(totals, j - 1, me)
        es = jnp.where(j < me, jnp.exp(jnp.minimum(gap - cums_ref[pl.ds(j, 1), :], 0.0)), 0.0)
        x = nn(q, wide(view, feat_at, nf)) * feat_scale
        weight = (1.0 + x + 0.5 * x * x) * es
        for h in range(0, rows, LANES):
            den += weight[:, h : h + LANES]
        num += nn(weight.astype(bf16), view[rows : 2 * rows, :])
        return num, den

    num, den = over_partners(
        count, forward, (jnp.zeros((rows, dh), f32), jnp.zeros((rows, LANES), f32))
    )
    x = nn(q, wide(own_ref, feat_at, nf)) * feat_scale
    e = jnp.where(at_col <= at_row, jnp.exp(jnp.minimum(cum_c - own_cum, 0.0)), 0.0)
    weight = (1.0 + x + 0.5 * x * x) * e
    num = num * growth + nn(weight.astype(bf16), own_ref[rows : 2 * rows, :])
    den = den * growth
    for h in range(0, rows, LANES):
        den += weight[:, h : h + LANES]
    rden = 1.0 / jnp.sum(den, axis=1, keepdims=True)
    linear = num * rden
    att_ref[...] = (linear + windowed).astype(bf16)
    do_f = do.astype(f32)
    delta_w = jnp.sum(do_f * windowed, axis=1, keepdims=True)
    delta_l = jnp.sum(do_f * linear, axis=1, keepdims=True)
    lse = top + jnp.log(total)
    lane = lax.broadcasted_iota(jnp.int32, (rows, LANES), 1)
    sheet = jnp.where(lane == 0, lse, 0.0)
    sheet = jnp.where(lane == 1, delta_w, sheet)
    sheet = jnp.where(lane == 2, rden, sheet)
    sheet = jnp.where(lane == 3, delta_l, sheet)
    sheet = jnp.where(lane == 4, cum_c, sheet)
    sheet_ref[...] = sheet
    stat_ref[...] = jnp.transpose(sheet)[0:8, :]


def gradient_kernel(count, place_ref, *rest):
    recvs = rest[:-6]
    own_ref, query_ref, feat_ref, sheet_ref, stat_ref, grad_ref = rest[-6:]

    def recv(d):
        return recvs[d - 1] if len(recvs) > 1 else recvs[0].at[d - 1]

    me = place_ref[0]
    rows = feat_ref.shape[0]
    dh = LANES
    nf = feat_ref.shape[1] // 2
    feat_at = 2 * rows
    scale = dh ** (-0.5)
    feat_scale = nf ** (-0.5)
    at_row, at_col = iotas(rows)
    apart = at_row - at_col
    wq, wk = query_ref[0:rows, :], own_ref[0:rows, :]
    do, v = query_ref[rows : 2 * rows, :], own_ref[rows : 2 * rows, :]
    q, k = feat_ref[:, :nf], feat_ref[:, nf:]
    lse_c, dw_c = sheet_ref[:, 0:1], sheet_ref[:, 1:2]
    rden_c, dl_c, cum_c = sheet_ref[:, 2:3], sheet_ref[:, 3:4], sheet_ref[:, 4:5]
    totals = jnp.concatenate([stat_ref[j, 4:5, rows - 1 : rows] for j in range(count)], axis=0)
    own_cum = stat_ref[me, 4:5, :]
    growth_c = jnp.exp(cum_c) * rden_c
    tail_c = jnp.exp(own_cum[:, rows - 1 : rows] - cum_c)

    def pick(flag, a, b):
        return jnp.where(flag, a, b)

    s = nt(wq, wk) * scale
    causal = at_col <= at_row
    p = jnp.where(causal, jnp.exp(s - lse_c), 0.0)
    dp = nt(do, v)
    dwq = nn((p * (dp - dw_c)).astype(bf16), wk)
    x = nn(q, wide(own_ref, feat_at, nf)) * feat_scale
    e = jnp.where(causal, jnp.exp(jnp.minimum(cum_c - own_cum, 0.0)), 0.0) * rden_c
    dx = (dp - dl_c) * e * (1.0 + x)
    dqt = nt(wide(own_ref, feat_at, nf), dx.astype(bf16))

    s = nt(wk, wq) * scale
    causal = at_row <= at_col
    p = jnp.where(causal, jnp.exp(s - stat_ref[me, 0:1, :]), 0.0)
    dp = nt(v, do)
    dwk = nn((p * (dp - stat_ref[me, 1:2, :])).astype(bf16), wq)
    x = nn(k, wide(query_ref, feat_at, nf)) * feat_scale
    e = jnp.where(causal, jnp.exp(jnp.minimum(own_cum - cum_c, 0.0)), 0.0) * stat_ref[me, 2:3, :]
    dx = (dp - stat_ref[me, 3:4, :]) * e * (1.0 + x)
    dkt = nt(wide(query_ref, feat_at, nf), dx.astype(bf16))
    dv = nn((p + (1.0 + x + 0.5 * x * x) * e).astype(bf16), do)

    def step(d, carry):
        dwq, dqt, dwk, dkt, dv = carry
        j = partner(me, d, count)
        view = recv(d)
        mine = j < me
        sign = pick(mine, 1, -1)
        limit = WINDOW - jnp.abs(me - j) * rows
        rows_w = pick(mine, wq, wk)
        rows_v = pick(mine, do, v)
        rows_f = pick(mine, q, k)
        other_w = view[0:rows, :]
        other_v = view[rows : 2 * rows, :]
        other_f = wide(view, feat_at, nf)
        st = stat_ref[j]
        zero = jnp.zeros((1, rows), f32)
        cum = st[4:5, :]
        gap = between(totals, jnp.minimum(me, j), jnp.maximum(me, j))
        e_r = jnp.exp(jnp.minimum(gap + pick(mine, cum[:, rows - 1 : rows] - cum, cum), 0.0))
        e_r = e_r * pick(mine, 1.0, st[2:3, :])
        e_c = pick(mine, growth_c, tail_c)

        s = nt(rows_w, other_w) * scale
        p = jnp.exp(s - pick(mine, lse_c, 0.0) - pick(mine, zero, st[0:1, :]))
        p = jnp.where(apart * sign < limit, p, 0.0)
        dp = nt(rows_v, other_v)
        ds = p * (dp - pick(mine, dw_c, 0.0) - pick(mine, zero, st[1:2, :]))
        more_w = nn(ds.astype(bf16), other_w)
        x = nn(rows_f, other_f) * feat_scale
        e = e_r * e_c
        dx = (dp - pick(mine, dl_c, 0.0) - pick(mine, zero, st[3:4, :])) * e * (1.0 + x)
        more_f = nt(other_f, dx.astype(bf16))
        more_v = nn((p + (1.0 + x + 0.5 * x * x) * e).astype(bf16), other_v)
        dwq = dwq + pick(mine, more_w, 0.0)
        dwk = dwk + pick(mine, 0.0, more_w)
        dqt = dqt + pick(mine, more_f, 0.0)
        dkt = dkt + pick(mine, 0.0, more_f)
        dv = dv + pick(mine, 0.0, more_v)
        return dwq, dqt, dwk, dkt, dv

    dwq, dqt, dwk, dkt, dv = over_partners(count, step, (dwq, dqt, dwk, dkt, dv))
    grad_ref[0:rows, :] = (dwq * scale).astype(bf16)
    grad_ref[rows : 2 * rows, :] = (dwk * scale).astype(bf16)
    grad_ref[2 * rows : 3 * rows, :] = dv.astype(bf16)
    dft = (jnp.concatenate([dqt, dkt], axis=0) * feat_scale).astype(bf16)
    put_wide(grad_ref, 3 * rows, dft)


def merge_kernel(by_head, place_ref, grad_ref, weight_ref, *rest):
    out_ref, cat_ref, feat_ref = rest[-3:]
    heads = grad_ref.shape[0]
    rows = cat_ref.shape[0]
    nf2 = feat_ref.shape[1] // heads
    lanes = 3 * LANES

    @pl.when(pl.program_id(0) == 0)
    def _():
        for h in range(heads):
            for part in range(3):
                at = h * lanes + part * LANES
                cat_ref[:, at : at + LANES] = grad_ref[h, part * rows : (part + 1) * rows, :]
        dft = jnp.concatenate([wide(grad_ref.at[h], 3 * rows, nf2) for h in range(heads)], axis=0)
        feat_ref[...] = jnp.transpose(dft.astype(f32)).astype(bf16)

    pieces = weight_ref.shape[1 if by_head else 0]

    def stacked(part):
        def one(h, p):
            return weight_ref[(h, p) + part] if by_head else weight_ref[(p, h) + part]

        return jnp.concatenate(
            [jnp.concatenate([one(h, p) for h in range(heads)], axis=0) for p in range(pieces)],
            axis=1,
        )

    total = nn(cat_ref[...], stacked((slice(0, lanes), slice(None))))
    total += nn(feat_ref[...], stacked((slice(lanes, None), slice(None))))
    out_ref[...] = total.astype(bf16)


VMEM = pl.BlockSpec(memory_space=pltpu.VMEM)
SMEM = pl.BlockSpec(memory_space=pltpu.SMEM)
ANY = pl.BlockSpec(memory_space=pl.ANY)
HBM = pl.BlockSpec(memory_space=pltpu.HBM)
params = pltpu.CompilerParams(vmem_limit_bytes=48 * 1024 * 1024)
full = pltpu.CompilerParams(vmem_limit_bytes=60 * 1024 * 1024)


def cost(flops, nbytes, exps=0):
    return pl.CostEstimate(flops=flops, bytes_accessed=nbytes, transcendentals=exps)


def merge(place, grads, weights, by_head, group, rows, dim, half=None, before=None):
    pieces, heads, columns, tile = weights.shape
    block = (group, heads, columns, tile)
    weight_at = lambda i, place: (i, 0, 0, 0)
    if by_head:
        pieces, heads = heads, pieces
        block = (heads, group, columns, tile)
        weight_at = lambda i, place: (0, i, 0, 0)
    steps = pieces // group

    def at(i, place):
        if half is None:
            return (0, i)
        return (0, (place[2] if half == 0 else 1 - place[2]) * steps + i)

    in_specs = [
        pl.BlockSpec(grads.shape, lambda i, place: (0, 0, 0)),
        pl.BlockSpec(block, weight_at),
    ]
    args = [place, grads, weights]
    aliases = {}
    if before is not None:
        in_specs.append(ANY)
        aliases = {len(args): 0}
        args.append(before)
    return pl.pallas_call(
        lambda *refs: merge_kernel(by_head, *refs),
        out_shape=jax.ShapeDtypeStruct((rows, dim), bf16),
        grid_spec=pltpu.PrefetchScalarGridSpec(
            num_scalar_prefetch=1,
            grid=(steps,),
            in_specs=in_specs,
            out_specs=pl.BlockSpec((rows, group * tile), at),
            scratch_shapes=[
                pltpu.VMEM((rows, 3 * LANES * heads), bf16),
                pltpu.VMEM((rows, (columns - 3 * LANES) * heads), bf16),
            ],
        ),
        input_output_aliases=aliases,
        compiler_params=full,
        cost_estimate=cost(rows * pieces * tile * heads * columns, weights.size * 2),
        name="head_sum",
    )(*args)


def per_device(tokens, feature_weight, window_weight, value_weight, log_decay, out_grad):
    rows, dim = tokens.shape
    nf2 = feature_weight.shape[1]
    nf = nf2 // 2
    dh = value_weight.shape[1]
    columns = 3 * dh + nf2
    chips, count = lax.axis_size("chip"), lax.axis_size(CTX)
    heads = lax.axis_size("tp")
    chip, core = lax.axis_index("chip"), lax.axis_index("core")
    me = lax.axis_index(CTX)
    tile = 2 * LANES
    spread = count * tile == dim
    pieces = 1 if spread else dim // tile
    piece = core * chips + chip if spread else 0 * me
    place = jnp.stack([me, piece, core, lax.axis_index("tp")]).astype(jnp.int32)
    fw_t = feature_weight.T
    packed = pl.pallas_call(
        pack_kernel,
        out_shape=jax.ShapeDtypeStruct((pieces, columns, tile), bf16),
        in_specs=[SMEM] + [HBM] * 3,
        out_specs=VMEM,
        scratch_shapes=[
            pltpu.VMEM((pieces * tile, 2 * dh), bf16),
            pltpu.VMEM((pieces * tile, dh), bf16),
            pltpu.VMEM((nf2, pieces * tile), bf16),
            pltpu.SemaphoreType.DMA((3,)),
        ],
        compiler_params=full,
        cost_estimate=cost(1, 2 * columns * tile * pieces * 2),
        name="pack",
    )(place, window_weight, value_weight, fw_t)
    weights = lax.all_gather(packed[0], ("chip", "tp")) if spread else lax.all_gather(packed, "tp")

    payload = 2 * rows + 2 * nf + 16
    block = jax.ShapeDtypeStruct((payload, LANES), bf16)
    *sends, own, query, feat, cum = pl.pallas_call(
        project_kernel,
        out_shape=[block] * (chips + 2)
        + [
            jax.ShapeDtypeStruct((rows, nf2), bf16),
            jax.ShapeDtypeStruct((rows, 1), f32),
        ],
        in_specs=[SMEM] + [HBM] * 6,
        out_specs=[VMEM] * (chips + 4),
        scratch_shapes=[
            pltpu.VMEM((rows, dim), bf16),
            pltpu.VMEM((nf2, dim), bf16),
            pltpu.VMEM((dim, 2 * dh), bf16),
            pltpu.VMEM((dim, dh), bf16),
            pltpu.VMEM((1, rows), f32),
            pltpu.VMEM((rows, dh), bf16),
            pltpu.SemaphoreType.DMA((CHUNKS, 4)),
            pltpu.SemaphoreType.DMA((2,)),
        ],
        compiler_params=params,
        cost_estimate=cost(2 * rows * dim * columns, 4 * 1024 * 1024),
        name="project",
    )(place, tokens, fw_t, window_weight, value_weight, log_decay.T, out_grad)

    swap = [(0, 1), (1, 0)]
    recv = {1: None}
    for d in range(1, chips):
        recv[2 * d] = lax.ppermute(sends[d], "chip", [(i, i ^ d) for i in range(chips)])
    recv[1] = lax.ppermute(sends[0], "core", swap)
    for d in range(1, chips):
        recv[2 * d + 1] = lax.ppermute(recv[2 * d], "core", swap)
    recv = [recv[d] for d in range(1, count)]
    if count > 8:
        recv = [jnp.stack(recv)]

    attended, stat, sheet = pl.pallas_call(
        lambda *refs: query_kernel(count, *refs),
        out_shape=(
            jax.ShapeDtypeStruct((rows, dh), bf16),
            jax.ShapeDtypeStruct((8, rows), f32),
            jax.ShapeDtypeStruct((rows, LANES), f32),
        ),
        in_specs=[SMEM] + [VMEM] * (len(recv) + 4),
        out_specs=[VMEM] * 3,
        scratch_shapes=[
            pltpu.VMEM((count, 2 * rows, dh), bf16),
            pltpu.VMEM((WINDOW // rows + 1, rows, rows), f32),
            pltpu.VMEM((count, rows), f32),
        ],
        compiler_params=params,
        cost_estimate=cost(10**9, 2 * 1024 * 1024, 10**6),
        name="query_side",
    )(place, *recv, own, query, feat, cum)
    stats = lax.all_gather(lax.all_gather(stat, "core"), "chip").reshape(count, -1, rows)
    grads = pl.pallas_call(
        lambda *refs: gradient_kernel(count, *refs),
        out_shape=jax.ShapeDtypeStruct((3 * rows + nf2 * rows // LANES, LANES), bf16),
        in_specs=[SMEM] + [VMEM] * (len(recv) + 5),
        out_specs=VMEM,
        compiler_params=params,
        cost_estimate=cost(10**9, 2 * 1024 * 1024, 10**6),
        name="gradients",
    )(place, *recv, own, query, feat, sheet, stats)
    grads = lax.all_gather(grads, "tp")
    if not spread:
        return (attended, merge(place, grads, weights, True, 1, rows, dim))
    weights, grads = lax.optimization_barrier((weights, grads))
    weights = weights.reshape(chips, -1, columns, tile)
    swapped = lax.ppermute(weights, "core", swap)
    total = merge(place, grads, weights, False, 2, rows, dim, 0)
    return (attended, merge(place, grads, swapped, False, 2, rows, dim, 1, total))


def solution(mesh):
    ctx, tp = mesh.devices.shape
    split = Mesh(mesh.devices.reshape(ctx // 2, 2, tp), ("chip", "core", "tp"))
    in_specs = (
        P(CTX, None),
        P(None, "tp"),
        P(None, "tp"),
        P(None, "tp"),
        P(CTX, "tp"),
        P(CTX, "tp"),
    )
    out_specs = (P(CTX, "tp"), P(CTX, None))
    return jax.shard_map(
        per_device, mesh=split, in_specs=in_specs, out_specs=out_specs, check_vma=False
    )
```

```python
import jax
import jax.numpy as jnp
from jax import lax
from jax.experimental import pallas as pl
from jax.experimental.pallas import tpu as pltpu
from jax.sharding import Mesh
from jax.sharding import PartitionSpec as P

WINDOW = 1024
LANES = 128
MASKED = -1e30
CTX = ("chip", "core")
CHUNKS = 4
f32 = jnp.float32
bf16 = jnp.bfloat16


def nn(a, b):
    return lax.dot_general(a, b, (((1,), (0,)), ((), ())), preferred_element_type=f32)


def nt(a, b):
    return lax.dot_general(a, b, (((1,), (1,)), ((), ())), preferred_element_type=f32)


def partner(me, d, count):
    assert count & (count - 1) == 0
    return jnp.bitwise_xor(me, d)


def wide(view, start, count):
    return jnp.concatenate(
        [view[start : start + count, :], view[start + count : start + 2 * count, :]], axis=1
    )


def put_wide(ref, start, value):
    count = value.shape[0]
    for half in range(value.shape[1] // LANES):
        ref[start + half * count : start + (half + 1) * count, :] = value[
            :, half * LANES : (half + 1) * LANES
        ]


def cum_row(view, start):
    tail = view[start : start + 16, :].astype(f32)
    first = tail[0:1] + tail[2:3] + tail[4:5]
    second = tail[1:2] + tail[3:4] + tail[5:6]
    return jnp.concatenate([first, second], axis=1)


def iotas(rows):
    return (
        lax.broadcasted_iota(jnp.int32, (rows, rows), 0),
        lax.broadcasted_iota(jnp.int32, (rows, rows), 1),
    )


def block_index():
    return lax.axis_index("chip") * lax.axis_size("core") + lax.axis_index("core")


def project_kernel(tok_hbm, fw_hbm, ww_hbm, vw_hbm, ld_hbm, do_hbm, *rest):
    *sends, keys_ref, query_ref, feat_ref, cum_ref = rest[:-8]
    tok_ref, fw_ref, ww_ref, vw_ref, ld_ref, do_ref, sems, small = rest[-8:]
    me = block_index()
    rows, dim = tok_ref.shape
    dh = do_ref.shape[1]
    nf = fw_ref.shape[0] // 2
    span = dim // CHUNKS
    copies = []
    for c in range(CHUNKS):
        part = pl.ds(c * span, span)
        copies.append([
            pltpu.make_async_copy(tok_hbm.at[:, part], tok_ref.at[:, part], sems.at[c, 0]),
            pltpu.make_async_copy(ww_hbm.at[part, :], ww_ref.at[part, :], sems.at[c, 1]),
            pltpu.make_async_copy(vw_hbm.at[part, :], vw_ref.at[part, :], sems.at[c, 2]),
            pltpu.make_async_copy(fw_hbm.at[:, part], fw_ref.at[:, part], sems.at[c, 3]),
        ])
    others = [
        pltpu.make_async_copy(ld_hbm, ld_ref, small.at[0]),
        pltpu.make_async_copy(do_hbm, do_ref, small.at[1]),
    ]
    for copy in copies[0] + others:
        copy.start()
    for group in copies[1:]:
        for copy in group:
            copy.start()
    for copy in others:
        copy.wait()
    at_row, at_col = iotas(rows)
    ld_r = ld_ref[...]
    ld_c = jnp.sum(jnp.where(at_row == at_col, ld_r, 0.0), axis=1, keepdims=True)
    cum_r = jnp.sum(jnp.where(at_row <= at_col, ld_c, 0.0), axis=0, keepdims=True)
    cum_ref[...] = jnp.sum(jnp.where(at_col <= at_row, ld_r, 0.0), axis=1, keepdims=True)
    high = cum_r.astype(bf16)
    left = cum_r - high.astype(f32)
    mid = left.astype(bf16)
    low = (left - mid.astype(f32)).astype(bf16)
    pieces = [t[:, h : h + LANES].astype(f32) for t in (high, mid, low) for h in range(0, rows, LANES)]
    tail = jnp.concatenate(pieces + [jnp.zeros((10, LANES), f32)], axis=0).astype(bf16)

    feat = jnp.zeros((rows, 2 * nf), f32)
    main = jnp.zeros((rows, 3 * dh), f32)
    for c in range(CHUNKS):
        for copy in copies[c]:
            copy.wait()
        part = slice(c * span, (c + 1) * span)
        tok = tok_ref[:, part]
        feat += nt(tok, fw_ref[:, part])
        main += nn(tok, jnp.concatenate([ww_ref[part, :], vw_ref[part, :]], axis=1))
    feat = feat.astype(bf16)
    window = main[:, : 2 * dh].astype(bf16)
    values = main[:, 2 * dh :].astype(bf16)
    feat_ref[...] = feat
    small_row, small_col = iotas(2 * nf)
    feat_t = nt((small_row == small_col).astype(bf16), feat).astype(bf16)
    feat_at = 2 * rows
    tail_at = feat_at + 2 * nf

    def put_keys(ref):
        ref[0:rows, :] = window[:, dh:]
        ref[rows : 2 * rows, :] = values
        put_wide(ref, feat_at, feat_t[nf:, :])
        ref[tail_at : tail_at + 16, :] = tail

    def put_query(ref):
        ref[0:rows, :] = window[:, :dh]
        ref[rows : 2 * rows, :] = do_ref[...]
        put_wide(ref, feat_at, feat_t[:nf, :])
        ref[tail_at : tail_at + 16, :] = tail

    put_keys(keys_ref)
    put_query(query_ref)
    for at, ref in enumerate(sends):
        later = jnp.bitwise_xor(me, max(2 * at, 1)) > me
        pl.when(later)(lambda ref=ref: put_keys(ref))
        pl.when(jnp.logical_not(later))(lambda ref=ref: put_query(ref))


def pack_kernel(ww_hbm, vw_hbm, fw_hbm, own_ref, *rest):
    sends, sems = rest[:-1], rest[-1]
    head, core = lax.axis_index("tp"), lax.axis_index("core")
    nf2 = fw_hbm.shape[0]
    tile = (own_ref.shape[1] * LANES) // (3 * LANES + nf2)
    parts = [(own_ref.at[k], 2 * head + k) for k in range(2)]
    parts += [(ref, 2 * jnp.bitwise_xor(head, t + 1) + core) for t, ref in enumerate(sends)]
    copies = []
    for n, (ref, piece) in enumerate(parts):
        rows = pl.ds(pl.multiple_of(piece * tile, tile), tile)
        moves = [
            (ww_hbm.at[rows, pl.ds(0, LANES)], ref.at[pl.ds(0, tile), :]),
            (ww_hbm.at[rows, pl.ds(LANES, LANES)], ref.at[pl.ds(tile, tile), :]),
            (vw_hbm.at[rows, :], ref.at[pl.ds(2 * tile, tile), :]),
        ]
        for m in range(tile // LANES):
            lanes = pl.ds(pl.multiple_of(piece * tile + m * LANES, LANES), LANES)
            moves.append((fw_hbm.at[:, lanes], ref.at[pl.ds(3 * tile + m * nf2, nf2), :]))
        for m, (src, dst) in enumerate(moves):
            copies.append(pltpu.make_async_copy(src, dst, sems.at[n, m]))
    for copy in copies:
        copy.start()
    for copy in copies:
        copy.wait()


def between(totals, low, high):
    at = lax.broadcasted_iota(jnp.int32, totals.shape, 0)
    return jnp.sum(jnp.where((at > low) & (at < high), totals, 0.0), axis=0, keepdims=True)


def over_partners(count, body, carry):
    if count <= 8:
        for d in range(1, count):
            carry = body(d, carry)
        return carry
    return lax.fori_loop(1, count, body, carry)


def query_kernel(count, *rest):
    recvs = rest[: -10]
    (own_ref, query_ref, feat_ref, cum_ref, att_ref, stat_ref, sheet_ref, near_ref, p_ref,
     cums_ref) = rest[-10:]

    def recv(d):
        return recvs[d - 1] if len(recvs) > 1 else recvs[0].at[d - 1]

    me = block_index()
    rows, dh = att_ref.shape
    nf = feat_ref.shape[1] // 2
    back = WINDOW // rows
    feat_at = 2 * rows
    tail_at = feat_at + 2 * nf
    scale = dh ** (-0.5)
    feat_scale = nf ** (-0.5)
    wq = query_ref[0:rows, :]
    do = query_ref[rows : 2 * rows, :]
    q = feat_ref[:, :nf]
    at_row, at_col = iotas(rows)
    own_cum = cum_row(own_ref, tail_at)
    cums_ref[pl.ds(me, 1), :] = own_cum
    near_ref[me] = own_ref[0 : 2 * rows, :]

    def gather(d, carry):
        j = partner(me, d, count)
        view = recv(d)
        near_ref[j] = view[0 : 2 * rows, :]
        cums_ref[pl.ds(j, 1), :] = cum_row(view, tail_at)
        return carry

    over_partners(count, gather, 0)

    def near(w):
        return near_ref.at[jnp.maximum(me - back + w, 0)]

    top = jnp.full((rows, LANES), MASKED, f32)
    for w in range(back + 1):
        keys = own_ref[0:rows, :] if w == back else near(w)[0:rows, :]
        s = nt(wq, keys) * scale
        if w == back:
            s = jnp.where(at_col <= at_row, s, MASKED)
        elif w == 0:
            s = jnp.where((at_col > at_row) & (me >= back), s, MASKED)
        else:
            s = jnp.where(me >= back - w, s, MASKED)
        p_ref[w] = s
        for h in range(0, rows, LANES):
            top = jnp.maximum(top, s[:, h : h + LANES])
    top = jnp.max(top, axis=1, keepdims=True)
    total = jnp.zeros((rows, LANES), f32)
    out = jnp.zeros((rows, dh), f32)
    for w in range(back + 1):
        p = jnp.exp(p_ref[w] - top)
        for h in range(0, rows, LANES):
            total += p[:, h : h + LANES]
        vals = own_ref[rows : 2 * rows, :] if w == back else near(w)[rows : 2 * rows, :]
        out += nn(p.astype(bf16), vals)
    total = jnp.sum(total, axis=1, keepdims=True)
    windowed = out * (1.0 / total)

    cum_c = cum_ref[...]
    growth = jnp.exp(cum_c)
    totals = cums_ref[:, rows - 1 : rows]

    def forward(d, carry):
        num, den = carry
        j = partner(me, d, count)
        view = recv(d)
        gap = between(totals, j - 1, me)
        es = jnp.where(j < me, jnp.exp(jnp.minimum(gap - cums_ref[pl.ds(j, 1), :], 0.0)), 0.0)
        x = nn(q, wide(view, feat_at, nf)) * feat_scale
        weight = (1.0 + x + 0.5 * x * x) * es
        for h in range(0, rows, LANES):
            den += weight[:, h : h + LANES]
        num += nn(weight.astype(bf16), view[rows : 2 * rows, :])
        return num, den

    num, den = over_partners(
        count, forward, (jnp.zeros((rows, dh), f32), jnp.zeros((rows, LANES), f32))
    )
    x = nn(q, wide(own_ref, feat_at, nf)) * feat_scale
    e = jnp.where(at_col <= at_row, jnp.exp(jnp.minimum(cum_c - own_cum, 0.0)), 0.0)
    weight = (1.0 + x + 0.5 * x * x) * e
    num = num * growth + nn(weight.astype(bf16), own_ref[rows : 2 * rows, :])
    den = den * growth
    for h in range(0, rows, LANES):
        den += weight[:, h : h + LANES]
    rden = 1.0 / jnp.sum(den, axis=1, keepdims=True)
    linear = num * rden
    att_ref[...] = (linear + windowed).astype(bf16)
    do_f = do.astype(f32)
    delta_w = jnp.sum(do_f * windowed, axis=1, keepdims=True)
    delta_l = jnp.sum(do_f * linear, axis=1, keepdims=True)
    lse = top + jnp.log(total)
    lane = lax.broadcasted_iota(jnp.int32, (rows, LANES), 1)
    sheet = jnp.where(lane == 0, lse, 0.0)
    sheet = jnp.where(lane == 1, delta_w, sheet)
    sheet = jnp.where(lane == 2, rden, sheet)
    sheet = jnp.where(lane == 3, delta_l, sheet)
    sheet = jnp.where(lane == 4, cum_c, sheet)
    sheet_ref[...] = sheet
    stat_ref[...] = jnp.transpose(sheet)[0:8, :]


def gradient_kernel(count, *rest):
    parts = len(rest) - 7 >> 1
    recvs, stats = rest[:parts], rest[parts : 2 * parts]
    own_ref, query_ref, feat_ref, sheet_ref, mine_ref, grad_ref, total_ref = rest[2 * parts :]

    def recv(d):
        return recvs[d - 1] if len(recvs) > 1 else recvs[0].at[d - 1]

    def stat(d):
        return stats[d - 1] if len(stats) > 1 else stats[0].at[d - 1]

    me = block_index()
    rows = feat_ref.shape[0]
    dh = LANES
    nf = feat_ref.shape[1] // 2
    feat_at = 2 * rows
    scale = dh ** (-0.5)
    feat_scale = nf ** (-0.5)
    at_row, at_col = iotas(rows)
    apart = at_row - at_col
    wq, wk = query_ref[0:rows, :], own_ref[0:rows, :]
    do, v = query_ref[rows : 2 * rows, :], own_ref[rows : 2 * rows, :]
    q, k = feat_ref[:, :nf], feat_ref[:, nf:]
    lse_c, dw_c = sheet_ref[:, 0:1], sheet_ref[:, 1:2]
    rden_c, dl_c, cum_c = sheet_ref[:, 2:3], sheet_ref[:, 3:4], sheet_ref[:, 4:5]
    own_cum = mine_ref[4:5, :]
    total_ref[pl.ds(me, 1), :] = own_cum[:, rows - LANES :]

    def place(d, carry):
        total_ref[pl.ds(partner(me, d, count), 1), :] = stat(d)[4:5, rows - LANES :]
        return carry

    over_partners(count, place, 0)
    totals = total_ref[:, LANES - 1 :]
    growth_c = jnp.exp(cum_c) * rden_c
    tail_c = jnp.exp(own_cum[:, rows - 1 : rows] - cum_c)

    def pick(flag, a, b):
        return jnp.where(flag, a, b)

    s = nt(wq, wk) * scale
    causal = at_col <= at_row
    p = jnp.where(causal, jnp.exp(s - lse_c), 0.0)
    dp = nt(do, v)
    dwq = nn((p * (dp - dw_c)).astype(bf16), wk)
    x = nn(q, wide(own_ref, feat_at, nf)) * feat_scale
    e = jnp.where(causal, jnp.exp(jnp.minimum(cum_c - own_cum, 0.0)), 0.0) * rden_c
    dx = (dp - dl_c) * e * (1.0 + x)
    dqt = nt(wide(own_ref, feat_at, nf), dx.astype(bf16))

    s = nt(wk, wq) * scale
    causal = at_row <= at_col
    p = jnp.where(causal, jnp.exp(s - mine_ref[0:1, :]), 0.0)
    dp = nt(v, do)
    dwk = nn((p * (dp - mine_ref[1:2, :])).astype(bf16), wq)
    x = nn(k, wide(query_ref, feat_at, nf)) * feat_scale
    e = jnp.where(causal, jnp.exp(jnp.minimum(own_cum - cum_c, 0.0)), 0.0) * mine_ref[2:3, :]
    dx = (dp - mine_ref[3:4, :]) * e * (1.0 + x)
    dkt = nt(wide(query_ref, feat_at, nf), dx.astype(bf16))
    dv = nn((p + (1.0 + x + 0.5 * x * x) * e).astype(bf16), do)

    def step(d, carry):
        dwq, dqt, dwk, dkt, dv = carry
        j = partner(me, d, count)
        view = recv(d)
        mine = j < me
        sign = pick(mine, 1, -1)
        limit = WINDOW - jnp.abs(me - j) * rows
        rows_w = pick(mine, wq, wk)
        rows_v = pick(mine, do, v)
        rows_f = pick(mine, q, k)
        other_w = view[0:rows, :]
        other_v = view[rows : 2 * rows, :]
        other_f = wide(view, feat_at, nf)
        st = stat(d)
        zero = jnp.zeros((1, rows), f32)
        cum = st[4:5, :]
        gap = between(totals, jnp.minimum(me, j), jnp.maximum(me, j))
        e_r = jnp.exp(jnp.minimum(gap + pick(mine, cum[:, rows - 1 : rows] - cum, cum), 0.0))
        e_r = e_r * pick(mine, 1.0, st[2:3, :])
        e_c = pick(mine, growth_c, tail_c)

        s = nt(rows_w, other_w) * scale
        p = jnp.exp(s - pick(mine, lse_c, 0.0) - pick(mine, zero, st[0:1, :]))
        p = jnp.where(apart * sign < limit, p, 0.0)
        dp = nt(rows_v, other_v)
        ds = p * (dp - pick(mine, dw_c, 0.0) - pick(mine, zero, st[1:2, :]))
        more_w = nn(ds.astype(bf16), other_w)
        x = nn(rows_f, other_f) * feat_scale
        e = e_r * e_c
        dx = (dp - pick(mine, dl_c, 0.0) - pick(mine, zero, st[3:4, :])) * e * (1.0 + x)
        more_f = nt(other_f, dx.astype(bf16))
        more_v = nn((p + (1.0 + x + 0.5 * x * x) * e).astype(bf16), other_v)
        dwq = dwq + pick(mine, more_w, 0.0)
        dwk = dwk + pick(mine, 0.0, more_w)
        dqt = dqt + pick(mine, more_f, 0.0)
        dkt = dkt + pick(mine, 0.0, more_f)
        dv = dv + pick(mine, 0.0, more_v)
        return dwq, dqt, dwk, dkt, dv

    dwq, dqt, dwk, dkt, dv = over_partners(count, step, (dwq, dqt, dwk, dkt, dv))
    grad_ref[0:rows, :] = (dwq * scale).astype(bf16)
    grad_ref[rows : 2 * rows, :] = (dwk * scale).astype(bf16)
    grad_ref[2 * rows : 3 * rows, :] = dv.astype(bf16)
    dft = (jnp.concatenate([dqt, dkt], axis=0) * feat_scale).astype(bf16)
    put_wide(grad_ref, 3 * rows, dft)


def gather_rows(grad_ref, order, cat_ref, feat_ref):
    rows = cat_ref.shape[0]
    nf2 = feat_ref.shape[1] // len(order)
    for at, h in enumerate(order):
        for part in range(3):
            lane = (3 * at + part) * LANES
            cat_ref[:, lane : lane + LANES] = grad_ref[h, part * rows : (part + 1) * rows, :]
    dft = jnp.concatenate([wide(grad_ref.at[h], 3 * rows, nf2) for h in order], axis=0)
    feat_ref[...] = jnp.transpose(dft.astype(f32)).astype(bf16)


def share_kernel(grad_ref, own_ref, *rest):
    heads = grad_ref.shape[0]
    near, far = rest[: heads - 1], rest[heads - 1 : 2 * heads - 2]
    first_ref, second_ref, cat_ref, feat_ref = rest[-4:]
    rows = cat_ref.shape[0]
    tile = first_ref.shape[1]
    nf2 = feat_ref.shape[1] // heads
    head, core = lax.axis_index("tp"), lax.axis_index("core")
    gather_rows(
        grad_ref, [head] + [jnp.bitwise_xor(head, t) for t in range(1, heads)], cat_ref, feat_ref
    )

    def product(out_ref, views):
        main = jnp.concatenate(
            [v[m * tile : (m + 1) * tile, :] for v in views for m in range(3)], axis=1
        )
        feats = jnp.concatenate([wide(v, 3 * tile, nf2) for v in views], axis=0)
        out_ref[...] = (nt(cat_ref[...], main) + nn(feat_ref[...], feats)).astype(bf16)

    for flag, ours, theirs in ((0, first_ref, second_ref), (1, second_ref, first_ref)):

        @pl.when(core == flag)
        def _():
            product(ours, [own_ref.at[flag], *near])
            product(theirs, [own_ref.at[1 - flag], *far])


def lay_kernel(first_ref, second_ref, out_ref):
    shares, _, tile = first_ref.shape
    for z in range(shares):
        at = 2 * z * tile
        out_ref[:, at : at + tile] = first_ref[z]
        out_ref[:, at + tile : at + 2 * tile] = second_ref[z]


def merge_kernel(grad_ref, weight_ref, out_ref, cat_ref, feat_ref):
    heads = grad_ref.shape[0]
    tile = out_ref.shape[1]
    lanes = 3 * LANES
    nf2 = feat_ref.shape[1] // heads

    @pl.when(pl.program_id(0) == 0)
    def _():
        gather_rows(grad_ref, range(heads), cat_ref, feat_ref)

    views = [weight_ref.at[h] for h in range(heads)]
    main = jnp.concatenate([v[:, 0:lanes] for v in views], axis=1)
    feats = jnp.concatenate([v[:, lanes:] for v in views], axis=1)
    out_ref[...] = (nt(cat_ref[...], main) + nt(feat_ref[...], feats)).astype(bf16)


VMEM = pl.BlockSpec(memory_space=pltpu.VMEM)
HBM = pl.BlockSpec(memory_space=pltpu.HBM)
params = pltpu.CompilerParams(vmem_limit_bytes=32 * 1024 * 1024)


def in_hbm(*arrays):
    return [pltpu.with_memory_space_constraint(a, pltpu.HBM) for a in arrays]


def cost(flops, nbytes, exps=0):
    return pl.CostEstimate(flops=flops, bytes_accessed=nbytes, transcendentals=exps)


def merge(grads, weights, rows, dim):
    heads, _, columns = weights.shape
    tile = 2 * LANES
    return pl.pallas_call(
        merge_kernel,
        out_shape=jax.ShapeDtypeStruct((rows, dim), bf16),
        grid=(dim // tile,),
        in_specs=[
            pl.BlockSpec(grads.shape, lambda i: (0, 0, 0)),
            pl.BlockSpec((heads, tile, columns), lambda i: (0, i, 0)),
        ],
        out_specs=pl.BlockSpec((rows, tile), lambda i: (0, i)),
        scratch_shapes=[
            pltpu.VMEM((rows, 3 * LANES * heads), bf16),
            pltpu.VMEM((rows, (columns - 3 * LANES) * heads), bf16),
        ],
        compiler_params=params,
        cost_estimate=cost(2 * rows * dim * heads * columns, heads * dim * columns * 2),
        name="head_sum",
    )(grads, weights)


def per_device(tokens, feature_weight, window_weight, value_weight, log_decay, out_grad):
    rows, dim = tokens.shape
    nf2 = feature_weight.shape[1]
    nf = nf2 // 2
    dh = value_weight.shape[1]
    columns = 3 * dh + nf2
    chips, count, heads = lax.axis_size("chip"), lax.axis_size(CTX), lax.axis_size("tp")
    tile = 2 * LANES
    fw_t = feature_weight.T

    payload = 2 * rows + 2 * nf + 16
    block = jax.ShapeDtypeStruct((payload, LANES), bf16)
    *sends, own, query, feat, cum = pl.pallas_call(
        project_kernel,
        out_shape=[block] * (chips + 2)
        + [
            jax.ShapeDtypeStruct((rows, nf2), bf16),
            jax.ShapeDtypeStruct((rows, 1), f32),
        ],
        in_specs=[HBM] * 6,
        out_specs=[VMEM] * (chips + 4),
        scratch_shapes=[
            pltpu.VMEM((rows, dim), bf16),
            pltpu.VMEM((nf2, dim), bf16),
            pltpu.VMEM((dim, 2 * dh), bf16),
            pltpu.VMEM((dim, dh), bf16),
            pltpu.VMEM((1, rows), f32),
            pltpu.VMEM((rows, dh), bf16),
            pltpu.SemaphoreType.DMA((CHUNKS, 4)),
            pltpu.SemaphoreType.DMA((2,)),
        ],
        compiler_params=params,
        cost_estimate=cost(2 * rows * dim * columns, 4 * 1024 * 1024),
        name="project",
    )(*in_hbm(tokens, fw_t, window_weight, value_weight, log_decay.T, out_grad))

    shared = heads & (heads - 1) == 0 and 2 * tile * heads == dim
    if shared:
        sources, _ = lax.optimization_barrier(((window_weight, value_weight, fw_t), sends[0]))
        area = 3 * tile + nf2 * tile // LANES
        own_weights, *packed = pl.pallas_call(
            pack_kernel,
            out_shape=[jax.ShapeDtypeStruct((2, area, LANES), bf16)]
            + [jax.ShapeDtypeStruct((area, LANES), bf16)] * (heads - 1),
            in_specs=[HBM] * 3,
            out_specs=[VMEM] * heads,
            scratch_shapes=[pltpu.SemaphoreType.DMA((heads + 1, 3 + tile // LANES))],
            compiler_params=params,
            cost_estimate=cost(1, 2 * columns * tile * (heads + 1) * 2),
            name="pack",
        )(*in_hbm(*sources))
        near = [
            lax.ppermute(packed[t - 1], "tp", [(z, z ^ t) for z in range(heads)])
            for t in range(1, heads)
        ]

    swap = [(0, 1), (1, 0)]
    recv = {}
    for d in range(1, chips):
        recv[2 * d] = lax.ppermute(sends[d], "chip", [(i, i ^ d) for i in range(chips)])
    recv[1] = lax.ppermute(sends[0], "core", swap)
    for d in range(1, chips):
        recv[2 * d + 1] = lax.ppermute(recv[2 * d], "core", swap)
    recv = [recv[d] for d in range(1, count)]
    if count > 8:
        recv = [jnp.stack(recv)]

    attended, stat, sheet = pl.pallas_call(
        lambda *refs: query_kernel(count, *refs),
        out_shape=(
            jax.ShapeDtypeStruct((rows, dh), bf16),
            jax.ShapeDtypeStruct((8, rows), f32),
            jax.ShapeDtypeStruct((rows, LANES), f32),
        ),
        in_specs=[VMEM] * (len(recv) + 4),
        out_specs=[VMEM] * 3,
        scratch_shapes=[
            pltpu.VMEM((count, 2 * rows, dh), bf16),
            pltpu.VMEM((WINDOW // rows + 1, rows, rows), f32),
            pltpu.VMEM((count, rows), f32),
        ],
        compiler_params=params,
        cost_estimate=cost(10**9, 2 * 1024 * 1024, 10**6),
        name="query_side",
    )(*recv, own, query, feat, cum)
    stats = [
        lax.ppermute(stat, CTX, [(i, i ^ d) for i in range(count)]) for d in range(1, count)
    ]
    if count > 8:
        stats = [jnp.stack(stats)]
    grads = pl.pallas_call(
        lambda *refs: gradient_kernel(count, *refs),
        out_shape=jax.ShapeDtypeStruct((3 * rows + nf2 * rows // LANES, LANES), bf16),
        in_specs=[VMEM] * (2 * len(recv) + 5),
        out_specs=VMEM,
        scratch_shapes=[pltpu.VMEM((count, LANES), f32)],
        compiler_params=params,
        cost_estimate=cost(10**9, 2 * 1024 * 1024, 10**6),
        name="gradients",
    )(*recv, *stats, own, query, feat, sheet, stat)
    if not shared:
        weights = jnp.concatenate([window_weight, value_weight, feature_weight], axis=1)
        weights = lax.all_gather(weights, "tp")
        return (attended, merge(lax.all_gather(grads, "tp"), weights, rows, dim))

    near, grads = lax.optimization_barrier((near, grads))
    far = [lax.ppermute(n, "core", swap) for n in near]
    grads = lax.all_gather(grads, "tp")
    tiles = pl.pallas_call(
        share_kernel,
        out_shape=[jax.ShapeDtypeStruct((rows, tile), bf16)] * 2,
        in_specs=[VMEM] * (2 * heads),
        out_specs=[VMEM] * 2,
        scratch_shapes=[
            pltpu.VMEM((rows, 3 * LANES * heads), bf16),
            pltpu.VMEM((rows, nf2 * heads), bf16),
        ],
        compiler_params=params,
        cost_estimate=cost(4 * rows * tile * heads * columns, 4 * heads * tile * columns),
        name="share",
    )(grads, own_weights, *near, *far)
    first, second = [lax.all_gather(t, "tp") for t in tiles]
    total = pl.pallas_call(
        lay_kernel,
        out_shape=jax.ShapeDtypeStruct((rows, dim), bf16),
        in_specs=[VMEM] * 2,
        out_specs=VMEM,
        compiler_params=params,
        cost_estimate=cost(1, 4 * rows * dim),
        name="lay",
    )(first, second)
    return (attended, total)


def solution(mesh):
    ctx, tp = mesh.devices.shape
    split = Mesh(mesh.devices.reshape(ctx // 2, 2, tp), ("chip", "core", "tp"))
    in_specs = (
        P(CTX, None),
        P(None, "tp"),
        P(None, "tp"),
        P(None, "tp"),
        P(CTX, "tp"),
        P(CTX, "tp"),
    )
    out_specs = (P(CTX, "tp"), P(CTX, None))
    return jax.shard_map(
        per_device, mesh=split, in_specs=in_specs, out_specs=out_specs, check_vma=False
    )
```

```python
import jax
import jax.numpy as jnp
from jax import lax
from jax.experimental import pallas as pl
from jax.experimental.pallas import tpu as pltpu
from jax.sharding import Mesh
from jax.sharding import PartitionSpec as P

WINDOW = 1024
LANES = 128
MASKED = -1e30
CTX = ("chip", "core")
CHUNKS = 4
f32 = jnp.float32
bf16 = jnp.bfloat16


def nn(a, b):
    return lax.dot_general(a, b, (((1,), (0,)), ((), ())), preferred_element_type=f32)


def nt(a, b):
    return lax.dot_general(a, b, (((1,), (1,)), ((), ())), preferred_element_type=f32)


def partner(me, d, count):
    assert count & (count - 1) == 0
    return jnp.bitwise_xor(me, d)


def wide(view, start, count):
    return jnp.concatenate(
        [view[start : start + count, :], view[start + count : start + 2 * count, :]], axis=1
    )


def put_wide(ref, start, value):
    count = value.shape[0]
    for half in range(value.shape[1] // LANES):
        ref[start + half * count : start + (half + 1) * count, :] = value[
            :, half * LANES : (half + 1) * LANES
        ]


def cum_row(view, start):
    tail = view[start : start + 16, :].astype(f32)
    first = tail[0:1] + tail[2:3] + tail[4:5]
    second = tail[1:2] + tail[3:4] + tail[5:6]
    return jnp.concatenate([first, second], axis=1)


def iotas(rows):
    return (
        lax.broadcasted_iota(jnp.int32, (rows, rows), 0),
        lax.broadcasted_iota(jnp.int32, (rows, rows), 1),
    )


def block_index():
    return lax.axis_index("chip") * lax.axis_size("core") + lax.axis_index("core")


def project_kernel(tok_hbm, fw_hbm, ww_hbm, vw_hbm, ld_hbm, do_hbm, *rest):
    *sends, keys_ref, query_ref, feat_ref, cum_ref = rest[:-8]
    tok_ref, fw_ref, ww_ref, vw_ref, ld_ref, do_ref, sems, small = rest[-8:]
    me = block_index()
    rows, dim = tok_ref.shape
    dh = do_ref.shape[1]
    nf = fw_ref.shape[0] // 2
    span = dim // CHUNKS
    copies = []
    for c in range(CHUNKS):
        part = pl.ds(c * span, span)
        copies.append([
            pltpu.make_async_copy(tok_hbm.at[:, part], tok_ref.at[:, part], sems.at[c, 0]),
            pltpu.make_async_copy(ww_hbm.at[part, :], ww_ref.at[part, :], sems.at[c, 1]),
            pltpu.make_async_copy(vw_hbm.at[part, :], vw_ref.at[part, :], sems.at[c, 2]),
            pltpu.make_async_copy(fw_hbm.at[:, part], fw_ref.at[:, part], sems.at[c, 3]),
        ])
    others = [
        pltpu.make_async_copy(ld_hbm, ld_ref, small.at[0]),
        pltpu.make_async_copy(do_hbm, do_ref, small.at[1]),
    ]
    for copy in copies[0] + others:
        copy.start()
    for group in copies[1:]:
        for copy in group:
            copy.start()
    for copy in others:
        copy.wait()
    at_row, at_col = iotas(rows)
    ld_r = ld_ref[...]
    ld_c = jnp.sum(jnp.where(at_row == at_col, ld_r, 0.0), axis=1, keepdims=True)
    cum_r = jnp.sum(jnp.where(at_row <= at_col, ld_c, 0.0), axis=0, keepdims=True)
    cum_ref[...] = jnp.sum(jnp.where(at_col <= at_row, ld_r, 0.0), axis=1, keepdims=True)
    high = cum_r.astype(bf16)
    left = cum_r - high.astype(f32)
    mid = left.astype(bf16)
    low = (left - mid.astype(f32)).astype(bf16)
    pieces = [t[:, h : h + LANES].astype(f32) for t in (high, mid, low) for h in range(0, rows, LANES)]
    tail = jnp.concatenate(pieces + [jnp.zeros((10, LANES), f32)], axis=0).astype(bf16)

    feat = jnp.zeros((rows, 2 * nf), f32)
    main = jnp.zeros((rows, 3 * dh), f32)
    for c in range(CHUNKS):
        for copy in copies[c]:
            copy.wait()
        part = slice(c * span, (c + 1) * span)
        tok = tok_ref[:, part]
        feat += nt(tok, fw_ref[:, part])
        main += nn(tok, jnp.concatenate([ww_ref[part, :], vw_ref[part, :]], axis=1))
    feat = feat.astype(bf16)
    window = main[:, : 2 * dh].astype(bf16)
    values = main[:, 2 * dh :].astype(bf16)
    feat_ref[...] = feat
    small_row, small_col = iotas(2 * nf)
    feat_t = nt((small_row == small_col).astype(bf16), feat).astype(bf16)
    feat_at = 2 * rows
    tail_at = feat_at + 2 * nf

    def put_keys(ref):
        ref[0:rows, :] = window[:, dh:]
        ref[rows : 2 * rows, :] = values
        put_wide(ref, feat_at, feat_t[nf:, :])
        ref[tail_at : tail_at + 16, :] = tail

    def put_query(ref):
        ref[0:rows, :] = window[:, :dh]
        ref[rows : 2 * rows, :] = do_ref[...]
        put_wide(ref, feat_at, feat_t[:nf, :])
        ref[tail_at : tail_at + 16, :] = tail

    put_keys(keys_ref)
    put_query(query_ref)
    for at, ref in enumerate(sends):
        later = jnp.bitwise_xor(me, max(2 * at, 1)) > me
        pl.when(later)(lambda ref=ref: put_keys(ref))
        pl.when(jnp.logical_not(later))(lambda ref=ref: put_query(ref))


def pack_kernel(ww_hbm, vw_hbm, fw_hbm, own_ref, *rest):
    sends, sems = rest[:-1], rest[-1]
    head, core = lax.axis_index("tp"), lax.axis_index("core")
    nf2, dim = fw_hbm.shape
    common, share = columns_of(dim, len(sends) + 1)
    parts = [(own_ref.at[k], head, k) for k in range(2)]
    parts += [(ref, jnp.bitwise_xor(head, t + 1), core) for t, ref in enumerate(sends)]
    copies = []
    for n, (ref, to, k) in enumerate(parts):
        first = k * common
        rest_at = 2 * common + to * 2 * share
        moves = []
        for at, start, size, chunks in (
            (0, first, common, first),
            (area(common, nf2), rest_at + k * share, share, rest_at + k * LANES),
        ):
            rows = pl.ds(pl.multiple_of(start, 64), size)
            moves += [
                (ww_hbm.at[rows, pl.ds(0, LANES)], ref.at[pl.ds(at, size), :]),
                (ww_hbm.at[rows, pl.ds(LANES, LANES)], ref.at[pl.ds(at + size, size), :]),
                (vw_hbm.at[rows, :], ref.at[pl.ds(at + 2 * size, size), :]),
            ]
            for m in range(2):
                lanes = pl.ds(pl.multiple_of(chunks + m * LANES, LANES), LANES)
                moves.append((fw_hbm.at[:, lanes], ref.at[pl.ds(at + 3 * size + m * nf2, nf2), :]))
        for m, (src, dst) in enumerate(moves):
            copies.append(pltpu.make_async_copy(src, dst, sems.at[n, m]))
    for copy in copies:
        copy.start()
    for copy in copies:
        copy.wait()


def columns_of(dim, heads):
    return dim // 8, dim * 3 // 4 // heads // 2


def area(size, nf2):
    return 3 * size + 2 * nf2


def between(totals, low, high):
    at = lax.broadcasted_iota(jnp.int32, totals.shape, 0)
    return jnp.sum(jnp.where((at > low) & (at < high), totals, 0.0), axis=0, keepdims=True)


def over_partners(count, body, carry):
    if count <= 8:
        for d in range(1, count):
            carry = body(d, carry)
        return carry
    return lax.fori_loop(1, count, body, carry)


def query_kernel(count, *rest):
    recvs = rest[: -10]
    (own_ref, query_ref, feat_ref, cum_ref, att_ref, stat_ref, sheet_ref, near_ref, p_ref,
     cums_ref) = rest[-10:]

    def recv(d):
        return recvs[d - 1] if len(recvs) > 1 else recvs[0].at[d - 1]

    me = block_index()
    rows, dh = att_ref.shape
    nf = feat_ref.shape[1] // 2
    back = WINDOW // rows
    feat_at = 2 * rows
    tail_at = feat_at + 2 * nf
    scale = dh ** (-0.5)
    feat_scale = nf ** (-0.5)
    wq = query_ref[0:rows, :]
    do = query_ref[rows : 2 * rows, :]
    q = feat_ref[:, :nf]
    at_row, at_col = iotas(rows)
    own_cum = cum_row(own_ref, tail_at)
    cums_ref[pl.ds(me, 1), :] = own_cum
    near_ref[me] = own_ref[0 : 2 * rows, :]

    def gather(d, carry):
        j = partner(me, d, count)
        view = recv(d)
        near_ref[j] = view[0 : 2 * rows, :]
        cums_ref[pl.ds(j, 1), :] = cum_row(view, tail_at)
        return carry

    over_partners(count, gather, 0)

    def near(w):
        return near_ref.at[jnp.maximum(me - back + w, 0)]

    top = jnp.full((rows, LANES), MASKED, f32)
    for w in range(back + 1):
        keys = own_ref[0:rows, :] if w == back else near(w)[0:rows, :]
        s = nt(wq, keys) * scale
        if w == back:
            s = jnp.where(at_col <= at_row, s, MASKED)
        elif w == 0:
            s = jnp.where((at_col > at_row) & (me >= back), s, MASKED)
        else:
            s = jnp.where(me >= back - w, s, MASKED)
        p_ref[w] = s
        for h in range(0, rows, LANES):
            top = jnp.maximum(top, s[:, h : h + LANES])
    top = jnp.max(top, axis=1, keepdims=True)
    total = jnp.zeros((rows, LANES), f32)
    out = jnp.zeros((rows, dh), f32)
    for w in range(back + 1):
        p = jnp.exp(p_ref[w] - top)
        for h in range(0, rows, LANES):
            total += p[:, h : h + LANES]
        vals = own_ref[rows : 2 * rows, :] if w == back else near(w)[rows : 2 * rows, :]
        out += nn(p.astype(bf16), vals)
    total = jnp.sum(total, axis=1, keepdims=True)
    windowed = out * (1.0 / total)

    cum_c = cum_ref[...]
    growth = jnp.exp(cum_c)
    totals = cums_ref[:, rows - 1 : rows]

    def forward(d, carry):
        num, den = carry
        j = partner(me, d, count)
        view = recv(d)
        gap = between(totals, j - 1, me)
        es = jnp.where(j < me, jnp.exp(jnp.minimum(gap - cums_ref[pl.ds(j, 1), :], 0.0)), 0.0)
        x = nn(q, wide(view, feat_at, nf)) * feat_scale
        weight = (1.0 + x + 0.5 * x * x) * es
        for h in range(0, rows, LANES):
            den += weight[:, h : h + LANES]
        num += nn(weight.astype(bf16), view[rows : 2 * rows, :])
        return num, den

    num, den = over_partners(
        count, forward, (jnp.zeros((rows, dh), f32), jnp.zeros((rows, LANES), f32))
    )
    x = nn(q, wide(own_ref, feat_at, nf)) * feat_scale
    e = jnp.where(at_col <= at_row, jnp.exp(jnp.minimum(cum_c - own_cum, 0.0)), 0.0)
    weight = (1.0 + x + 0.5 * x * x) * e
    num = num * growth + nn(weight.astype(bf16), own_ref[rows : 2 * rows, :])
    den = den * growth
    for h in range(0, rows, LANES):
        den += weight[:, h : h + LANES]
    rden = 1.0 / jnp.sum(den, axis=1, keepdims=True)
    linear = num * rden
    att_ref[...] = (linear + windowed).astype(bf16)
    do_f = do.astype(f32)
    delta_w = jnp.sum(do_f * windowed, axis=1, keepdims=True)
    delta_l = jnp.sum(do_f * linear, axis=1, keepdims=True)
    lse = top + jnp.log(total)
    lane = lax.broadcasted_iota(jnp.int32, (rows, LANES), 1)
    sheet = jnp.where(lane == 0, lse, 0.0)
    sheet = jnp.where(lane == 1, delta_w, sheet)
    sheet = jnp.where(lane == 2, rden, sheet)
    sheet = jnp.where(lane == 3, delta_l, sheet)
    sheet = jnp.where(lane == 4, cum_c, sheet)
    sheet_ref[...] = sheet
    stat_ref[...] = jnp.transpose(sheet)[0:8, :]


def gradient_kernel(count, *rest):
    recvs = rest[:-6]
    own_ref, query_ref, feat_ref, sheet_ref, stat_ref, grad_ref = rest[-6:]

    def recv(d):
        return recvs[d - 1] if len(recvs) > 1 else recvs[0].at[d - 1]

    me = block_index()
    rows = feat_ref.shape[0]
    dh = LANES
    nf = feat_ref.shape[1] // 2
    feat_at = 2 * rows
    scale = dh ** (-0.5)
    feat_scale = nf ** (-0.5)
    at_row, at_col = iotas(rows)
    apart = at_row - at_col
    wq, wk = query_ref[0:rows, :], own_ref[0:rows, :]
    do, v = query_ref[rows : 2 * rows, :], own_ref[rows : 2 * rows, :]
    q, k = feat_ref[:, :nf], feat_ref[:, nf:]
    lse_c, dw_c = sheet_ref[:, 0:1], sheet_ref[:, 1:2]
    rden_c, dl_c, cum_c = sheet_ref[:, 2:3], sheet_ref[:, 3:4], sheet_ref[:, 4:5]
    mine_ref = stat_ref.at[me]
    own_cum = mine_ref[4:5, :]
    totals = jnp.concatenate([stat_ref[j, 4:5, rows - 1 : rows] for j in range(count)], axis=0)
    growth_c = jnp.exp(cum_c) * rden_c
    tail_c = jnp.exp(own_cum[:, rows - 1 : rows] - cum_c)

    def pick(flag, a, b):
        return jnp.where(flag, a, b)

    s = nt(wq, wk) * scale
    causal = at_col <= at_row
    p = jnp.where(causal, jnp.exp(s - lse_c), 0.0)
    dp = nt(do, v)
    dwq = nn((p * (dp - dw_c)).astype(bf16), wk)
    x = nn(q, wide(own_ref, feat_at, nf)) * feat_scale
    e = jnp.where(causal, jnp.exp(jnp.minimum(cum_c - own_cum, 0.0)), 0.0) * rden_c
    dx = (dp - dl_c) * e * (1.0 + x)
    dqt = nt(wide(own_ref, feat_at, nf), dx.astype(bf16))

    s = nt(wk, wq) * scale
    causal = at_row <= at_col
    p = jnp.where(causal, jnp.exp(s - mine_ref[0:1, :]), 0.0)
    dp = nt(v, do)
    dwk = nn((p * (dp - mine_ref[1:2, :])).astype(bf16), wq)
    x = nn(k, wide(query_ref, feat_at, nf)) * feat_scale
    e = jnp.where(causal, jnp.exp(jnp.minimum(own_cum - cum_c, 0.0)), 0.0) * mine_ref[2:3, :]
    dx = (dp - mine_ref[3:4, :]) * e * (1.0 + x)
    dkt = nt(wide(query_ref, feat_at, nf), dx.astype(bf16))
    dv = nn((p + (1.0 + x + 0.5 * x * x) * e).astype(bf16), do)

    def step(d, carry):
        dwq, dqt, dwk, dkt, dv = carry
        j = partner(me, d, count)
        view = recv(d)
        mine = j < me
        sign = pick(mine, 1, -1)
        limit = WINDOW - jnp.abs(me - j) * rows
        rows_w = pick(mine, wq, wk)
        rows_v = pick(mine, do, v)
        rows_f = pick(mine, q, k)
        other_w = view[0:rows, :]
        other_v = view[rows : 2 * rows, :]
        other_f = wide(view, feat_at, nf)
        st = stat_ref[j]
        zero = jnp.zeros((1, rows), f32)
        cum = st[4:5, :]
        gap = between(totals, jnp.minimum(me, j), jnp.maximum(me, j))
        e_r = jnp.exp(jnp.minimum(gap + pick(mine, cum[:, rows - 1 : rows] - cum, cum), 0.0))
        e_r = e_r * pick(mine, 1.0, st[2:3, :])
        e_c = pick(mine, growth_c, tail_c)

        s = nt(rows_w, other_w) * scale
        p = jnp.exp(s - pick(mine, lse_c, 0.0) - pick(mine, zero, st[0:1, :]))
        p = jnp.where(apart * sign < limit, p, 0.0)
        dp = nt(rows_v, other_v)
        ds = p * (dp - pick(mine, dw_c, 0.0) - pick(mine, zero, st[1:2, :]))
        more_w = nn(ds.astype(bf16), other_w)
        x = nn(rows_f, other_f) * feat_scale
        e = e_r * e_c
        dx = (dp - pick(mine, dl_c, 0.0) - pick(mine, zero, st[3:4, :])) * e * (1.0 + x)
        more_f = nt(other_f, dx.astype(bf16))
        more_v = nn((p + (1.0 + x + 0.5 * x * x) * e).astype(bf16), other_v)
        dwq = dwq + pick(mine, more_w, 0.0)
        dwk = dwk + pick(mine, 0.0, more_w)
        dqt = dqt + pick(mine, more_f, 0.0)
        dkt = dkt + pick(mine, 0.0, more_f)
        dv = dv + pick(mine, 0.0, more_v)
        return dwq, dqt, dwk, dkt, dv

    dwq, dqt, dwk, dkt, dv = over_partners(count, step, (dwq, dqt, dwk, dkt, dv))
    grad_ref[0:rows, :] = (dwq * scale).astype(bf16)
    grad_ref[rows : 2 * rows, :] = (dwk * scale).astype(bf16)
    grad_ref[2 * rows : 3 * rows, :] = dv.astype(bf16)
    dft = (jnp.concatenate([dqt, dkt], axis=0) * feat_scale).astype(bf16)
    put_wide(grad_ref, 3 * rows, dft)


def gather_rows(grad_ref, order, cat_ref, feat_ref):
    rows = cat_ref.shape[0]
    nf2 = feat_ref.shape[1] // len(order)
    for at, h in enumerate(order):
        for part in range(3):
            lane = (3 * at + part) * LANES
            cat_ref[:, lane : lane + LANES] = grad_ref[h, part * rows : (part + 1) * rows, :]
    dft = jnp.concatenate([wide(grad_ref.at[h], 3 * rows, nf2) for h in order], axis=0)
    feat_ref[...] = jnp.transpose(dft.astype(f32)).astype(bf16)


def share_kernel(grad_ref, own_ref, *rest):
    heads = grad_ref.shape[0]
    near, far = rest[: heads - 1], rest[heads - 1 : 2 * heads - 2]
    common_ref, share_ref, cat_ref, feat_ref = rest[-4:]
    nf2 = feat_ref.shape[1] // heads
    head, core = lax.axis_index("tp"), lax.axis_index("core")
    gather_rows(
        grad_ref, [head] + [jnp.bitwise_xor(head, t) for t in range(1, heads)], cat_ref, feat_ref
    )
    common, share = common_ref.shape[1] // 2, share_ref.shape[1] // 2

    def product(sides, at, size, chunks):
        main = jnp.concatenate(
            [
                jnp.concatenate(
                    [v[at + m * size : at + (m + 1) * size, :] for v in views for m in range(3)],
                    axis=1,
                )
                for views in sides
            ],
            axis=0,
        )
        feats = jnp.concatenate(
            [
                jnp.concatenate(
                    [
                        sides[k][h][at + 3 * size + m * nf2 : at + 3 * size + (m + 1) * nf2, :]
                        for k, m in chunks
                    ],
                    axis=1,
                )
                for h in range(heads)
            ],
            axis=0,
        )
        return (nt(cat_ref[...], main) + nn(feat_ref[...], feats)).astype(bf16)

    for flag, zero, one in ((0, near, far), (1, far, near)):

        @pl.when(core == flag)
        def _():
            sides = [[own_ref.at[0], *zero], [own_ref.at[1], *one]]
            share_ref[...] = product(sides, area(common, nf2), share, ((0, 0), (0, 1), (1, 1)))
            common_ref[...] = product(sides, 0, common, ((0, 0), (0, 1), (1, 0), (1, 1)))


def lay_kernel(common_ref, share_ref, out_ref):
    first = common_ref.shape[1]
    shares, _, width = share_ref.shape
    out_ref[:, 0:first] = common_ref[...]
    for z in range(shares):
        out_ref[:, first + z * width : first + (z + 1) * width] = share_ref[z]


def merge_kernel(grad_ref, weight_ref, out_ref, cat_ref, feat_ref):
    heads = grad_ref.shape[0]
    tile = out_ref.shape[1]
    lanes = 3 * LANES
    nf2 = feat_ref.shape[1] // heads

    @pl.when(pl.program_id(0) == 0)
    def _():
        gather_rows(grad_ref, range(heads), cat_ref, feat_ref)

    views = [weight_ref.at[h] for h in range(heads)]
    main = jnp.concatenate([v[:, 0:lanes] for v in views], axis=1)
    feats = jnp.concatenate([v[:, lanes:] for v in views], axis=1)
    out_ref[...] = (nt(cat_ref[...], main) + nt(feat_ref[...], feats)).astype(bf16)


VMEM = pl.BlockSpec(memory_space=pltpu.VMEM)
HBM = pl.BlockSpec(memory_space=pltpu.HBM)
params = pltpu.CompilerParams(vmem_limit_bytes=32 * 1024 * 1024)


def in_hbm(*arrays):
    return [pltpu.with_memory_space_constraint(a, pltpu.HBM) for a in arrays]


def cost(flops, nbytes, exps=0):
    return pl.CostEstimate(flops=flops, bytes_accessed=nbytes, transcendentals=exps)


def merge(grads, weights, rows, dim):
    heads, _, columns = weights.shape
    tile = 2 * LANES
    return pl.pallas_call(
        merge_kernel,
        out_shape=jax.ShapeDtypeStruct((rows, dim), bf16),
        grid=(dim // tile,),
        in_specs=[
            pl.BlockSpec(grads.shape, lambda i: (0, 0, 0)),
            pl.BlockSpec((heads, tile, columns), lambda i: (0, i, 0)),
        ],
        out_specs=pl.BlockSpec((rows, tile), lambda i: (0, i)),
        scratch_shapes=[
            pltpu.VMEM((rows, 3 * LANES * heads), bf16),
            pltpu.VMEM((rows, (columns - 3 * LANES) * heads), bf16),
        ],
        compiler_params=params,
        cost_estimate=cost(2 * rows * dim * heads * columns, heads * dim * columns * 2),
        name="head_sum",
    )(grads, weights)


def per_device(tokens, feature_weight, window_weight, value_weight, log_decay, out_grad):
    rows, dim = tokens.shape
    nf2 = feature_weight.shape[1]
    nf = nf2 // 2
    dh = value_weight.shape[1]
    columns = 3 * dh + nf2
    chips, count, heads = lax.axis_size("chip"), lax.axis_size(CTX), lax.axis_size("tp")
    tile = 2 * LANES
    fw_t = feature_weight.T

    payload = 2 * rows + 2 * nf + 16
    block = jax.ShapeDtypeStruct((payload, LANES), bf16)
    *sends, own, query, feat, cum = pl.pallas_call(
        project_kernel,
        out_shape=[block] * (chips + 2)
        + [
            jax.ShapeDtypeStruct((rows, nf2), bf16),
            jax.ShapeDtypeStruct((rows, 1), f32),
        ],
        in_specs=[HBM] * 6,
        out_specs=[VMEM] * (chips + 4),
        scratch_shapes=[
            pltpu.VMEM((rows, dim), bf16),
            pltpu.VMEM((nf2, dim), bf16),
            pltpu.VMEM((dim, 2 * dh), bf16),
            pltpu.VMEM((dim, dh), bf16),
            pltpu.VMEM((1, rows), f32),
            pltpu.VMEM((rows, dh), bf16),
            pltpu.SemaphoreType.DMA((CHUNKS, 4)),
            pltpu.SemaphoreType.DMA((2,)),
        ],
        compiler_params=params,
        cost_estimate=cost(2 * rows * dim * columns, 4 * 1024 * 1024),
        name="project",
    )(*in_hbm(tokens, fw_t, window_weight, value_weight, log_decay.T, out_grad))

    common, share = columns_of(dim, heads)
    shared = heads & (heads - 1) == 0 and common == 2 * LANES and share * 2 == 3 * LANES
    if shared:
        sources, _ = lax.optimization_barrier(((window_weight, value_weight, fw_t), sends[0]))
        height = area(common, nf2) + area(share, nf2)
        own_weights, *packed = pl.pallas_call(
            pack_kernel,
            out_shape=[jax.ShapeDtypeStruct((2, height, LANES), bf16)]
            + [jax.ShapeDtypeStruct((height, LANES), bf16)] * (heads - 1),
            in_specs=[HBM] * 3,
            out_specs=[VMEM] * heads,
            scratch_shapes=[pltpu.SemaphoreType.DMA((heads + 1, 10))],
            compiler_params=params,
            cost_estimate=cost(1, 2 * height * LANES * (heads + 1) * 2),
            name="pack",
        )(*in_hbm(*sources))
        near = [
            lax.ppermute(packed[t - 1], "tp", [(z, z ^ t) for z in range(heads)])
            for t in range(1, heads)
        ]

    swap = [(0, 1), (1, 0)]
    recv = {}
    for d in range(1, chips):
        recv[2 * d] = lax.ppermute(sends[d], "chip", [(i, i ^ d) for i in range(chips)])
    recv[1] = lax.ppermute(sends[0], "core", swap)
    if shared:
        recv, packed = lax.optimization_barrier((recv, packed))
    for d in range(1, chips):
        recv[2 * d + 1] = lax.ppermute(recv[2 * d], "core", swap)
    recv = [recv[d] for d in range(1, count)]
    if count > 8:
        recv = [jnp.stack(recv)]

    attended, stat, sheet = pl.pallas_call(
        lambda *refs: query_kernel(count, *refs),
        out_shape=(
            jax.ShapeDtypeStruct((rows, dh), bf16),
            jax.ShapeDtypeStruct((8, rows), f32),
            jax.ShapeDtypeStruct((rows, LANES), f32),
        ),
        in_specs=[VMEM] * (len(recv) + 4),
        out_specs=[VMEM] * 3,
        scratch_shapes=[
            pltpu.VMEM((count, 2 * rows, dh), bf16),
            pltpu.VMEM((WINDOW // rows + 1, rows, rows), f32),
            pltpu.VMEM((count, rows), f32),
        ],
        compiler_params=params,
        cost_estimate=cost(10**9, 2 * 1024 * 1024, 10**6),
        name="query_side",
    )(*recv, own, query, feat, cum)
    stats = lax.all_gather(stat, CTX)
    grads = pl.pallas_call(
        lambda *refs: gradient_kernel(count, *refs),
        out_shape=jax.ShapeDtypeStruct((3 * rows + nf2 * rows // LANES, LANES), bf16),
        in_specs=[VMEM] * (len(recv) + 5),
        out_specs=VMEM,
        compiler_params=params,
        cost_estimate=cost(10**9, 2 * 1024 * 1024, 10**6),
        name="gradients",
    )(*recv, own, query, feat, sheet, stats)
    if not shared:
        weights = jnp.concatenate([window_weight, value_weight, feature_weight], axis=1)
        weights = lax.all_gather(weights, "tp")
        return (attended, merge(lax.all_gather(grads, "tp"), weights, rows, dim))

    near, grads = lax.optimization_barrier((near, grads))
    far = [lax.ppermute(n, "core", swap) for n in near]
    grads = lax.all_gather(grads, "tp")
    first, rest = pl.pallas_call(
        share_kernel,
        out_shape=[
            jax.ShapeDtypeStruct((rows, 2 * common), bf16),
            jax.ShapeDtypeStruct((rows, 2 * share), bf16),
        ],
        in_specs=[VMEM] * (2 * heads),
        out_specs=[VMEM] * 2,
        scratch_shapes=[
            pltpu.VMEM((rows, 3 * LANES * heads), bf16),
            pltpu.VMEM((rows, nf2 * heads), bf16),
        ],
        compiler_params=params,
        cost_estimate=cost(
            4 * rows * (common + share) * heads * columns, 4 * heads * height * LANES
        ),
        name="share",
    )(grads, own_weights, *near, *far)
    total = pl.pallas_call(
        lay_kernel,
        out_shape=jax.ShapeDtypeStruct((rows, dim), bf16),
        in_specs=[VMEM] * 2,
        out_specs=VMEM,
        compiler_params=params,
        cost_estimate=cost(1, 4 * rows * dim),
        name="lay",
    )(first, lax.all_gather(rest, "tp"))
    return (attended, total)


def solution(mesh):
    ctx, tp = mesh.devices.shape
    split = Mesh(mesh.devices.reshape(ctx // 2, 2, tp), ("chip", "core", "tp"))
    in_specs = (
        P(CTX, None),
        P(None, "tp"),
        P(None, "tp"),
        P(None, "tp"),
        P(CTX, "tp"),
        P(CTX, "tp"),
    )
    out_specs = (P(CTX, "tp"), P(CTX, None))
    return jax.shard_map(
        per_device, mesh=split, in_specs=in_specs, out_specs=out_specs, check_vma=False
    )
```

```python
import jax
import jax.numpy as jnp
from jax import lax
from jax.experimental import pallas as pl
from jax.experimental.pallas import tpu as pltpu
from jax.sharding import Mesh
from jax.sharding import PartitionSpec as P

WINDOW = 1024
LANES = 128
MASKED = -1e30
CTX = ("chip", "core")
CHUNKS = 4
f32 = jnp.float32
bf16 = jnp.bfloat16


def nn(a, b):
    return lax.dot_general(a, b, (((1,), (0,)), ((), ())), preferred_element_type=f32)


def nt(a, b):
    return lax.dot_general(a, b, (((1,), (1,)), ((), ())), preferred_element_type=f32)


def partner(me, d, count):
    assert count & (count - 1) == 0
    return jnp.bitwise_xor(me, d)


def wide(view, start, count):
    return jnp.concatenate(
        [view[start : start + count, :], view[start + count : start + 2 * count, :]], axis=1
    )


def put_wide(ref, start, value):
    count = value.shape[0]
    for half in range(value.shape[1] // LANES):
        ref[start + half * count : start + (half + 1) * count, :] = value[
            :, half * LANES : (half + 1) * LANES
        ]


def cum_row(view, start):
    tail = view[start : start + 16, :].astype(f32)
    first = tail[0:1] + tail[2:3] + tail[4:5]
    second = tail[1:2] + tail[3:4] + tail[5:6]
    return jnp.concatenate([first, second], axis=1)


def iotas(rows):
    return (
        lax.broadcasted_iota(jnp.int32, (rows, rows), 0),
        lax.broadcasted_iota(jnp.int32, (rows, rows), 1),
    )


def block_index():
    return lax.axis_index("chip") * lax.axis_size("core") + lax.axis_index("core")


def pack_copies(ww_hbm, vw_hbm, fw_hbm, own_ref, sends, sems):
    head, core = lax.axis_index("tp"), lax.axis_index("core")
    nf2 = fw_hbm.shape[0]
    tile = own_ref.shape[1] * LANES // (3 * LANES + nf2)
    parts = [(ref, 2 * jnp.bitwise_xor(head, t + 1) + core) for t, ref in enumerate(sends)]
    parts += [(own_ref.at[k], 2 * head + k) for k in range(2)]
    copies = []
    for n, (ref, piece) in enumerate(parts):
        rows = pl.ds(pl.multiple_of(piece * tile, tile), tile)
        moves = [
            (ww_hbm.at[rows, pl.ds(0, LANES)], ref.at[pl.ds(0, tile), :]),
            (ww_hbm.at[rows, pl.ds(LANES, LANES)], ref.at[pl.ds(tile, tile), :]),
            (vw_hbm.at[rows, :], ref.at[pl.ds(2 * tile, tile), :]),
        ]
        for m in range(tile // LANES):
            lanes = pl.ds(pl.multiple_of(piece * tile + m * LANES, LANES), LANES)
            moves.append((fw_hbm.at[:, lanes], ref.at[pl.ds(3 * tile + m * nf2, nf2), :]))
        for m, (src, dst) in enumerate(moves):
            copies.append(pltpu.make_async_copy(src, dst, sems.at[n, m]))
    return copies


def project_kernel(packs, tok_hbm, fw_hbm, ww_hbm, vw_hbm, ld_hbm, do_hbm, *rest):
    *sends, keys_ref, query_ref, feat_ref, cum_ref = rest[packs:-9]
    tok_ref, fw_ref, ww_ref, vw_ref, ld_ref, do_ref, sems, small, pack_sems = rest[-9:]
    me = block_index()
    rows, dim = tok_ref.shape
    dh = do_ref.shape[1]
    nf = fw_ref.shape[0] // 2
    span = dim // CHUNKS
    copies = []
    for c in range(CHUNKS):
        part = pl.ds(c * span, span)
        copies.append([
            pltpu.make_async_copy(tok_hbm.at[:, part], tok_ref.at[:, part], sems.at[c, 0]),
            pltpu.make_async_copy(ww_hbm.at[part, :], ww_ref.at[part, :], sems.at[c, 1]),
            pltpu.make_async_copy(vw_hbm.at[part, :], vw_ref.at[part, :], sems.at[c, 2]),
            pltpu.make_async_copy(fw_hbm.at[:, part], fw_ref.at[:, part], sems.at[c, 3]),
        ])
    others = [
        pltpu.make_async_copy(ld_hbm, ld_ref, small.at[0]),
        pltpu.make_async_copy(do_hbm, do_ref, small.at[1]),
    ]
    for copy in copies[0] + others:
        copy.start()
    for group in copies[1:]:
        for copy in group:
            copy.start()
    packing = pack_copies(ww_hbm, vw_hbm, fw_hbm, rest[0], rest[1:packs], pack_sems) if packs else []
    for copy in packing:
        copy.start()
    for copy in others:
        copy.wait()
    at_row, at_col = iotas(rows)
    ld_r = ld_ref[...]
    ld_c = jnp.sum(jnp.where(at_row == at_col, ld_r, 0.0), axis=1, keepdims=True)
    cum_r = jnp.sum(jnp.where(at_row <= at_col, ld_c, 0.0), axis=0, keepdims=True)
    cum_ref[...] = jnp.sum(jnp.where(at_col <= at_row, ld_r, 0.0), axis=1, keepdims=True)
    high = cum_r.astype(bf16)
    left = cum_r - high.astype(f32)
    mid = left.astype(bf16)
    low = (left - mid.astype(f32)).astype(bf16)
    pieces = [t[:, h : h + LANES].astype(f32) for t in (high, mid, low) for h in range(0, rows, LANES)]
    tail = jnp.concatenate(pieces + [jnp.zeros((10, LANES), f32)], axis=0).astype(bf16)

    feat = jnp.zeros((rows, 2 * nf), f32)
    main = jnp.zeros((rows, 3 * dh), f32)
    for c in range(CHUNKS):
        for copy in copies[c]:
            copy.wait()
        part = slice(c * span, (c + 1) * span)
        tok = tok_ref[:, part]
        feat += nt(tok, fw_ref[:, part])
        main += nn(tok, jnp.concatenate([ww_ref[part, :], vw_ref[part, :]], axis=1))
    feat = feat.astype(bf16)
    window = main[:, : 2 * dh].astype(bf16)
    values = main[:, 2 * dh :].astype(bf16)
    feat_ref[...] = feat
    small_row, small_col = iotas(2 * nf)
    feat_t = nt((small_row == small_col).astype(bf16), feat).astype(bf16)
    feat_at = 2 * rows
    tail_at = feat_at + 2 * nf

    def put_keys(ref):
        ref[0:rows, :] = window[:, dh:]
        ref[rows : 2 * rows, :] = values
        put_wide(ref, feat_at, feat_t[nf:, :])
        ref[tail_at : tail_at + 16, :] = tail

    def put_query(ref):
        ref[0:rows, :] = window[:, :dh]
        ref[rows : 2 * rows, :] = do_ref[...]
        put_wide(ref, feat_at, feat_t[:nf, :])
        ref[tail_at : tail_at + 16, :] = tail

    put_keys(keys_ref)
    put_query(query_ref)
    for at, ref in enumerate(sends):
        later = jnp.bitwise_xor(me, max(2 * at, 1)) > me
        pl.when(later)(lambda ref=ref: put_keys(ref))
        pl.when(jnp.logical_not(later))(lambda ref=ref: put_query(ref))
    for copy in packing:
        copy.wait()


def between(totals, low, high):
    at = lax.broadcasted_iota(jnp.int32, totals.shape, 0)
    return jnp.sum(jnp.where((at > low) & (at < high), totals, 0.0), axis=0, keepdims=True)


def over_partners(count, body, carry):
    if count <= 8:
        for d in range(1, count):
            carry = body(d, carry)
        return carry
    return lax.fori_loop(1, count, body, carry)


def query_kernel(count, *rest):
    recvs = rest[: -10]
    (own_ref, query_ref, feat_ref, cum_ref, att_ref, stat_ref, sheet_ref, near_ref, p_ref,
     cums_ref) = rest[-10:]

    def recv(d):
        return recvs[d - 1] if len(recvs) > 1 else recvs[0].at[d - 1]

    me = block_index()
    rows, dh = att_ref.shape
    nf = feat_ref.shape[1] // 2
    back = WINDOW // rows
    feat_at = 2 * rows
    tail_at = feat_at + 2 * nf
    scale = dh ** (-0.5)
    feat_scale = nf ** (-0.5)
    wq = query_ref[0:rows, :]
    do = query_ref[rows : 2 * rows, :]
    q = feat_ref[:, :nf]
    at_row, at_col = iotas(rows)
    own_cum = cum_row(own_ref, tail_at)
    cums_ref[pl.ds(me, 1), :] = own_cum
    near_ref[me] = own_ref[0 : 2 * rows, :]

    def gather(d, carry):
        j = partner(me, d, count)
        view = recv(d)
        near_ref[j] = view[0 : 2 * rows, :]
        cums_ref[pl.ds(j, 1), :] = cum_row(view, tail_at)
        return carry

    over_partners(count, gather, 0)

    def near(w):
        return near_ref.at[jnp.maximum(me - back + w, 0)]

    top = jnp.full((rows, LANES), MASKED, f32)
    for w in range(back + 1):
        keys = own_ref[0:rows, :] if w == back else near(w)[0:rows, :]
        s = nt(wq, keys) * scale
        if w == back:
            s = jnp.where(at_col <= at_row, s, MASKED)
        elif w == 0:
            s = jnp.where((at_col > at_row) & (me >= back), s, MASKED)
        else:
            s = jnp.where(me >= back - w, s, MASKED)
        p_ref[w] = s
        for h in range(0, rows, LANES):
            top = jnp.maximum(top, s[:, h : h + LANES])
    top = jnp.max(top, axis=1, keepdims=True)
    total = jnp.zeros((rows, LANES), f32)
    out = jnp.zeros((rows, dh), f32)
    for w in range(back + 1):
        p = jnp.exp(p_ref[w] - top)
        for h in range(0, rows, LANES):
            total += p[:, h : h + LANES]
        vals = own_ref[rows : 2 * rows, :] if w == back else near(w)[rows : 2 * rows, :]
        out += nn(p.astype(bf16), vals)
    total = jnp.sum(total, axis=1, keepdims=True)
    windowed = out * (1.0 / total)

    cum_c = cum_ref[...]
    growth = jnp.exp(cum_c)
    totals = cums_ref[:, rows - 1 : rows]

    def forward(d, carry):
        num, den = carry
        j = partner(me, d, count)
        view = recv(d)
        gap = between(totals, j - 1, me)
        es = jnp.where(j < me, jnp.exp(jnp.minimum(gap - cums_ref[pl.ds(j, 1), :], 0.0)), 0.0)
        x = nn(q, wide(view, feat_at, nf)) * feat_scale
        weight = (1.0 + x + 0.5 * x * x) * es
        for h in range(0, rows, LANES):
            den += weight[:, h : h + LANES]
        num += nn(weight.astype(bf16), view[rows : 2 * rows, :])
        return num, den

    num, den = over_partners(
        count, forward, (jnp.zeros((rows, dh), f32), jnp.zeros((rows, LANES), f32))
    )
    x = nn(q, wide(own_ref, feat_at, nf)) * feat_scale
    e = jnp.where(at_col <= at_row, jnp.exp(jnp.minimum(cum_c - own_cum, 0.0)), 0.0)
    weight = (1.0 + x + 0.5 * x * x) * e
    num = num * growth + nn(weight.astype(bf16), own_ref[rows : 2 * rows, :])
    den = den * growth
    for h in range(0, rows, LANES):
        den += weight[:, h : h + LANES]
    rden = 1.0 / jnp.sum(den, axis=1, keepdims=True)
    linear = num * rden
    att_ref[...] = (linear + windowed).astype(bf16)
    do_f = do.astype(f32)
    delta_w = jnp.sum(do_f * windowed, axis=1, keepdims=True)
    delta_l = jnp.sum(do_f * linear, axis=1, keepdims=True)
    lse = top + jnp.log(total)
    lane = lax.broadcasted_iota(jnp.int32, (rows, LANES), 1)
    sheet = jnp.where(lane == 0, lse, 0.0)
    sheet = jnp.where(lane == 1, delta_w, sheet)
    sheet = jnp.where(lane == 2, rden, sheet)
    sheet = jnp.where(lane == 3, delta_l, sheet)
    sheet = jnp.where(lane == 4, cum_c, sheet)
    sheet_ref[...] = sheet
    stat_ref[...] = jnp.transpose(sheet)[0:8, :]


def gradient_kernel(count, *rest):
    recvs = rest[:-6]
    own_ref, query_ref, feat_ref, sheet_ref, stat_ref, grad_ref = rest[-6:]

    def recv(d):
        return recvs[d - 1] if len(recvs) > 1 else recvs[0].at[d - 1]

    me = block_index()
    rows = feat_ref.shape[0]
    dh = LANES
    nf = feat_ref.shape[1] // 2
    feat_at = 2 * rows
    scale = dh ** (-0.5)
    feat_scale = nf ** (-0.5)
    at_row, at_col = iotas(rows)
    apart = at_row - at_col
    wq, wk = query_ref[0:rows, :], own_ref[0:rows, :]
    do, v = query_ref[rows : 2 * rows, :], own_ref[rows : 2 * rows, :]
    q, k = feat_ref[:, :nf], feat_ref[:, nf:]
    lse_c, dw_c = sheet_ref[:, 0:1], sheet_ref[:, 1:2]
    rden_c, dl_c, cum_c = sheet_ref[:, 2:3], sheet_ref[:, 3:4], sheet_ref[:, 4:5]
    mine_ref = stat_ref.at[me]
    own_cum = mine_ref[4:5, :]
    totals = jnp.concatenate([stat_ref[j, 4:5, rows - 1 : rows] for j in range(count)], axis=0)
    growth_c = jnp.exp(cum_c) * rden_c
    tail_c = jnp.exp(own_cum[:, rows - 1 : rows] - cum_c)

    def pick(flag, a, b):
        return jnp.where(flag, a, b)

    s = nt(wq, wk) * scale
    causal = at_col <= at_row
    p = jnp.where(causal, jnp.exp(s - lse_c), 0.0)
    dp = nt(do, v)
    dwq = nn((p * (dp - dw_c)).astype(bf16), wk)
    x = nn(q, wide(own_ref, feat_at, nf)) * feat_scale
    e = jnp.where(causal, jnp.exp(jnp.minimum(cum_c - own_cum, 0.0)), 0.0) * rden_c
    dx = (dp - dl_c) * e * (1.0 + x)
    dqt = nt(wide(own_ref, feat_at, nf), dx.astype(bf16))

    s = nt(wk, wq) * scale
    causal = at_row <= at_col
    p = jnp.where(causal, jnp.exp(s - mine_ref[0:1, :]), 0.0)
    dp = nt(v, do)
    dwk = nn((p * (dp - mine_ref[1:2, :])).astype(bf16), wq)
    x = nn(k, wide(query_ref, feat_at, nf)) * feat_scale
    e = jnp.where(causal, jnp.exp(jnp.minimum(own_cum - cum_c, 0.0)), 0.0) * mine_ref[2:3, :]
    dx = (dp - mine_ref[3:4, :]) * e * (1.0 + x)
    dkt = nt(wide(query_ref, feat_at, nf), dx.astype(bf16))
    dv = nn((p + (1.0 + x + 0.5 * x * x) * e).astype(bf16), do)

    def step(d, carry):
        dwq, dqt, dwk, dkt, dv = carry
        j = partner(me, d, count)
        view = recv(d)
        mine = j < me
        sign = pick(mine, 1, -1)
        limit = WINDOW - jnp.abs(me - j) * rows
        rows_w = pick(mine, wq, wk)
        rows_v = pick(mine, do, v)
        rows_f = pick(mine, q, k)
        other_w = view[0:rows, :]
        other_v = view[rows : 2 * rows, :]
        other_f = wide(view, feat_at, nf)
        st = stat_ref[j]
        zero = jnp.zeros((1, rows), f32)
        cum = st[4:5, :]
        gap = between(totals, jnp.minimum(me, j), jnp.maximum(me, j))
        e_r = jnp.exp(jnp.minimum(gap + pick(mine, cum[:, rows - 1 : rows] - cum, cum), 0.0))
        e_r = e_r * pick(mine, 1.0, st[2:3, :])
        e_c = pick(mine, growth_c, tail_c)

        s = nt(rows_w, other_w) * scale
        p = jnp.exp(s - pick(mine, lse_c, 0.0) - pick(mine, zero, st[0:1, :]))
        p = jnp.where(apart * sign < limit, p, 0.0)
        dp = nt(rows_v, other_v)
        ds = p * (dp - pick(mine, dw_c, 0.0) - pick(mine, zero, st[1:2, :]))
        more_w = nn(ds.astype(bf16), other_w)
        x = nn(rows_f, other_f) * feat_scale
        e = e_r * e_c
        dx = (dp - pick(mine, dl_c, 0.0) - pick(mine, zero, st[3:4, :])) * e * (1.0 + x)
        more_f = nt(other_f, dx.astype(bf16))
        more_v = nn((p + (1.0 + x + 0.5 * x * x) * e).astype(bf16), other_v)
        dwq = dwq + pick(mine, more_w, 0.0)
        dwk = dwk + pick(mine, 0.0, more_w)
        dqt = dqt + pick(mine, more_f, 0.0)
        dkt = dkt + pick(mine, 0.0, more_f)
        dv = dv + pick(mine, 0.0, more_v)
        return dwq, dqt, dwk, dkt, dv

    dwq, dqt, dwk, dkt, dv = over_partners(count, step, (dwq, dqt, dwk, dkt, dv))
    grad_ref[0:rows, :] = (dwq * scale).astype(bf16)
    grad_ref[rows : 2 * rows, :] = (dwk * scale).astype(bf16)
    grad_ref[2 * rows : 3 * rows, :] = dv.astype(bf16)
    dft = (jnp.concatenate([dqt, dkt], axis=0) * feat_scale).astype(bf16)
    put_wide(grad_ref, 3 * rows, dft)


def gather_rows(grad_ref, order, cat_ref, feat_ref):
    rows = cat_ref.shape[0]
    nf2 = feat_ref.shape[1] // len(order)
    for at, h in enumerate(order):
        for part in range(3):
            lane = (3 * at + part) * LANES
            cat_ref[:, lane : lane + LANES] = grad_ref[h, part * rows : (part + 1) * rows, :]
    dft = jnp.concatenate([wide(grad_ref.at[h], 3 * rows, nf2) for h in order], axis=0)
    feat_ref[...] = jnp.transpose(dft.astype(f32)).astype(bf16)


def share_kernel(grad_ref, own_ref, *rest):
    heads = grad_ref.shape[0]
    near, far = rest[: heads - 1], rest[heads - 1 : 2 * heads - 2]
    most_ref, last_ref, cat_ref, feat_ref = rest[-4:]
    nf2 = feat_ref.shape[1] // heads
    head, core = lax.axis_index("tp"), lax.axis_index("core")
    gather_rows(
        grad_ref, [head] + [jnp.bitwise_xor(head, t) for t in range(1, heads)], cat_ref, feat_ref
    )
    most = most_ref.shape[0]
    tile = most_ref.shape[1] // 2

    def product(k, views):
        main = jnp.concatenate(
            [v[m * tile : (m + 1) * tile, :] for v in views for m in range(3)], axis=1
        )
        feats = jnp.concatenate([wide(v, 3 * tile, nf2) for v in views], axis=0)
        out = (nt(cat_ref[...], main) + nn(feat_ref[...], feats)).astype(bf16)
        most_ref[:, k * tile : (k + 1) * tile] = out[:most]
        last_ref[:, k * tile : (k + 1) * tile] = out[most:]

    for flag, zero, one in ((0, near, far), (1, far, near)):

        @pl.when(core == flag)
        def _():
            product(0, [own_ref.at[0], *zero])
            product(1, [own_ref.at[1], *one])


def lay_kernel(most_ref, own_ref, *rest):
    *lasts, out_ref = rest
    shares, most, width = most_ref.shape
    head = lax.axis_index("tp")
    for z in range(shares):
        out_ref[0:most, z * width : (z + 1) * width] = most_ref[z]
    for t, ref in enumerate([own_ref, *lasts]):
        at = pl.multiple_of(jnp.bitwise_xor(head, t) * width, width)
        out_ref[most:, pl.ds(at, width)] = ref[...]


def merge_kernel(grad_ref, weight_ref, out_ref, cat_ref, feat_ref):
    heads = grad_ref.shape[0]
    tile = out_ref.shape[1]
    lanes = 3 * LANES
    nf2 = feat_ref.shape[1] // heads

    @pl.when(pl.program_id(0) == 0)
    def _():
        gather_rows(grad_ref, range(heads), cat_ref, feat_ref)

    views = [weight_ref.at[h] for h in range(heads)]
    main = jnp.concatenate([v[:, 0:lanes] for v in views], axis=1)
    feats = jnp.concatenate([v[:, lanes:] for v in views], axis=1)
    out_ref[...] = (nt(cat_ref[...], main) + nt(feat_ref[...], feats)).astype(bf16)


VMEM = pl.BlockSpec(memory_space=pltpu.VMEM)
HBM = pl.BlockSpec(memory_space=pltpu.HBM)
params = pltpu.CompilerParams(vmem_limit_bytes=32 * 1024 * 1024)


def in_hbm(*arrays):
    return [pltpu.with_memory_space_constraint(a, pltpu.HBM) for a in arrays]


def cost(flops, nbytes, exps=0):
    return pl.CostEstimate(flops=flops, bytes_accessed=nbytes, transcendentals=exps)


def merge(grads, weights, rows, dim):
    heads, _, columns = weights.shape
    tile = 2 * LANES
    return pl.pallas_call(
        merge_kernel,
        out_shape=jax.ShapeDtypeStruct((rows, dim), bf16),
        grid=(dim // tile,),
        in_specs=[
            pl.BlockSpec(grads.shape, lambda i: (0, 0, 0)),
            pl.BlockSpec((heads, tile, columns), lambda i: (0, i, 0)),
        ],
        out_specs=pl.BlockSpec((rows, tile), lambda i: (0, i)),
        scratch_shapes=[
            pltpu.VMEM((rows, 3 * LANES * heads), bf16),
            pltpu.VMEM((rows, (columns - 3 * LANES) * heads), bf16),
        ],
        compiler_params=params,
        cost_estimate=cost(2 * rows * dim * heads * columns, heads * dim * columns * 2),
        name="head_sum",
    )(grads, weights)


def per_device(tokens, feature_weight, window_weight, value_weight, log_decay, out_grad):
    rows, dim = tokens.shape
    nf2 = feature_weight.shape[1]
    nf = nf2 // 2
    dh = value_weight.shape[1]
    columns = 3 * dh + nf2
    chips, count, heads = lax.axis_size("chip"), lax.axis_size(CTX), lax.axis_size("tp")
    tile = 2 * LANES
    fw_t = feature_weight.T

    shared = heads & (heads - 1) == 0 and 2 * tile * heads == dim
    height = 3 * tile + nf2 * tile // LANES
    packs = []
    if shared:
        packs = [jax.ShapeDtypeStruct((2, height, LANES), bf16)]
        packs += [jax.ShapeDtypeStruct((height, LANES), bf16)] * (heads - 1)

    payload = 2 * rows + 2 * nf + 16
    block = jax.ShapeDtypeStruct((payload, LANES), bf16)
    outs = pl.pallas_call(
        lambda *refs: project_kernel(len(packs), *refs),
        out_shape=packs
        + [block] * (chips + 2)
        + [
            jax.ShapeDtypeStruct((rows, nf2), bf16),
            jax.ShapeDtypeStruct((rows, 1), f32),
        ],
        in_specs=[HBM] * 6,
        out_specs=[VMEM] * (len(packs) + chips + 4),
        scratch_shapes=[
            pltpu.VMEM((rows, dim), bf16),
            pltpu.VMEM((nf2, dim), bf16),
            pltpu.VMEM((dim, 2 * dh), bf16),
            pltpu.VMEM((dim, dh), bf16),
            pltpu.VMEM((1, rows), f32),
            pltpu.VMEM((rows, dh), bf16),
            pltpu.SemaphoreType.DMA((CHUNKS, 4)),
            pltpu.SemaphoreType.DMA((2,)),
            pltpu.SemaphoreType.DMA((heads + 1, 3 + tile // LANES)),
        ],
        compiler_params=params,
        cost_estimate=cost(2 * rows * dim * columns, 4 * 1024 * 1024),
        name="project",
    )(*in_hbm(tokens, fw_t, window_weight, value_weight, log_decay.T, out_grad))
    packed, (*sends, own, query, feat, cum) = outs[: len(packs)], outs[len(packs) :]
    near = [
        lax.ppermute(p, "tp", [(z, z ^ t) for z in range(heads)])
        for t, p in enumerate(packed)
        if t
    ]

    swap = [(0, 1), (1, 0)]
    recv = {}
    for d in range(1, chips):
        recv[2 * d] = lax.ppermute(sends[d], "chip", [(i, i ^ d) for i in range(chips)])
    recv[1] = lax.ppermute(sends[0], "core", swap)
    for d in range(1, chips):
        recv[2 * d + 1] = lax.ppermute(recv[2 * d], "core", swap)
    recv = [recv[d] for d in range(1, count)]
    if count > 8:
        recv = [jnp.stack(recv)]

    attended, stat, sheet = pl.pallas_call(
        lambda *refs: query_kernel(count, *refs),
        out_shape=(
            jax.ShapeDtypeStruct((rows, dh), bf16),
            jax.ShapeDtypeStruct((8, rows), f32),
            jax.ShapeDtypeStruct((rows, LANES), f32),
        ),
        in_specs=[VMEM] * (len(recv) + 4),
        out_specs=[VMEM] * 3,
        scratch_shapes=[
            pltpu.VMEM((count, 2 * rows, dh), bf16),
            pltpu.VMEM((WINDOW // rows + 1, rows, rows), f32),
            pltpu.VMEM((count, rows), f32),
        ],
        compiler_params=params,
        cost_estimate=cost(10**9, 2 * 1024 * 1024, 10**6),
        name="query_side",
    )(*recv, own, query, feat, cum)
    stats = lax.all_gather(stat, CTX)
    grads = pl.pallas_call(
        lambda *refs: gradient_kernel(count, *refs),
        out_shape=jax.ShapeDtypeStruct((3 * rows + nf2 * rows // LANES, LANES), bf16),
        in_specs=[VMEM] * (len(recv) + 5),
        out_specs=VMEM,
        compiler_params=params,
        cost_estimate=cost(10**9, 2 * 1024 * 1024, 10**6),
        name="gradients",
    )(*recv, own, query, feat, sheet, stats)
    if not shared:
        weights = jnp.concatenate([window_weight, value_weight, feature_weight], axis=1)
        weights = lax.all_gather(weights, "tp")
        return (attended, merge(lax.all_gather(grads, "tp"), weights, rows, dim))

    near, grads = lax.optimization_barrier((near, grads))
    far = [lax.ppermute(n, "core", swap) for n in near]
    grads = lax.all_gather(grads, "tp")
    last = 16
    sums, ends = pl.pallas_call(
        share_kernel,
        out_shape=[
            jax.ShapeDtypeStruct((rows - last, 2 * tile), bf16),
            jax.ShapeDtypeStruct((last, 2 * tile), bf16),
        ],
        in_specs=[VMEM] * (2 * heads),
        out_specs=[VMEM] * 2,
        scratch_shapes=[
            pltpu.VMEM((rows, 3 * LANES * heads), bf16),
            pltpu.VMEM((rows, nf2 * heads), bf16),
        ],
        compiler_params=params,
        cost_estimate=cost(4 * rows * tile * heads * columns, 4 * heads * height * LANES),
        name="share",
    )(grads, packed[0], *near, *far)
    others = [
        lax.ppermute(ends, "tp", [(z, z ^ t) for z in range(heads)]) for t in range(1, heads)
    ]
    total = pl.pallas_call(
        lay_kernel,
        out_shape=jax.ShapeDtypeStruct((rows, dim), bf16),
        in_specs=[VMEM] * (heads + 1),
        out_specs=VMEM,
        compiler_params=params,
        cost_estimate=cost(1, 4 * rows * dim),
        name="lay",
    )(lax.all_gather(sums, "tp"), ends, *others)
    return (attended, total)


def solution(mesh):
    ctx, tp = mesh.devices.shape
    split = Mesh(mesh.devices.reshape(ctx // 2, 2, tp), ("chip", "core", "tp"))
    in_specs = (
        P(CTX, None),
        P(None, "tp"),
        P(None, "tp"),
        P(None, "tp"),
        P(CTX, "tp"),
        P(CTX, "tp"),
    )
    out_specs = (P(CTX, "tp"), P(CTX, None))
    return jax.shard_map(
        per_device, mesh=split, in_specs=in_specs, out_specs=out_specs, check_vma=False
    )
```

```python
from functools import partial

import jax
import jax.numpy as jnp
from jax import lax
from jax.experimental import pallas as pl
from jax.experimental.pallas import tpu as pltpu
from jax.sharding import Mesh
from jax.sharding import PartitionSpec as P

WINDOW = 1024
LANES = 128
MASKED = -1e30
CHUNKS = 4
f32 = jnp.float32
bf16 = jnp.bfloat16


def nn(a, b):
    return lax.dot_general(a, b, (((1,), (0,)), ((), ())), preferred_element_type=f32)


def nt(a, b):
    return lax.dot_general(a, b, (((1,), (1,)), ((), ())), preferred_element_type=f32)


def partner(me, d, count):
    assert count & (count - 1) == 0
    return jnp.bitwise_xor(me, d)


def wide(view, start, count):
    return jnp.concatenate(
        [view[start : start + count, :], view[start + count : start + 2 * count, :]], axis=1
    )


def put_wide(ref, start, value):
    count = value.shape[0]
    for half in range(value.shape[1] // LANES):
        ref[start + half * count : start + (half + 1) * count, :] = value[
            :, half * LANES : (half + 1) * LANES
        ]


def cum_row(view, start):
    tail = view[start : start + 16, :].astype(f32)
    first = tail[0:1] + tail[2:3] + tail[4:5]
    second = tail[1:2] + tail[3:4] + tail[5:6]
    return jnp.concatenate([first, second], axis=1)


def iotas(rows):
    return (
        lax.broadcasted_iota(jnp.int32, (rows, rows), 0),
        lax.broadcasted_iota(jnp.int32, (rows, rows), 1),
    )


def block_index(ctx):
    place = 0
    for name in ctx:
        place = place * lax.axis_size(name) + lax.axis_index(name)
    return place


def project_kernel(ctx, tok_hbm, fw_hbm, ww_hbm, vw_hbm, ld_hbm, do_hbm, *rest):
    *sends, keys_ref, query_ref, feat_ref, cum_ref, ww_ref, vw_ref, fw_ref = rest[:-5]
    tok_ref, ld_ref, do_ref, sems, small = rest[-5:]
    me = block_index(ctx)
    rows, dim = tok_ref.shape
    dh = do_ref.shape[1]
    nf = fw_ref.shape[0] // 2
    span = dim // CHUNKS
    copies = []
    for c in range(CHUNKS):
        part = pl.ds(c * span, span)
        copies.append([
            pltpu.make_async_copy(tok_hbm.at[:, part], tok_ref.at[:, part], sems.at[c, 0]),
            pltpu.make_async_copy(ww_hbm.at[part, :], ww_ref.at[part, :], sems.at[c, 1]),
            pltpu.make_async_copy(vw_hbm.at[part, :], vw_ref.at[part, :], sems.at[c, 2]),
            pltpu.make_async_copy(fw_hbm.at[:, part], fw_ref.at[:, part], sems.at[c, 3]),
        ])
    others = [
        pltpu.make_async_copy(ld_hbm, ld_ref, small.at[0]),
        pltpu.make_async_copy(do_hbm, do_ref, small.at[1]),
    ]
    for copy in copies[0] + others:
        copy.start()
    for group in copies[1:]:
        for copy in group:
            copy.start()
    for copy in others:
        copy.wait()
    at_row, at_col = iotas(rows)
    ld_r = ld_ref[...]
    ld_c = jnp.sum(jnp.where(at_row == at_col, ld_r, 0.0), axis=1, keepdims=True)
    cum_r = jnp.sum(jnp.where(at_row <= at_col, ld_c, 0.0), axis=0, keepdims=True)
    cum_ref[...] = jnp.sum(jnp.where(at_col <= at_row, ld_r, 0.0), axis=1, keepdims=True)
    high = cum_r.astype(bf16)
    left = cum_r - high.astype(f32)
    mid = left.astype(bf16)
    low = (left - mid.astype(f32)).astype(bf16)
    pieces = [t[:, h : h + LANES].astype(f32) for t in (high, mid, low) for h in range(0, rows, LANES)]
    tail = jnp.concatenate(pieces + [jnp.zeros((10, LANES), f32)], axis=0).astype(bf16)

    feat = jnp.zeros((rows, 2 * nf), f32)
    main = jnp.zeros((rows, 3 * dh), f32)
    for c in range(CHUNKS):
        for copy in copies[c]:
            copy.wait()
        part = slice(c * span, (c + 1) * span)
        tok = tok_ref[:, part]
        feat += nt(tok, fw_ref[:, part])
        main += nn(tok, jnp.concatenate([ww_ref[part, :], vw_ref[part, :]], axis=1))
    feat = feat.astype(bf16)
    window = main[:, : 2 * dh].astype(bf16)
    values = main[:, 2 * dh :].astype(bf16)
    feat_ref[...] = feat
    small_row, small_col = iotas(2 * nf)
    feat_t = nt((small_row == small_col).astype(bf16), feat).astype(bf16)
    feat_at = 2 * rows
    tail_at = feat_at + 2 * nf

    def put_keys(ref):
        ref[0:rows, :] = window[:, dh:]
        ref[rows : 2 * rows, :] = values
        put_wide(ref, feat_at, feat_t[nf:, :])
        ref[tail_at : tail_at + 16, :] = tail

    def put_query(ref):
        ref[0:rows, :] = window[:, :dh]
        ref[rows : 2 * rows, :] = do_ref[...]
        put_wide(ref, feat_at, feat_t[:nf, :])
        ref[tail_at : tail_at + 16, :] = tail

    put_keys(keys_ref)
    put_query(query_ref)
    for at, ref in enumerate(sends):
        later = jnp.bitwise_xor(me, max(2 * at, 1)) > me
        pl.when(later)(lambda ref=ref: put_keys(ref))
        pl.when(jnp.logical_not(later))(lambda ref=ref: put_query(ref))

def between(totals, low, high):
    at = lax.broadcasted_iota(jnp.int32, totals.shape, 0)
    return jnp.sum(jnp.where((at > low) & (at < high), totals, 0.0), axis=0, keepdims=True)


def over_partners(count, body, carry):
    if count <= 8:
        for d in range(1, count):
            carry = body(d, carry)
        return carry
    return lax.fori_loop(1, count, body, carry)


def query_kernel(ctx, count, *rest):
    recvs = rest[: -10]
    (own_ref, query_ref, feat_ref, cum_ref, att_ref, stat_ref, sheet_ref, near_ref, p_ref,
     cums_ref) = rest[-10:]

    def recv(d):
        return recvs[d - 1] if len(recvs) > 1 else recvs[0].at[d - 1]

    me = block_index(ctx)
    rows, dh = att_ref.shape
    nf = feat_ref.shape[1] // 2
    back = WINDOW // rows
    feat_at = 2 * rows
    tail_at = feat_at + 2 * nf
    scale = dh ** (-0.5)
    feat_scale = nf ** (-0.5)
    wq = query_ref[0:rows, :]
    do = query_ref[rows : 2 * rows, :]
    q = feat_ref[:, :nf]
    at_row, at_col = iotas(rows)
    own_cum = cum_row(own_ref, tail_at)
    cums_ref[pl.ds(me, 1), :] = own_cum
    near_ref[me] = own_ref[0 : 2 * rows, :]

    def gather(d, carry):
        j = partner(me, d, count)
        view = recv(d)
        near_ref[j] = view[0 : 2 * rows, :]
        cums_ref[pl.ds(j, 1), :] = cum_row(view, tail_at)
        return carry

    over_partners(count, gather, 0)

    def near(w):
        return near_ref.at[jnp.maximum(me - back + w, 0)]

    top = jnp.full((rows, LANES), MASKED, f32)
    for w in range(back + 1):
        keys = own_ref[0:rows, :] if w == back else near(w)[0:rows, :]
        s = nt(wq, keys) * scale
        if w == back:
            s = jnp.where(at_col <= at_row, s, MASKED)
        elif w == 0:
            s = jnp.where((at_col > at_row) & (me >= back), s, MASKED)
        else:
            s = jnp.where(me >= back - w, s, MASKED)
        p_ref[w] = s
        for h in range(0, rows, LANES):
            top = jnp.maximum(top, s[:, h : h + LANES])
    top = jnp.max(top, axis=1, keepdims=True)
    total = jnp.zeros((rows, LANES), f32)
    out = jnp.zeros((rows, dh), f32)
    for w in range(back + 1):
        p = jnp.exp(p_ref[w] - top)
        for h in range(0, rows, LANES):
            total += p[:, h : h + LANES]
        vals = own_ref[rows : 2 * rows, :] if w == back else near(w)[rows : 2 * rows, :]
        out += nn(p.astype(bf16), vals)
    total = jnp.sum(total, axis=1, keepdims=True)
    windowed = out * (1.0 / total)

    cum_c = cum_ref[...]
    growth = jnp.exp(cum_c)
    totals = cums_ref[:, rows - 1 : rows]

    def forward(d, carry):
        num, den = carry
        j = partner(me, d, count)
        view = recv(d)
        gap = between(totals, j - 1, me)
        es = jnp.where(j < me, jnp.exp(jnp.minimum(gap - cums_ref[pl.ds(j, 1), :], 0.0)), 0.0)
        x = nn(q, wide(view, feat_at, nf)) * feat_scale
        weight = (1.0 + x + 0.5 * x * x) * es
        for h in range(0, rows, LANES):
            den += weight[:, h : h + LANES]
        num += nn(weight.astype(bf16), view[rows : 2 * rows, :])
        return num, den

    num, den = over_partners(
        count, forward, (jnp.zeros((rows, dh), f32), jnp.zeros((rows, LANES), f32))
    )
    x = nn(q, wide(own_ref, feat_at, nf)) * feat_scale
    e = jnp.where(at_col <= at_row, jnp.exp(jnp.minimum(cum_c - own_cum, 0.0)), 0.0)
    weight = (1.0 + x + 0.5 * x * x) * e
    num = num * growth + nn(weight.astype(bf16), own_ref[rows : 2 * rows, :])
    den = den * growth
    for h in range(0, rows, LANES):
        den += weight[:, h : h + LANES]
    rden = 1.0 / jnp.sum(den, axis=1, keepdims=True)
    linear = num * rden
    att_ref[...] = (linear + windowed).astype(bf16)
    do_f = do.astype(f32)
    delta_w = jnp.sum(do_f * windowed, axis=1, keepdims=True)
    delta_l = jnp.sum(do_f * linear, axis=1, keepdims=True)
    lse = top + jnp.log(total)
    lane = lax.broadcasted_iota(jnp.int32, (rows, LANES), 1)
    sheet = jnp.where(lane == 0, lse, 0.0)
    sheet = jnp.where(lane == 1, delta_w, sheet)
    sheet = jnp.where(lane == 2, rden, sheet)
    sheet = jnp.where(lane == 3, delta_l, sheet)
    sheet = jnp.where(lane == 4, cum_c, sheet)
    sheet_ref[...] = sheet
    stat_ref[...] = jnp.transpose(sheet)[0:8, :]


def gradient_kernel(ctx, count, recvs, *rest):
    recvs = rest[:recvs]
    own_ref, query_ref, feat_ref, sheet_ref, stat_ref, *rest = rest[len(recvs) :]

    def recv(d):
        return recvs[d - 1] if len(recvs) > 1 else recvs[0].at[d - 1]

    me = block_index(ctx)
    rows = feat_ref.shape[0]
    dh = LANES
    nf = feat_ref.shape[1] // 2
    feat_at = 2 * rows
    scale = dh ** (-0.5)
    feat_scale = nf ** (-0.5)
    at_row, at_col = iotas(rows)
    apart = at_row - at_col
    wq, wk = query_ref[0:rows, :], own_ref[0:rows, :]
    do, v = query_ref[rows : 2 * rows, :], own_ref[rows : 2 * rows, :]
    q, k = feat_ref[:, :nf], feat_ref[:, nf:]
    lse_c, dw_c = sheet_ref[:, 0:1], sheet_ref[:, 1:2]
    rden_c, dl_c, cum_c = sheet_ref[:, 2:3], sheet_ref[:, 3:4], sheet_ref[:, 4:5]
    mine_ref = stat_ref.at[me]
    own_cum = mine_ref[4:5, :]
    totals = jnp.concatenate([stat_ref[j, 4:5, rows - 1 : rows] for j in range(count)], axis=0)
    growth_c = jnp.exp(cum_c) * rden_c
    tail_c = jnp.exp(own_cum[:, rows - 1 : rows] - cum_c)

    def pick(flag, a, b):
        return jnp.where(flag, a, b)

    s = nt(wq, wk) * scale
    causal = at_col <= at_row
    p = jnp.where(causal, jnp.exp(s - lse_c), 0.0)
    dp = nt(do, v)
    dwq = nn((p * (dp - dw_c)).astype(bf16), wk)
    x = nn(q, wide(own_ref, feat_at, nf)) * feat_scale
    e = jnp.where(causal, jnp.exp(jnp.minimum(cum_c - own_cum, 0.0)), 0.0) * rden_c
    dx = (dp - dl_c) * e * (1.0 + x)
    dqt = nt(wide(own_ref, feat_at, nf), dx.astype(bf16))

    s = nt(wk, wq) * scale
    causal = at_row <= at_col
    p = jnp.where(causal, jnp.exp(s - mine_ref[0:1, :]), 0.0)
    dp = nt(v, do)
    dwk = nn((p * (dp - mine_ref[1:2, :])).astype(bf16), wq)
    x = nn(k, wide(query_ref, feat_at, nf)) * feat_scale
    e = jnp.where(causal, jnp.exp(jnp.minimum(own_cum - cum_c, 0.0)), 0.0) * mine_ref[2:3, :]
    dx = (dp - mine_ref[3:4, :]) * e * (1.0 + x)
    dkt = nt(wide(query_ref, feat_at, nf), dx.astype(bf16))
    dv = nn((p + (1.0 + x + 0.5 * x * x) * e).astype(bf16), do)

    def step(d, carry):
        dwq, dqt, dwk, dkt, dv = carry
        j = partner(me, d, count)
        view = recv(d)
        mine = j < me
        sign = pick(mine, 1, -1)
        limit = WINDOW - jnp.abs(me - j) * rows
        rows_w = pick(mine, wq, wk)
        rows_v = pick(mine, do, v)
        rows_f = pick(mine, q, k)
        other_w = view[0:rows, :]
        other_v = view[rows : 2 * rows, :]
        other_f = wide(view, feat_at, nf)
        st = stat_ref[j]
        zero = jnp.zeros((1, rows), f32)
        cum = st[4:5, :]
        gap = between(totals, jnp.minimum(me, j), jnp.maximum(me, j))
        e_r = jnp.exp(jnp.minimum(gap + pick(mine, cum[:, rows - 1 : rows] - cum, cum), 0.0))
        e_r = e_r * pick(mine, 1.0, st[2:3, :])
        e_c = pick(mine, growth_c, tail_c)

        s = nt(rows_w, other_w) * scale
        p = jnp.exp(s - pick(mine, lse_c, 0.0) - pick(mine, zero, st[0:1, :]))
        p = jnp.where(apart * sign < limit, p, 0.0)
        dp = nt(rows_v, other_v)
        ds = p * (dp - pick(mine, dw_c, 0.0) - pick(mine, zero, st[1:2, :]))
        more_w = nn(ds.astype(bf16), other_w)
        x = nn(rows_f, other_f) * feat_scale
        e = e_r * e_c
        dx = (dp - pick(mine, dl_c, 0.0) - pick(mine, zero, st[3:4, :])) * e * (1.0 + x)
        more_f = nt(other_f, dx.astype(bf16))
        more_v = nn((p + (1.0 + x + 0.5 * x * x) * e).astype(bf16), other_v)
        dwq = dwq + pick(mine, more_w, 0.0)
        dwk = dwk + pick(mine, 0.0, more_w)
        dqt = dqt + pick(mine, more_f, 0.0)
        dkt = dkt + pick(mine, 0.0, more_f)
        dv = dv + pick(mine, 0.0, more_v)
        return dwq, dqt, dwk, dkt, dv

    dwq, dqt, dwk, dkt, dv = over_partners(count, step, (dwq, dqt, dwk, dkt, dv))
    dwq, dwk = (dwq * scale).astype(bf16), (dwk * scale).astype(bf16)
    dv = dv.astype(bf16)
    dft = (jnp.concatenate([dqt, dkt], axis=0) * feat_scale).astype(bf16)
    if len(rest) == 1:
        grad_ref = rest[0]
        grad_ref[0:rows, :] = dwq
        grad_ref[rows : 2 * rows, :] = dwk
        grad_ref[2 * rows : 3 * rows, :] = dv
        put_wide(grad_ref, 3 * rows, dft)
        return

    ww_ref, vw_ref, fw_ref, part_ref, *sends = rest
    head = lax.axis_index("tp")
    share = part_ref.shape[1]
    dw = jnp.concatenate([dwq, dwk], axis=1)
    padded = jnp.concatenate([dft.astype(f32), jnp.zeros((LANES - 2 * nf, rows), f32)], axis=0)
    df = jnp.transpose(padded)[:, : 2 * nf].astype(bf16)
    for t, ref in enumerate([part_ref, *sends]):
        part = pl.ds(pl.multiple_of(jnp.bitwise_xor(head, t) * share, share), share)
        product = nt(dw, ww_ref[part, :]) + nt(dv, vw_ref[part, :]) + nn(df, fw_ref[:, part])
        ref[...] = product.astype(ref.dtype)


def add_kernel(part_ref, *rest):
    *others, most_ref, last_ref = rest
    total = part_ref[...]
    for ref in others:
        total += ref[...].astype(f32)
    most = most_ref.shape[0]
    total = total.astype(bf16)
    most_ref[...] = total[:most]
    last_ref[...] = total[most:]


def gather_rows(grad_ref, order, cat_ref, feat_ref):
    rows = cat_ref.shape[0]
    nf2 = feat_ref.shape[1] // len(order)
    for at, h in enumerate(order):
        for part in range(3):
            lane = (3 * at + part) * LANES
            cat_ref[:, lane : lane + LANES] = grad_ref[h, part * rows : (part + 1) * rows, :]
    dft = jnp.concatenate([wide(grad_ref.at[h], 3 * rows, nf2) for h in order], axis=0)
    feat_ref[...] = jnp.transpose(dft.astype(f32)).astype(bf16)


def lay_kernel(most_ref, own_ref, *rest):
    *lasts, out_ref = rest
    shares, most, width = most_ref.shape
    head = lax.axis_index("tp")
    for z in range(shares):
        out_ref[0:most, z * width : (z + 1) * width] = most_ref[z]
    for t, ref in enumerate([own_ref, *lasts]):
        at = pl.multiple_of(jnp.bitwise_xor(head, t) * width, width)
        out_ref[most:, pl.ds(at, width)] = ref[...]


def merge_kernel(grad_ref, weight_ref, out_ref, cat_ref, feat_ref):
    heads = grad_ref.shape[0]
    tile = out_ref.shape[1]
    lanes = 3 * LANES
    nf2 = feat_ref.shape[1] // heads

    @pl.when(pl.program_id(0) == 0)
    def _():
        gather_rows(grad_ref, range(heads), cat_ref, feat_ref)

    views = [weight_ref.at[h] for h in range(heads)]
    main = jnp.concatenate([v[:, 0:lanes] for v in views], axis=1)
    feats = jnp.concatenate([v[:, lanes:] for v in views], axis=1)
    out_ref[...] = (nt(cat_ref[...], main) + nt(feat_ref[...], feats)).astype(bf16)


VMEM = pl.BlockSpec(memory_space=pltpu.VMEM)
HBM = pl.BlockSpec(memory_space=pltpu.HBM)
params = pltpu.CompilerParams(vmem_limit_bytes=32 * 1024 * 1024)


def in_hbm(*arrays):
    return [pltpu.with_memory_space_constraint(a, pltpu.HBM) for a in arrays]


def cost(flops, nbytes, exps=0):
    return pl.CostEstimate(flops=flops, bytes_accessed=nbytes, transcendentals=exps)


def merge(grads, weights, rows, dim):
    heads, _, columns = weights.shape
    tile = 2 * LANES
    return pl.pallas_call(
        merge_kernel,
        out_shape=jax.ShapeDtypeStruct((rows, dim), bf16),
        grid=(dim // tile,),
        in_specs=[
            pl.BlockSpec(grads.shape, lambda i: (0, 0, 0)),
            pl.BlockSpec((heads, tile, columns), lambda i: (0, i, 0)),
        ],
        out_specs=pl.BlockSpec((rows, tile), lambda i: (0, i)),
        scratch_shapes=[
            pltpu.VMEM((rows, 3 * LANES * heads), bf16),
            pltpu.VMEM((rows, (columns - 3 * LANES) * heads), bf16),
        ],
        compiler_params=params,
        cost_estimate=cost(2 * rows * dim * heads * columns, heads * dim * columns * 2),
        name="head_sum",
    )(grads, weights)


def per_device(ctx, tokens, feature_weight, window_weight, value_weight, log_decay, out_grad):
    rows, dim = tokens.shape
    nf2 = feature_weight.shape[1]
    nf = nf2 // 2
    dh = value_weight.shape[1]
    columns = 3 * dh + nf2
    chips, count, heads = lax.axis_size(ctx[:-1]), lax.axis_size(ctx), lax.axis_size("tp")
    fw_t = feature_weight.T

    payload = 2 * rows + 2 * nf + 16
    block = jax.ShapeDtypeStruct((payload, LANES), bf16)
    *sends, own, query, feat, cum, ww, vw, fw = pl.pallas_call(
        partial(project_kernel, ctx),
        out_shape=[block] * (chips + 2)
        + [
            jax.ShapeDtypeStruct((rows, nf2), bf16),
            jax.ShapeDtypeStruct((rows, 1), f32),
            jax.ShapeDtypeStruct((dim, 2 * dh), bf16),
            jax.ShapeDtypeStruct((dim, dh), bf16),
            jax.ShapeDtypeStruct((nf2, dim), bf16),
        ],
        in_specs=[HBM] * 6,
        out_specs=[VMEM] * (chips + 7),
        scratch_shapes=[
            pltpu.VMEM((rows, dim), bf16),
            pltpu.VMEM((1, rows), f32),
            pltpu.VMEM((rows, dh), bf16),
            pltpu.SemaphoreType.DMA((CHUNKS, 4)),
            pltpu.SemaphoreType.DMA((2,)),
        ],
        compiler_params=params,
        cost_estimate=cost(2 * rows * dim * columns, 4 * 1024 * 1024),
        name="project",
    )(*in_hbm(tokens, fw_t, window_weight, value_weight, log_decay.T, out_grad))

    swap = [(0, 1), (1, 0)]
    recv = {}
    for d in range(1, chips):
        recv[2 * d] = lax.ppermute(sends[d], ctx[:-1], [(i, i ^ d) for i in range(chips)])
    recv[1] = lax.ppermute(sends[0], "core", swap)
    for d in range(1, chips):
        recv[2 * d + 1] = lax.ppermute(recv[2 * d], "core", swap)
    recv = [recv[d] for d in range(1, count)]
    if count > 8:
        recv = [jnp.stack(recv)]

    attended, stat, sheet = pl.pallas_call(
        lambda *refs: query_kernel(ctx, count, *refs),
        out_shape=(
            jax.ShapeDtypeStruct((rows, dh), bf16),
            jax.ShapeDtypeStruct((8, rows), f32),
            jax.ShapeDtypeStruct((rows, LANES), f32),
        ),
        in_specs=[VMEM] * (len(recv) + 4),
        out_specs=[VMEM] * 3,
        scratch_shapes=[
            pltpu.VMEM((count, 2 * rows, dh), bf16),
            pltpu.VMEM((WINDOW // rows + 1, rows, rows), f32),
            pltpu.VMEM((count, rows), f32),
        ],
        compiler_params=params,
        cost_estimate=cost(10**9, 2 * 1024 * 1024, 10**6),
        name="query_side",
    )(*recv, own, query, feat, cum)
    stats = stat
    for name in reversed(ctx):
        stats = lax.all_gather(stats, name, tiled=True)
    stats = stats.reshape(count, -1, rows)

    share = dim // heads
    shared = heads & (heads - 1) == 0 and share % LANES == 0
    args = [*recv, own, query, feat, sheet, stats]
    if shared:
        args += [ww, vw, fw]
        out_shape = [jax.ShapeDtypeStruct((rows, share), f32)]
        out_shape += [jax.ShapeDtypeStruct((rows, share), bf16)] * (heads - 1)
    else:
        out_shape = [jax.ShapeDtypeStruct((3 * rows + nf2 * rows // LANES, LANES), bf16)]
    grads = pl.pallas_call(
        lambda *refs: gradient_kernel(ctx, count, len(recv), *refs),
        out_shape=out_shape,
        in_specs=[VMEM] * len(args),
        out_specs=[VMEM] * len(out_shape),
        compiler_params=params,
        cost_estimate=cost(10**9, 2 * 1024 * 1024, 10**6),
        name="gradients",
    )(*args)
    if not shared:
        weights = jnp.concatenate([window_weight, value_weight, feature_weight], axis=1)
        weights = lax.all_gather(weights, "tp")
        return (attended, merge(lax.all_gather(grads[0], "tp"), weights, rows, dim))

    def passed_on(parts):
        return [
            lax.ppermute(parts[t], "tp", [(z, z ^ t) for z in range(heads)])
            for t in range(heads - 1, 0, -1)
        ][::-1]

    last = 16
    sums, ends = pl.pallas_call(
        add_kernel,
        out_shape=[
            jax.ShapeDtypeStruct((rows - last, share), bf16),
            jax.ShapeDtypeStruct((last, share), bf16),
        ],
        in_specs=[VMEM] * heads,
        out_specs=[VMEM] * 2,
        compiler_params=params,
        cost_estimate=cost(rows * share * heads, 2 * rows * share * heads),
        name="add",
    )(grads[0], *passed_on(grads))
    others = passed_on([ends] * heads)
    total = pl.pallas_call(
        lay_kernel,
        out_shape=jax.ShapeDtypeStruct((rows, dim), bf16),
        in_specs=[VMEM] * (heads + 1),
        out_specs=VMEM,
        compiler_params=params,
        cost_estimate=cost(1, 4 * rows * dim),
        name="lay",
    )(lax.all_gather(sums, "tp"), ends, *others)
    return (attended, total)


def solution(mesh):
    blocks, tp = mesh.devices.shape
    bits = blocks.bit_length() - 1
    assert blocks == 2**bits
    ctx = tuple(f"half{i}" for i in range(bits - 1)) + ("core",)
    split = Mesh(mesh.devices.reshape((2,) * bits + (tp,)), (*ctx, "tp"))
    in_specs = (
        P(ctx, None),
        P(None, "tp"),
        P(None, "tp"),
        P(None, "tp"),
        P(ctx, "tp"),
        P(ctx, "tp"),
    )
    out_specs = (P(ctx, "tp"), P(ctx, None))
    return jax.shard_map(
        partial(per_device, ctx),
        mesh=split,
        in_specs=in_specs,
        out_specs=out_specs,
        check_vma=False,
    )
```

```python
from functools import partial

import jax
import jax.numpy as jnp
from jax import lax
from jax.experimental import pallas as pl
from jax.experimental.pallas import tpu as pltpu
from jax.sharding import Mesh
from jax.sharding import PartitionSpec as P

WINDOW = 1024
LANES = 128
MASKED = -1e30
CHUNKS = 4
f32 = jnp.float32
bf16 = jnp.bfloat16


def nn(a, b):
    return lax.dot_general(a, b, (((1,), (0,)), ((), ())), preferred_element_type=f32)


def nt(a, b):
    return lax.dot_general(a, b, (((1,), (1,)), ((), ())), preferred_element_type=f32)


def partner(me, d, count):
    assert count & (count - 1) == 0
    return jnp.bitwise_xor(me, d)


def wide(view, start, count):
    return jnp.concatenate(
        [view[start : start + count, :], view[start + count : start + 2 * count, :]], axis=1
    )


def put_wide(ref, start, value):
    count = value.shape[0]
    for half in range(value.shape[1] // LANES):
        ref[start + half * count : start + (half + 1) * count, :] = value[
            :, half * LANES : (half + 1) * LANES
        ]


def cum_row(view, start):
    tail = view[start : start + 16, :].astype(f32)
    first = tail[0:1] + tail[2:3] + tail[4:5]
    second = tail[1:2] + tail[3:4] + tail[5:6]
    return jnp.concatenate([first, second], axis=1)


def iotas(rows):
    return (
        lax.broadcasted_iota(jnp.int32, (rows, rows), 0),
        lax.broadcasted_iota(jnp.int32, (rows, rows), 1),
    )


def block_index(ctx):
    place = 0
    for name in ctx:
        place = place * lax.axis_size(name) + lax.axis_index(name)
    return place


def project_kernel(ctx, tok_hbm, fw_hbm, ww_hbm, vw_hbm, ld_hbm, do_hbm, *rest):
    *sends, keys_ref, query_ref, feat_ref, cum_ref, ww_ref, vw_ref, fw_ref = rest[:-5]
    tok_ref, ld_ref, do_ref, sems, small = rest[-5:]
    me = block_index(ctx)
    rows, dim = tok_ref.shape
    dh = do_ref.shape[1]
    nf = fw_ref.shape[0] // 2
    span = dim // CHUNKS
    copies = []
    for c in range(CHUNKS):
        part = pl.ds(c * span, span)
        copies.append([
            pltpu.make_async_copy(tok_hbm.at[:, part], tok_ref.at[:, part], sems.at[c, 0]),
            pltpu.make_async_copy(ww_hbm.at[part, :], ww_ref.at[part, :], sems.at[c, 1]),
            pltpu.make_async_copy(vw_hbm.at[part, :], vw_ref.at[part, :], sems.at[c, 2]),
            pltpu.make_async_copy(fw_hbm.at[:, part], fw_ref.at[:, part], sems.at[c, 3]),
        ])
    others = [
        pltpu.make_async_copy(ld_hbm, ld_ref, small.at[0]),
        pltpu.make_async_copy(do_hbm, do_ref, small.at[1]),
    ]
    for copy in others:
        copy.start()
    for group in copies:
        for at, copy in enumerate(group):
            copy.start(priority=min(at, 1))
    for copy in others:
        copy.wait()
    at_row, at_col = iotas(rows)
    ld_r = ld_ref[...]
    ld_c = jnp.sum(jnp.where(at_row == at_col, ld_r, 0.0), axis=1, keepdims=True)
    cum_r = jnp.sum(jnp.where(at_row <= at_col, ld_c, 0.0), axis=0, keepdims=True)
    cum_ref[...] = jnp.sum(jnp.where(at_col <= at_row, ld_r, 0.0), axis=1, keepdims=True)
    high = cum_r.astype(bf16)
    left = cum_r - high.astype(f32)
    mid = left.astype(bf16)
    low = (left - mid.astype(f32)).astype(bf16)
    pieces = [t[:, h : h + LANES].astype(f32) for t in (high, mid, low) for h in range(0, rows, LANES)]
    tail = jnp.concatenate(pieces + [jnp.zeros((10, LANES), f32)], axis=0).astype(bf16)

    feat = jnp.zeros((rows, 2 * nf), f32)
    main = jnp.zeros((rows, 3 * dh), f32)
    for c in range(CHUNKS):
        for copy in copies[c]:
            copy.wait()
        part = slice(c * span, (c + 1) * span)
        tok = tok_ref[:, part]
        feat += nt(tok, fw_ref[:, part])
        main += nn(tok, jnp.concatenate([ww_ref[part, :], vw_ref[part, :]], axis=1))
    feat = feat.astype(bf16)
    window = main[:, : 2 * dh].astype(bf16)
    values = main[:, 2 * dh :].astype(bf16)
    feat_ref[...] = feat
    small_row, small_col = iotas(2 * nf)
    feat_t = nt((small_row == small_col).astype(bf16), feat).astype(bf16)
    feat_at = 2 * rows
    tail_at = feat_at + 2 * nf

    def put_keys(ref):
        ref[0:rows, :] = window[:, dh:]
        ref[rows : 2 * rows, :] = values
        put_wide(ref, feat_at, feat_t[nf:, :])
        ref[tail_at : tail_at + 16, :] = tail

    def put_query(ref):
        ref[0:rows, :] = window[:, :dh]
        ref[rows : 2 * rows, :] = do_ref[...]
        put_wide(ref, feat_at, feat_t[:nf, :])
        ref[tail_at : tail_at + 16, :] = tail

    put_keys(keys_ref)
    put_query(query_ref)
    for at, ref in enumerate(sends):
        later = jnp.bitwise_xor(me, max(2 * at, 1)) > me
        pl.when(later)(lambda ref=ref: put_keys(ref))
        pl.when(jnp.logical_not(later))(lambda ref=ref: put_query(ref))

def between(totals, low, high):
    at = lax.broadcasted_iota(jnp.int32, totals.shape, 0)
    return jnp.sum(jnp.where((at > low) & (at < high), totals, 0.0), axis=0, keepdims=True)


def over_partners(count, body, carry):
    if count <= 8:
        for d in range(1, count):
            carry = body(d, carry)
        return carry
    return lax.fori_loop(1, count, body, carry)


def query_kernel(ctx, count, *rest):
    recvs = rest[: -10]
    (own_ref, query_ref, feat_ref, cum_ref, att_ref, stat_ref, sheet_ref, near_ref, p_ref,
     cums_ref) = rest[-10:]

    def recv(d):
        return recvs[d - 1] if len(recvs) > 1 else recvs[0].at[d - 1]

    me = block_index(ctx)
    rows, dh = att_ref.shape
    nf = feat_ref.shape[1] // 2
    back = WINDOW // rows
    feat_at = 2 * rows
    tail_at = feat_at + 2 * nf
    scale = dh ** (-0.5)
    feat_scale = nf ** (-0.5)
    wq = query_ref[0:rows, :]
    do = query_ref[rows : 2 * rows, :]
    q = feat_ref[:, :nf]
    at_row, at_col = iotas(rows)
    own_cum = cum_row(own_ref, tail_at)
    cums_ref[pl.ds(me, 1), :] = own_cum
    near_ref[me] = own_ref[0 : 2 * rows, :]

    def gather(d, carry):
        j = partner(me, d, count)
        view = recv(d)
        near_ref[j] = view[0 : 2 * rows, :]
        cums_ref[pl.ds(j, 1), :] = cum_row(view, tail_at)
        return carry

    over_partners(count, gather, 0)

    def near(w):
        return near_ref.at[jnp.maximum(me - back + w, 0)]

    top = jnp.full((rows, LANES), MASKED, f32)
    for w in range(back + 1):
        keys = own_ref[0:rows, :] if w == back else near(w)[0:rows, :]
        s = nt(wq, keys) * scale
        if w == back:
            s = jnp.where(at_col <= at_row, s, MASKED)
        elif w == 0:
            s = jnp.where((at_col > at_row) & (me >= back), s, MASKED)
        else:
            s = jnp.where(me >= back - w, s, MASKED)
        p_ref[w] = s
        for h in range(0, rows, LANES):
            top = jnp.maximum(top, s[:, h : h + LANES])
    top = jnp.max(top, axis=1, keepdims=True)
    total = jnp.zeros((rows, LANES), f32)
    out = jnp.zeros((rows, dh), f32)
    for w in range(back + 1):
        p = jnp.exp(p_ref[w] - top)
        for h in range(0, rows, LANES):
            total += p[:, h : h + LANES]
        vals = own_ref[rows : 2 * rows, :] if w == back else near(w)[rows : 2 * rows, :]
        out += nn(p.astype(bf16), vals)
    total = jnp.sum(total, axis=1, keepdims=True)
    windowed = out * (1.0 / total)

    cum_c = cum_ref[...]
    growth = jnp.exp(cum_c)
    totals = cums_ref[:, rows - 1 : rows]

    def forward(d, carry):
        num, den = carry
        j = partner(me, d, count)
        view = recv(d)
        gap = between(totals, j - 1, me)
        es = jnp.where(j < me, jnp.exp(jnp.minimum(gap - cums_ref[pl.ds(j, 1), :], 0.0)), 0.0)
        x = nn(q, wide(view, feat_at, nf)) * feat_scale
        weight = (1.0 + x + 0.5 * x * x) * es
        for h in range(0, rows, LANES):
            den += weight[:, h : h + LANES]
        num += nn(weight.astype(bf16), view[rows : 2 * rows, :])
        return num, den

    num, den = over_partners(
        count, forward, (jnp.zeros((rows, dh), f32), jnp.zeros((rows, LANES), f32))
    )
    x = nn(q, wide(own_ref, feat_at, nf)) * feat_scale
    e = jnp.where(at_col <= at_row, jnp.exp(jnp.minimum(cum_c - own_cum, 0.0)), 0.0)
    weight = (1.0 + x + 0.5 * x * x) * e
    num = num * growth + nn(weight.astype(bf16), own_ref[rows : 2 * rows, :])
    den = den * growth
    for h in range(0, rows, LANES):
        den += weight[:, h : h + LANES]
    rden = 1.0 / jnp.sum(den, axis=1, keepdims=True)
    linear = num * rden
    att_ref[...] = (linear + windowed).astype(bf16)
    do_f = do.astype(f32)
    delta_w = jnp.sum(do_f * windowed, axis=1, keepdims=True)
    delta_l = jnp.sum(do_f * linear, axis=1, keepdims=True)
    lse = top + jnp.log(total)
    lane = lax.broadcasted_iota(jnp.int32, (rows, LANES), 1)
    sheet = jnp.where(lane == 0, lse, 0.0)
    sheet = jnp.where(lane == 1, delta_w, sheet)
    sheet = jnp.where(lane == 2, rden, sheet)
    sheet = jnp.where(lane == 3, delta_l, sheet)
    sheet = jnp.where(lane == 4, cum_c, sheet)
    sheet_ref[...] = sheet
    stat_ref[...] = jnp.transpose(sheet)[0:8, :]


def gradient_kernel(ctx, count, recvs, stats, *rest):
    recvs, rest = rest[:recvs], rest[recvs:]
    stats, rest = rest[:stats], rest[stats:]
    own_ref, query_ref, feat_ref, sheet_ref, *rest, total_ref = rest

    def recv(d):
        return recvs[d - 1] if len(recvs) > 1 else recvs[0].at[d - 1]

    me = block_index(ctx)
    rows = feat_ref.shape[0]
    dh = LANES
    nf = feat_ref.shape[1] // 2
    feat_at = 2 * rows
    scale = dh ** (-0.5)
    feat_scale = nf ** (-0.5)
    at_row, at_col = iotas(rows)
    apart = at_row - at_col
    wq, wk = query_ref[0:rows, :], own_ref[0:rows, :]
    do, v = query_ref[rows : 2 * rows, :], own_ref[rows : 2 * rows, :]
    q, k = feat_ref[:, :nf], feat_ref[:, nf:]
    lse_c, dw_c = sheet_ref[:, 0:1], sheet_ref[:, 1:2]
    rden_c, dl_c, cum_c = sheet_ref[:, 2:3], sheet_ref[:, 3:4], sheet_ref[:, 4:5]
    def stat(d):
        if len(stats) == 1:
            return stats[0].at[pl.ds(pl.multiple_of(8 * d, 8), 8)]
        at = d.bit_length()
        return stats[at].at[pl.ds(8 * (d - (1 << at >> 1)), 8)]

    mine_ref = stat(0)
    own_cum = mine_ref[4:5, :]
    total_ref[pl.ds(me, 1), :] = own_cum[:, rows - LANES :]

    def place(d, carry):
        total_ref[pl.ds(partner(me, d, count), 1), :] = stat(d)[4:5, rows - LANES :]
        return carry

    over_partners(count, place, 0)
    totals = total_ref[:, LANES - 1 :]
    growth_c = jnp.exp(cum_c) * rden_c
    tail_c = jnp.exp(own_cum[:, rows - 1 : rows] - cum_c)

    def pick(flag, a, b):
        return jnp.where(flag, a, b)

    s = nt(wq, wk) * scale
    causal = at_col <= at_row
    p = jnp.where(causal, jnp.exp(s - lse_c), 0.0)
    dp = nt(do, v)
    dwq = nn((p * (dp - dw_c)).astype(bf16), wk)
    x = nn(q, wide(own_ref, feat_at, nf)) * feat_scale
    e = jnp.where(causal, jnp.exp(jnp.minimum(cum_c - own_cum, 0.0)), 0.0) * rden_c
    dx = (dp - dl_c) * e * (1.0 + x)
    dqt = nt(wide(own_ref, feat_at, nf), dx.astype(bf16))

    s = nt(wk, wq) * scale
    causal = at_row <= at_col
    p = jnp.where(causal, jnp.exp(s - mine_ref[0:1, :]), 0.0)
    dp = nt(v, do)
    dwk = nn((p * (dp - mine_ref[1:2, :])).astype(bf16), wq)
    x = nn(k, wide(query_ref, feat_at, nf)) * feat_scale
    e = jnp.where(causal, jnp.exp(jnp.minimum(own_cum - cum_c, 0.0)), 0.0) * mine_ref[2:3, :]
    dx = (dp - mine_ref[3:4, :]) * e * (1.0 + x)
    dkt = nt(wide(query_ref, feat_at, nf), dx.astype(bf16))
    dv = nn((p + (1.0 + x + 0.5 * x * x) * e).astype(bf16), do)

    def step(d, carry):
        dwq, dqt, dwk, dkt, dv = carry
        j = partner(me, d, count)
        view = recv(d)
        mine = j < me
        sign = pick(mine, 1, -1)
        limit = WINDOW - jnp.abs(me - j) * rows
        rows_w = pick(mine, wq, wk)
        rows_v = pick(mine, do, v)
        rows_f = pick(mine, q, k)
        other_w = view[0:rows, :]
        other_v = view[rows : 2 * rows, :]
        other_f = wide(view, feat_at, nf)
        st = stat(d)
        zero = jnp.zeros((1, rows), f32)
        cum = st[4:5, :]
        gap = between(totals, jnp.minimum(me, j), jnp.maximum(me, j))
        e_r = jnp.exp(jnp.minimum(gap + pick(mine, cum[:, rows - 1 : rows] - cum, cum), 0.0))
        e_r = e_r * pick(mine, 1.0, st[2:3, :])
        e_c = pick(mine, growth_c, tail_c)

        s = nt(rows_w, other_w) * scale
        p = jnp.exp(s - pick(mine, lse_c, 0.0) - pick(mine, zero, st[0:1, :]))
        p = jnp.where(apart * sign < limit, p, 0.0)
        dp = nt(rows_v, other_v)
        ds = p * (dp - pick(mine, dw_c, 0.0) - pick(mine, zero, st[1:2, :]))
        more_w = nn(ds.astype(bf16), other_w)
        x = nn(rows_f, other_f) * feat_scale
        e = e_r * e_c
        dx = (dp - pick(mine, dl_c, 0.0) - pick(mine, zero, st[3:4, :])) * e * (1.0 + x)
        more_f = nt(other_f, dx.astype(bf16))
        more_v = nn((p + (1.0 + x + 0.5 * x * x) * e).astype(bf16), other_v)
        dwq = dwq + pick(mine, more_w, 0.0)
        dwk = dwk + pick(mine, 0.0, more_w)
        dqt = dqt + pick(mine, more_f, 0.0)
        dkt = dkt + pick(mine, 0.0, more_f)
        dv = dv + pick(mine, 0.0, more_v)
        return dwq, dqt, dwk, dkt, dv

    dwq, dqt, dwk, dkt, dv = over_partners(count, step, (dwq, dqt, dwk, dkt, dv))
    dwq, dwk = (dwq * scale).astype(bf16), (dwk * scale).astype(bf16)
    dv = dv.astype(bf16)
    dft = (jnp.concatenate([dqt, dkt], axis=0) * feat_scale).astype(bf16)
    if len(rest) == 1:
        grad_ref = rest[0]
        grad_ref[0:rows, :] = dwq
        grad_ref[rows : 2 * rows, :] = dwk
        grad_ref[2 * rows : 3 * rows, :] = dv
        put_wide(grad_ref, 3 * rows, dft)
        return

    ww_ref, vw_ref, fw_ref, *parts = rest
    head = lax.axis_index("tp")
    half, share = parts[0].shape
    dw = jnp.concatenate([dwq, dwk], axis=1)
    padded = jnp.concatenate([dft.astype(f32), jnp.zeros((LANES - 2 * nf, rows), f32)], axis=0)
    df = jnp.transpose(padded)[:, : 2 * nf].astype(bf16)
    for t in range(len(parts) // 2):
        part = pl.ds(pl.multiple_of(jnp.bitwise_xor(head, t) * share, share), share)
        product = nt(dw, ww_ref[part, :]) + nt(dv, vw_ref[part, :]) + nn(df, fw_ref[:, part])
        for h in range(2):
            ref = parts[2 * t + h]
            ref[...] = product[h * half : (h + 1) * half].astype(ref.dtype)


def add_kernel(part_ref, *rest):
    *others, out_ref = rest
    total = part_ref[...]
    for ref in others:
        total += ref[...].astype(f32)
    out_ref[...] = total.astype(bf16)


def lay_kernel(half, sums_ref, *rest):
    out_ref, sems = rest[-2:]
    shares, rows, width = sums_ref.shape
    at = pl.ds(half * rows, rows)
    copies = [
        pltpu.make_async_copy(
            sums_ref.at[z], out_ref.at[at, pl.ds(z * width, width)], sems.at[z]
        )
        for z in range(shares)
    ]
    for copy in copies:
        copy.start()
    for copy in copies:
        copy.wait()


def gather_rows(grad_ref, order, cat_ref, feat_ref):
    rows = cat_ref.shape[0]
    nf2 = feat_ref.shape[1] // len(order)
    for at, h in enumerate(order):
        for part in range(3):
            lane = (3 * at + part) * LANES
            cat_ref[:, lane : lane + LANES] = grad_ref[h, part * rows : (part + 1) * rows, :]
    dft = jnp.concatenate([wide(grad_ref.at[h], 3 * rows, nf2) for h in order], axis=0)
    feat_ref[...] = jnp.transpose(dft.astype(f32)).astype(bf16)


def merge_kernel(grad_ref, weight_ref, out_ref, cat_ref, feat_ref):
    heads = grad_ref.shape[0]
    tile = out_ref.shape[1]
    lanes = 3 * LANES
    nf2 = feat_ref.shape[1] // heads

    @pl.when(pl.program_id(0) == 0)
    def _():
        gather_rows(grad_ref, range(heads), cat_ref, feat_ref)

    views = [weight_ref.at[h] for h in range(heads)]
    main = jnp.concatenate([v[:, 0:lanes] for v in views], axis=1)
    feats = jnp.concatenate([v[:, lanes:] for v in views], axis=1)
    out_ref[...] = (nt(cat_ref[...], main) + nt(feat_ref[...], feats)).astype(bf16)


VMEM = pl.BlockSpec(memory_space=pltpu.VMEM)
HBM = pl.BlockSpec(memory_space=pltpu.HBM)
ANY = pl.BlockSpec(memory_space=pl.ANY)
params = pltpu.CompilerParams(vmem_limit_bytes=32 * 1024 * 1024)


def in_hbm(*arrays):
    return [pltpu.with_memory_space_constraint(a, pltpu.HBM) for a in arrays]


def cost(flops, nbytes, exps=0):
    return pl.CostEstimate(flops=flops, bytes_accessed=nbytes, transcendentals=exps)


def merge(grads, weights, rows, dim):
    heads, _, columns = weights.shape
    tile = 2 * LANES
    return pl.pallas_call(
        merge_kernel,
        out_shape=jax.ShapeDtypeStruct((rows, dim), bf16),
        grid=(dim // tile,),
        in_specs=[
            pl.BlockSpec(grads.shape, lambda i: (0, 0, 0)),
            pl.BlockSpec((heads, tile, columns), lambda i: (0, i, 0)),
        ],
        out_specs=pl.BlockSpec((rows, tile), lambda i: (0, i)),
        scratch_shapes=[
            pltpu.VMEM((rows, 3 * LANES * heads), bf16),
            pltpu.VMEM((rows, (columns - 3 * LANES) * heads), bf16),
        ],
        compiler_params=params,
        cost_estimate=cost(2 * rows * dim * heads * columns, heads * dim * columns * 2),
        name="head_sum",
    )(grads, weights)


def per_device(ctx, tokens, feature_weight, window_weight, value_weight, log_decay, out_grad):
    rows, dim = tokens.shape
    nf2 = feature_weight.shape[1]
    nf = nf2 // 2
    dh = value_weight.shape[1]
    columns = 3 * dh + nf2
    chips, count, heads = lax.axis_size(ctx[:-1]), lax.axis_size(ctx), lax.axis_size("tp")
    fw_t = feature_weight.T

    payload = 2 * rows + 2 * nf + 16
    block = jax.ShapeDtypeStruct((payload, LANES), bf16)
    *sends, own, query, feat, cum, ww, vw, fw = pl.pallas_call(
        partial(project_kernel, ctx),
        out_shape=[block] * (chips + 2)
        + [
            jax.ShapeDtypeStruct((rows, nf2), bf16),
            jax.ShapeDtypeStruct((rows, 1), f32),
            jax.ShapeDtypeStruct((dim, 2 * dh), bf16),
            jax.ShapeDtypeStruct((dim, dh), bf16),
            jax.ShapeDtypeStruct((nf2, dim), bf16),
        ],
        in_specs=[HBM] * 6,
        out_specs=[VMEM] * (chips + 7),
        scratch_shapes=[
            pltpu.VMEM((rows, dim), bf16),
            pltpu.VMEM((1, rows), f32),
            pltpu.VMEM((rows, dh), bf16),
            pltpu.SemaphoreType.DMA((CHUNKS, 4)),
            pltpu.SemaphoreType.DMA((2,)),
        ],
        compiler_params=params,
        cost_estimate=cost(2 * rows * dim * columns, 4 * 1024 * 1024),
        name="project",
    )(*in_hbm(tokens, fw_t, window_weight, value_weight, log_decay.T, out_grad))

    swap = [(0, 1), (1, 0)]
    recv = {}
    for d in range(1, chips):
        recv[2 * d] = lax.ppermute(sends[d], ctx[:-1], [(i, i ^ d) for i in range(chips)])
    recv[1] = lax.ppermute(sends[0], "core", swap)
    for d in range(1, chips):
        recv[2 * d + 1] = lax.ppermute(recv[2 * d], "core", swap)
    recv = [recv[d] for d in range(1, count)]
    if count > 8:
        recv = [jnp.stack(recv)]

    attended, stat, sheet = pl.pallas_call(
        lambda *refs: query_kernel(ctx, count, *refs),
        out_shape=(
            jax.ShapeDtypeStruct((rows, dh), bf16),
            jax.ShapeDtypeStruct((8, rows), f32),
            jax.ShapeDtypeStruct((rows, LANES), f32),
        ),
        in_specs=[VMEM] * (len(recv) + 4),
        out_specs=[VMEM] * 3,
        scratch_shapes=[
            pltpu.VMEM((count, 2 * rows, dh), bf16),
            pltpu.VMEM((WINDOW // rows + 1, rows, rows), f32),
            pltpu.VMEM((count, rows), f32),
        ],
        compiler_params=params,
        cost_estimate=cost(10**9, 2 * 1024 * 1024, 10**6),
        name="query_side",
    )(*recv, own, query, feat, cum)
    stats = [stat]
    for name in reversed(ctx):
        held = stats[0] if len(stats) == 1 else jnp.concatenate(stats, axis=0)
        stats.append(lax.ppermute(held, name, swap))
    if count > 8:
        stats = [jnp.concatenate(stats, axis=0)]

    share = dim // heads
    shared = heads & (heads - 1) == 0 and share % LANES == 0
    args = [*recv, *stats, own, query, feat, sheet]
    if shared:
        args += [ww, vw, fw]
        out_shape = [jax.ShapeDtypeStruct((rows // 2, share), f32)] * 2
        out_shape += [jax.ShapeDtypeStruct((rows // 2, share), bf16)] * (2 * heads - 2)
    else:
        out_shape = [jax.ShapeDtypeStruct((3 * rows + nf2 * rows // LANES, LANES), bf16)]
    grads = pl.pallas_call(
        lambda *refs: gradient_kernel(ctx, count, len(recv), len(stats), *refs),
        out_shape=out_shape,
        in_specs=[VMEM] * len(args),
        out_specs=[VMEM] * len(out_shape),
        scratch_shapes=[pltpu.VMEM((count, LANES), f32)],
        compiler_params=params,
        cost_estimate=cost(10**9, 2 * 1024 * 1024, 10**6),
        name="gradients",
    )(*args)
    if not shared:
        weights = jnp.concatenate([window_weight, value_weight, feature_weight], axis=1)
        weights = lax.all_gather(weights, "tp")
        return (attended, merge(lax.all_gather(grads[0], "tp"), weights, rows, dim))

    def sum_of(half):
        others = [
            lax.ppermute(grads[2 * t + half], "tp", [(z, z ^ t) for z in range(heads)])
            for t in range(heads - 1, 0, -1)
        ]
        return pl.pallas_call(
            add_kernel,
            out_shape=jax.ShapeDtypeStruct((rows // 2, share), bf16),
            in_specs=[VMEM] * heads,
            out_specs=VMEM,
            compiler_params=params,
            cost_estimate=cost(rows * share * heads, 2 * rows * share * heads),
            name="add",
        )(grads[half], *others)

    def lay(half, sums, before):
        return pl.pallas_call(
            partial(lay_kernel, half),
            out_shape=jax.ShapeDtypeStruct((rows, dim), bf16),
            in_specs=[VMEM] + [ANY] * len(before),
            out_specs=ANY,
            scratch_shapes=[pltpu.SemaphoreType.DMA((heads,))],
            input_output_aliases={1: 0} if before else {},
            compiler_params=params,
            cost_estimate=cost(1, 2 * rows * dim),
            name="lay",
        )(sums, *before)

    halves = [sum_of(half) for half in range(2)]
    first = lay(0, lax.all_gather(halves[0], "tp"), [])
    return (attended, lay(1, lax.all_gather(halves[1], "tp"), [first]))


def solution(mesh):
    blocks, tp = mesh.devices.shape
    bits = blocks.bit_length() - 1
    assert blocks == 2**bits
    ctx = tuple(f"half{i}" for i in range(bits - 1)) + ("core",)
    split = Mesh(mesh.devices.reshape((2,) * bits + (tp,)), (*ctx, "tp"))
    in_specs = (
        P(ctx, None),
        P(None, "tp"),
        P(None, "tp"),
        P(None, "tp"),
        P(ctx, "tp"),
        P(ctx, "tp"),
    )
    out_specs = (P(ctx, "tp"), P(ctx, None))
    return jax.shard_map(
        partial(per_device, ctx),
        mesh=split,
        in_specs=in_specs,
        out_specs=out_specs,
        check_vma=False,
    )
```

```python
from functools import partial

import jax
import jax.numpy as jnp
from jax import lax
from jax.experimental import pallas as pl
from jax.experimental.pallas import tpu as pltpu
from jax.sharding import Mesh
from jax.sharding import PartitionSpec as P

WINDOW = 1024
LANES = 128
MASKED = -1e30
CHUNKS = 4
f32 = jnp.float32
bf16 = jnp.bfloat16


def nn(a, b):
    return lax.dot_general(a, b, (((1,), (0,)), ((), ())), preferred_element_type=f32)


def nt(a, b):
    return lax.dot_general(a, b, (((1,), (1,)), ((), ())), preferred_element_type=f32)


def partner(me, d, count):
    assert count & (count - 1) == 0
    return jnp.bitwise_xor(me, d)


def wide(view, start, count):
    return jnp.concatenate(
        [view[start : start + count, :], view[start + count : start + 2 * count, :]], axis=1
    )


def put_wide(ref, start, value):
    count = value.shape[0]
    for half in range(value.shape[1] // LANES):
        ref[start + half * count : start + (half + 1) * count, :] = value[
            :, half * LANES : (half + 1) * LANES
        ]


def cum_row(view, start):
    tail = view[start : start + 16, :].astype(f32)
    first = tail[0:1] + tail[2:3] + tail[4:5]
    second = tail[1:2] + tail[3:4] + tail[5:6]
    return jnp.concatenate([first, second], axis=1)


def iotas(rows):
    return (
        lax.broadcasted_iota(jnp.int32, (rows, rows), 0),
        lax.broadcasted_iota(jnp.int32, (rows, rows), 1),
    )


def block_index(ctx):
    place = 0
    for name in ctx:
        place = place * lax.axis_size(name) + lax.axis_index(name)
    return place


def project_kernel(ctx, tok_hbm, fw_hbm, ww_hbm, vw_hbm, ld_hbm, do_hbm, *rest):
    *sends, keys_ref, query_ref, feat_ref, cum_ref, ww_ref, vw_ref, fw_ref = rest[:-5]
    tok_ref, ld_ref, do_ref, sems, small = rest[-5:]
    me = block_index(ctx)
    rows, dim = tok_ref.shape
    dh = do_ref.shape[1]
    nf = fw_ref.shape[0] // 2
    span = dim // CHUNKS
    copies = []
    for c in range(CHUNKS):
        part = pl.ds(c * span, span)
        copies.append([
            pltpu.make_async_copy(tok_hbm.at[:, part], tok_ref.at[:, part], sems.at[c, 0]),
            pltpu.make_async_copy(ww_hbm.at[part, :], ww_ref.at[part, :], sems.at[c, 1]),
            pltpu.make_async_copy(vw_hbm.at[part, :], vw_ref.at[part, :], sems.at[c, 2]),
            pltpu.make_async_copy(fw_hbm.at[:, part], fw_ref.at[:, part], sems.at[c, 3]),
        ])
    others = [
        pltpu.make_async_copy(ld_hbm, ld_ref, small.at[0]),
        pltpu.make_async_copy(do_hbm, do_ref, small.at[1]),
    ]
    for copy in others:
        copy.start()
    for group in copies:
        for at, copy in enumerate(group):
            copy.start(priority=min(at, 1))
    for copy in others:
        copy.wait()
    at_row, at_col = iotas(rows)
    ld_r = ld_ref[...]
    ld_c = jnp.sum(jnp.where(at_row == at_col, ld_r, 0.0), axis=1, keepdims=True)
    cum_r = jnp.sum(jnp.where(at_row <= at_col, ld_c, 0.0), axis=0, keepdims=True)
    cum_ref[...] = jnp.sum(jnp.where(at_col <= at_row, ld_r, 0.0), axis=1, keepdims=True)
    high = cum_r.astype(bf16)
    left = cum_r - high.astype(f32)
    mid = left.astype(bf16)
    low = (left - mid.astype(f32)).astype(bf16)
    pieces = [t[:, h : h + LANES].astype(f32) for t in (high, mid, low) for h in range(0, rows, LANES)]
    tail = jnp.concatenate(pieces + [jnp.zeros((10, LANES), f32)], axis=0).astype(bf16)

    feat = jnp.zeros((rows, 2 * nf), f32)
    main = jnp.zeros((rows, 3 * dh), f32)
    for c in range(CHUNKS):
        for copy in copies[c]:
            copy.wait()
        part = slice(c * span, (c + 1) * span)
        tok = tok_ref[:, part]
        feat += nt(tok, fw_ref[:, part])
        main += nn(tok, jnp.concatenate([ww_ref[part, :], vw_ref[part, :]], axis=1))
    feat = feat.astype(bf16)
    window = main[:, : 2 * dh].astype(bf16)
    values = main[:, 2 * dh :].astype(bf16)
    feat_ref[...] = feat
    small_row, small_col = iotas(2 * nf)
    feat_t = nt((small_row == small_col).astype(bf16), feat).astype(bf16)
    feat_at = 2 * rows
    tail_at = feat_at + 2 * nf

    def put_keys(ref):
        ref[0:rows, :] = window[:, dh:]
        ref[rows : 2 * rows, :] = values
        put_wide(ref, feat_at, feat_t[nf:, :])
        ref[tail_at : tail_at + 16, :] = tail

    def put_query(ref):
        ref[0:rows, :] = window[:, :dh]
        ref[rows : 2 * rows, :] = do_ref[...]
        put_wide(ref, feat_at, feat_t[:nf, :])
        ref[tail_at : tail_at + 16, :] = tail

    put_keys(keys_ref)
    put_query(query_ref)
    for at, ref in enumerate(sends):
        later = jnp.bitwise_xor(me, max(2 * at, 1)) > me
        pl.when(later)(lambda ref=ref: put_keys(ref))
        pl.when(jnp.logical_not(later))(lambda ref=ref: put_query(ref))

def pack_kernel(ctx, ww_hbm, vw_hbm, fw_hbm, out_ref, sems):
    nf2, dim = fw_hbm.shape
    tile = 2 * LANES
    at = pl.multiple_of(block_index(ctx) * tile, tile)
    rows = pl.ds(at, tile)
    moves = [
        (ww_hbm.at[rows, pl.ds(0, LANES)], out_ref.at[pl.ds(0, tile), :]),
        (ww_hbm.at[rows, pl.ds(LANES, LANES)], out_ref.at[pl.ds(tile, tile), :]),
        (vw_hbm.at[rows, :], out_ref.at[pl.ds(2 * tile, tile), :]),
    ]
    for m in range(2):
        lanes = pl.ds(pl.multiple_of(at + m * LANES, LANES), LANES)
        moves.append((fw_hbm.at[:, lanes], out_ref.at[pl.ds(3 * tile + m * nf2, nf2), :]))
    copies = [
        pltpu.make_async_copy(src, dst, sems.at[n]) for n, (src, dst) in enumerate(moves)
    ]
    for copy in copies:
        copy.start()
    used = 3 * tile + 2 * nf2
    out_ref[used:, :] = jnp.zeros((out_ref.shape[0] - used, LANES), bf16)
    for copy in copies:
        copy.wait()


def others_kernel(pack_hbm, out_ref, sems):
    head = lax.axis_index("tp")
    others, used, _ = out_ref.shape
    copies = [
        pltpu.make_async_copy(
            pack_hbm.at[jnp.bitwise_xor(head, t + 1), pl.ds(0, used), :], out_ref.at[t], sems.at[t]
        )
        for t in range(others)
    ]
    for copy in copies:
        copy.start()
    for copy in copies:
        copy.wait()


def between(totals, low, high):
    at = lax.broadcasted_iota(jnp.int32, totals.shape, 0)
    return jnp.sum(jnp.where((at > low) & (at < high), totals, 0.0), axis=0, keepdims=True)


def over_partners(count, body, carry):
    if count <= 8:
        for d in range(1, count):
            carry = body(d, carry)
        return carry
    return lax.fori_loop(1, count, body, carry)


def query_kernel(ctx, count, *rest):
    recvs = rest[: -10]
    (own_ref, query_ref, feat_ref, cum_ref, att_ref, stat_ref, sheet_ref, near_ref, p_ref,
     cums_ref) = rest[-10:]

    def recv(d):
        return recvs[d - 1] if len(recvs) > 1 else recvs[0].at[d - 1]

    me = block_index(ctx)
    rows, dh = att_ref.shape
    nf = feat_ref.shape[1] // 2
    back = WINDOW // rows
    feat_at = 2 * rows
    tail_at = feat_at + 2 * nf
    scale = dh ** (-0.5)
    feat_scale = nf ** (-0.5)
    wq = query_ref[0:rows, :]
    do = query_ref[rows : 2 * rows, :]
    q = feat_ref[:, :nf]
    at_row, at_col = iotas(rows)
    own_cum = cum_row(own_ref, tail_at)
    cums_ref[pl.ds(me, 1), :] = own_cum
    near_ref[me] = own_ref[0 : 2 * rows, :]

    def gather(d, carry):
        j = partner(me, d, count)
        view = recv(d)
        near_ref[j] = view[0 : 2 * rows, :]
        cums_ref[pl.ds(j, 1), :] = cum_row(view, tail_at)
        return carry

    over_partners(count, gather, 0)

    def near(w):
        return near_ref.at[jnp.maximum(me - back + w, 0)]

    top = jnp.full((rows, LANES), MASKED, f32)
    for w in range(back + 1):
        keys = own_ref[0:rows, :] if w == back else near(w)[0:rows, :]
        s = nt(wq, keys) * scale
        if w == back:
            s = jnp.where(at_col <= at_row, s, MASKED)
        elif w == 0:
            s = jnp.where((at_col > at_row) & (me >= back), s, MASKED)
        else:
            s = jnp.where(me >= back - w, s, MASKED)
        p_ref[w] = s
        for h in range(0, rows, LANES):
            top = jnp.maximum(top, s[:, h : h + LANES])
    top = jnp.max(top, axis=1, keepdims=True)
    total = jnp.zeros((rows, LANES), f32)
    out = jnp.zeros((rows, dh), f32)
    for w in range(back + 1):
        p = jnp.exp(p_ref[w] - top)
        for h in range(0, rows, LANES):
            total += p[:, h : h + LANES]
        vals = own_ref[rows : 2 * rows, :] if w == back else near(w)[rows : 2 * rows, :]
        out += nn(p.astype(bf16), vals)
    total = jnp.sum(total, axis=1, keepdims=True)
    windowed = out * (1.0 / total)

    cum_c = cum_ref[...]
    growth = jnp.exp(cum_c)
    totals = cums_ref[:, rows - 1 : rows]

    def forward(d, carry):
        num, den = carry
        j = partner(me, d, count)
        view = recv(d)
        gap = between(totals, j - 1, me)
        es = jnp.where(j < me, jnp.exp(jnp.minimum(gap - cums_ref[pl.ds(j, 1), :], 0.0)), 0.0)
        x = nn(q, wide(view, feat_at, nf)) * feat_scale
        weight = (1.0 + x + 0.5 * x * x) * es
        for h in range(0, rows, LANES):
            den += weight[:, h : h + LANES]
        num += nn(weight.astype(bf16), view[rows : 2 * rows, :])
        return num, den

    num, den = over_partners(
        count, forward, (jnp.zeros((rows, dh), f32), jnp.zeros((rows, LANES), f32))
    )
    x = nn(q, wide(own_ref, feat_at, nf)) * feat_scale
    e = jnp.where(at_col <= at_row, jnp.exp(jnp.minimum(cum_c - own_cum, 0.0)), 0.0)
    weight = (1.0 + x + 0.5 * x * x) * e
    num = num * growth + nn(weight.astype(bf16), own_ref[rows : 2 * rows, :])
    den = den * growth
    for h in range(0, rows, LANES):
        den += weight[:, h : h + LANES]
    rden = 1.0 / jnp.sum(den, axis=1, keepdims=True)
    linear = num * rden
    att_ref[...] = (linear + windowed).astype(bf16)
    do_f = do.astype(f32)
    delta_w = jnp.sum(do_f * windowed, axis=1, keepdims=True)
    delta_l = jnp.sum(do_f * linear, axis=1, keepdims=True)
    lse = top + jnp.log(total)
    lane = lax.broadcasted_iota(jnp.int32, (rows, LANES), 1)
    sheet = jnp.where(lane == 0, lse, 0.0)
    sheet = jnp.where(lane == 1, delta_w, sheet)
    sheet = jnp.where(lane == 2, rden, sheet)
    sheet = jnp.where(lane == 3, delta_l, sheet)
    sheet = jnp.where(lane == 4, cum_c, sheet)
    sheet_ref[...] = sheet
    stat_ref[...] = jnp.transpose(sheet)[0:8, :]


def gradient_kernel(ctx, count, recvs, stats, *rest):
    recvs, rest = rest[:recvs], rest[recvs:]
    stats, rest = rest[:stats], rest[stats:]
    own_ref, query_ref, feat_ref, sheet_ref, *rest, total_ref = rest

    def recv(d):
        return recvs[d - 1] if len(recvs) > 1 else recvs[0].at[d - 1]

    me = block_index(ctx)
    rows = feat_ref.shape[0]
    dh = LANES
    nf = feat_ref.shape[1] // 2
    feat_at = 2 * rows
    scale = dh ** (-0.5)
    feat_scale = nf ** (-0.5)
    at_row, at_col = iotas(rows)
    apart = at_row - at_col
    wq, wk = query_ref[0:rows, :], own_ref[0:rows, :]
    do, v = query_ref[rows : 2 * rows, :], own_ref[rows : 2 * rows, :]
    q, k = feat_ref[:, :nf], feat_ref[:, nf:]
    lse_c, dw_c = sheet_ref[:, 0:1], sheet_ref[:, 1:2]
    rden_c, dl_c, cum_c = sheet_ref[:, 2:3], sheet_ref[:, 3:4], sheet_ref[:, 4:5]
    def stat(d):
        if len(stats) == 1:
            return stats[0].at[pl.ds(pl.multiple_of(8 * d, 8), 8)]
        at = d.bit_length()
        return stats[at].at[pl.ds(8 * (d - (1 << at >> 1)), 8)]

    mine_ref = stat(0)
    own_cum = mine_ref[4:5, :]
    total_ref[pl.ds(me, 1), :] = own_cum[:, rows - LANES :]

    def place(d, carry):
        total_ref[pl.ds(partner(me, d, count), 1), :] = stat(d)[4:5, rows - LANES :]
        return carry

    over_partners(count, place, 0)
    totals = total_ref[:, LANES - 1 :]
    growth_c = jnp.exp(cum_c) * rden_c
    tail_c = jnp.exp(own_cum[:, rows - 1 : rows] - cum_c)

    def pick(flag, a, b):
        return jnp.where(flag, a, b)

    s = nt(wq, wk) * scale
    causal = at_col <= at_row
    p = jnp.where(causal, jnp.exp(s - lse_c), 0.0)
    dp = nt(do, v)
    dwq = nn((p * (dp - dw_c)).astype(bf16), wk)
    x = nn(q, wide(own_ref, feat_at, nf)) * feat_scale
    e = jnp.where(causal, jnp.exp(jnp.minimum(cum_c - own_cum, 0.0)), 0.0) * rden_c
    dx = (dp - dl_c) * e * (1.0 + x)
    dqt = nt(wide(own_ref, feat_at, nf), dx.astype(bf16))

    s = nt(wk, wq) * scale
    causal = at_row <= at_col
    p = jnp.where(causal, jnp.exp(s - mine_ref[0:1, :]), 0.0)
    dp = nt(v, do)
    dwk = nn((p * (dp - mine_ref[1:2, :])).astype(bf16), wq)
    x = nn(k, wide(query_ref, feat_at, nf)) * feat_scale
    e = jnp.where(causal, jnp.exp(jnp.minimum(own_cum - cum_c, 0.0)), 0.0) * mine_ref[2:3, :]
    dx = (dp - mine_ref[3:4, :]) * e * (1.0 + x)
    dkt = nt(wide(query_ref, feat_at, nf), dx.astype(bf16))
    dv = nn((p + (1.0 + x + 0.5 * x * x) * e).astype(bf16), do)

    def step(d, carry):
        dwq, dqt, dwk, dkt, dv = carry
        j = partner(me, d, count)
        view = recv(d)
        mine = j < me
        sign = pick(mine, 1, -1)
        limit = WINDOW - jnp.abs(me - j) * rows
        rows_w = pick(mine, wq, wk)
        rows_v = pick(mine, do, v)
        rows_f = pick(mine, q, k)
        other_w = view[0:rows, :]
        other_v = view[rows : 2 * rows, :]
        other_f = wide(view, feat_at, nf)
        st = stat(d)
        zero = jnp.zeros((1, rows), f32)
        cum = st[4:5, :]
        gap = between(totals, jnp.minimum(me, j), jnp.maximum(me, j))
        e_r = jnp.exp(jnp.minimum(gap + pick(mine, cum[:, rows - 1 : rows] - cum, cum), 0.0))
        e_r = e_r * pick(mine, 1.0, st[2:3, :])
        e_c = pick(mine, growth_c, tail_c)

        s = nt(rows_w, other_w) * scale
        p = jnp.exp(s - pick(mine, lse_c, 0.0) - pick(mine, zero, st[0:1, :]))
        p = jnp.where(apart * sign < limit, p, 0.0)
        dp = nt(rows_v, other_v)
        ds = p * (dp - pick(mine, dw_c, 0.0) - pick(mine, zero, st[1:2, :]))
        more_w = nn(ds.astype(bf16), other_w)
        x = nn(rows_f, other_f) * feat_scale
        e = e_r * e_c
        dx = (dp - pick(mine, dl_c, 0.0) - pick(mine, zero, st[3:4, :])) * e * (1.0 + x)
        more_f = nt(other_f, dx.astype(bf16))
        more_v = nn((p + (1.0 + x + 0.5 * x * x) * e).astype(bf16), other_v)
        dwq = dwq + pick(mine, more_w, 0.0)
        dwk = dwk + pick(mine, 0.0, more_w)
        dqt = dqt + pick(mine, more_f, 0.0)
        dkt = dkt + pick(mine, 0.0, more_f)
        dv = dv + pick(mine, 0.0, more_v)
        return dwq, dqt, dwk, dkt, dv

    dwq, dqt, dwk, dkt, dv = over_partners(count, step, (dwq, dqt, dwk, dkt, dv))
    dwq, dwk = (dwq * scale).astype(bf16), (dwk * scale).astype(bf16)
    dv = dv.astype(bf16)
    dft = (jnp.concatenate([dqt, dkt], axis=0) * feat_scale).astype(bf16)
    (grad_ref,) = rest
    grad_ref[0:rows, :] = dwq
    grad_ref[rows : 2 * rows, :] = dwk
    grad_ref[2 * rows : 3 * rows, :] = dv
    put_wide(grad_ref, 3 * rows, dft)


def gather_rows(grad_ref, order, cat_ref, feat_ref):
    rows = cat_ref.shape[0]
    nf2 = feat_ref.shape[1] // len(order)
    for at, h in enumerate(order):
        for part in range(3):
            lane = (3 * at + part) * LANES
            cat_ref[:, lane : lane + LANES] = grad_ref[h, part * rows : (part + 1) * rows, :]
    dft = jnp.concatenate([wide(grad_ref.at[h], 3 * rows, nf2) for h in order], axis=0)
    feat_ref[...] = jnp.transpose(dft.astype(f32)).astype(bf16)


def columns_kernel(ctx, side, grad_ref, ww_ref, vw_ref, fw_ref, *rest):
    pieces = rest[: ww_ref.shape[0] // (4 * LANES)]
    out_ref, cat_ref, feat_ref, tile_ref, sems = rest[-5:]
    heads = grad_ref.shape[0]
    nf2 = fw_ref.shape[0]
    tile = 2 * LANES
    head, me = lax.axis_index("tp"), block_index(ctx)
    gather_rows(
        grad_ref, [head] + [jnp.bitwise_xor(head, t) for t in range(1, heads)], cat_ref, feat_ref
    )
    copies = []
    for d, ref in enumerate(pieces):
        at = pl.multiple_of(jnp.bitwise_xor(me, 2 * d + side) * tile, tile)
        part = pl.ds(at, tile)
        main = [ww_ref[part, :], vw_ref[part, :]]
        main += [
            ref[t, m * tile : (m + 1) * tile, :] for t in range(heads - 1) for m in range(3)
        ]
        feats = [fw_ref[:, part]] + [wide(ref.at[t], 3 * tile, nf2) for t in range(heads - 1)]
        total = nt(cat_ref[...], jnp.concatenate(main, axis=1))
        total += nn(feat_ref[...], jnp.concatenate(feats, axis=0))
        tile_ref[d] = total.astype(bf16)
        copies.append(pltpu.make_async_copy(tile_ref.at[d], out_ref.at[:, part], sems.at[d]))
        copies[-1].start()
    for copy in copies:
        copy.wait()


def merge_kernel(grad_ref, weight_ref, out_ref, cat_ref, feat_ref):
    heads = grad_ref.shape[0]
    tile = out_ref.shape[1]
    lanes = 3 * LANES
    nf2 = feat_ref.shape[1] // heads

    @pl.when(pl.program_id(0) == 0)
    def _():
        gather_rows(grad_ref, range(heads), cat_ref, feat_ref)

    views = [weight_ref.at[h] for h in range(heads)]
    main = jnp.concatenate([v[:, 0:lanes] for v in views], axis=1)
    feats = jnp.concatenate([v[:, lanes:] for v in views], axis=1)
    out_ref[...] = (nt(cat_ref[...], main) + nt(feat_ref[...], feats)).astype(bf16)


VMEM = pl.BlockSpec(memory_space=pltpu.VMEM)
HBM = pl.BlockSpec(memory_space=pltpu.HBM)
ANY = pl.BlockSpec(memory_space=pl.ANY)
params = pltpu.CompilerParams(vmem_limit_bytes=32 * 1024 * 1024)


def in_hbm(*arrays):
    return [pltpu.with_memory_space_constraint(a, pltpu.HBM) for a in arrays]


def cost(flops, nbytes, exps=0):
    return pl.CostEstimate(flops=flops, bytes_accessed=nbytes, transcendentals=exps)


def merge(grads, weights, rows, dim):
    heads, _, columns = weights.shape
    tile = 2 * LANES
    return pl.pallas_call(
        merge_kernel,
        out_shape=jax.ShapeDtypeStruct((rows, dim), bf16),
        grid=(dim // tile,),
        in_specs=[
            pl.BlockSpec(grads.shape, lambda i: (0, 0, 0)),
            pl.BlockSpec((heads, tile, columns), lambda i: (0, i, 0)),
        ],
        out_specs=pl.BlockSpec((rows, tile), lambda i: (0, i)),
        scratch_shapes=[
            pltpu.VMEM((rows, 3 * LANES * heads), bf16),
            pltpu.VMEM((rows, (columns - 3 * LANES) * heads), bf16),
        ],
        compiler_params=params,
        cost_estimate=cost(2 * rows * dim * heads * columns, heads * dim * columns * 2),
        name="head_sum",
    )(grads, weights)


def per_device(ctx, tokens, feature_weight, window_weight, value_weight, log_decay, out_grad):
    rows, dim = tokens.shape
    nf2 = feature_weight.shape[1]
    nf = nf2 // 2
    dh = value_weight.shape[1]
    columns = 3 * dh + nf2
    chips, count, heads = lax.axis_size(ctx[:-1]), lax.axis_size(ctx), lax.axis_size("tp")
    fw_t = feature_weight.T
    tile = 2 * LANES
    spread = heads == 4 and count * tile == dim and count == 8
    if spread:
        packed = pl.pallas_call(
            partial(pack_kernel, ctx),
            out_shape=jax.ShapeDtypeStruct((4 * tile, LANES), bf16),
            in_specs=[HBM] * 3,
            out_specs=VMEM,
            scratch_shapes=[pltpu.SemaphoreType.DMA((5,))],
            compiler_params=params,
            cost_estimate=cost(1, 4 * columns * tile),
            name="pack",
        )(*in_hbm(window_weight, value_weight, fw_t))
        weights = lax.all_gather(packed, "tp")

    payload = 2 * rows + 2 * nf + 16
    block = jax.ShapeDtypeStruct((payload, LANES), bf16)
    *sends, own, query, feat, cum, ww, vw, fw = pl.pallas_call(
        partial(project_kernel, ctx),
        out_shape=[block] * (chips + 2)
        + [
            jax.ShapeDtypeStruct((rows, nf2), bf16),
            jax.ShapeDtypeStruct((rows, 1), f32),
            jax.ShapeDtypeStruct((dim, 2 * dh), bf16),
            jax.ShapeDtypeStruct((dim, dh), bf16),
            jax.ShapeDtypeStruct((nf2, dim), bf16),
        ],
        in_specs=[HBM] * 6,
        out_specs=[VMEM] * (chips + 7),
        scratch_shapes=[
            pltpu.VMEM((rows, dim), bf16),
            pltpu.VMEM((1, rows), f32),
            pltpu.VMEM((rows, dh), bf16),
            pltpu.SemaphoreType.DMA((CHUNKS, 4)),
            pltpu.SemaphoreType.DMA((2,)),
        ],
        compiler_params=params,
        cost_estimate=cost(2 * rows * dim * columns, 4 * 1024 * 1024),
        name="project",
    )(*in_hbm(tokens, fw_t, window_weight, value_weight, log_decay.T, out_grad))

    swap = [(0, 1), (1, 0)]
    recv = {}
    for d in range(1, chips):
        recv[2 * d] = lax.ppermute(sends[d], ctx[:-1], [(i, i ^ d) for i in range(chips)])
    recv[1] = lax.ppermute(sends[0], "core", swap)
    for d in range(1, chips):
        recv[2 * d + 1] = lax.ppermute(recv[2 * d], "core", swap)
    recv = [recv[d] for d in range(1, count)]
    if count > 8:
        recv = [jnp.stack(recv)]

    attended, stat, sheet = pl.pallas_call(
        lambda *refs: query_kernel(ctx, count, *refs),
        out_shape=(
            jax.ShapeDtypeStruct((rows, dh), bf16),
            jax.ShapeDtypeStruct((8, rows), f32),
            jax.ShapeDtypeStruct((rows, LANES), f32),
        ),
        in_specs=[VMEM] * (len(recv) + 4),
        out_specs=[VMEM] * 3,
        scratch_shapes=[
            pltpu.VMEM((count, 2 * rows, dh), bf16),
            pltpu.VMEM((WINDOW // rows + 1, rows, rows), f32),
            pltpu.VMEM((count, rows), f32),
        ],
        compiler_params=params,
        cost_estimate=cost(10**9, 2 * 1024 * 1024, 10**6),
        name="query_side",
    )(*recv, own, query, feat, cum)
    stats = [stat]
    for name in reversed(ctx):
        held = stats[0] if len(stats) == 1 else jnp.concatenate(stats, axis=0)
        stats.append(lax.ppermute(held, name, swap))
    if count > 8:
        stats = [jnp.concatenate(stats, axis=0)]

    grads = pl.pallas_call(
        lambda *refs: gradient_kernel(ctx, count, len(recv), len(stats), *refs),
        out_shape=jax.ShapeDtypeStruct((3 * rows + nf2 * rows // LANES, LANES), bf16),
        in_specs=[VMEM] * (len(recv) + len(stats) + 4),
        out_specs=VMEM,
        scratch_shapes=[pltpu.VMEM((count, LANES), f32)],
        compiler_params=params,
        cost_estimate=cost(10**9, 2 * 1024 * 1024, 10**6),
        name="gradients",
    )(*recv, *stats, own, query, feat, sheet)
    if not spread:
        weights = jnp.concatenate([window_weight, value_weight, feature_weight], axis=1)
        weights = lax.all_gather(weights, "tp")
        return (attended, merge(lax.all_gather(grads, "tp"), weights, rows, dim))

    weights, grads = lax.optimization_barrier((weights, grads))
    pieces = [
        pl.pallas_call(
            others_kernel,
            out_shape=jax.ShapeDtypeStruct((heads - 1, columns * tile // LANES, LANES), bf16),
            in_specs=[HBM],
            out_specs=VMEM,
            scratch_shapes=[pltpu.SemaphoreType.DMA((heads - 1,))],
            compiler_params=params,
            cost_estimate=cost(1, heads * columns * tile * 4),
            name="others",
        )(*in_hbm(weights))
    ]
    pieces[0], grads = lax.optimization_barrier((pieces[0], grads))
    for d in range(1, chips):
        pieces.append(
            lax.ppermute(pieces[0], ctx[:-1], [(i, i ^ d) for i in range(chips)])
        )
    grads = lax.all_gather(grads, "tp")
    swapped = [lax.ppermute(p, "core", swap) for p in pieces]

    def columns_of(side, pieces, before):
        return pl.pallas_call(
            partial(columns_kernel, ctx, side),
            out_shape=jax.ShapeDtypeStruct((rows, dim), bf16),
            in_specs=[VMEM] * (4 + chips) + [ANY] * len(before),
            out_specs=ANY,
            scratch_shapes=[
                pltpu.VMEM((rows, 3 * LANES * heads), bf16),
                pltpu.VMEM((rows, nf2 * heads), bf16),
                pltpu.VMEM((chips, rows, tile), bf16),
                pltpu.SemaphoreType.DMA((chips,)),
            ],
            input_output_aliases={4 + chips: 0} if before else {},
            compiler_params=params,
            cost_estimate=cost(rows * dim * heads * columns, heads * dim * columns),
            name="columns",
        )(grads, ww, vw, fw, *pieces, *before)

    first = columns_of(0, pieces, [])
    return (attended, columns_of(1, swapped, [first]))


def solution(mesh):
    blocks, tp = mesh.devices.shape
    bits = blocks.bit_length() - 1
    assert blocks == 2**bits
    ctx = tuple(f"half{i}" for i in range(bits - 1)) + ("core",)
    split = Mesh(mesh.devices.reshape((2,) * bits + (tp,)), (*ctx, "tp"))
    in_specs = (
        P(ctx, None),
        P(None, "tp"),
        P(None, "tp"),
        P(None, "tp"),
        P(ctx, "tp"),
        P(ctx, "tp"),
    )
    out_specs = (P(ctx, "tp"), P(ctx, None))
    return jax.shard_map(
        partial(per_device, ctx),
        mesh=split,
        in_specs=in_specs,
        out_specs=out_specs,
        check_vma=False,
    )
```

```python
from functools import partial

import jax
import jax.numpy as jnp
from jax import lax
from jax.experimental import pallas as pl
from jax.experimental.pallas import tpu as pltpu
from jax.sharding import Mesh
from jax.sharding import PartitionSpec as P

WINDOW = 1024
LANES = 128
MASKED = -1e30
CHUNKS = 4
f32 = jnp.float32
bf16 = jnp.bfloat16


def nn(a, b):
    return lax.dot_general(a, b, (((1,), (0,)), ((), ())), preferred_element_type=f32)


def nt(a, b):
    return lax.dot_general(a, b, (((1,), (1,)), ((), ())), preferred_element_type=f32)


def partner(me, d, count):
    assert count & (count - 1) == 0
    return jnp.bitwise_xor(me, d)


def wide(view, start, count):
    return jnp.concatenate(
        [view[start : start + count, :], view[start + count : start + 2 * count, :]], axis=1
    )


def put_wide(ref, start, value):
    count = value.shape[0]
    for half in range(value.shape[1] // LANES):
        ref[start + half * count : start + (half + 1) * count, :] = value[
            :, half * LANES : (half + 1) * LANES
        ]


def cum_row(view, start):
    tail = view[start : start + 16, :].astype(f32)
    first = tail[0:1] + tail[2:3] + tail[4:5]
    second = tail[1:2] + tail[3:4] + tail[5:6]
    return jnp.concatenate([first, second], axis=1)


def iotas(rows):
    return (
        lax.broadcasted_iota(jnp.int32, (rows, rows), 0),
        lax.broadcasted_iota(jnp.int32, (rows, rows), 1),
    )


def block_index(ctx):
    place = 0
    for name in ctx:
        place = place * lax.axis_size(name) + lax.axis_index(name)
    return place


def project_kernel(ctx, tok_hbm, fw_hbm, ww_hbm, vw_hbm, ld_hbm, do_hbm, *rest):
    *sends, keys_ref, query_ref, feat_ref, cum_ref, ww_ref, vw_ref, fw_ref = rest[:-5]
    tok_ref, ld_ref, do_ref, sems, small = rest[-5:]
    me = block_index(ctx)
    rows, dim = tok_ref.shape
    dh = do_ref.shape[1]
    nf = fw_ref.shape[0] // 2
    span = dim // CHUNKS
    copies = []
    for c in range(CHUNKS):
        part = pl.ds(c * span, span)
        copies.append([
            pltpu.make_async_copy(tok_hbm.at[:, part], tok_ref.at[:, part], sems.at[c, 0]),
            pltpu.make_async_copy(ww_hbm.at[part, :], ww_ref.at[part, :], sems.at[c, 1]),
            pltpu.make_async_copy(vw_hbm.at[part, :], vw_ref.at[part, :], sems.at[c, 2]),
            pltpu.make_async_copy(fw_hbm.at[:, part], fw_ref.at[:, part], sems.at[c, 3]),
        ])
    others = [
        pltpu.make_async_copy(ld_hbm, ld_ref, small.at[0]),
        pltpu.make_async_copy(do_hbm, do_ref, small.at[1]),
    ]
    for copy in others:
        copy.start()
    for group in copies:
        for at, copy in enumerate(group):
            copy.start(priority=min(at, 1))
    for copy in others:
        copy.wait()
    at_row, at_col = iotas(rows)
    ld_r = ld_ref[...]
    ld_c = jnp.sum(jnp.where(at_row == at_col, ld_r, 0.0), axis=1, keepdims=True)
    cum_r = jnp.sum(jnp.where(at_row <= at_col, ld_c, 0.0), axis=0, keepdims=True)
    cum_ref[...] = jnp.sum(jnp.where(at_col <= at_row, ld_r, 0.0), axis=1, keepdims=True)
    high = cum_r.astype(bf16)
    left = cum_r - high.astype(f32)
    mid = left.astype(bf16)
    low = (left - mid.astype(f32)).astype(bf16)
    pieces = [t[:, h : h + LANES].astype(f32) for t in (high, mid, low) for h in range(0, rows, LANES)]
    tail = jnp.concatenate(pieces + [jnp.zeros((10, LANES), f32)], axis=0).astype(bf16)

    feat = jnp.zeros((rows, 2 * nf), f32)
    main = jnp.zeros((rows, 3 * dh), f32)
    for c in range(CHUNKS):
        for copy in copies[c]:
            copy.wait()
        part = slice(c * span, (c + 1) * span)
        tok = tok_ref[:, part]
        feat += nt(tok, fw_ref[:, part])
        main += nn(tok, jnp.concatenate([ww_ref[part, :], vw_ref[part, :]], axis=1))
    feat = feat.astype(bf16)
    window = main[:, : 2 * dh].astype(bf16)
    values = main[:, 2 * dh :].astype(bf16)
    feat_ref[...] = feat
    small_row, small_col = iotas(2 * nf)
    feat_t = nt((small_row == small_col).astype(bf16), feat).astype(bf16)
    feat_at = 2 * rows
    tail_at = feat_at + 2 * nf

    def put_keys(ref):
        ref[0:rows, :] = window[:, dh:]
        ref[rows : 2 * rows, :] = values
        put_wide(ref, feat_at, feat_t[nf:, :])
        ref[tail_at : tail_at + 16, :] = tail

    def put_query(ref):
        ref[0:rows, :] = window[:, :dh]
        ref[rows : 2 * rows, :] = do_ref[...]
        put_wide(ref, feat_at, feat_t[:nf, :])
        ref[tail_at : tail_at + 16, :] = tail

    put_keys(keys_ref)
    put_query(query_ref)
    for at, ref in enumerate(sends):
        later = jnp.bitwise_xor(me, max(2 * at, 1)) > me
        pl.when(later)(lambda ref=ref: put_keys(ref))
        pl.when(jnp.logical_not(later))(lambda ref=ref: put_query(ref))

def pack_kernel(ctx, ww_hbm, vw_hbm, fw_hbm, out_ref, sems):
    nf2, dim = fw_hbm.shape
    tile = 2 * LANES
    at = pl.multiple_of(block_index(ctx) * tile, tile)
    rows = pl.ds(at, tile)
    moves = [
        (ww_hbm.at[rows, pl.ds(0, LANES)], out_ref.at[pl.ds(0, tile), :]),
        (ww_hbm.at[rows, pl.ds(LANES, LANES)], out_ref.at[pl.ds(tile, tile), :]),
        (vw_hbm.at[rows, :], out_ref.at[pl.ds(2 * tile, tile), :]),
    ]
    for m in range(2):
        lanes = pl.ds(pl.multiple_of(at + m * LANES, LANES), LANES)
        moves.append((fw_hbm.at[:, lanes], out_ref.at[pl.ds(3 * tile + m * nf2, nf2), :]))
    copies = [
        pltpu.make_async_copy(src, dst, sems.at[n]) for n, (src, dst) in enumerate(moves)
    ]
    for copy in copies:
        copy.start()
    for copy in copies:
        copy.wait()


def stack_kernel(*refs):
    *parts, out_ref = refs
    for t, ref in enumerate(parts):
        out_ref[t] = ref[...]


def between(totals, low, high):
    at = lax.broadcasted_iota(jnp.int32, totals.shape, 0)
    return jnp.sum(jnp.where((at > low) & (at < high), totals, 0.0), axis=0, keepdims=True)


def over_partners(count, body, carry):
    if count <= 8:
        for d in range(1, count):
            carry = body(d, carry)
        return carry
    return lax.fori_loop(1, count, body, carry)


def query_kernel(ctx, count, *rest):
    recvs = rest[: -10]
    (own_ref, query_ref, feat_ref, cum_ref, att_ref, stat_ref, sheet_ref, near_ref, p_ref,
     cums_ref) = rest[-10:]

    def recv(d):
        return recvs[d - 1] if len(recvs) > 1 else recvs[0].at[d - 1]

    me = block_index(ctx)
    rows, dh = att_ref.shape
    nf = feat_ref.shape[1] // 2
    back = WINDOW // rows
    feat_at = 2 * rows
    tail_at = feat_at + 2 * nf
    scale = dh ** (-0.5)
    feat_scale = nf ** (-0.5)
    wq = query_ref[0:rows, :]
    do = query_ref[rows : 2 * rows, :]
    q = feat_ref[:, :nf]
    at_row, at_col = iotas(rows)
    own_cum = cum_row(own_ref, tail_at)
    cums_ref[pl.ds(me, 1), :] = own_cum
    near_ref[me] = own_ref[0 : 2 * rows, :]

    def gather(d, carry):
        j = partner(me, d, count)
        view = recv(d)
        near_ref[j] = view[0 : 2 * rows, :]
        cums_ref[pl.ds(j, 1), :] = cum_row(view, tail_at)
        return carry

    over_partners(count, gather, 0)

    def near(w):
        return near_ref.at[jnp.maximum(me - back + w, 0)]

    top = jnp.full((rows, LANES), MASKED, f32)
    for w in range(back + 1):
        keys = own_ref[0:rows, :] if w == back else near(w)[0:rows, :]
        s = nt(wq, keys) * scale
        if w == back:
            s = jnp.where(at_col <= at_row, s, MASKED)
        elif w == 0:
            s = jnp.where((at_col > at_row) & (me >= back), s, MASKED)
        else:
            s = jnp.where(me >= back - w, s, MASKED)
        p_ref[w] = s
        for h in range(0, rows, LANES):
            top = jnp.maximum(top, s[:, h : h + LANES])
    top = jnp.max(top, axis=1, keepdims=True)
    total = jnp.zeros((rows, LANES), f32)
    out = jnp.zeros((rows, dh), f32)
    for w in range(back + 1):
        p = jnp.exp(p_ref[w] - top)
        for h in range(0, rows, LANES):
            total += p[:, h : h + LANES]
        vals = own_ref[rows : 2 * rows, :] if w == back else near(w)[rows : 2 * rows, :]
        out += nn(p.astype(bf16), vals)
    total = jnp.sum(total, axis=1, keepdims=True)
    windowed = out * (1.0 / total)

    cum_c = cum_ref[...]
    growth = jnp.exp(cum_c)
    totals = cums_ref[:, rows - 1 : rows]

    def forward(d, carry):
        num, den = carry
        j = partner(me, d, count)
        view = recv(d)
        gap = between(totals, j - 1, me)
        es = jnp.where(j < me, jnp.exp(jnp.minimum(gap - cums_ref[pl.ds(j, 1), :], 0.0)), 0.0)
        x = nn(q, wide(view, feat_at, nf)) * feat_scale
        weight = (1.0 + x + 0.5 * x * x) * es
        for h in range(0, rows, LANES):
            den += weight[:, h : h + LANES]
        num += nn(weight.astype(bf16), view[rows : 2 * rows, :])
        return num, den

    num, den = over_partners(
        count, forward, (jnp.zeros((rows, dh), f32), jnp.zeros((rows, LANES), f32))
    )
    x = nn(q, wide(own_ref, feat_at, nf)) * feat_scale
    e = jnp.where(at_col <= at_row, jnp.exp(jnp.minimum(cum_c - own_cum, 0.0)), 0.0)
    weight = (1.0 + x + 0.5 * x * x) * e
    num = num * growth + nn(weight.astype(bf16), own_ref[rows : 2 * rows, :])
    den = den * growth
    for h in range(0, rows, LANES):
        den += weight[:, h : h + LANES]
    rden = 1.0 / jnp.sum(den, axis=1, keepdims=True)
    linear = num * rden
    att_ref[...] = (linear + windowed).astype(bf16)
    do_f = do.astype(f32)
    delta_w = jnp.sum(do_f * windowed, axis=1, keepdims=True)
    delta_l = jnp.sum(do_f * linear, axis=1, keepdims=True)
    lse = top + jnp.log(total)
    lane = lax.broadcasted_iota(jnp.int32, (rows, LANES), 1)
    sheet = jnp.where(lane == 0, lse, 0.0)
    sheet = jnp.where(lane == 1, delta_w, sheet)
    sheet = jnp.where(lane == 2, rden, sheet)
    sheet = jnp.where(lane == 3, delta_l, sheet)
    sheet = jnp.where(lane == 4, cum_c, sheet)
    sheet_ref[...] = sheet
    stat_ref[...] = jnp.transpose(sheet)[0:8, :]


def gradient_kernel(ctx, count, recvs, stats, *rest):
    recvs, rest = rest[:recvs], rest[recvs:]
    stats, rest = rest[:stats], rest[stats:]
    own_ref, query_ref, feat_ref, sheet_ref, *rest, total_ref = rest

    def recv(d):
        return recvs[d - 1] if len(recvs) > 1 else recvs[0].at[d - 1]

    me = block_index(ctx)
    rows = feat_ref.shape[0]
    dh = LANES
    nf = feat_ref.shape[1] // 2
    feat_at = 2 * rows
    scale = dh ** (-0.5)
    feat_scale = nf ** (-0.5)
    at_row, at_col = iotas(rows)
    apart = at_row - at_col
    wq, wk = query_ref[0:rows, :], own_ref[0:rows, :]
    do, v = query_ref[rows : 2 * rows, :], own_ref[rows : 2 * rows, :]
    q, k = feat_ref[:, :nf], feat_ref[:, nf:]
    lse_c, dw_c = sheet_ref[:, 0:1], sheet_ref[:, 1:2]
    rden_c, dl_c, cum_c = sheet_ref[:, 2:3], sheet_ref[:, 3:4], sheet_ref[:, 4:5]
    def stat(d):
        if len(stats) == 1:
            return stats[0].at[pl.ds(pl.multiple_of(8 * d, 8), 8)]
        at = d.bit_length()
        return stats[at].at[pl.ds(8 * (d - (1 << at >> 1)), 8)]

    mine_ref = stat(0)
    own_cum = mine_ref[4:5, :]
    total_ref[pl.ds(me, 1), :] = own_cum[:, rows - LANES :]

    def place(d, carry):
        total_ref[pl.ds(partner(me, d, count), 1), :] = stat(d)[4:5, rows - LANES :]
        return carry

    over_partners(count, place, 0)
    totals = total_ref[:, LANES - 1 :]
    growth_c = jnp.exp(cum_c) * rden_c
    tail_c = jnp.exp(own_cum[:, rows - 1 : rows] - cum_c)

    def pick(flag, a, b):
        return jnp.where(flag, a, b)

    s = nt(wq, wk) * scale
    causal = at_col <= at_row
    p = jnp.where(causal, jnp.exp(s - lse_c), 0.0)
    dp = nt(do, v)
    dwq = nn((p * (dp - dw_c)).astype(bf16), wk)
    x = nn(q, wide(own_ref, feat_at, nf)) * feat_scale
    e = jnp.where(causal, jnp.exp(jnp.minimum(cum_c - own_cum, 0.0)), 0.0) * rden_c
    dx = (dp - dl_c) * e * (1.0 + x)
    dqt = nt(wide(own_ref, feat_at, nf), dx.astype(bf16))

    s = nt(wk, wq) * scale
    causal = at_row <= at_col
    p = jnp.where(causal, jnp.exp(s - mine_ref[0:1, :]), 0.0)
    dp = nt(v, do)
    dwk = nn((p * (dp - mine_ref[1:2, :])).astype(bf16), wq)
    x = nn(k, wide(query_ref, feat_at, nf)) * feat_scale
    e = jnp.where(causal, jnp.exp(jnp.minimum(own_cum - cum_c, 0.0)), 0.0) * mine_ref[2:3, :]
    dx = (dp - mine_ref[3:4, :]) * e * (1.0 + x)
    dkt = nt(wide(query_ref, feat_at, nf), dx.astype(bf16))
    dv = nn((p + (1.0 + x + 0.5 * x * x) * e).astype(bf16), do)

    def step(d, carry):
        dwq, dqt, dwk, dkt, dv = carry
        j = partner(me, d, count)
        view = recv(d)
        mine = j < me
        sign = pick(mine, 1, -1)
        limit = WINDOW - jnp.abs(me - j) * rows
        rows_w = pick(mine, wq, wk)
        rows_v = pick(mine, do, v)
        rows_f = pick(mine, q, k)
        other_w = view[0:rows, :]
        other_v = view[rows : 2 * rows, :]
        other_f = wide(view, feat_at, nf)
        st = stat(d)
        zero = jnp.zeros((1, rows), f32)
        cum = st[4:5, :]
        gap = between(totals, jnp.minimum(me, j), jnp.maximum(me, j))
        e_r = jnp.exp(jnp.minimum(gap + pick(mine, cum[:, rows - 1 : rows] - cum, cum), 0.0))
        e_r = e_r * pick(mine, 1.0, st[2:3, :])
        e_c = pick(mine, growth_c, tail_c)

        s = nt(rows_w, other_w) * scale
        p = jnp.exp(s - pick(mine, lse_c, 0.0) - pick(mine, zero, st[0:1, :]))
        p = jnp.where(apart * sign < limit, p, 0.0)
        dp = nt(rows_v, other_v)
        ds = p * (dp - pick(mine, dw_c, 0.0) - pick(mine, zero, st[1:2, :]))
        more_w = nn(ds.astype(bf16), other_w)
        x = nn(rows_f, other_f) * feat_scale
        e = e_r * e_c
        dx = (dp - pick(mine, dl_c, 0.0) - pick(mine, zero, st[3:4, :])) * e * (1.0 + x)
        more_f = nt(other_f, dx.astype(bf16))
        more_v = nn((p + (1.0 + x + 0.5 * x * x) * e).astype(bf16), other_v)
        dwq = dwq + pick(mine, more_w, 0.0)
        dwk = dwk + pick(mine, 0.0, more_w)
        dqt = dqt + pick(mine, more_f, 0.0)
        dkt = dkt + pick(mine, 0.0, more_f)
        dv = dv + pick(mine, 0.0, more_v)
        return dwq, dqt, dwk, dkt, dv

    dwq, dqt, dwk, dkt, dv = over_partners(count, step, (dwq, dqt, dwk, dkt, dv))
    dwq, dwk = (dwq * scale).astype(bf16), (dwk * scale).astype(bf16)
    dv = dv.astype(bf16)
    dft = (jnp.concatenate([dqt, dkt], axis=0) * feat_scale).astype(bf16)
    (grad_ref,) = rest
    grad_ref[0:rows, :] = dwq
    grad_ref[rows : 2 * rows, :] = dwk
    grad_ref[2 * rows : 3 * rows, :] = dv
    put_wide(grad_ref, 3 * rows, dft)


def gather_rows(grad_ref, order, cat_ref, feat_ref):
    rows = cat_ref.shape[0]
    nf2 = feat_ref.shape[1] // len(order)
    for at, h in enumerate(order):
        for part in range(3):
            lane = (3 * at + part) * LANES
            cat_ref[:, lane : lane + LANES] = grad_ref[h, part * rows : (part + 1) * rows, :]
    dft = jnp.concatenate([wide(grad_ref.at[h], 3 * rows, nf2) for h in order], axis=0)
    feat_ref[...] = jnp.transpose(dft.astype(f32)).astype(bf16)


def columns_kernel(ctx, side, grad_ref, ww_ref, vw_ref, fw_ref, *rest):
    pieces = rest[: ww_ref.shape[0] // (4 * LANES)]
    out_ref, cat_ref, feat_ref, tile_ref, sems = rest[-5:]
    heads = grad_ref.shape[0]
    nf2 = fw_ref.shape[0]
    tile = 2 * LANES
    head, me = lax.axis_index("tp"), block_index(ctx)
    gather_rows(
        grad_ref, [head] + [jnp.bitwise_xor(head, t) for t in range(1, heads)], cat_ref, feat_ref
    )
    copies = []
    for d, ref in enumerate(pieces):
        at = pl.multiple_of(jnp.bitwise_xor(me, 2 * d + side) * tile, tile)
        part = pl.ds(at, tile)
        main = [ww_ref[part, :], vw_ref[part, :]]
        main += [
            ref[t, m * tile : (m + 1) * tile, :] for t in range(heads - 1) for m in range(3)
        ]
        feats = [fw_ref[:, part]] + [wide(ref.at[t], 3 * tile, nf2) for t in range(heads - 1)]
        total = nt(cat_ref[...], jnp.concatenate(main, axis=1))
        total += nn(feat_ref[...], jnp.concatenate(feats, axis=0))
        tile_ref[d] = total.astype(bf16)
        copies.append(pltpu.make_async_copy(tile_ref.at[d], out_ref.at[:, part], sems.at[d]))
        copies[-1].start()
    for copy in copies:
        copy.wait()


def merge_kernel(grad_ref, weight_ref, out_ref, cat_ref, feat_ref):
    heads = grad_ref.shape[0]
    tile = out_ref.shape[1]
    lanes = 3 * LANES
    nf2 = feat_ref.shape[1] // heads

    @pl.when(pl.program_id(0) == 0)
    def _():
        gather_rows(grad_ref, range(heads), cat_ref, feat_ref)

    views = [weight_ref.at[h] for h in range(heads)]
    main = jnp.concatenate([v[:, 0:lanes] for v in views], axis=1)
    feats = jnp.concatenate([v[:, lanes:] for v in views], axis=1)
    out_ref[...] = (nt(cat_ref[...], main) + nt(feat_ref[...], feats)).astype(bf16)


VMEM = pl.BlockSpec(memory_space=pltpu.VMEM)
HBM = pl.BlockSpec(memory_space=pltpu.HBM)
ANY = pl.BlockSpec(memory_space=pl.ANY)
params = pltpu.CompilerParams(vmem_limit_bytes=32 * 1024 * 1024)


def in_hbm(*arrays):
    return [pltpu.with_memory_space_constraint(a, pltpu.HBM) for a in arrays]


def cost(flops, nbytes, exps=0):
    return pl.CostEstimate(flops=flops, bytes_accessed=nbytes, transcendentals=exps)


def merge(grads, weights, rows, dim):
    heads, _, columns = weights.shape
    tile = 2 * LANES
    return pl.pallas_call(
        merge_kernel,
        out_shape=jax.ShapeDtypeStruct((rows, dim), bf16),
        grid=(dim // tile,),
        in_specs=[
            pl.BlockSpec(grads.shape, lambda i: (0, 0, 0)),
            pl.BlockSpec((heads, tile, columns), lambda i: (0, i, 0)),
        ],
        out_specs=pl.BlockSpec((rows, tile), lambda i: (0, i)),
        scratch_shapes=[
            pltpu.VMEM((rows, 3 * LANES * heads), bf16),
            pltpu.VMEM((rows, (columns - 3 * LANES) * heads), bf16),
        ],
        compiler_params=params,
        cost_estimate=cost(2 * rows * dim * heads * columns, heads * dim * columns * 2),
        name="head_sum",
    )(grads, weights)


def per_device(ctx, tokens, feature_weight, window_weight, value_weight, log_decay, out_grad):
    rows, dim = tokens.shape
    nf2 = feature_weight.shape[1]
    nf = nf2 // 2
    dh = value_weight.shape[1]
    columns = 3 * dh + nf2
    chips, count, heads = lax.axis_size(ctx[:-1]), lax.axis_size(ctx), lax.axis_size("tp")
    fw_t = feature_weight.T
    tile = 2 * LANES
    spread = heads == 4 and count * tile == dim and count == 8
    if spread:
        packed = pl.pallas_call(
            partial(pack_kernel, ctx),
            out_shape=jax.ShapeDtypeStruct((columns * tile // LANES, LANES), bf16),
            in_specs=[HBM] * 3,
            out_specs=VMEM,
            scratch_shapes=[pltpu.SemaphoreType.DMA((5,))],
            compiler_params=params,
            cost_estimate=cost(1, 4 * columns * tile),
            name="pack",
        )(*in_hbm(window_weight, value_weight, fw_t))
        near = [
            lax.ppermute(packed, "tp", [(z, z ^ t) for z in range(heads)])
            for t in range(1, heads)
        ]
        pieces = [
            pl.pallas_call(
                stack_kernel,
                out_shape=jax.ShapeDtypeStruct((heads - 1, *packed.shape), bf16),
                in_specs=[VMEM] * (heads - 1),
                out_specs=VMEM,
                compiler_params=params,
                cost_estimate=cost(1, 4 * packed.size * heads),
                name="stack",
            )(*near)
        ]
        for d in range(1, chips):
            pieces.append(
                lax.ppermute(pieces[0], ctx[:-1], [(i, i ^ d) for i in range(chips)])
            )

    payload = 2 * rows + 2 * nf + 16
    block = jax.ShapeDtypeStruct((payload, LANES), bf16)
    *sends, own, query, feat, cum, ww, vw, fw = pl.pallas_call(
        partial(project_kernel, ctx),
        out_shape=[block] * (chips + 2)
        + [
            jax.ShapeDtypeStruct((rows, nf2), bf16),
            jax.ShapeDtypeStruct((rows, 1), f32),
            jax.ShapeDtypeStruct((dim, 2 * dh), bf16),
            jax.ShapeDtypeStruct((dim, dh), bf16),
            jax.ShapeDtypeStruct((nf2, dim), bf16),
        ],
        in_specs=[HBM] * 6,
        out_specs=[VMEM] * (chips + 7),
        scratch_shapes=[
            pltpu.VMEM((rows, dim), bf16),
            pltpu.VMEM((1, rows), f32),
            pltpu.VMEM((rows, dh), bf16),
            pltpu.SemaphoreType.DMA((CHUNKS, 4)),
            pltpu.SemaphoreType.DMA((2,)),
        ],
        compiler_params=params,
        cost_estimate=cost(1, 1024),
        name="project",
    )(*in_hbm(tokens, fw_t, window_weight, value_weight, log_decay.T, out_grad))

    swap = [(0, 1), (1, 0)]
    recv = {}
    for d in range(1, chips):
        recv[2 * d] = lax.ppermute(sends[d], ctx[:-1], [(i, i ^ d) for i in range(chips)])
    recv[1] = lax.ppermute(sends[0], "core", swap)
    for d in range(1, chips):
        recv[2 * d + 1] = lax.ppermute(recv[2 * d], "core", swap)
    recv = [recv[d] for d in range(1, count)]
    if count > 8:
        recv = [jnp.stack(recv)]

    attended, stat, sheet = pl.pallas_call(
        lambda *refs: query_kernel(ctx, count, *refs),
        out_shape=(
            jax.ShapeDtypeStruct((rows, dh), bf16),
            jax.ShapeDtypeStruct((8, rows), f32),
            jax.ShapeDtypeStruct((rows, LANES), f32),
        ),
        in_specs=[VMEM] * (len(recv) + 4),
        out_specs=[VMEM] * 3,
        scratch_shapes=[
            pltpu.VMEM((count, 2 * rows, dh), bf16),
            pltpu.VMEM((WINDOW // rows + 1, rows, rows), f32),
            pltpu.VMEM((count, rows), f32),
        ],
        compiler_params=params,
        cost_estimate=cost(1, 1024),
        name="query_side",
    )(*recv, own, query, feat, cum)
    stats = [stat]
    for name in reversed(ctx):
        held = stats[0] if len(stats) == 1 else jnp.concatenate(stats, axis=0)
        stats.append(lax.ppermute(held, name, swap))
    if count > 8:
        stats = [jnp.concatenate(stats, axis=0)]

    grads = pl.pallas_call(
        lambda *refs: gradient_kernel(ctx, count, len(recv), len(stats), *refs),
        out_shape=jax.ShapeDtypeStruct((3 * rows + nf2 * rows // LANES, LANES), bf16),
        in_specs=[VMEM] * (len(recv) + len(stats) + 4),
        out_specs=VMEM,
        scratch_shapes=[pltpu.VMEM((count, LANES), f32)],
        compiler_params=params,
        cost_estimate=cost(1, 1024),
        name="gradients",
    )(*recv, *stats, own, query, feat, sheet)
    if not spread:
        weights = jnp.concatenate([window_weight, value_weight, feature_weight], axis=1)
        weights = lax.all_gather(weights, "tp")
        return (attended, merge(lax.all_gather(grads, "tp"), weights, rows, dim))

    grads = lax.all_gather(grads, "tp")
    pieces, grads = lax.optimization_barrier((pieces, grads))
    swapped = [lax.ppermute(p, "core", swap) for p in pieces]

    def columns_of(side, pieces, before):
        return pl.pallas_call(
            partial(columns_kernel, ctx, side),
            out_shape=jax.ShapeDtypeStruct((rows, dim), bf16),
            in_specs=[VMEM] * (4 + chips) + [ANY] * len(before),
            out_specs=ANY,
            scratch_shapes=[
                pltpu.VMEM((rows, 3 * LANES * heads), bf16),
                pltpu.VMEM((rows, nf2 * heads), bf16),
                pltpu.VMEM((chips, rows, tile), bf16),
                pltpu.SemaphoreType.DMA((chips,)),
            ],
            input_output_aliases={4 + chips: 0} if before else {},
            compiler_params=params,
            cost_estimate=cost(rows * dim * heads * columns, heads * dim * columns),
            name="columns",
        )(grads, ww, vw, fw, *pieces, *before)

    first = columns_of(0, pieces, [])
    return (attended, columns_of(1, swapped, [first]))


def solution(mesh):
    blocks, tp = mesh.devices.shape
    bits = blocks.bit_length() - 1
    assert blocks == 2**bits
    ctx = tuple(f"half{i}" for i in range(bits - 1)) + ("core",)
    split = Mesh(mesh.devices.reshape((2,) * bits + (tp,)), (*ctx, "tp"))
    in_specs = (
        P(ctx, None),
        P(None, "tp"),
        P(None, "tp"),
        P(None, "tp"),
        P(ctx, "tp"),
        P(ctx, "tp"),
    )
    out_specs = (P(ctx, "tp"), P(ctx, None))
    return jax.shard_map(
        partial(per_device, ctx),
        mesh=split,
        in_specs=in_specs,
        out_specs=out_specs,
        check_vma=False,
    )
```

```python
from functools import partial

import jax
import jax.numpy as jnp
from jax import lax
from jax.experimental import pallas as pl
from jax.experimental.pallas import tpu as pltpu
from jax.sharding import Mesh
from jax.sharding import PartitionSpec as P

WINDOW = 1024
LANES = 128
MASKED = -1e30
CHUNKS = 4
f32 = jnp.float32
bf16 = jnp.bfloat16


def nn(a, b):
    return lax.dot_general(a, b, (((1,), (0,)), ((), ())), preferred_element_type=f32)


def nt(a, b):
    return lax.dot_general(a, b, (((1,), (1,)), ((), ())), preferred_element_type=f32)


def partner(me, d, count):
    assert count & (count - 1) == 0
    return jnp.bitwise_xor(me, d)


def wide(view, start, count):
    return jnp.concatenate(
        [view[start : start + count, :], view[start + count : start + 2 * count, :]], axis=1
    )


def put_wide(ref, start, value):
    count = value.shape[0]
    for half in range(value.shape[1] // LANES):
        ref[start + half * count : start + (half + 1) * count, :] = value[
            :, half * LANES : (half + 1) * LANES
        ]


def cum_row(view, start):
    tail = view[start : start + 16, :].astype(f32)
    first = tail[0:1] + tail[2:3] + tail[4:5]
    second = tail[1:2] + tail[3:4] + tail[5:6]
    return jnp.concatenate([first, second], axis=1)


def iotas(rows):
    return (
        lax.broadcasted_iota(jnp.int32, (rows, rows), 0),
        lax.broadcasted_iota(jnp.int32, (rows, rows), 1),
    )


def block_index(ctx):
    place = 0
    for name in ctx:
        place = place * lax.axis_size(name) + lax.axis_index(name)
    return place


def pack_copies(ctx, ww_hbm, vw_hbm, fw_hbm, out_ref, sems):
    nf2 = fw_hbm.shape[0]
    tile = 2 * LANES
    at = pl.multiple_of(block_index(ctx) * tile, tile)
    rows = pl.ds(at, tile)
    moves = [
        (ww_hbm.at[rows, pl.ds(0, LANES)], out_ref.at[pl.ds(0, tile), :]),
        (ww_hbm.at[rows, pl.ds(LANES, LANES)], out_ref.at[pl.ds(tile, tile), :]),
        (vw_hbm.at[rows, :], out_ref.at[pl.ds(2 * tile, tile), :]),
    ]
    for m in range(2):
        lanes = pl.ds(pl.multiple_of(at + m * LANES, LANES), LANES)
        moves.append((fw_hbm.at[:, lanes], out_ref.at[pl.ds(3 * tile + m * nf2, nf2), :]))
    return [pltpu.make_async_copy(src, dst, sems.at[n]) for n, (src, dst) in enumerate(moves)]


def project_kernel(ctx, packs, tok_hbm, fw_hbm, ww_hbm, vw_hbm, ld_hbm, do_hbm, *rest):
    *sends, keys_ref, query_ref, feat_ref, cum_ref, ww_ref, vw_ref, fw_ref = rest[packs:-6]
    tok_ref, ld_ref, do_ref, sems, small, pack_sems = rest[-6:]
    me = block_index(ctx)
    rows, dim = tok_ref.shape
    dh = do_ref.shape[1]
    nf = fw_ref.shape[0] // 2
    span = dim // CHUNKS
    copies = []
    for c in range(CHUNKS):
        part = pl.ds(c * span, span)
        copies.append([
            pltpu.make_async_copy(tok_hbm.at[:, part], tok_ref.at[:, part], sems.at[c, 0]),
            pltpu.make_async_copy(ww_hbm.at[part, :], ww_ref.at[part, :], sems.at[c, 1]),
            pltpu.make_async_copy(vw_hbm.at[part, :], vw_ref.at[part, :], sems.at[c, 2]),
            pltpu.make_async_copy(fw_hbm.at[:, part], fw_ref.at[:, part], sems.at[c, 3]),
        ])
    others = [
        pltpu.make_async_copy(ld_hbm, ld_ref, small.at[0]),
        pltpu.make_async_copy(do_hbm, do_ref, small.at[1]),
    ]
    for copy in others:
        copy.start()
    for group in copies:
        for at, copy in enumerate(group):
            copy.start(priority=min(at, 1))
    packing = pack_copies(ctx, ww_hbm, vw_hbm, fw_hbm, rest[0], pack_sems) if packs else []
    for copy in packing:
        copy.start()
    for copy in others:
        copy.wait()
    at_row, at_col = iotas(rows)
    ld_r = ld_ref[...]
    ld_c = jnp.sum(jnp.where(at_row == at_col, ld_r, 0.0), axis=1, keepdims=True)
    cum_r = jnp.sum(jnp.where(at_row <= at_col, ld_c, 0.0), axis=0, keepdims=True)
    cum_ref[...] = jnp.sum(jnp.where(at_col <= at_row, ld_r, 0.0), axis=1, keepdims=True)
    high = cum_r.astype(bf16)
    left = cum_r - high.astype(f32)
    mid = left.astype(bf16)
    low = (left - mid.astype(f32)).astype(bf16)
    pieces = [t[:, h : h + LANES].astype(f32) for t in (high, mid, low) for h in range(0, rows, LANES)]
    tail = jnp.concatenate(pieces + [jnp.zeros((10, LANES), f32)], axis=0).astype(bf16)

    feat = jnp.zeros((rows, 2 * nf), f32)
    main = jnp.zeros((rows, 3 * dh), f32)
    for c in range(CHUNKS):
        for copy in copies[c]:
            copy.wait()
        part = slice(c * span, (c + 1) * span)
        tok = tok_ref[:, part]
        feat += nt(tok, fw_ref[:, part])
        main += nn(tok, jnp.concatenate([ww_ref[part, :], vw_ref[part, :]], axis=1))
    feat = feat.astype(bf16)
    window = main[:, : 2 * dh].astype(bf16)
    values = main[:, 2 * dh :].astype(bf16)
    feat_ref[...] = feat
    small_row, small_col = iotas(2 * nf)
    feat_t = nt((small_row == small_col).astype(bf16), feat).astype(bf16)
    feat_at = 2 * rows
    tail_at = feat_at + 2 * nf

    def put_keys(ref):
        ref[0:rows, :] = window[:, dh:]
        ref[rows : 2 * rows, :] = values
        put_wide(ref, feat_at, feat_t[nf:, :])
        ref[tail_at : tail_at + 16, :] = tail

    def put_query(ref):
        ref[0:rows, :] = window[:, :dh]
        ref[rows : 2 * rows, :] = do_ref[...]
        put_wide(ref, feat_at, feat_t[:nf, :])
        ref[tail_at : tail_at + 16, :] = tail

    put_keys(keys_ref)
    put_query(query_ref)
    for at, ref in enumerate(sends):
        later = jnp.bitwise_xor(me, max(2 * at, 1)) > me
        pl.when(later)(lambda ref=ref: put_keys(ref))
        pl.when(jnp.logical_not(later))(lambda ref=ref: put_query(ref))
    for copy in packing:
        copy.wait()

def stack_kernel(*refs):
    *parts, out_ref = refs
    for t, ref in enumerate(parts):
        out_ref[t] = ref[...]


def between(totals, low, high):
    at = lax.broadcasted_iota(jnp.int32, totals.shape, 0)
    return jnp.sum(jnp.where((at > low) & (at < high), totals, 0.0), axis=0, keepdims=True)


def over_partners(count, body, carry):
    if count <= 8:
        for d in range(1, count):
            carry = body(d, carry)
        return carry
    return lax.fori_loop(1, count, body, carry)


def query_kernel(ctx, count, *rest):
    recvs = rest[: -10]
    (own_ref, query_ref, feat_ref, cum_ref, att_ref, stat_ref, sheet_ref, near_ref, p_ref,
     cums_ref) = rest[-10:]

    def recv(d):
        return recvs[d - 1] if len(recvs) > 1 else recvs[0].at[d - 1]

    me = block_index(ctx)
    rows, dh = att_ref.shape
    nf = feat_ref.shape[1] // 2
    back = WINDOW // rows
    feat_at = 2 * rows
    tail_at = feat_at + 2 * nf
    scale = dh ** (-0.5)
    feat_scale = nf ** (-0.5)
    wq = query_ref[0:rows, :]
    do = query_ref[rows : 2 * rows, :]
    q = feat_ref[:, :nf]
    at_row, at_col = iotas(rows)
    own_cum = cum_row(own_ref, tail_at)
    cums_ref[pl.ds(me, 1), :] = own_cum
    near_ref[me] = own_ref[0 : 2 * rows, :]

    def gather(d, carry):
        j = partner(me, d, count)
        view = recv(d)
        near_ref[j] = view[0 : 2 * rows, :]
        cums_ref[pl.ds(j, 1), :] = cum_row(view, tail_at)
        return carry

    over_partners(count, gather, 0)

    def near(w):
        return near_ref.at[jnp.maximum(me - back + w, 0)]

    top = jnp.full((rows, LANES), MASKED, f32)
    for w in range(back + 1):
        keys = own_ref[0:rows, :] if w == back else near(w)[0:rows, :]
        s = nt(wq, keys) * scale
        if w == back:
            s = jnp.where(at_col <= at_row, s, MASKED)
        elif w == 0:
            s = jnp.where((at_col > at_row) & (me >= back), s, MASKED)
        else:
            s = jnp.where(me >= back - w, s, MASKED)
        p_ref[w] = s
        for h in range(0, rows, LANES):
            top = jnp.maximum(top, s[:, h : h + LANES])
    top = jnp.max(top, axis=1, keepdims=True)
    total = jnp.zeros((rows, LANES), f32)
    out = jnp.zeros((rows, dh), f32)
    for w in range(back + 1):
        p = jnp.exp(p_ref[w] - top)
        for h in range(0, rows, LANES):
            total += p[:, h : h + LANES]
        vals = own_ref[rows : 2 * rows, :] if w == back else near(w)[rows : 2 * rows, :]
        out += nn(p.astype(bf16), vals)
    total = jnp.sum(total, axis=1, keepdims=True)
    windowed = out * (1.0 / total)

    cum_c = cum_ref[...]
    growth = jnp.exp(cum_c)
    totals = cums_ref[:, rows - 1 : rows]

    def forward(d, carry):
        num, den = carry
        j = partner(me, d, count)
        view = recv(d)
        gap = between(totals, j - 1, me)
        es = jnp.where(j < me, jnp.exp(jnp.minimum(gap - cums_ref[pl.ds(j, 1), :], 0.0)), 0.0)
        x = nn(q, wide(view, feat_at, nf)) * feat_scale
        weight = (1.0 + x + 0.5 * x * x) * es
        for h in range(0, rows, LANES):
            den += weight[:, h : h + LANES]
        num += nn(weight.astype(bf16), view[rows : 2 * rows, :])
        return num, den

    num, den = over_partners(
        count, forward, (jnp.zeros((rows, dh), f32), jnp.zeros((rows, LANES), f32))
    )
    x = nn(q, wide(own_ref, feat_at, nf)) * feat_scale
    e = jnp.where(at_col <= at_row, jnp.exp(jnp.minimum(cum_c - own_cum, 0.0)), 0.0)
    weight = (1.0 + x + 0.5 * x * x) * e
    num = num * growth + nn(weight.astype(bf16), own_ref[rows : 2 * rows, :])
    den = den * growth
    for h in range(0, rows, LANES):
        den += weight[:, h : h + LANES]
    rden = 1.0 / jnp.sum(den, axis=1, keepdims=True)
    linear = num * rden
    att_ref[...] = (linear + windowed).astype(bf16)
    do_f = do.astype(f32)
    delta_w = jnp.sum(do_f * windowed, axis=1, keepdims=True)
    delta_l = jnp.sum(do_f * linear, axis=1, keepdims=True)
    lse = top + jnp.log(total)
    lane = lax.broadcasted_iota(jnp.int32, (rows, LANES), 1)
    sheet = jnp.where(lane == 0, lse, 0.0)
    sheet = jnp.where(lane == 1, delta_w, sheet)
    sheet = jnp.where(lane == 2, rden, sheet)
    sheet = jnp.where(lane == 3, delta_l, sheet)
    sheet = jnp.where(lane == 4, cum_c, sheet)
    sheet_ref[...] = sheet
    stat_ref[...] = jnp.transpose(sheet)[0:8, :]


def gradient_kernel(ctx, count, recvs, stats, *rest):
    recvs, rest = rest[:recvs], rest[recvs:]
    stats, rest = rest[:stats], rest[stats:]
    own_ref, query_ref, feat_ref, sheet_ref, *rest, total_ref = rest

    def recv(d):
        return recvs[d - 1] if len(recvs) > 1 else recvs[0].at[d - 1]

    me = block_index(ctx)
    rows = feat_ref.shape[0]
    dh = LANES
    nf = feat_ref.shape[1] // 2
    feat_at = 2 * rows
    scale = dh ** (-0.5)
    feat_scale = nf ** (-0.5)
    at_row, at_col = iotas(rows)
    apart = at_row - at_col
    wq, wk = query_ref[0:rows, :], own_ref[0:rows, :]
    do, v = query_ref[rows : 2 * rows, :], own_ref[rows : 2 * rows, :]
    q, k = feat_ref[:, :nf], feat_ref[:, nf:]
    lse_c, dw_c = sheet_ref[:, 0:1], sheet_ref[:, 1:2]
    rden_c, dl_c, cum_c = sheet_ref[:, 2:3], sheet_ref[:, 3:4], sheet_ref[:, 4:5]
    def stat(d):
        if len(stats) == 1:
            return stats[0].at[pl.ds(pl.multiple_of(8 * d, 8), 8)]
        at = d.bit_length()
        return stats[at].at[pl.ds(8 * (d - (1 << at >> 1)), 8)]

    mine_ref = stat(0)
    own_cum = mine_ref[4:5, :]
    total_ref[pl.ds(me, 1), :] = own_cum[:, rows - LANES :]

    def place(d, carry):
        total_ref[pl.ds(partner(me, d, count), 1), :] = stat(d)[4:5, rows - LANES :]
        return carry

    over_partners(count, place, 0)
    totals = total_ref[:, LANES - 1 :]
    growth_c = jnp.exp(cum_c) * rden_c
    tail_c = jnp.exp(own_cum[:, rows - 1 : rows] - cum_c)

    def pick(flag, a, b):
        return jnp.where(flag, a, b)

    s = nt(wq, wk) * scale
    causal = at_col <= at_row
    p = jnp.where(causal, jnp.exp(s - lse_c), 0.0)
    dp = nt(do, v)
    dwq = nn((p * (dp - dw_c)).astype(bf16), wk)
    x = nn(q, wide(own_ref, feat_at, nf)) * feat_scale
    e = jnp.where(causal, jnp.exp(jnp.minimum(cum_c - own_cum, 0.0)), 0.0) * rden_c
    dx = (dp - dl_c) * e * (1.0 + x)
    dqt = nt(wide(own_ref, feat_at, nf), dx.astype(bf16))

    s = nt(wk, wq) * scale
    causal = at_row <= at_col
    p = jnp.where(causal, jnp.exp(s - mine_ref[0:1, :]), 0.0)
    dp = nt(v, do)
    dwk = nn((p * (dp - mine_ref[1:2, :])).astype(bf16), wq)
    x = nn(k, wide(query_ref, feat_at, nf)) * feat_scale
    e = jnp.where(causal, jnp.exp(jnp.minimum(own_cum - cum_c, 0.0)), 0.0) * mine_ref[2:3, :]
    dx = (dp - mine_ref[3:4, :]) * e * (1.0 + x)
    dkt = nt(wide(query_ref, feat_at, nf), dx.astype(bf16))
    dv = nn((p + (1.0 + x + 0.5 * x * x) * e).astype(bf16), do)

    def step(d, carry):
        dwq, dqt, dwk, dkt, dv = carry
        j = partner(me, d, count)
        view = recv(d)
        mine = j < me
        sign = pick(mine, 1, -1)
        limit = WINDOW - jnp.abs(me - j) * rows
        rows_w = pick(mine, wq, wk)
        rows_v = pick(mine, do, v)
        rows_f = pick(mine, q, k)
        other_w = view[0:rows, :]
        other_v = view[rows : 2 * rows, :]
        other_f = wide(view, feat_at, nf)
        st = stat(d)
        zero = jnp.zeros((1, rows), f32)
        cum = st[4:5, :]
        gap = between(totals, jnp.minimum(me, j), jnp.maximum(me, j))
        e_r = jnp.exp(jnp.minimum(gap + pick(mine, cum[:, rows - 1 : rows] - cum, cum), 0.0))
        e_r = e_r * pick(mine, 1.0, st[2:3, :])
        e_c = pick(mine, growth_c, tail_c)

        s = nt(rows_w, other_w) * scale
        p = jnp.exp(s - pick(mine, lse_c, 0.0) - pick(mine, zero, st[0:1, :]))
        p = jnp.where(apart * sign < limit, p, 0.0)
        dp = nt(rows_v, other_v)
        ds = p * (dp - pick(mine, dw_c, 0.0) - pick(mine, zero, st[1:2, :]))
        more_w = nn(ds.astype(bf16), other_w)
        x = nn(rows_f, other_f) * feat_scale
        e = e_r * e_c
        dx = (dp - pick(mine, dl_c, 0.0) - pick(mine, zero, st[3:4, :])) * e * (1.0 + x)
        more_f = nt(other_f, dx.astype(bf16))
        more_v = nn((p + (1.0 + x + 0.5 * x * x) * e).astype(bf16), other_v)
        dwq = dwq + pick(mine, more_w, 0.0)
        dwk = dwk + pick(mine, 0.0, more_w)
        dqt = dqt + pick(mine, more_f, 0.0)
        dkt = dkt + pick(mine, 0.0, more_f)
        dv = dv + pick(mine, 0.0, more_v)
        return dwq, dqt, dwk, dkt, dv

    dwq, dqt, dwk, dkt, dv = over_partners(count, step, (dwq, dqt, dwk, dkt, dv))
    dwq, dwk = (dwq * scale).astype(bf16), (dwk * scale).astype(bf16)
    dv = dv.astype(bf16)
    dft = (jnp.concatenate([dqt, dkt], axis=0) * feat_scale).astype(bf16)
    (grad_ref,) = rest
    grad_ref[0:rows, :] = dwq
    grad_ref[rows : 2 * rows, :] = dwk
    grad_ref[2 * rows : 3 * rows, :] = dv
    put_wide(grad_ref, 3 * rows, dft)


def gather_rows(grad_ref, order, cat_ref, feat_ref):
    rows = cat_ref.shape[0]
    nf2 = feat_ref.shape[1] // len(order)
    for at, h in enumerate(order):
        for part in range(3):
            lane = (3 * at + part) * LANES
            cat_ref[:, lane : lane + LANES] = grad_ref[h, part * rows : (part + 1) * rows, :]
    dft = jnp.concatenate([wide(grad_ref.at[h], 3 * rows, nf2) for h in order], axis=0)
    feat_ref[...] = jnp.transpose(dft.astype(f32)).astype(bf16)


def columns_kernel(ctx, side, grad_ref, ww_ref, vw_ref, fw_ref, *rest):
    pieces = rest[: ww_ref.shape[0] // (4 * LANES)]
    out_ref, cat_ref, feat_ref, tile_ref, sems = rest[-5:]
    heads = grad_ref.shape[0]
    nf2 = fw_ref.shape[0]
    tile = 2 * LANES
    head, me = lax.axis_index("tp"), block_index(ctx)
    gather_rows(
        grad_ref, [head] + [jnp.bitwise_xor(head, t) for t in range(1, heads)], cat_ref, feat_ref
    )
    copies = []
    for d, ref in enumerate(pieces):
        at = pl.multiple_of(jnp.bitwise_xor(me, 2 * d + side) * tile, tile)
        part = pl.ds(at, tile)
        main = [ww_ref[part, :], vw_ref[part, :]]
        main += [
            ref[t, m * tile : (m + 1) * tile, :] for t in range(heads - 1) for m in range(3)
        ]
        feats = [fw_ref[:, part]] + [wide(ref.at[t], 3 * tile, nf2) for t in range(heads - 1)]
        total = nt(cat_ref[...], jnp.concatenate(main, axis=1))
        total += nn(feat_ref[...], jnp.concatenate(feats, axis=0))
        tile_ref[d] = total.astype(bf16)
        copies.append(pltpu.make_async_copy(tile_ref.at[d], out_ref.at[:, part], sems.at[d]))
        copies[-1].start()
    for copy in copies:
        copy.wait()


def merge_kernel(grad_ref, weight_ref, out_ref, cat_ref, feat_ref):
    heads = grad_ref.shape[0]
    tile = out_ref.shape[1]
    lanes = 3 * LANES
    nf2 = feat_ref.shape[1] // heads

    @pl.when(pl.program_id(0) == 0)
    def _():
        gather_rows(grad_ref, range(heads), cat_ref, feat_ref)

    views = [weight_ref.at[h] for h in range(heads)]
    main = jnp.concatenate([v[:, 0:lanes] for v in views], axis=1)
    feats = jnp.concatenate([v[:, lanes:] for v in views], axis=1)
    out_ref[...] = (nt(cat_ref[...], main) + nt(feat_ref[...], feats)).astype(bf16)


VMEM = pl.BlockSpec(memory_space=pltpu.VMEM)
HBM = pl.BlockSpec(memory_space=pltpu.HBM)
ANY = pl.BlockSpec(memory_space=pl.ANY)
params = pltpu.CompilerParams(vmem_limit_bytes=32 * 1024 * 1024)


def in_hbm(*arrays):
    return [pltpu.with_memory_space_constraint(a, pltpu.HBM) for a in arrays]


def cost(flops, nbytes, exps=0):
    return pl.CostEstimate(flops=flops, bytes_accessed=nbytes, transcendentals=exps)


def merge(grads, weights, rows, dim):
    heads, _, columns = weights.shape
    tile = 2 * LANES
    return pl.pallas_call(
        merge_kernel,
        out_shape=jax.ShapeDtypeStruct((rows, dim), bf16),
        grid=(dim // tile,),
        in_specs=[
            pl.BlockSpec(grads.shape, lambda i: (0, 0, 0)),
            pl.BlockSpec((heads, tile, columns), lambda i: (0, i, 0)),
        ],
        out_specs=pl.BlockSpec((rows, tile), lambda i: (0, i)),
        scratch_shapes=[
            pltpu.VMEM((rows, 3 * LANES * heads), bf16),
            pltpu.VMEM((rows, (columns - 3 * LANES) * heads), bf16),
        ],
        compiler_params=params,
        cost_estimate=cost(2 * rows * dim * heads * columns, heads * dim * columns * 2),
        name="head_sum",
    )(grads, weights)


def per_device(ctx, tokens, feature_weight, window_weight, value_weight, log_decay, out_grad):
    rows, dim = tokens.shape
    nf2 = feature_weight.shape[1]
    nf = nf2 // 2
    dh = value_weight.shape[1]
    columns = 3 * dh + nf2
    chips, count, heads = lax.axis_size(ctx[:-1]), lax.axis_size(ctx), lax.axis_size("tp")
    fw_t = feature_weight.T
    tile = 2 * LANES
    spread = heads == 4 and count * tile == dim and count == 8
    packs = []
    if spread:
        packs = [jax.ShapeDtypeStruct((columns * tile // LANES, LANES), bf16)]

    payload = 2 * rows + 2 * nf + 16
    block = jax.ShapeDtypeStruct((payload, LANES), bf16)
    outs = pl.pallas_call(
        partial(project_kernel, ctx, len(packs)),
        out_shape=packs
        + [block] * (chips + 2)
        + [
            jax.ShapeDtypeStruct((rows, nf2), bf16),
            jax.ShapeDtypeStruct((rows, 1), f32),
            jax.ShapeDtypeStruct((dim, 2 * dh), bf16),
            jax.ShapeDtypeStruct((dim, dh), bf16),
            jax.ShapeDtypeStruct((nf2, dim), bf16),
        ],
        in_specs=[HBM] * 6,
        out_specs=[VMEM] * (len(packs) + chips + 7),
        scratch_shapes=[
            pltpu.VMEM((rows, dim), bf16),
            pltpu.VMEM((1, rows), f32),
            pltpu.VMEM((rows, dh), bf16),
            pltpu.SemaphoreType.DMA((CHUNKS, 4)),
            pltpu.SemaphoreType.DMA((2,)),
            pltpu.SemaphoreType.DMA((5,)),
        ],
        compiler_params=params,
        cost_estimate=cost(1, 1024),
        name="project",
    )(*in_hbm(tokens, fw_t, window_weight, value_weight, log_decay.T, out_grad))
    *sends, own, query, feat, cum, ww, vw, fw = outs[len(packs) :]

    swap = [(0, 1), (1, 0)]
    recv = {}
    for d in range(1, chips):
        recv[2 * d] = lax.ppermute(sends[d], ctx[:-1], [(i, i ^ d) for i in range(chips)])
    recv[1] = lax.ppermute(sends[0], "core", swap)
    for d in range(1, chips):
        recv[2 * d + 1] = lax.ppermute(recv[2 * d], "core", swap)
    recv = [recv[d] for d in range(1, count)]
    if count > 8:
        recv = [jnp.stack(recv)]

    if spread:
        near = [
            lax.ppermute(outs[0], "tp", [(z, z ^ t) for z in range(heads)])
            for t in range(1, heads)
        ]
        near[:2], own = lax.optimization_barrier((near[:2], own))

    attended, stat, sheet = pl.pallas_call(
        lambda *refs: query_kernel(ctx, count, *refs),
        out_shape=(
            jax.ShapeDtypeStruct((rows, dh), bf16),
            jax.ShapeDtypeStruct((8, rows), f32),
            jax.ShapeDtypeStruct((rows, LANES), f32),
        ),
        in_specs=[VMEM] * (len(recv) + 4),
        out_specs=[VMEM] * 3,
        scratch_shapes=[
            pltpu.VMEM((count, 2 * rows, dh), bf16),
            pltpu.VMEM((WINDOW // rows + 1, rows, rows), f32),
            pltpu.VMEM((count, rows), f32),
        ],
        compiler_params=params,
        cost_estimate=cost(1, 1024),
        name="query_side",
    )(*recv, own, query, feat, cum)
    stats = [stat]
    for name in reversed(ctx):
        held = stats[0] if len(stats) == 1 else jnp.concatenate(stats, axis=0)
        stats.append(lax.ppermute(held, name, swap))
    if count > 8:
        stats = [jnp.concatenate(stats, axis=0)]

    if spread:
        near, stats = lax.optimization_barrier((near, stats))
        pieces = [
            pl.pallas_call(
                stack_kernel,
                out_shape=jax.ShapeDtypeStruct((heads - 1, *packs[0].shape), bf16),
                in_specs=[VMEM] * (heads - 1),
                out_specs=VMEM,
                compiler_params=params,
                cost_estimate=cost(1, 1024),
                name="stack",
            )(*near)
        ]
        for d in range(1, chips):
            pieces.append(
                lax.ppermute(pieces[0], ctx[:-1], [(i, i ^ d) for i in range(chips)])
            )
        first, sheet = lax.optimization_barrier((pieces[0], sheet))
        pieces[0] = first

    grads = pl.pallas_call(
        lambda *refs: gradient_kernel(ctx, count, len(recv), len(stats), *refs),
        out_shape=jax.ShapeDtypeStruct((3 * rows + nf2 * rows // LANES, LANES), bf16),
        in_specs=[VMEM] * (len(recv) + len(stats) + 4),
        out_specs=VMEM,
        scratch_shapes=[pltpu.VMEM((count, LANES), f32)],
        compiler_params=params,
        cost_estimate=cost(1, 1024),
        name="gradients",
    )(*recv, *stats, own, query, feat, sheet)
    if not spread:
        weights = jnp.concatenate([window_weight, value_weight, feature_weight], axis=1)
        weights = lax.all_gather(weights, "tp")
        return (attended, merge(lax.all_gather(grads, "tp"), weights, rows, dim))

    grads = lax.all_gather(grads, "tp")
    pieces, grads = lax.optimization_barrier((pieces, grads))
    swapped = [lax.ppermute(p, "core", swap) for p in pieces]

    def columns_of(side, pieces, before):
        return pl.pallas_call(
            partial(columns_kernel, ctx, side),
            out_shape=jax.ShapeDtypeStruct((rows, dim), bf16),
            in_specs=[VMEM] * (4 + chips) + [ANY] * len(before),
            out_specs=ANY,
            scratch_shapes=[
                pltpu.VMEM((rows, 3 * LANES * heads), bf16),
                pltpu.VMEM((rows, nf2 * heads), bf16),
                pltpu.VMEM((chips, rows, tile), bf16),
                pltpu.SemaphoreType.DMA((chips,)),
            ],
            input_output_aliases={4 + chips: 0} if before else {},
            compiler_params=params,
            cost_estimate=cost(rows * dim * heads * columns, heads * dim * columns),
            name="columns",
        )(grads, ww, vw, fw, *pieces, *before)

    first = columns_of(0, pieces, [])
    return (attended, columns_of(1, swapped, [first]))


def solution(mesh):
    blocks, tp = mesh.devices.shape
    bits = blocks.bit_length() - 1
    assert blocks == 2**bits
    ctx = tuple(f"half{i}" for i in range(bits - 1)) + ("core",)
    split = Mesh(mesh.devices.reshape((2,) * bits + (tp,)), (*ctx, "tp"))
    in_specs = (
        P(ctx, None),
        P(None, "tp"),
        P(None, "tp"),
        P(None, "tp"),
        P(ctx, "tp"),
        P(ctx, "tp"),
    )
    out_specs = (P(ctx, "tp"), P(ctx, None))
    return jax.shard_map(
        partial(per_device, ctx),
        mesh=split,
        in_specs=in_specs,
        out_specs=out_specs,
        check_vma=False,
    )
```

```python
from functools import partial

import jax
import jax.numpy as jnp
from jax import lax
from jax.experimental import pallas as pl
from jax.experimental.pallas import tpu as pltpu
from jax.sharding import Mesh
from jax.sharding import PartitionSpec as P

WINDOW = 1024
LANES = 128
MASKED = -1e30
CHUNKS = 4
f32 = jnp.float32
bf16 = jnp.bfloat16


def nn(a, b):
    return lax.dot_general(a, b, (((1,), (0,)), ((), ())), preferred_element_type=f32)


def nt(a, b):
    return lax.dot_general(a, b, (((1,), (1,)), ((), ())), preferred_element_type=f32)


def partner(me, d, count):
    assert count & (count - 1) == 0
    return jnp.bitwise_xor(me, d)


def wide(view, start, count):
    return jnp.concatenate(
        [view[start : start + count, :], view[start + count : start + 2 * count, :]], axis=1
    )


def put_wide(ref, start, value):
    count = value.shape[0]
    for half in range(value.shape[1] // LANES):
        ref[start + half * count : start + (half + 1) * count, :] = value[
            :, half * LANES : (half + 1) * LANES
        ]


def cum_row(view, start):
    tail = view[start : start + 16, :].astype(f32)
    first = tail[0:1] + tail[2:3] + tail[4:5]
    second = tail[1:2] + tail[3:4] + tail[5:6]
    return jnp.concatenate([first, second], axis=1)


def iotas(rows):
    return (
        lax.broadcasted_iota(jnp.int32, (rows, rows), 0),
        lax.broadcasted_iota(jnp.int32, (rows, rows), 1),
    )


def block_index(ctx):
    place = 0
    for name in ctx:
        place = place * lax.axis_size(name) + lax.axis_index(name)
    return place


def pack_copies(ctx, ww_hbm, vw_hbm, fw_hbm, out_ref, sems):
    nf2 = fw_hbm.shape[0]
    tile = 2 * LANES
    at = pl.multiple_of(block_index(ctx) * tile, tile)
    rows = pl.ds(at, tile)
    moves = [
        (ww_hbm.at[rows, pl.ds(0, LANES)], out_ref.at[pl.ds(0, tile), :]),
        (ww_hbm.at[rows, pl.ds(LANES, LANES)], out_ref.at[pl.ds(tile, tile), :]),
        (vw_hbm.at[rows, :], out_ref.at[pl.ds(2 * tile, tile), :]),
    ]
    for m in range(2):
        lanes = pl.ds(pl.multiple_of(at + m * LANES, LANES), LANES)
        moves.append((fw_hbm.at[:, lanes], out_ref.at[pl.ds(3 * tile + m * nf2, nf2), :]))
    return [pltpu.make_async_copy(src, dst, sems.at[n]) for n, (src, dst) in enumerate(moves)]


def project_kernel(ctx, packs, tok_hbm, fw_hbm, ww_hbm, vw_hbm, ld_hbm, do_hbm, *rest):
    *sends, keys_ref, query_ref, feat_ref, cum_ref, ww_ref, vw_ref, fw_ref = rest[packs:-6]
    tok_ref, ld_ref, do_ref, sems, small, pack_sems = rest[-6:]
    me = block_index(ctx)
    rows, dim = tok_ref.shape
    dh = do_ref.shape[1]
    nf = fw_ref.shape[0] // 2
    span = dim // CHUNKS
    copies = []
    for c in range(CHUNKS):
        part = pl.ds(c * span, span)
        copies.append([
            pltpu.make_async_copy(tok_hbm.at[:, part], tok_ref.at[:, part], sems.at[c, 0]),
            pltpu.make_async_copy(ww_hbm.at[part, :], ww_ref.at[part, :], sems.at[c, 1]),
            pltpu.make_async_copy(vw_hbm.at[part, :], vw_ref.at[part, :], sems.at[c, 2]),
            pltpu.make_async_copy(fw_hbm.at[:, part], fw_ref.at[:, part], sems.at[c, 3]),
        ])
    others = [
        pltpu.make_async_copy(ld_hbm, ld_ref, small.at[0]),
        pltpu.make_async_copy(do_hbm, do_ref, small.at[1]),
    ]
    for copy in others:
        copy.start()
    for group in copies:
        for at, copy in enumerate(group):
            copy.start(priority=min(at, 1))
    packing = pack_copies(ctx, ww_hbm, vw_hbm, fw_hbm, rest[0], pack_sems) if packs else []
    for copy in packing:
        copy.start()
    for copy in others:
        copy.wait()
    at_row, at_col = iotas(rows)
    ld_r = ld_ref[...]
    ld_c = jnp.sum(jnp.where(at_row == at_col, ld_r, 0.0), axis=1, keepdims=True)
    cum_r = jnp.sum(jnp.where(at_row <= at_col, ld_c, 0.0), axis=0, keepdims=True)
    cum_ref[...] = jnp.sum(jnp.where(at_col <= at_row, ld_r, 0.0), axis=1, keepdims=True)
    high = cum_r.astype(bf16)
    left = cum_r - high.astype(f32)
    mid = left.astype(bf16)
    low = (left - mid.astype(f32)).astype(bf16)
    pieces = [t[:, h : h + LANES].astype(f32) for t in (high, mid, low) for h in range(0, rows, LANES)]
    tail = jnp.concatenate(pieces + [jnp.zeros((10, LANES), f32)], axis=0).astype(bf16)

    feat = jnp.zeros((rows, 2 * nf), f32)
    main = jnp.zeros((rows, 3 * dh), f32)
    for c in range(CHUNKS):
        for copy in copies[c]:
            copy.wait()
        part = slice(c * span, (c + 1) * span)
        tok = tok_ref[:, part]
        feat += nt(tok, fw_ref[:, part])
        main += nn(tok, jnp.concatenate([ww_ref[part, :], vw_ref[part, :]], axis=1))
    feat = feat.astype(bf16)
    window = main[:, : 2 * dh].astype(bf16)
    values = main[:, 2 * dh :].astype(bf16)
    feat_ref[...] = feat
    small_row, small_col = iotas(2 * nf)
    feat_t = nt((small_row == small_col).astype(bf16), feat).astype(bf16)
    feat_at = 2 * rows
    tail_at = feat_at + 2 * nf

    def put_keys(ref):
        ref[0:rows, :] = window[:, dh:]
        ref[rows : 2 * rows, :] = values
        put_wide(ref, feat_at, feat_t[nf:, :])
        ref[tail_at : tail_at + 16, :] = tail

    def put_query(ref):
        ref[0:rows, :] = window[:, :dh]
        ref[rows : 2 * rows, :] = do_ref[...]
        put_wide(ref, feat_at, feat_t[:nf, :])
        ref[tail_at : tail_at + 16, :] = tail

    put_keys(keys_ref)
    put_query(query_ref)
    for at, ref in enumerate(sends):
        later = jnp.bitwise_xor(me, max(2 * at, 1)) > me
        pl.when(later)(lambda ref=ref: put_keys(ref))
        pl.when(jnp.logical_not(later))(lambda ref=ref: put_query(ref))
    for copy in packing:
        copy.wait()

def stack_kernel(*refs):
    *parts, out_ref = refs
    for t, ref in enumerate(parts):
        out_ref[t] = ref[...]


def between(totals, low, high):
    at = lax.broadcasted_iota(jnp.int32, totals.shape, 0)
    return jnp.sum(jnp.where((at > low) & (at < high), totals, 0.0), axis=0, keepdims=True)


def over_partners(count, body, carry):
    if count <= 8:
        for d in range(1, count):
            carry = body(d, carry)
        return carry
    return lax.fori_loop(1, count, body, carry)


def query_kernel(ctx, count, *rest):
    recvs = rest[: -10]
    (own_ref, query_ref, feat_ref, cum_ref, att_ref, stat_ref, sheet_ref, near_ref, p_ref,
     cums_ref) = rest[-10:]

    def recv(d):
        return recvs[d - 1] if len(recvs) > 1 else recvs[0].at[d - 1]

    me = block_index(ctx)
    rows, dh = att_ref.shape
    nf = feat_ref.shape[1] // 2
    back = WINDOW // rows
    feat_at = 2 * rows
    tail_at = feat_at + 2 * nf
    scale = dh ** (-0.5)
    feat_scale = nf ** (-0.5)
    wq = query_ref[0:rows, :]
    do = query_ref[rows : 2 * rows, :]
    q = feat_ref[:, :nf]
    at_row, at_col = iotas(rows)
    own_cum = cum_row(own_ref, tail_at)
    cums_ref[pl.ds(me, 1), :] = own_cum
    near_ref[me] = own_ref[0 : 2 * rows, :]

    def gather(d, carry):
        j = partner(me, d, count)
        view = recv(d)
        near_ref[j] = view[0 : 2 * rows, :]
        cums_ref[pl.ds(j, 1), :] = cum_row(view, tail_at)
        return carry

    over_partners(count, gather, 0)

    def near(w):
        return near_ref.at[jnp.maximum(me - back + w, 0)]

    top = jnp.full((rows, LANES), MASKED, f32)
    for w in range(back + 1):
        keys = own_ref[0:rows, :] if w == back else near(w)[0:rows, :]
        s = nt(wq, keys) * scale
        if w == back:
            s = jnp.where(at_col <= at_row, s, MASKED)
        elif w == 0:
            s = jnp.where((at_col > at_row) & (me >= back), s, MASKED)
        else:
            s = jnp.where(me >= back - w, s, MASKED)
        p_ref[w] = s
        for h in range(0, rows, LANES):
            top = jnp.maximum(top, s[:, h : h + LANES])
    top = jnp.max(top, axis=1, keepdims=True)
    total = jnp.zeros((rows, LANES), f32)
    out = jnp.zeros((rows, dh), f32)
    for w in range(back + 1):
        p = jnp.exp(p_ref[w] - top)
        for h in range(0, rows, LANES):
            total += p[:, h : h + LANES]
        vals = own_ref[rows : 2 * rows, :] if w == back else near(w)[rows : 2 * rows, :]
        out += nn(p.astype(bf16), vals)
    total = jnp.sum(total, axis=1, keepdims=True)
    windowed = out * (1.0 / total)

    cum_c = cum_ref[...]
    growth = jnp.exp(cum_c)
    totals = cums_ref[:, rows - 1 : rows]

    def forward(d, carry):
        num, den = carry
        j = partner(me, d, count)
        view = recv(d)
        gap = between(totals, j - 1, me)
        es = jnp.where(j < me, jnp.exp(jnp.minimum(gap - cums_ref[pl.ds(j, 1), :], 0.0)), 0.0)
        x = nn(q, wide(view, feat_at, nf)) * feat_scale
        weight = (1.0 + x + 0.5 * x * x) * es
        for h in range(0, rows, LANES):
            den += weight[:, h : h + LANES]
        num += nn(weight.astype(bf16), view[rows : 2 * rows, :])
        return num, den

    num, den = over_partners(
        count, forward, (jnp.zeros((rows, dh), f32), jnp.zeros((rows, LANES), f32))
    )
    x = nn(q, wide(own_ref, feat_at, nf)) * feat_scale
    e = jnp.where(at_col <= at_row, jnp.exp(jnp.minimum(cum_c - own_cum, 0.0)), 0.0)
    weight = (1.0 + x + 0.5 * x * x) * e
    num = num * growth + nn(weight.astype(bf16), own_ref[rows : 2 * rows, :])
    den = den * growth
    for h in range(0, rows, LANES):
        den += weight[:, h : h + LANES]
    rden = 1.0 / jnp.sum(den, axis=1, keepdims=True)
    linear = num * rden
    att_ref[...] = (linear + windowed).astype(bf16)
    do_f = do.astype(f32)
    delta_w = jnp.sum(do_f * windowed, axis=1, keepdims=True)
    delta_l = jnp.sum(do_f * linear, axis=1, keepdims=True)
    lse = top + jnp.log(total)
    lane = lax.broadcasted_iota(jnp.int32, (rows, LANES), 1)
    sheet = jnp.where(lane == 0, lse, 0.0)
    sheet = jnp.where(lane == 1, delta_w, sheet)
    sheet = jnp.where(lane == 2, rden, sheet)
    sheet = jnp.where(lane == 3, delta_l, sheet)
    sheet = jnp.where(lane == 4, cum_c, sheet)
    sheet_ref[...] = sheet
    stat_ref[...] = jnp.transpose(sheet)[0:8, :]


def gradient_kernel(ctx, count, recvs, stats, *rest):
    recvs, rest = rest[:recvs], rest[recvs:]
    stats, rest = rest[:stats], rest[stats:]
    own_ref, query_ref, feat_ref, sheet_ref, *rest, total_ref = rest

    def recv(d):
        return recvs[d - 1] if len(recvs) > 1 else recvs[0].at[d - 1]

    me = block_index(ctx)
    rows = feat_ref.shape[0]
    dh = LANES
    nf = feat_ref.shape[1] // 2
    feat_at = 2 * rows
    scale = dh ** (-0.5)
    feat_scale = nf ** (-0.5)
    at_row, at_col = iotas(rows)
    apart = at_row - at_col
    wq, wk = query_ref[0:rows, :], own_ref[0:rows, :]
    do, v = query_ref[rows : 2 * rows, :], own_ref[rows : 2 * rows, :]
    q, k = feat_ref[:, :nf], feat_ref[:, nf:]
    lse_c, dw_c = sheet_ref[:, 0:1], sheet_ref[:, 1:2]
    rden_c, dl_c, cum_c = sheet_ref[:, 2:3], sheet_ref[:, 3:4], sheet_ref[:, 4:5]
    def stat(d):
        if len(stats) == 1:
            return stats[0].at[pl.ds(pl.multiple_of(8 * d, 8), 8)]
        at = d.bit_length()
        return stats[at].at[pl.ds(8 * (d - (1 << at >> 1)), 8)]

    mine_ref = stat(0)
    own_cum = mine_ref[4:5, :]
    total_ref[pl.ds(me, 1), :] = own_cum[:, rows - LANES :]

    def place(d, carry):
        total_ref[pl.ds(partner(me, d, count), 1), :] = stat(d)[4:5, rows - LANES :]
        return carry

    over_partners(count, place, 0)
    totals = total_ref[:, LANES - 1 :]
    growth_c = jnp.exp(cum_c) * rden_c
    tail_c = jnp.exp(own_cum[:, rows - 1 : rows] - cum_c)

    def pick(flag, a, b):
        return jnp.where(flag, a, b)

    s = nt(wq, wk) * scale
    causal = at_col <= at_row
    p = jnp.where(causal, jnp.exp(s - lse_c), 0.0)
    dp = nt(do, v)
    dwq = nn((p * (dp - dw_c)).astype(bf16), wk)
    x = nn(q, wide(own_ref, feat_at, nf)) * feat_scale
    e = jnp.where(causal, jnp.exp(jnp.minimum(cum_c - own_cum, 0.0)), 0.0) * rden_c
    dx = (dp - dl_c) * e * (1.0 + x)
    dqt = nt(wide(own_ref, feat_at, nf), dx.astype(bf16))

    s = nt(wk, wq) * scale
    causal = at_row <= at_col
    p = jnp.where(causal, jnp.exp(s - mine_ref[0:1, :]), 0.0)
    dp = nt(v, do)
    dwk = nn((p * (dp - mine_ref[1:2, :])).astype(bf16), wq)
    x = nn(k, wide(query_ref, feat_at, nf)) * feat_scale
    e = jnp.where(causal, jnp.exp(jnp.minimum(own_cum - cum_c, 0.0)), 0.0) * mine_ref[2:3, :]
    dx = (dp - mine_ref[3:4, :]) * e * (1.0 + x)
    dkt = nt(wide(query_ref, feat_at, nf), dx.astype(bf16))
    dv = nn((p + (1.0 + x + 0.5 * x * x) * e).astype(bf16), do)

    def step(d, carry):
        dwq, dqt, dwk, dkt, dv = carry
        j = partner(me, d, count)
        view = recv(d)
        mine = j < me
        sign = pick(mine, 1, -1)
        limit = WINDOW - jnp.abs(me - j) * rows
        rows_w = pick(mine, wq, wk)
        rows_v = pick(mine, do, v)
        rows_f = pick(mine, q, k)
        other_w = view[0:rows, :]
        other_v = view[rows : 2 * rows, :]
        other_f = wide(view, feat_at, nf)
        st = stat(d)
        zero = jnp.zeros((1, rows), f32)
        cum = st[4:5, :]
        gap = between(totals, jnp.minimum(me, j), jnp.maximum(me, j))
        e_r = jnp.exp(jnp.minimum(gap + pick(mine, cum[:, rows - 1 : rows] - cum, cum), 0.0))
        e_r = e_r * pick(mine, 1.0, st[2:3, :])
        e_c = pick(mine, growth_c, tail_c)

        s = nt(rows_w, other_w) * scale
        p = jnp.exp(s - pick(mine, lse_c, 0.0) - pick(mine, zero, st[0:1, :]))
        p = jnp.where(apart * sign < limit, p, 0.0)
        dp = nt(rows_v, other_v)
        ds = p * (dp - pick(mine, dw_c, 0.0) - pick(mine, zero, st[1:2, :]))
        more_w = nn(ds.astype(bf16), other_w)
        x = nn(rows_f, other_f) * feat_scale
        e = e_r * e_c
        dx = (dp - pick(mine, dl_c, 0.0) - pick(mine, zero, st[3:4, :])) * e * (1.0 + x)
        more_f = nt(other_f, dx.astype(bf16))
        more_v = nn((p + (1.0 + x + 0.5 * x * x) * e).astype(bf16), other_v)
        dwq = dwq + pick(mine, more_w, 0.0)
        dwk = dwk + pick(mine, 0.0, more_w)
        dqt = dqt + pick(mine, more_f, 0.0)
        dkt = dkt + pick(mine, 0.0, more_f)
        dv = dv + pick(mine, 0.0, more_v)
        return dwq, dqt, dwk, dkt, dv

    dwq, dqt, dwk, dkt, dv = over_partners(count, step, (dwq, dqt, dwk, dkt, dv))
    dwq, dwk = (dwq * scale).astype(bf16), (dwk * scale).astype(bf16)
    dv = dv.astype(bf16)
    dft = (jnp.concatenate([dqt, dkt], axis=0) * feat_scale).astype(bf16)
    (grad_ref,) = rest
    grad_ref[0:rows, :] = dwq
    grad_ref[rows : 2 * rows, :] = dwk
    grad_ref[2 * rows : 3 * rows, :] = dv
    put_wide(grad_ref, 3 * rows, dft)


def gather_rows(grad_ref, order, cat_ref, feat_ref):
    rows = cat_ref.shape[0]
    nf2 = feat_ref.shape[1] // len(order)
    for at, h in enumerate(order):
        for part in range(3):
            lane = (3 * at + part) * LANES
            cat_ref[:, lane : lane + LANES] = grad_ref[h, part * rows : (part + 1) * rows, :]
    dft = jnp.concatenate([wide(grad_ref.at[h], 3 * rows, nf2) for h in order], axis=0)
    feat_ref[...] = jnp.transpose(dft.astype(f32)).astype(bf16)


def cat_kernel(grad_ref, cat_ref, feat_ref):
    heads = grad_ref.shape[0]
    head = lax.axis_index("tp")
    order = [head] + [jnp.bitwise_xor(head, t) for t in range(1, heads)]
    gather_rows(grad_ref, order, cat_ref, feat_ref)


def columns_kernel(ctx, distances, cat_ref, feat_ref, ww_ref, vw_ref, fw_ref, *rest):
    pieces = rest[: len(distances)]
    out_ref, tile_ref, sems = rest[-3:]
    nf2 = fw_ref.shape[0]
    heads = feat_ref.shape[1] // nf2
    tile = 2 * LANES
    me = block_index(ctx)
    copies = []
    for n, (e, ref) in enumerate(zip(distances, pieces)):
        part = pl.ds(pl.multiple_of(jnp.bitwise_xor(me, e) * tile, tile), tile)
        main = [ww_ref[part, :], vw_ref[part, :]]
        main += [
            ref[t, m * tile : (m + 1) * tile, :] for t in range(heads - 1) for m in range(3)
        ]
        feats = [fw_ref[:, part]] + [wide(ref.at[t], 3 * tile, nf2) for t in range(heads - 1)]
        total = nt(cat_ref[...], jnp.concatenate(main, axis=1))
        total += nn(feat_ref[...], jnp.concatenate(feats, axis=0))
        tile_ref[n] = total.astype(bf16)
        copies.append(pltpu.make_async_copy(tile_ref.at[n], out_ref.at[:, part], sems.at[n]))
        copies[-1].start()
    for copy in copies:
        copy.wait()


def merge_kernel(grad_ref, weight_ref, out_ref, cat_ref, feat_ref):
    heads = grad_ref.shape[0]
    tile = out_ref.shape[1]
    lanes = 3 * LANES
    nf2 = feat_ref.shape[1] // heads

    @pl.when(pl.program_id(0) == 0)
    def _():
        gather_rows(grad_ref, range(heads), cat_ref, feat_ref)

    views = [weight_ref.at[h] for h in range(heads)]
    main = jnp.concatenate([v[:, 0:lanes] for v in views], axis=1)
    feats = jnp.concatenate([v[:, lanes:] for v in views], axis=1)
    out_ref[...] = (nt(cat_ref[...], main) + nt(feat_ref[...], feats)).astype(bf16)


VMEM = pl.BlockSpec(memory_space=pltpu.VMEM)
HBM = pl.BlockSpec(memory_space=pltpu.HBM)
ANY = pl.BlockSpec(memory_space=pl.ANY)
params = pltpu.CompilerParams(vmem_limit_bytes=32 * 1024 * 1024)


def in_hbm(*arrays):
    return [pltpu.with_memory_space_constraint(a, pltpu.HBM) for a in arrays]


def cost(flops, nbytes, exps=0):
    return pl.CostEstimate(flops=flops, bytes_accessed=nbytes, transcendentals=exps)


def merge(grads, weights, rows, dim):
    heads, _, columns = weights.shape
    tile = 2 * LANES
    return pl.pallas_call(
        merge_kernel,
        out_shape=jax.ShapeDtypeStruct((rows, dim), bf16),
        grid=(dim // tile,),
        in_specs=[
            pl.BlockSpec(grads.shape, lambda i: (0, 0, 0)),
            pl.BlockSpec((heads, tile, columns), lambda i: (0, i, 0)),
        ],
        out_specs=pl.BlockSpec((rows, tile), lambda i: (0, i)),
        scratch_shapes=[
            pltpu.VMEM((rows, 3 * LANES * heads), bf16),
            pltpu.VMEM((rows, (columns - 3 * LANES) * heads), bf16),
        ],
        compiler_params=params,
        cost_estimate=cost(2 * rows * dim * heads * columns, heads * dim * columns * 2),
        name="head_sum",
    )(grads, weights)


def per_device(ctx, tokens, feature_weight, window_weight, value_weight, log_decay, out_grad):
    rows, dim = tokens.shape
    nf2 = feature_weight.shape[1]
    nf = nf2 // 2
    dh = value_weight.shape[1]
    columns = 3 * dh + nf2
    chips, count, heads = lax.axis_size(ctx[:-1]), lax.axis_size(ctx), lax.axis_size("tp")
    fw_t = feature_weight.T
    tile = 2 * LANES
    spread = heads == 4 and count * tile == dim and count == 8
    packs = []
    if spread:
        packs = [jax.ShapeDtypeStruct((columns * tile // LANES, LANES), bf16)]

    payload = 2 * rows + 2 * nf + 16
    block = jax.ShapeDtypeStruct((payload, LANES), bf16)
    outs = pl.pallas_call(
        partial(project_kernel, ctx, len(packs)),
        out_shape=packs
        + [block] * (chips + 2)
        + [
            jax.ShapeDtypeStruct((rows, nf2), bf16),
            jax.ShapeDtypeStruct((rows, 1), f32),
            jax.ShapeDtypeStruct((dim, 2 * dh), bf16),
            jax.ShapeDtypeStruct((dim, dh), bf16),
            jax.ShapeDtypeStruct((nf2, dim), bf16),
        ],
        in_specs=[HBM] * 6,
        out_specs=[VMEM] * (len(packs) + chips + 7),
        scratch_shapes=[
            pltpu.VMEM((rows, dim), bf16),
            pltpu.VMEM((1, rows), f32),
            pltpu.VMEM((rows, dh), bf16),
            pltpu.SemaphoreType.DMA((CHUNKS, 4)),
            pltpu.SemaphoreType.DMA((2,)),
            pltpu.SemaphoreType.DMA((5,)),
        ],
        compiler_params=params,
        cost_estimate=cost(1, 1024),
        name="project",
    )(*in_hbm(tokens, fw_t, window_weight, value_weight, log_decay.T, out_grad))
    *sends, own, query, feat, cum, ww, vw, fw = outs[len(packs) :]

    swap = [(0, 1), (1, 0)]
    recv = {}
    for d in range(1, chips):
        recv[2 * d] = lax.ppermute(sends[d], ctx[:-1], [(i, i ^ d) for i in range(chips)])
    recv[1] = lax.ppermute(sends[0], "core", swap)
    for d in range(1, chips):
        recv[2 * d + 1] = lax.ppermute(recv[2 * d], "core", swap)
    recv = [recv[d] for d in range(1, count)]
    if count > 8:
        recv = [jnp.stack(recv)]

    if spread:
        near = [
            lax.ppermute(outs[0], "tp", [(z, z ^ t) for z in range(heads)])
            for t in range(1, heads)
        ]
        near[1], own = lax.optimization_barrier((near[1], own))

    attended, stat, sheet = pl.pallas_call(
        lambda *refs: query_kernel(ctx, count, *refs),
        out_shape=(
            jax.ShapeDtypeStruct((rows, dh), bf16),
            jax.ShapeDtypeStruct((8, rows), f32),
            jax.ShapeDtypeStruct((rows, LANES), f32),
        ),
        in_specs=[VMEM] * (len(recv) + 4),
        out_specs=[VMEM] * 3,
        scratch_shapes=[
            pltpu.VMEM((count, 2 * rows, dh), bf16),
            pltpu.VMEM((WINDOW // rows + 1, rows, rows), f32),
            pltpu.VMEM((count, rows), f32),
        ],
        compiler_params=params,
        cost_estimate=cost(1, 1024),
        name="query_side",
    )(*recv, own, query, feat, cum)
    stats = [stat]
    for name in reversed(ctx):
        if spread and len(stats) == 2:
            near, stats = lax.optimization_barrier((near, stats))
        held = stats[0] if len(stats) == 1 else jnp.concatenate(stats, axis=0)
        stats.append(lax.ppermute(held, name, swap))
    if count > 8:
        stats = [jnp.concatenate(stats, axis=0)]

    if spread:
        near, stats = lax.optimization_barrier((near, stats))
        pieces = [
            pl.pallas_call(
                stack_kernel,
                out_shape=jax.ShapeDtypeStruct((heads - 1, *packs[0].shape), bf16),
                in_specs=[VMEM] * (heads - 1),
                out_specs=VMEM,
                compiler_params=params,
                cost_estimate=cost(1, 1024),
                name="stack",
            )(*near)
        ]
        for d in range(1, chips):
            pieces.append(
                lax.ppermute(pieces[0], ctx[:-1], [(i, i ^ d) for i in range(chips)])
            )
        first, sheet = lax.optimization_barrier((pieces[0], sheet))
        pieces[0] = first

    grads = pl.pallas_call(
        lambda *refs: gradient_kernel(ctx, count, len(recv), len(stats), *refs),
        out_shape=jax.ShapeDtypeStruct((3 * rows + nf2 * rows // LANES, LANES), bf16),
        in_specs=[VMEM] * (len(recv) + len(stats) + 4),
        out_specs=VMEM,
        scratch_shapes=[pltpu.VMEM((count, LANES), f32)],
        compiler_params=params,
        cost_estimate=cost(1, 1024),
        name="gradients",
    )(*recv, *stats, own, query, feat, sheet)
    if not spread:
        weights = jnp.concatenate([window_weight, value_weight, feature_weight], axis=1)
        weights = lax.all_gather(weights, "tp")
        return (attended, merge(lax.all_gather(grads, "tp"), weights, rows, dim))

    swapped = {0: lax.ppermute(pieces[0], "core", swap)}
    swapped[0], grads = lax.optimization_barrier((swapped[0], grads))
    grads = lax.all_gather(grads, "tp")
    cat, feats = pl.pallas_call(
        cat_kernel,
        out_shape=[
            jax.ShapeDtypeStruct((rows, 3 * LANES * heads), bf16),
            jax.ShapeDtypeStruct((rows, nf2 * heads), bf16),
        ],
        in_specs=[VMEM],
        out_specs=[VMEM] * 2,
        compiler_params=params,
        cost_estimate=cost(1, 1024),
        name="cat",
    )(grads)
    total = []
    groups = [(0, 1)]
    for d in range(1, chips):
        groups.append((2 * d - 1, 2 * d) if d > 1 else (2 * d,))
    groups.append((2 * chips - 1,))
    for d, distances in enumerate(groups):
        if 0 < d < chips:
            if d < 3:
                late = slice(d, d + 1 if d == 1 else chips)
                pieces[late], total = lax.optimization_barrier((pieces[late], total))
            swapped[d] = lax.ppermute(pieces[d], "core", swap)
        parts = [(swapped if e % 2 else pieces)[e // 2] for e in distances]
        args = [cat, feats, ww, vw, fw, *parts, *total]
        total = [
            pl.pallas_call(
                partial(columns_kernel, ctx, distances),
                out_shape=jax.ShapeDtypeStruct((rows, dim), bf16),
                in_specs=[VMEM] * (5 + len(parts)) + [ANY] * len(total),
                out_specs=ANY,
                scratch_shapes=[
                    pltpu.VMEM((len(parts), rows, tile), bf16),
                    pltpu.SemaphoreType.DMA((len(parts),)),
                ],
                input_output_aliases={len(args) - 1: 0} if total else {},
                compiler_params=params,
                cost_estimate=cost(1, 1024),
                name="columns",
            )(*args)
        ]
    return (attended, total[0])


def solution(mesh):
    blocks, tp = mesh.devices.shape
    bits = blocks.bit_length() - 1
    assert blocks == 2**bits
    ctx = tuple(f"half{i}" for i in range(bits - 1)) + ("core",)
    split = Mesh(mesh.devices.reshape((2,) * bits + (tp,)), (*ctx, "tp"))
    in_specs = (
        P(ctx, None),
        P(None, "tp"),
        P(None, "tp"),
        P(None, "tp"),
        P(ctx, "tp"),
        P(ctx, "tp"),
    )
    out_specs = (P(ctx, "tp"), P(ctx, None))
    return jax.shard_map(
        partial(per_device, ctx),
        mesh=split,
        in_specs=in_specs,
        out_specs=out_specs,
        check_vma=False,
    )
```

```python
from functools import partial

import jax
import jax.numpy as jnp
from jax import lax
from jax.experimental import pallas as pl
from jax.experimental.pallas import tpu as pltpu
from jax.sharding import Mesh
from jax.sharding import PartitionSpec as P

WINDOW = 1024
LANES = 128
MASKED = -1e30
CHUNKS = 4
f32 = jnp.float32
bf16 = jnp.bfloat16


def nn(a, b):
    return lax.dot_general(a, b, (((1,), (0,)), ((), ())), preferred_element_type=f32)


def nt(a, b):
    return lax.dot_general(a, b, (((1,), (1,)), ((), ())), preferred_element_type=f32)


def partner(me, d, count):
    assert count & (count - 1) == 0
    return jnp.bitwise_xor(me, d)


def wide(view, start, count):
    return jnp.concatenate(
        [view[start : start + count, :], view[start + count : start + 2 * count, :]], axis=1
    )


def put_wide(ref, start, value):
    count = value.shape[0]
    for half in range(value.shape[1] // LANES):
        ref[start + half * count : start + (half + 1) * count, :] = value[
            :, half * LANES : (half + 1) * LANES
        ]


def cum_row(view, start):
    tail = view[start : start + 16, :].astype(f32)
    first = tail[0:1] + tail[2:3] + tail[4:5]
    second = tail[1:2] + tail[3:4] + tail[5:6]
    return jnp.concatenate([first, second], axis=1)


def iotas(rows):
    return (
        lax.broadcasted_iota(jnp.int32, (rows, rows), 0),
        lax.broadcasted_iota(jnp.int32, (rows, rows), 1),
    )


def block_index(ctx):
    place = 0
    for name in ctx:
        place = place * lax.axis_size(name) + lax.axis_index(name)
    return place


def pack_copies(ctx, ww_hbm, vw_hbm, fw_hbm, out_ref, sems):
    nf2 = fw_hbm.shape[0]
    tile = 2 * LANES
    at = pl.multiple_of(block_index(ctx) * tile, tile)
    rows = pl.ds(at, tile)
    moves = [
        (ww_hbm.at[rows, pl.ds(0, LANES)], out_ref.at[pl.ds(0, tile), :]),
        (ww_hbm.at[rows, pl.ds(LANES, LANES)], out_ref.at[pl.ds(tile, tile), :]),
        (vw_hbm.at[rows, :], out_ref.at[pl.ds(2 * tile, tile), :]),
    ]
    for m in range(2):
        lanes = pl.ds(pl.multiple_of(at + m * LANES, LANES), LANES)
        moves.append((fw_hbm.at[:, lanes], out_ref.at[pl.ds(3 * tile + m * nf2, nf2), :]))
    return [pltpu.make_async_copy(src, dst, sems.at[n]) for n, (src, dst) in enumerate(moves)]


def project_kernel(ctx, packs, tok_hbm, fw_hbm, ww_hbm, vw_hbm, ld_hbm, do_hbm, *rest):
    *sends, keys_ref, query_ref, feat_ref, cum_ref, ww_ref, vw_ref, fw_ref = rest[packs:-6]
    tok_ref, ld_ref, do_ref, sems, small, pack_sems = rest[-6:]
    me = block_index(ctx)
    rows, dim = tok_ref.shape
    dh = do_ref.shape[1]
    nf = fw_ref.shape[0] // 2
    span = dim // CHUNKS
    copies = []
    for c in range(CHUNKS):
        part = pl.ds(c * span, span)
        copies.append([
            pltpu.make_async_copy(tok_hbm.at[:, part], tok_ref.at[:, part], sems.at[c, 0]),
            pltpu.make_async_copy(ww_hbm.at[part, :], ww_ref.at[part, :], sems.at[c, 1]),
            pltpu.make_async_copy(vw_hbm.at[part, :], vw_ref.at[part, :], sems.at[c, 2]),
            pltpu.make_async_copy(fw_hbm.at[:, part], fw_ref.at[:, part], sems.at[c, 3]),
        ])
    others = [
        pltpu.make_async_copy(ld_hbm, ld_ref, small.at[0]),
        pltpu.make_async_copy(do_hbm, do_ref, small.at[1]),
    ]
    for copy in others:
        copy.start()
    for group in copies:
        for at, copy in enumerate(group):
            copy.start(priority=min(at, 1))
    packing = pack_copies(ctx, ww_hbm, vw_hbm, fw_hbm, rest[0], pack_sems) if packs else []
    for copy in packing:
        copy.start()
    for copy in others:
        copy.wait()
    at_row, at_col = iotas(rows)
    ld_r = ld_ref[...]
    ld_c = jnp.sum(jnp.where(at_row == at_col, ld_r, 0.0), axis=1, keepdims=True)
    cum_r = jnp.sum(jnp.where(at_row <= at_col, ld_c, 0.0), axis=0, keepdims=True)
    cum_ref[...] = jnp.sum(jnp.where(at_col <= at_row, ld_r, 0.0), axis=1, keepdims=True)
    high = cum_r.astype(bf16)
    left = cum_r - high.astype(f32)
    mid = left.astype(bf16)
    low = (left - mid.astype(f32)).astype(bf16)
    pieces = [t[:, h : h + LANES].astype(f32) for t in (high, mid, low) for h in range(0, rows, LANES)]
    tail = jnp.concatenate(pieces + [jnp.zeros((10, LANES), f32)], axis=0).astype(bf16)

    feat = jnp.zeros((rows, 2 * nf), f32)
    main = jnp.zeros((rows, 3 * dh), f32)
    for c in range(CHUNKS):
        for copy in copies[c]:
            copy.wait()
        part = slice(c * span, (c + 1) * span)
        tok = tok_ref[:, part]
        feat += nt(tok, fw_ref[:, part])
        main += nn(tok, jnp.concatenate([ww_ref[part, :], vw_ref[part, :]], axis=1))
    feat = feat.astype(bf16)
    window = main[:, : 2 * dh].astype(bf16)
    values = main[:, 2 * dh :].astype(bf16)
    feat_ref[...] = feat
    small_row, small_col = iotas(2 * nf)
    feat_t = nt((small_row == small_col).astype(bf16), feat).astype(bf16)
    feat_at = 2 * rows
    tail_at = feat_at + 2 * nf

    def put_keys(ref):
        ref[0:rows, :] = window[:, dh:]
        ref[rows : 2 * rows, :] = values
        put_wide(ref, feat_at, feat_t[nf:, :])
        ref[tail_at : tail_at + 16, :] = tail

    def put_query(ref):
        ref[0:rows, :] = window[:, :dh]
        ref[rows : 2 * rows, :] = do_ref[...]
        put_wide(ref, feat_at, feat_t[:nf, :])
        ref[tail_at : tail_at + 16, :] = tail

    put_keys(keys_ref)
    put_query(query_ref)
    for at, ref in enumerate(sends):
        later = jnp.bitwise_xor(me, max(2 * at, 1)) > me
        pl.when(later)(lambda ref=ref: put_keys(ref))
        pl.when(jnp.logical_not(later))(lambda ref=ref: put_query(ref))
    for copy in packing:
        copy.wait()

def stack_kernel(*refs):
    *parts, out_ref = refs
    for t, ref in enumerate(parts):
        out_ref[t] = ref[...]


def between(totals, low, high):
    at = lax.broadcasted_iota(jnp.int32, totals.shape, 0)
    return jnp.sum(jnp.where((at > low) & (at < high), totals, 0.0), axis=0, keepdims=True)


def over_partners(count, body, carry):
    if count <= 8:
        for d in range(1, count):
            carry = body(d, carry)
        return carry
    return lax.fori_loop(1, count, body, carry)


def query_kernel(ctx, count, *rest):
    recvs = rest[: -10]
    (own_ref, query_ref, feat_ref, cum_ref, att_ref, stat_ref, sheet_ref, near_ref, p_ref,
     cums_ref) = rest[-10:]

    def recv(d):
        return recvs[d - 1] if len(recvs) > 1 else recvs[0].at[d - 1]

    me = block_index(ctx)
    rows, dh = att_ref.shape
    nf = feat_ref.shape[1] // 2
    back = WINDOW // rows
    feat_at = 2 * rows
    tail_at = feat_at + 2 * nf
    scale = dh ** (-0.5)
    feat_scale = nf ** (-0.5)
    wq = query_ref[0:rows, :]
    do = query_ref[rows : 2 * rows, :]
    q = feat_ref[:, :nf]
    at_row, at_col = iotas(rows)
    own_cum = cum_row(own_ref, tail_at)
    cums_ref[pl.ds(me, 1), :] = own_cum
    near_ref[me] = own_ref[0 : 2 * rows, :]

    def gather(d, carry):
        j = partner(me, d, count)
        view = recv(d)
        near_ref[j] = view[0 : 2 * rows, :]
        cums_ref[pl.ds(j, 1), :] = cum_row(view, tail_at)
        return carry

    over_partners(count, gather, 0)

    def near(w):
        return near_ref.at[jnp.maximum(me - back + w, 0)]

    top = jnp.full((rows, LANES), MASKED, f32)
    for w in range(back + 1):
        keys = own_ref[0:rows, :] if w == back else near(w)[0:rows, :]
        s = nt(wq, keys) * scale
        if w == back:
            s = jnp.where(at_col <= at_row, s, MASKED)
        elif w == 0:
            s = jnp.where((at_col > at_row) & (me >= back), s, MASKED)
        else:
            s = jnp.where(me >= back - w, s, MASKED)
        p_ref[w] = s
        for h in range(0, rows, LANES):
            top = jnp.maximum(top, s[:, h : h + LANES])
    top = jnp.max(top, axis=1, keepdims=True)
    total = jnp.zeros((rows, LANES), f32)
    out = jnp.zeros((rows, dh), f32)
    for w in range(back + 1):
        p = jnp.exp(p_ref[w] - top)
        for h in range(0, rows, LANES):
            total += p[:, h : h + LANES]
        vals = own_ref[rows : 2 * rows, :] if w == back else near(w)[rows : 2 * rows, :]
        out += nn(p.astype(bf16), vals)
    total = jnp.sum(total, axis=1, keepdims=True)
    windowed = out * (1.0 / total)

    cum_c = cum_ref[...]
    growth = jnp.exp(cum_c)
    totals = cums_ref[:, rows - 1 : rows]

    def forward(d, carry):
        num, den = carry
        j = partner(me, d, count)
        view = recv(d)
        gap = between(totals, j - 1, me)
        es = jnp.where(j < me, jnp.exp(jnp.minimum(gap - cums_ref[pl.ds(j, 1), :], 0.0)), 0.0)
        x = nn(q, wide(view, feat_at, nf)) * feat_scale
        weight = (1.0 + x + 0.5 * x * x) * es
        for h in range(0, rows, LANES):
            den += weight[:, h : h + LANES]
        num += nn(weight.astype(bf16), view[rows : 2 * rows, :])
        return num, den

    num, den = over_partners(
        count, forward, (jnp.zeros((rows, dh), f32), jnp.zeros((rows, LANES), f32))
    )
    x = nn(q, wide(own_ref, feat_at, nf)) * feat_scale
    e = jnp.where(at_col <= at_row, jnp.exp(jnp.minimum(cum_c - own_cum, 0.0)), 0.0)
    weight = (1.0 + x + 0.5 * x * x) * e
    num = num * growth + nn(weight.astype(bf16), own_ref[rows : 2 * rows, :])
    den = den * growth
    for h in range(0, rows, LANES):
        den += weight[:, h : h + LANES]
    rden = 1.0 / jnp.sum(den, axis=1, keepdims=True)
    linear = num * rden
    att_ref[...] = (linear + windowed).astype(bf16)
    do_f = do.astype(f32)
    delta_w = jnp.sum(do_f * windowed, axis=1, keepdims=True)
    delta_l = jnp.sum(do_f * linear, axis=1, keepdims=True)
    lse = top + jnp.log(total)
    lane = lax.broadcasted_iota(jnp.int32, (rows, LANES), 1)
    sheet = jnp.where(lane == 0, lse, 0.0)
    sheet = jnp.where(lane == 1, delta_w, sheet)
    sheet = jnp.where(lane == 2, rden, sheet)
    sheet = jnp.where(lane == 3, delta_l, sheet)
    sheet = jnp.where(lane == 4, cum_c, sheet)
    sheet_ref[...] = sheet
    stat_ref[...] = jnp.transpose(sheet)[0:8, :]


def gradient_kernel(ctx, count, recvs, stats, *rest):
    recvs, rest = rest[:recvs], rest[recvs:]
    stats, rest = rest[:stats], rest[stats:]
    own_ref, query_ref, feat_ref, sheet_ref, *rest, total_ref = rest

    def recv(d):
        return recvs[d - 1] if len(recvs) > 1 else recvs[0].at[d - 1]

    me = block_index(ctx)
    rows = feat_ref.shape[0]
    dh = LANES
    nf = feat_ref.shape[1] // 2
    feat_at = 2 * rows
    scale = dh ** (-0.5)
    feat_scale = nf ** (-0.5)
    at_row, at_col = iotas(rows)
    apart = at_row - at_col
    wq, wk = query_ref[0:rows, :], own_ref[0:rows, :]
    do, v = query_ref[rows : 2 * rows, :], own_ref[rows : 2 * rows, :]
    q, k = feat_ref[:, :nf], feat_ref[:, nf:]
    lse_c, dw_c = sheet_ref[:, 0:1], sheet_ref[:, 1:2]
    rden_c, dl_c, cum_c = sheet_ref[:, 2:3], sheet_ref[:, 3:4], sheet_ref[:, 4:5]
    def stat(d):
        if len(stats) == 1:
            return stats[0].at[pl.ds(pl.multiple_of(8 * d, 8), 8)]
        at = d.bit_length()
        return stats[at].at[pl.ds(8 * (d - (1 << at >> 1)), 8)]

    mine_ref = stat(0)
    own_cum = mine_ref[4:5, :]
    total_ref[pl.ds(me, 1), :] = own_cum[:, rows - LANES :]

    def place(d, carry):
        total_ref[pl.ds(partner(me, d, count), 1), :] = stat(d)[4:5, rows - LANES :]
        return carry

    over_partners(count, place, 0)
    totals = total_ref[:, LANES - 1 :]
    growth_c = jnp.exp(cum_c) * rden_c
    tail_c = jnp.exp(own_cum[:, rows - 1 : rows] - cum_c)

    def pick(flag, a, b):
        return jnp.where(flag, a, b)

    s = nt(wq, wk) * scale
    causal = at_col <= at_row
    p = jnp.where(causal, jnp.exp(s - lse_c), 0.0)
    dp = nt(do, v)
    dwq = nn((p * (dp - dw_c)).astype(bf16), wk)
    x = nn(q, wide(own_ref, feat_at, nf)) * feat_scale
    e = jnp.where(causal, jnp.exp(jnp.minimum(cum_c - own_cum, 0.0)), 0.0) * rden_c
    dx = (dp - dl_c) * e * (1.0 + x)
    dqt = nt(wide(own_ref, feat_at, nf), dx.astype(bf16))

    s = nt(wk, wq) * scale
    causal = at_row <= at_col
    p = jnp.where(causal, jnp.exp(s - mine_ref[0:1, :]), 0.0)
    dp = nt(v, do)
    dwk = nn((p * (dp - mine_ref[1:2, :])).astype(bf16), wq)
    x = nn(k, wide(query_ref, feat_at, nf)) * feat_scale
    e = jnp.where(causal, jnp.exp(jnp.minimum(own_cum - cum_c, 0.0)), 0.0) * mine_ref[2:3, :]
    dx = (dp - mine_ref[3:4, :]) * e * (1.0 + x)
    dkt = nt(wide(query_ref, feat_at, nf), dx.astype(bf16))
    dv = nn((p + (1.0 + x + 0.5 * x * x) * e).astype(bf16), do)

    def step(d, carry):
        dwq, dqt, dwk, dkt, dv = carry
        j = partner(me, d, count)
        view = recv(d)
        mine = j < me
        sign = pick(mine, 1, -1)
        limit = WINDOW - jnp.abs(me - j) * rows
        rows_w = pick(mine, wq, wk)
        rows_v = pick(mine, do, v)
        rows_f = pick(mine, q, k)
        other_w = view[0:rows, :]
        other_v = view[rows : 2 * rows, :]
        other_f = wide(view, feat_at, nf)
        st = stat(d)
        zero = jnp.zeros((1, rows), f32)
        cum = st[4:5, :]
        gap = between(totals, jnp.minimum(me, j), jnp.maximum(me, j))
        e_r = jnp.exp(jnp.minimum(gap + pick(mine, cum[:, rows - 1 : rows] - cum, cum), 0.0))
        e_r = e_r * pick(mine, 1.0, st[2:3, :])
        e_c = pick(mine, growth_c, tail_c)

        s = nt(rows_w, other_w) * scale
        p = jnp.exp(s - pick(mine, lse_c, 0.0) - pick(mine, zero, st[0:1, :]))
        p = jnp.where(apart * sign < limit, p, 0.0)
        dp = nt(rows_v, other_v)
        ds = p * (dp - pick(mine, dw_c, 0.0) - pick(mine, zero, st[1:2, :]))
        more_w = nn(ds.astype(bf16), other_w)
        x = nn(rows_f, other_f) * feat_scale
        e = e_r * e_c
        dx = (dp - pick(mine, dl_c, 0.0) - pick(mine, zero, st[3:4, :])) * e * (1.0 + x)
        more_f = nt(other_f, dx.astype(bf16))
        more_v = nn((p + (1.0 + x + 0.5 * x * x) * e).astype(bf16), other_v)
        dwq = dwq + pick(mine, more_w, 0.0)
        dwk = dwk + pick(mine, 0.0, more_w)
        dqt = dqt + pick(mine, more_f, 0.0)
        dkt = dkt + pick(mine, 0.0, more_f)
        dv = dv + pick(mine, 0.0, more_v)
        return dwq, dqt, dwk, dkt, dv

    dwq, dqt, dwk, dkt, dv = over_partners(count, step, (dwq, dqt, dwk, dkt, dv))
    dwq, dwk = (dwq * scale).astype(bf16), (dwk * scale).astype(bf16)
    dv = dv.astype(bf16)
    dft = (jnp.concatenate([dqt, dkt], axis=0) * feat_scale).astype(bf16)
    (grad_ref,) = rest
    grad_ref[0:rows, :] = dwq
    grad_ref[rows : 2 * rows, :] = dwk
    grad_ref[2 * rows : 3 * rows, :] = dv
    put_wide(grad_ref, 3 * rows, dft)


def gather_rows(grad_ref, order, cat_ref, feat_ref):
    rows = cat_ref.shape[0]
    nf2 = feat_ref.shape[1] // len(order)
    for at, h in enumerate(order):
        for part in range(3):
            lane = (3 * at + part) * LANES
            cat_ref[:, lane : lane + LANES] = grad_ref[h, part * rows : (part + 1) * rows, :]
    dft = jnp.concatenate([wide(grad_ref.at[h], 3 * rows, nf2) for h in order], axis=0)
    feat_ref[...] = jnp.transpose(dft.astype(f32)).astype(bf16)


def cat_kernel(grad_ref, cat_ref, feat_ref):
    heads = grad_ref.shape[0]
    head = lax.axis_index("tp")
    order = [head] + [jnp.bitwise_xor(head, t) for t in range(1, heads)]
    gather_rows(grad_ref, order, cat_ref, feat_ref)


def columns_kernel(ctx, distances, cat_ref, feat_ref, ww_ref, vw_ref, fw_ref, *rest):
    pieces = rest[: len(distances)]
    out_ref, tile_ref, sems = rest[-3:]
    nf2 = fw_ref.shape[0]
    heads = feat_ref.shape[1] // nf2
    tile = 2 * LANES
    me = block_index(ctx)
    copies = []
    for n, (e, ref) in enumerate(zip(distances, pieces)):
        part = pl.ds(pl.multiple_of(jnp.bitwise_xor(me, e) * tile, tile), tile)
        main = [ww_ref[part, :], vw_ref[part, :]]
        main += [
            ref[t, m * tile : (m + 1) * tile, :] for t in range(heads - 1) for m in range(3)
        ]
        feats = [fw_ref[:, part]] + [wide(ref.at[t], 3 * tile, nf2) for t in range(heads - 1)]
        total = nt(cat_ref[...], jnp.concatenate(main, axis=1))
        total += nn(feat_ref[...], jnp.concatenate(feats, axis=0))
        tile_ref[n] = total.astype(bf16)
        copies.append(pltpu.make_async_copy(tile_ref.at[n], out_ref.at[:, part], sems.at[n]))
        copies[-1].start()
    for copy in copies:
        copy.wait()


def merge_kernel(grad_ref, weight_ref, out_ref, cat_ref, feat_ref):
    heads = grad_ref.shape[0]
    tile = out_ref.shape[1]
    lanes = 3 * LANES
    nf2 = feat_ref.shape[1] // heads

    @pl.when(pl.program_id(0) == 0)
    def _():
        gather_rows(grad_ref, range(heads), cat_ref, feat_ref)

    views = [weight_ref.at[h] for h in range(heads)]
    main = jnp.concatenate([v[:, 0:lanes] for v in views], axis=1)
    feats = jnp.concatenate([v[:, lanes:] for v in views], axis=1)
    out_ref[...] = (nt(cat_ref[...], main) + nt(feat_ref[...], feats)).astype(bf16)


VMEM = pl.BlockSpec(memory_space=pltpu.VMEM)
HBM = pl.BlockSpec(memory_space=pltpu.HBM)
ANY = pl.BlockSpec(memory_space=pl.ANY)
params = pltpu.CompilerParams(vmem_limit_bytes=32 * 1024 * 1024)


def in_hbm(*arrays):
    return [pltpu.with_memory_space_constraint(a, pltpu.HBM) for a in arrays]


def cost(flops, nbytes, exps=0):
    return pl.CostEstimate(flops=flops, bytes_accessed=nbytes, transcendentals=exps)


def merge(grads, weights, rows, dim):
    heads, _, columns = weights.shape
    tile = 2 * LANES
    return pl.pallas_call(
        merge_kernel,
        out_shape=jax.ShapeDtypeStruct((rows, dim), bf16),
        grid=(dim // tile,),
        in_specs=[
            pl.BlockSpec(grads.shape, lambda i: (0, 0, 0)),
            pl.BlockSpec((heads, tile, columns), lambda i: (0, i, 0)),
        ],
        out_specs=pl.BlockSpec((rows, tile), lambda i: (0, i)),
        scratch_shapes=[
            pltpu.VMEM((rows, 3 * LANES * heads), bf16),
            pltpu.VMEM((rows, (columns - 3 * LANES) * heads), bf16),
        ],
        compiler_params=params,
        cost_estimate=cost(2 * rows * dim * heads * columns, heads * dim * columns * 2),
        name="head_sum",
    )(grads, weights)


def per_device(ctx, tokens, feature_weight, window_weight, value_weight, log_decay, out_grad):
    rows, dim = tokens.shape
    nf2 = feature_weight.shape[1]
    nf = nf2 // 2
    dh = value_weight.shape[1]
    columns = 3 * dh + nf2
    chips, count, heads = lax.axis_size(ctx[:-1]), lax.axis_size(ctx), lax.axis_size("tp")
    fw_t = feature_weight.T
    tile = 2 * LANES
    spread = heads == 4 and count * tile == dim and count == 8
    packs = []
    if spread:
        packs = [jax.ShapeDtypeStruct((columns * tile // LANES, LANES), bf16)]

    payload = 2 * rows + 2 * nf + 16
    block = jax.ShapeDtypeStruct((payload, LANES), bf16)
    outs = pl.pallas_call(
        partial(project_kernel, ctx, len(packs)),
        out_shape=packs
        + [block] * (chips + 2)
        + [
            jax.ShapeDtypeStruct((rows, nf2), bf16),
            jax.ShapeDtypeStruct((rows, 1), f32),
            jax.ShapeDtypeStruct((dim, 2 * dh), bf16),
            jax.ShapeDtypeStruct((dim, dh), bf16),
            jax.ShapeDtypeStruct((nf2, dim), bf16),
        ],
        in_specs=[HBM] * 6,
        out_specs=[VMEM] * (len(packs) + chips + 7),
        scratch_shapes=[
            pltpu.VMEM((rows, dim), bf16),
            pltpu.VMEM((1, rows), f32),
            pltpu.VMEM((rows, dh), bf16),
            pltpu.SemaphoreType.DMA((CHUNKS, 4)),
            pltpu.SemaphoreType.DMA((2,)),
            pltpu.SemaphoreType.DMA((5,)),
        ],
        compiler_params=params,
        cost_estimate=cost(1, 1024),
        name="project",
    )(*in_hbm(tokens, fw_t, window_weight, value_weight, log_decay.T, out_grad))
    *sends, own, query, feat, cum, ww, vw, fw = outs[len(packs) :]

    swap = [(0, 1), (1, 0)]
    recv = {}
    for d in range(1, chips):
        recv[2 * d] = lax.ppermute(sends[d], ctx[:-1], [(i, i ^ d) for i in range(chips)])
    recv[1] = lax.ppermute(sends[0], "core", swap)
    for d in range(1, chips):
        recv[2 * d + 1] = lax.ppermute(recv[2 * d], "core", swap)
    recv = [recv[d] for d in range(1, count)]
    if count > 8:
        recv = [jnp.stack(recv)]

    if spread:
        near = [
            lax.ppermute(outs[0], "tp", [(z, z ^ t) for z in range(heads)])
            for t in range(1, heads)
        ]

    attended, stat, sheet = pl.pallas_call(
        lambda *refs: query_kernel(ctx, count, *refs),
        out_shape=(
            jax.ShapeDtypeStruct((rows, dh), bf16),
            jax.ShapeDtypeStruct((8, rows), f32),
            jax.ShapeDtypeStruct((rows, LANES), f32),
        ),
        in_specs=[VMEM] * (len(recv) + 4),
        out_specs=[VMEM] * 3,
        scratch_shapes=[
            pltpu.VMEM((count, 2 * rows, dh), bf16),
            pltpu.VMEM((WINDOW // rows + 1, rows, rows), f32),
            pltpu.VMEM((count, rows), f32),
        ],
        compiler_params=params,
        cost_estimate=cost(1, 1024),
        name="query_side",
    )(*recv, own, query, feat, cum)
    stats = [stat]
    for name in reversed(ctx):
        if spread and len(stats) == 2:
            near, stats = lax.optimization_barrier((near, stats))
        held = stats[0] if len(stats) == 1 else jnp.concatenate(stats, axis=0)
        stats.append(lax.ppermute(held, name, swap))
    if count > 8:
        stats = [jnp.concatenate(stats, axis=0)]

    if spread:
        near, stats = lax.optimization_barrier((near, stats))
        pieces = [
            pl.pallas_call(
                stack_kernel,
                out_shape=jax.ShapeDtypeStruct((heads - 1, *packs[0].shape), bf16),
                in_specs=[VMEM] * (heads - 1),
                out_specs=VMEM,
                compiler_params=params,
                cost_estimate=cost(1, 1024),
                name="stack",
            )(*near)
        ]
        for d in range(1, chips):
            pieces.append(
                lax.ppermute(pieces[0], ctx[:-1], [(i, i ^ d) for i in range(chips)])
            )
        first, sheet = lax.optimization_barrier((pieces[0], sheet))
        pieces[0] = first

    grads = pl.pallas_call(
        lambda *refs: gradient_kernel(ctx, count, len(recv), len(stats), *refs),
        out_shape=jax.ShapeDtypeStruct((3 * rows + nf2 * rows // LANES, LANES), bf16),
        in_specs=[VMEM] * (len(recv) + len(stats) + 4),
        out_specs=VMEM,
        scratch_shapes=[pltpu.VMEM((count, LANES), f32)],
        compiler_params=params,
        cost_estimate=cost(1, 1024),
        name="gradients",
    )(*recv, *stats, own, query, feat, sheet)
    if not spread:
        weights = jnp.concatenate([window_weight, value_weight, feature_weight], axis=1)
        weights = lax.all_gather(weights, "tp")
        return (attended, merge(lax.all_gather(grads, "tp"), weights, rows, dim))

    swapped = {0: lax.ppermute(pieces[0], "core", swap)}
    swapped[0], grads = lax.optimization_barrier((swapped[0], grads))
    grads = lax.all_gather(grads, "tp")
    cat, feats = pl.pallas_call(
        cat_kernel,
        out_shape=[
            jax.ShapeDtypeStruct((rows, 3 * LANES * heads), bf16),
            jax.ShapeDtypeStruct((rows, nf2 * heads), bf16),
        ],
        in_specs=[VMEM],
        out_specs=[VMEM] * 2,
        compiler_params=params,
        cost_estimate=cost(1, 1024),
        name="cat",
    )(grads)
    total = []
    for distances in ((0, 1), (2,), (3, 4, 6), (5, 7)):
        if distances == (2,):
            pieces[1], total = lax.optimization_barrier((pieces[1], total))
            swapped[1] = lax.ppermute(pieces[1], "core", swap)
        if distances == (3, 4, 6):
            pieces[2:], total = lax.optimization_barrier((pieces[2:], total))
            for d in range(2, chips):
                swapped[d] = lax.ppermute(pieces[d], "core", swap)
        parts = [(swapped if e % 2 else pieces)[e // 2] for e in distances]
        args = [cat, feats, ww, vw, fw, *parts, *total]
        total = [
            pl.pallas_call(
                partial(columns_kernel, ctx, distances),
                out_shape=jax.ShapeDtypeStruct((rows, dim), bf16),
                in_specs=[VMEM] * (5 + len(parts)) + [ANY] * len(total),
                out_specs=ANY,
                scratch_shapes=[
                    pltpu.VMEM((len(parts), rows, tile), bf16),
                    pltpu.SemaphoreType.DMA((len(parts),)),
                ],
                input_output_aliases={len(args) - 1: 0} if total else {},
                compiler_params=params,
                cost_estimate=cost(1, 1024),
                name="columns",
            )(*args)
        ]
    return (attended, total[0])


def solution(mesh):
    blocks, tp = mesh.devices.shape
    bits = blocks.bit_length() - 1
    assert blocks == 2**bits
    ctx = tuple(f"half{i}" for i in range(bits - 1)) + ("core",)
    split = Mesh(mesh.devices.reshape((2,) * bits + (tp,)), (*ctx, "tp"))
    in_specs = (
        P(ctx, None),
        P(None, "tp"),
        P(None, "tp"),
        P(None, "tp"),
        P(ctx, "tp"),
        P(ctx, "tp"),
    )
    out_specs = (P(ctx, "tp"), P(ctx, None))
    return jax.shard_map(
        partial(per_device, ctx),
        mesh=split,
        in_specs=in_specs,
        out_specs=out_specs,
        check_vma=False,
    )
```

```python
from functools import partial

import jax
import jax.numpy as jnp
from jax import lax
from jax.experimental import pallas as pl
from jax.experimental.pallas import tpu as pltpu
from jax.sharding import Mesh
from jax.sharding import PartitionSpec as P

WINDOW = 1024
LANES = 128
MASKED = -1e30
CHUNKS = 4
f32 = jnp.float32
bf16 = jnp.bfloat16


def nn(a, b):
    return lax.dot_general(a, b, (((1,), (0,)), ((), ())), preferred_element_type=f32)


def nt(a, b):
    return lax.dot_general(a, b, (((1,), (1,)), ((), ())), preferred_element_type=f32)


def partner(me, d, count):
    assert count & (count - 1) == 0
    return jnp.bitwise_xor(me, d)


def wide(view, start, count):
    return jnp.concatenate(
        [view[start : start + count, :], view[start + count : start + 2 * count, :]], axis=1
    )


def put_wide(ref, start, value):
    count = value.shape[0]
    for half in range(value.shape[1] // LANES):
        ref[start + half * count : start + (half + 1) * count, :] = value[
            :, half * LANES : (half + 1) * LANES
        ]


def cum_row(view, start):
    tail = view[start : start + 16, :].astype(f32)
    first = tail[0:1] + tail[2:3] + tail[4:5]
    second = tail[1:2] + tail[3:4] + tail[5:6]
    return jnp.concatenate([first, second], axis=1)


def iotas(rows):
    return (
        lax.broadcasted_iota(jnp.int32, (rows, rows), 0),
        lax.broadcasted_iota(jnp.int32, (rows, rows), 1),
    )


def block_index(ctx):
    place = 0
    for name in ctx:
        place = place * lax.axis_size(name) + lax.axis_index(name)
    return place


def pack_copies(ctx, distance, ww_hbm, vw_hbm, fw_hbm, out_ref, sems):
    nf2 = fw_hbm.shape[0]
    tile = 2 * LANES
    at = pl.multiple_of(jnp.bitwise_xor(block_index(ctx), distance) * tile, tile)
    rows = pl.ds(at, tile)
    moves = [
        (ww_hbm.at[rows, pl.ds(0, LANES)], out_ref.at[pl.ds(0, tile), :]),
        (ww_hbm.at[rows, pl.ds(LANES, LANES)], out_ref.at[pl.ds(tile, tile), :]),
        (vw_hbm.at[rows, :], out_ref.at[pl.ds(2 * tile, tile), :]),
    ]
    for m in range(2):
        lanes = pl.ds(pl.multiple_of(at + m * LANES, LANES), LANES)
        moves.append((fw_hbm.at[:, lanes], out_ref.at[pl.ds(3 * tile + m * nf2, nf2), :]))
    return [pltpu.make_async_copy(src, dst, sems.at[n]) for n, (src, dst) in enumerate(moves)]


def project_kernel(ctx, packs, tok_hbm, fw_hbm, ww_hbm, vw_hbm, ld_hbm, do_hbm, *rest):
    *sends, keys_ref, query_ref, feat_ref, cum_ref, ww_ref, vw_ref, fw_ref = rest[packs:-6]
    tok_ref, ld_ref, do_ref, sems, small, pack_sems = rest[-6:]
    me = block_index(ctx)
    rows, dim = tok_ref.shape
    dh = do_ref.shape[1]
    nf = fw_ref.shape[0] // 2
    span = dim // CHUNKS
    copies = []
    for c in range(CHUNKS):
        part = pl.ds(c * span, span)
        copies.append([
            pltpu.make_async_copy(tok_hbm.at[:, part], tok_ref.at[:, part], sems.at[c, 0]),
            pltpu.make_async_copy(ww_hbm.at[part, :], ww_ref.at[part, :], sems.at[c, 1]),
            pltpu.make_async_copy(vw_hbm.at[part, :], vw_ref.at[part, :], sems.at[c, 2]),
            pltpu.make_async_copy(fw_hbm.at[:, part], fw_ref.at[:, part], sems.at[c, 3]),
        ])
    others = [
        pltpu.make_async_copy(ld_hbm, ld_ref, small.at[0]),
        pltpu.make_async_copy(do_hbm, do_ref, small.at[1]),
    ]
    for copy in others:
        copy.start()
    for group in copies:
        for at, copy in enumerate(group):
            copy.start(priority=min(at, 1))
    packing = pack_copies(ctx, 0, ww_hbm, vw_hbm, fw_hbm, rest[0], pack_sems) if packs else []
    for copy in packing:
        copy.start()
    for copy in others:
        copy.wait()
    at_row, at_col = iotas(rows)
    ld_r = ld_ref[...]
    ld_c = jnp.sum(jnp.where(at_row == at_col, ld_r, 0.0), axis=1, keepdims=True)
    cum_r = jnp.sum(jnp.where(at_row <= at_col, ld_c, 0.0), axis=0, keepdims=True)
    cum_ref[...] = jnp.sum(jnp.where(at_col <= at_row, ld_r, 0.0), axis=1, keepdims=True)
    high = cum_r.astype(bf16)
    left = cum_r - high.astype(f32)
    mid = left.astype(bf16)
    low = (left - mid.astype(f32)).astype(bf16)
    pieces = [t[:, h : h + LANES].astype(f32) for t in (high, mid, low) for h in range(0, rows, LANES)]
    tail = jnp.concatenate(pieces + [jnp.zeros((10, LANES), f32)], axis=0).astype(bf16)

    feat = jnp.zeros((rows, 2 * nf), f32)
    main = jnp.zeros((rows, 3 * dh), f32)
    for c in range(CHUNKS):
        for copy in copies[c]:
            copy.wait()
        part = slice(c * span, (c + 1) * span)
        tok = tok_ref[:, part]
        feat += nt(tok, fw_ref[:, part])
        main += nn(tok, jnp.concatenate([ww_ref[part, :], vw_ref[part, :]], axis=1))
    feat = feat.astype(bf16)
    window = main[:, : 2 * dh].astype(bf16)
    values = main[:, 2 * dh :].astype(bf16)
    feat_ref[...] = feat
    small_row, small_col = iotas(2 * nf)
    feat_t = nt((small_row == small_col).astype(bf16), feat).astype(bf16)
    feat_at = 2 * rows
    tail_at = feat_at + 2 * nf

    def put_keys(ref):
        ref[0:rows, :] = window[:, dh:]
        ref[rows : 2 * rows, :] = values
        put_wide(ref, feat_at, feat_t[nf:, :])
        ref[tail_at : tail_at + 16, :] = tail

    def put_query(ref):
        ref[0:rows, :] = window[:, :dh]
        ref[rows : 2 * rows, :] = do_ref[...]
        put_wide(ref, feat_at, feat_t[:nf, :])
        ref[tail_at : tail_at + 16, :] = tail

    put_keys(keys_ref)
    put_query(query_ref)
    for at, ref in enumerate(sends):
        later = jnp.bitwise_xor(me, max(2 * at, 1)) > me
        pl.when(later)(lambda ref=ref: put_keys(ref))
        pl.when(jnp.logical_not(later))(lambda ref=ref: put_query(ref))
    for copy in packing:
        copy.wait()

def stack_kernel(*refs):
    *parts, out_ref = refs
    for t, ref in enumerate(parts):
        out_ref[t] = ref[...]


def between(totals, low, high):
    at = lax.broadcasted_iota(jnp.int32, totals.shape, 0)
    return jnp.sum(jnp.where((at > low) & (at < high), totals, 0.0), axis=0, keepdims=True)


def over_partners(count, body, carry):
    if count <= 8:
        for d in range(1, count):
            carry = body(d, carry)
        return carry
    return lax.fori_loop(1, count, body, carry)


def query_kernel(ctx, count, recvs, *rest):
    recvs, rest = rest[:recvs], rest[recvs:]
    own_ref, query_ref, feat_ref, cum_ref, *rest = rest
    near_ref, p_ref, cums_ref, sems = rest[-4:]
    packing = []
    if len(rest) > 7:
        *weights, pack_ref = rest[:3] + rest[6:7]
        rest = rest[3:]
        for n in range(pack_ref.shape[0]):
            packing += pack_copies(ctx, 2 * n, *weights, pack_ref.at[n], sems.at[n])
    for copy in packing:
        copy.start()
    att_ref, stat_ref, sheet_ref = rest[:3]

    def recv(d):
        return recvs[d - 1] if len(recvs) > 1 else recvs[0].at[d - 1]

    me = block_index(ctx)
    rows, dh = att_ref.shape
    nf = feat_ref.shape[1] // 2
    back = WINDOW // rows
    feat_at = 2 * rows
    tail_at = feat_at + 2 * nf
    scale = dh ** (-0.5)
    feat_scale = nf ** (-0.5)
    wq = query_ref[0:rows, :]
    do = query_ref[rows : 2 * rows, :]
    q = feat_ref[:, :nf]
    at_row, at_col = iotas(rows)
    own_cum = cum_row(own_ref, tail_at)
    cums_ref[pl.ds(me, 1), :] = own_cum
    near_ref[me] = own_ref[0 : 2 * rows, :]

    def gather(d, carry):
        j = partner(me, d, count)
        view = recv(d)
        near_ref[j] = view[0 : 2 * rows, :]
        cums_ref[pl.ds(j, 1), :] = cum_row(view, tail_at)
        return carry

    over_partners(count, gather, 0)

    def near(w):
        return near_ref.at[jnp.maximum(me - back + w, 0)]

    top = jnp.full((rows, LANES), MASKED, f32)
    for w in range(back + 1):
        keys = own_ref[0:rows, :] if w == back else near(w)[0:rows, :]
        s = nt(wq, keys) * scale
        if w == back:
            s = jnp.where(at_col <= at_row, s, MASKED)
        elif w == 0:
            s = jnp.where((at_col > at_row) & (me >= back), s, MASKED)
        else:
            s = jnp.where(me >= back - w, s, MASKED)
        p_ref[w] = s
        for h in range(0, rows, LANES):
            top = jnp.maximum(top, s[:, h : h + LANES])
    top = jnp.max(top, axis=1, keepdims=True)
    total = jnp.zeros((rows, LANES), f32)
    out = jnp.zeros((rows, dh), f32)
    for w in range(back + 1):
        p = jnp.exp(p_ref[w] - top)
        for h in range(0, rows, LANES):
            total += p[:, h : h + LANES]
        vals = own_ref[rows : 2 * rows, :] if w == back else near(w)[rows : 2 * rows, :]
        out += nn(p.astype(bf16), vals)
    total = jnp.sum(total, axis=1, keepdims=True)
    windowed = out * (1.0 / total)

    cum_c = cum_ref[...]
    growth = jnp.exp(cum_c)
    totals = cums_ref[:, rows - 1 : rows]

    def forward(d, carry):
        num, den = carry
        j = partner(me, d, count)
        view = recv(d)
        gap = between(totals, j - 1, me)
        es = jnp.where(j < me, jnp.exp(jnp.minimum(gap - cums_ref[pl.ds(j, 1), :], 0.0)), 0.0)
        x = nn(q, wide(view, feat_at, nf)) * feat_scale
        weight = (1.0 + x + 0.5 * x * x) * es
        for h in range(0, rows, LANES):
            den += weight[:, h : h + LANES]
        num += nn(weight.astype(bf16), view[rows : 2 * rows, :])
        return num, den

    num, den = over_partners(
        count, forward, (jnp.zeros((rows, dh), f32), jnp.zeros((rows, LANES), f32))
    )
    x = nn(q, wide(own_ref, feat_at, nf)) * feat_scale
    e = jnp.where(at_col <= at_row, jnp.exp(jnp.minimum(cum_c - own_cum, 0.0)), 0.0)
    weight = (1.0 + x + 0.5 * x * x) * e
    num = num * growth + nn(weight.astype(bf16), own_ref[rows : 2 * rows, :])
    den = den * growth
    for h in range(0, rows, LANES):
        den += weight[:, h : h + LANES]
    rden = 1.0 / jnp.sum(den, axis=1, keepdims=True)
    linear = num * rden
    att_ref[...] = (linear + windowed).astype(bf16)
    do_f = do.astype(f32)
    delta_w = jnp.sum(do_f * windowed, axis=1, keepdims=True)
    delta_l = jnp.sum(do_f * linear, axis=1, keepdims=True)
    lse = top + jnp.log(total)
    lane = lax.broadcasted_iota(jnp.int32, (rows, LANES), 1)
    sheet = jnp.where(lane == 0, lse, 0.0)
    sheet = jnp.where(lane == 1, delta_w, sheet)
    sheet = jnp.where(lane == 2, rden, sheet)
    sheet = jnp.where(lane == 3, delta_l, sheet)
    sheet = jnp.where(lane == 4, cum_c, sheet)
    sheet_ref[...] = sheet
    stat_ref[...] = jnp.transpose(sheet)[0:8, :]
    for copy in packing:
        copy.wait()


def gradient_kernel(ctx, count, recvs, *rest):
    recvs, rest = rest[:recvs], rest[recvs:]
    own_ref, query_ref, feat_ref, sheet_ref, stat_ref, *rest, total_ref = rest

    def recv(d):
        return recvs[d - 1] if len(recvs) > 1 else recvs[0].at[d - 1]

    me = block_index(ctx)
    rows = feat_ref.shape[0]
    dh = LANES
    nf = feat_ref.shape[1] // 2
    feat_at = 2 * rows
    scale = dh ** (-0.5)
    feat_scale = nf ** (-0.5)
    at_row, at_col = iotas(rows)
    apart = at_row - at_col
    wq, wk = query_ref[0:rows, :], own_ref[0:rows, :]
    do, v = query_ref[rows : 2 * rows, :], own_ref[rows : 2 * rows, :]
    q, k = feat_ref[:, :nf], feat_ref[:, nf:]
    lse_c, dw_c = sheet_ref[:, 0:1], sheet_ref[:, 1:2]
    rden_c, dl_c, cum_c = sheet_ref[:, 2:3], sheet_ref[:, 3:4], sheet_ref[:, 4:5]
    def stat(d):
        return stat_ref.at[partner(me, d, count)]

    mine_ref = stat(0)
    own_cum = mine_ref[4:5, :]
    total_ref[pl.ds(me, 1), :] = own_cum[:, rows - LANES :]

    def place(d, carry):
        total_ref[pl.ds(partner(me, d, count), 1), :] = stat(d)[4:5, rows - LANES :]
        return carry

    over_partners(count, place, 0)
    totals = total_ref[:, LANES - 1 :]
    growth_c = jnp.exp(cum_c) * rden_c
    tail_c = jnp.exp(own_cum[:, rows - 1 : rows] - cum_c)

    def pick(flag, a, b):
        return jnp.where(flag, a, b)

    s = nt(wq, wk) * scale
    causal = at_col <= at_row
    p = jnp.where(causal, jnp.exp(s - lse_c), 0.0)
    dp = nt(do, v)
    dwq = nn((p * (dp - dw_c)).astype(bf16), wk)
    x = nn(q, wide(own_ref, feat_at, nf)) * feat_scale
    e = jnp.where(causal, jnp.exp(jnp.minimum(cum_c - own_cum, 0.0)), 0.0) * rden_c
    dx = (dp - dl_c) * e * (1.0 + x)
    dqt = nt(wide(own_ref, feat_at, nf), dx.astype(bf16))

    s = nt(wk, wq) * scale
    causal = at_row <= at_col
    p = jnp.where(causal, jnp.exp(s - mine_ref[0:1, :]), 0.0)
    dp = nt(v, do)
    dwk = nn((p * (dp - mine_ref[1:2, :])).astype(bf16), wq)
    x = nn(k, wide(query_ref, feat_at, nf)) * feat_scale
    e = jnp.where(causal, jnp.exp(jnp.minimum(own_cum - cum_c, 0.0)), 0.0) * mine_ref[2:3, :]
    dx = (dp - mine_ref[3:4, :]) * e * (1.0 + x)
    dkt = nt(wide(query_ref, feat_at, nf), dx.astype(bf16))
    dv = nn((p + (1.0 + x + 0.5 * x * x) * e).astype(bf16), do)

    def step(d, carry):
        dwq, dqt, dwk, dkt, dv = carry
        j = partner(me, d, count)
        view = recv(d)
        mine = j < me
        sign = pick(mine, 1, -1)
        limit = WINDOW - jnp.abs(me - j) * rows
        rows_w = pick(mine, wq, wk)
        rows_v = pick(mine, do, v)
        rows_f = pick(mine, q, k)
        other_w = view[0:rows, :]
        other_v = view[rows : 2 * rows, :]
        other_f = wide(view, feat_at, nf)
        st = stat(d)
        zero = jnp.zeros((1, rows), f32)
        cum = st[4:5, :]
        gap = between(totals, jnp.minimum(me, j), jnp.maximum(me, j))
        e_r = jnp.exp(jnp.minimum(gap + pick(mine, cum[:, rows - 1 : rows] - cum, cum), 0.0))
        e_r = e_r * pick(mine, 1.0, st[2:3, :])
        e_c = pick(mine, growth_c, tail_c)

        s = nt(rows_w, other_w) * scale
        p = jnp.exp(s - pick(mine, lse_c, 0.0) - pick(mine, zero, st[0:1, :]))
        p = jnp.where(apart * sign < limit, p, 0.0)
        dp = nt(rows_v, other_v)
        ds = p * (dp - pick(mine, dw_c, 0.0) - pick(mine, zero, st[1:2, :]))
        more_w = nn(ds.astype(bf16), other_w)
        x = nn(rows_f, other_f) * feat_scale
        e = e_r * e_c
        dx = (dp - pick(mine, dl_c, 0.0) - pick(mine, zero, st[3:4, :])) * e * (1.0 + x)
        more_f = nt(other_f, dx.astype(bf16))
        more_v = nn((p + (1.0 + x + 0.5 * x * x) * e).astype(bf16), other_v)
        dwq = dwq + pick(mine, more_w, 0.0)
        dwk = dwk + pick(mine, 0.0, more_w)
        dqt = dqt + pick(mine, more_f, 0.0)
        dkt = dkt + pick(mine, 0.0, more_f)
        dv = dv + pick(mine, 0.0, more_v)
        return dwq, dqt, dwk, dkt, dv

    dwq, dqt, dwk, dkt, dv = over_partners(count, step, (dwq, dqt, dwk, dkt, dv))
    dwq, dwk = (dwq * scale).astype(bf16), (dwk * scale).astype(bf16)
    dv = dv.astype(bf16)
    dft = (jnp.concatenate([dqt, dkt], axis=0) * feat_scale).astype(bf16)
    (grad_ref,) = rest
    grad_ref[0:rows, :] = dwq
    grad_ref[rows : 2 * rows, :] = dwk
    grad_ref[2 * rows : 3 * rows, :] = dv
    put_wide(grad_ref, 3 * rows, dft)


def gather_rows(grad_ref, order, cat_ref, feat_ref):
    rows = cat_ref.shape[0]
    nf2 = feat_ref.shape[1] // len(order)
    for at, h in enumerate(order):
        for part in range(3):
            lane = (3 * at + part) * LANES
            cat_ref[:, lane : lane + LANES] = grad_ref[h, part * rows : (part + 1) * rows, :]
    dft = jnp.concatenate([wide(grad_ref.at[h], 3 * rows, nf2) for h in order], axis=0)
    feat_ref[...] = jnp.transpose(dft.astype(f32)).astype(bf16)


def cat_kernel(grad_ref, cat_ref, feat_ref):
    heads = grad_ref.shape[0]
    head = lax.axis_index("tp")
    order = [head] + [jnp.bitwise_xor(head, t) for t in range(1, heads)]
    gather_rows(grad_ref, order, cat_ref, feat_ref)


def columns_kernel(ctx, distances, cat_ref, feat_ref, ww_ref, vw_ref, fw_ref, *rest):
    pieces, firsts = rest[: len(distances)], rest[len(distances) : len(distances) + 2]
    out_ref, tile_ref, sems = rest[-3:]
    nf2 = fw_ref.shape[0]
    heads = feat_ref.shape[1] // nf2
    tile = 2 * LANES
    me = block_index(ctx)
    copies = []
    for n, (e, ref) in enumerate(zip(distances, pieces)):
        part = pl.ds(pl.multiple_of(jnp.bitwise_xor(me, e) * tile, tile), tile)
        views = [firsts[e % 2].at[e // 2]] + [ref.at[t] for t in range(heads - 2)]
        main = [ww_ref[part, :], vw_ref[part, :]]
        main += [v[m * tile : (m + 1) * tile, :] for v in views for m in range(3)]
        feats = [fw_ref[:, part]] + [wide(v, 3 * tile, nf2) for v in views]
        total = nt(cat_ref[...], jnp.concatenate(main, axis=1))
        total += nn(feat_ref[...], jnp.concatenate(feats, axis=0))
        tile_ref[n] = total.astype(bf16)
        copies.append(pltpu.make_async_copy(tile_ref.at[n], out_ref.at[:, part], sems.at[n]))
        copies[-1].start()
    for copy in copies:
        copy.wait()


def merge_kernel(grad_ref, weight_ref, out_ref, cat_ref, feat_ref):
    heads = grad_ref.shape[0]
    tile = out_ref.shape[1]
    lanes = 3 * LANES
    nf2 = feat_ref.shape[1] // heads

    @pl.when(pl.program_id(0) == 0)
    def _():
        gather_rows(grad_ref, range(heads), cat_ref, feat_ref)

    views = [weight_ref.at[h] for h in range(heads)]
    main = jnp.concatenate([v[:, 0:lanes] for v in views], axis=1)
    feats = jnp.concatenate([v[:, lanes:] for v in views], axis=1)
    out_ref[...] = (nt(cat_ref[...], main) + nt(feat_ref[...], feats)).astype(bf16)


VMEM = pl.BlockSpec(memory_space=pltpu.VMEM)
HBM = pl.BlockSpec(memory_space=pltpu.HBM)
ANY = pl.BlockSpec(memory_space=pl.ANY)
params = pltpu.CompilerParams(vmem_limit_bytes=32 * 1024 * 1024)


def in_hbm(*arrays):
    return [pltpu.with_memory_space_constraint(a, pltpu.HBM) for a in arrays]


def cost(flops, nbytes, exps=0):
    return pl.CostEstimate(flops=flops, bytes_accessed=nbytes, transcendentals=exps)


def merge(grads, weights, rows, dim):
    heads, _, columns = weights.shape
    tile = 2 * LANES
    return pl.pallas_call(
        merge_kernel,
        out_shape=jax.ShapeDtypeStruct((rows, dim), bf16),
        grid=(dim // tile,),
        in_specs=[
            pl.BlockSpec(grads.shape, lambda i: (0, 0, 0)),
            pl.BlockSpec((heads, tile, columns), lambda i: (0, i, 0)),
        ],
        out_specs=pl.BlockSpec((rows, tile), lambda i: (0, i)),
        scratch_shapes=[
            pltpu.VMEM((rows, 3 * LANES * heads), bf16),
            pltpu.VMEM((rows, (columns - 3 * LANES) * heads), bf16),
        ],
        compiler_params=params,
        cost_estimate=cost(2 * rows * dim * heads * columns, heads * dim * columns * 2),
        name="head_sum",
    )(grads, weights)


def per_device(ctx, tokens, feature_weight, window_weight, value_weight, log_decay, out_grad):
    rows, dim = tokens.shape
    nf2 = feature_weight.shape[1]
    nf = nf2 // 2
    dh = value_weight.shape[1]
    columns = 3 * dh + nf2
    chips, count, heads = lax.axis_size(ctx[:-1]), lax.axis_size(ctx), lax.axis_size("tp")
    fw_t = feature_weight.T
    tile = 2 * LANES
    spread = heads == 4 and count * tile == dim and count == 8
    packs = []
    if spread:
        packs = [jax.ShapeDtypeStruct((columns * tile // LANES, LANES), bf16)]

    payload = 2 * rows + 2 * nf + 16
    block = jax.ShapeDtypeStruct((payload, LANES), bf16)
    outs = pl.pallas_call(
        partial(project_kernel, ctx, len(packs)),
        out_shape=packs
        + [block] * (chips + 2)
        + [
            jax.ShapeDtypeStruct((rows, nf2), bf16),
            jax.ShapeDtypeStruct((rows, 1), f32),
            jax.ShapeDtypeStruct((dim, 2 * dh), bf16),
            jax.ShapeDtypeStruct((dim, dh), bf16),
            jax.ShapeDtypeStruct((nf2, dim), bf16),
        ],
        in_specs=[HBM] * 6,
        out_specs=[VMEM] * (len(packs) + chips + 7),
        scratch_shapes=[
            pltpu.VMEM((rows, dim), bf16),
            pltpu.VMEM((1, rows), f32),
            pltpu.VMEM((rows, dh), bf16),
            pltpu.SemaphoreType.DMA((CHUNKS, 4)),
            pltpu.SemaphoreType.DMA((2,)),
            pltpu.SemaphoreType.DMA((5,)),
        ],
        compiler_params=params,
        cost_estimate=cost(1, 1024),
        name="project",
    )(*in_hbm(tokens, fw_t, window_weight, value_weight, log_decay.T, out_grad))
    *sends, own, query, feat, cum, ww, vw, fw = outs[len(packs) :]

    swap = [(0, 1), (1, 0)]
    recv = {}
    for d in range(1, chips):
        recv[2 * d] = lax.ppermute(sends[d], ctx[:-1], [(i, i ^ d) for i in range(chips)])
    recv[1] = lax.ppermute(sends[0], "core", swap)
    for d in range(1, chips):
        recv[2 * d + 1] = lax.ppermute(recv[2 * d], "core", swap)
    recv = [recv[d] for d in range(1, count)]
    if count > 8:
        recv = [jnp.stack(recv)]

    first_pack, first_args = [], []
    if spread:
        across = lax.ppermute(outs[0], "tp", [(z, z ^ 2) for z in range(heads)])
        across, own = lax.optimization_barrier((across, own))
        near = [across, lax.ppermute(across, "tp", [(z, z ^ 1) for z in range(heads)])]
        first_pack = [jax.ShapeDtypeStruct((chips, *packs[0].shape), bf16)]
        first_args = in_hbm(window_weight, value_weight, fw_t)

    attended, stat, sheet, *first = pl.pallas_call(
        lambda *refs: query_kernel(ctx, count, len(recv), *refs),
        out_shape=[
            jax.ShapeDtypeStruct((rows, dh), bf16),
            jax.ShapeDtypeStruct((8, rows), f32),
            jax.ShapeDtypeStruct((rows, LANES), f32),
            *first_pack,
        ],
        in_specs=[VMEM] * (len(recv) + 4) + [HBM] * len(first_args),
        out_specs=[VMEM] * (3 + len(first_pack)),
        scratch_shapes=[
            pltpu.VMEM((count, 2 * rows, dh), bf16),
            pltpu.VMEM((WINDOW // rows + 1, rows, rows), f32),
            pltpu.VMEM((count, rows), f32),
            pltpu.SemaphoreType.DMA((chips, 5)),
        ],
        compiler_params=params,
        cost_estimate=cost(1, 1024),
        name="query_side",
    )(*recv, own, query, feat, cum, *first_args)
    if spread:
        near, stat, first = lax.optimization_barrier((near, stat, first))
    stats = lax.all_gather(stat, ctx)

    if spread:
        first = lax.ppermute(first[0], "tp", [(z, z ^ 1) for z in range(heads)])
        near, stats = lax.optimization_barrier((near, stats))
        pieces = [
            pl.pallas_call(
                stack_kernel,
                out_shape=jax.ShapeDtypeStruct((heads - 2, *packs[0].shape), bf16),
                in_specs=[VMEM] * (heads - 2),
                out_specs=VMEM,
                compiler_params=params,
                cost_estimate=cost(1, 1024),
                name="stack",
            )(*near)
        ]
        for d in range(1, chips):
            pieces.append(
                lax.ppermute(pieces[0], ctx[:-1], [(i, i ^ d) for i in range(chips)])
            )
        pieces[0], sheet = lax.optimization_barrier((pieces[0], sheet))

    grads = pl.pallas_call(
        lambda *refs: gradient_kernel(ctx, count, len(recv), *refs),
        out_shape=jax.ShapeDtypeStruct((3 * rows + nf2 * rows // LANES, LANES), bf16),
        in_specs=[VMEM] * (len(recv) + 5),
        out_specs=VMEM,
        scratch_shapes=[pltpu.VMEM((count, LANES), f32)],
        compiler_params=params,
        cost_estimate=cost(1, 1024),
        name="gradients",
    )(*recv, own, query, feat, sheet, stats)
    if not spread:
        weights = jnp.concatenate([window_weight, value_weight, feature_weight], axis=1)
        weights = lax.all_gather(weights, "tp")
        return (attended, merge(lax.all_gather(grads, "tp"), weights, rows, dim))

    first, grads = lax.optimization_barrier((first, grads))
    swapped = [lax.ppermute(pieces[0], "core", swap)]
    firsts = [first, lax.ppermute(first, "core", swap)]
    grads = lax.all_gather(grads, "tp")
    cat, feats = pl.pallas_call(
        cat_kernel,
        out_shape=[
            jax.ShapeDtypeStruct((rows, 3 * LANES * heads), bf16),
            jax.ShapeDtypeStruct((rows, nf2 * heads), bf16),
        ],
        in_specs=[VMEM],
        out_specs=[VMEM] * 2,
        compiler_params=params,
        cost_estimate=cost(1, 1024),
        name="cat",
    )(grads)
    pieces, _ = lax.optimization_barrier((pieces, cat))
    swapped += [lax.ppermute(p, "core", swap) for p in pieces[1:]]

    total = []
    for distances in ((0, 1, 2, 4, 6), (3, 5, 7)):
        parts = [(swapped if e % 2 else pieces)[e // 2] for e in distances]
        args = [cat, feats, ww, vw, fw, *parts, *firsts, *total]
        total = [
            pl.pallas_call(
                partial(columns_kernel, ctx, distances),
                out_shape=jax.ShapeDtypeStruct((rows, dim), bf16),
                in_specs=[VMEM] * (7 + len(parts)) + [ANY] * len(total),
                out_specs=ANY,
                scratch_shapes=[
                    pltpu.VMEM((len(parts), rows, tile), bf16),
                    pltpu.SemaphoreType.DMA((len(parts),)),
                ],
                input_output_aliases={len(args) - 1: 0} if total else {},
                compiler_params=params,
                cost_estimate=cost(1, 1024),
                name="columns",
            )(*args)
        ]
    return (attended, total[0])


def solution(mesh):
    blocks, tp = mesh.devices.shape
    bits = blocks.bit_length() - 1
    assert blocks == 2**bits
    ctx = tuple(f"half{i}" for i in range(bits - 1)) + ("core",)
    split = Mesh(mesh.devices.reshape((2,) * bits + (tp,)), (*ctx, "tp"))
    in_specs = (
        P(ctx, None),
        P(None, "tp"),
        P(None, "tp"),
        P(None, "tp"),
        P(ctx, "tp"),
        P(ctx, "tp"),
    )
    out_specs = (P(ctx, "tp"), P(ctx, None))
    return jax.shard_map(
        partial(per_device, ctx),
        mesh=split,
        in_specs=in_specs,
        out_specs=out_specs,
        check_vma=False,
    )
```

```python
from functools import partial

import jax
import jax.numpy as jnp
from jax import lax
from jax.experimental import pallas as pl
from jax.experimental.pallas import tpu as pltpu
from jax.sharding import Mesh
from jax.sharding import PartitionSpec as P

WINDOW = 1024
LANES = 128
MASKED = -1e30
CHUNKS = 4
f32 = jnp.float32
bf16 = jnp.bfloat16


def nn(a, b):
    return lax.dot_general(a, b, (((1,), (0,)), ((), ())), preferred_element_type=f32)


def nt(a, b):
    return lax.dot_general(a, b, (((1,), (1,)), ((), ())), preferred_element_type=f32)


def partner(me, d, count):
    assert count & (count - 1) == 0
    return jnp.bitwise_xor(me, d)


def wide(view, start, count):
    return jnp.concatenate(
        [view[start : start + count, :], view[start + count : start + 2 * count, :]], axis=1
    )


def put_wide(ref, start, value):
    count = value.shape[0]
    for half in range(value.shape[1] // LANES):
        ref[start + half * count : start + (half + 1) * count, :] = value[
            :, half * LANES : (half + 1) * LANES
        ]


def cum_row(view, start):
    tail = view[start : start + 16, :].astype(f32)
    first = tail[0:1] + tail[2:3] + tail[4:5]
    second = tail[1:2] + tail[3:4] + tail[5:6]
    return jnp.concatenate([first, second], axis=1)


def iotas(rows):
    return (
        lax.broadcasted_iota(jnp.int32, (rows, rows), 0),
        lax.broadcasted_iota(jnp.int32, (rows, rows), 1),
    )


def block_index(ctx):
    place = 0
    for name in ctx:
        place = place * lax.axis_size(name) + lax.axis_index(name)
    return place


def pack(me, ww_ref, vw_ref, fw_ref, out_ref):
    nf2 = fw_ref.shape[0]
    tile = 2 * LANES
    at = pl.multiple_of(me * tile, tile)
    rows = pl.ds(at, tile)
    out_ref[0:tile, :] = ww_ref[rows, 0:LANES]
    out_ref[tile : 2 * tile, :] = ww_ref[rows, LANES:]
    out_ref[2 * tile : 3 * tile, :] = vw_ref[rows, :]
    put_wide(out_ref, 3 * tile, fw_ref[:, rows])


def project_kernel(ctx, packs, tok_hbm, fw_hbm, ww_hbm, vw_hbm, ld_hbm, do_hbm, *rest):
    *sends, keys_ref, query_ref, feat_ref, cum_ref, ww_ref, vw_ref, fw_ref = rest[packs:-5]
    tok_ref, ld_ref, do_ref, sems, small = rest[-5:]
    me = block_index(ctx)
    rows, dim = tok_ref.shape
    dh = do_ref.shape[1]
    nf = fw_ref.shape[0] // 2
    span = dim // CHUNKS
    copies = []
    for c in range(CHUNKS):
        part = pl.ds(c * span, span)
        copies.append([
            pltpu.make_async_copy(tok_hbm.at[:, part], tok_ref.at[:, part], sems.at[c, 0]),
            pltpu.make_async_copy(ww_hbm.at[part, :], ww_ref.at[part, :], sems.at[c, 1]),
            pltpu.make_async_copy(vw_hbm.at[part, :], vw_ref.at[part, :], sems.at[c, 2]),
            pltpu.make_async_copy(fw_hbm.at[:, part], fw_ref.at[:, part], sems.at[c, 3]),
        ])
    others = [
        pltpu.make_async_copy(ld_hbm, ld_ref, small.at[0]),
        pltpu.make_async_copy(do_hbm, do_ref, small.at[1]),
    ]
    for copy in others:
        copy.start()
    for group in copies:
        for at, copy in enumerate(group):
            copy.start(priority=min(at, 1))
    for copy in others:
        copy.wait()
    at_row, at_col = iotas(rows)
    ld_r = ld_ref[...]
    ld_c = jnp.sum(jnp.where(at_row == at_col, ld_r, 0.0), axis=1, keepdims=True)
    cum_r = jnp.sum(jnp.where(at_row <= at_col, ld_c, 0.0), axis=0, keepdims=True)
    cum_ref[...] = jnp.sum(jnp.where(at_col <= at_row, ld_r, 0.0), axis=1, keepdims=True)
    high = cum_r.astype(bf16)
    left = cum_r - high.astype(f32)
    mid = left.astype(bf16)
    low = (left - mid.astype(f32)).astype(bf16)
    pieces = [t[:, h : h + LANES].astype(f32) for t in (high, mid, low) for h in range(0, rows, LANES)]
    tail = jnp.concatenate(pieces + [jnp.zeros((10, LANES), f32)], axis=0).astype(bf16)

    feat = jnp.zeros((rows, 2 * nf), f32)
    main = jnp.zeros((rows, 3 * dh), f32)
    for c in range(CHUNKS):
        for copy in copies[c]:
            copy.wait()
        part = slice(c * span, (c + 1) * span)
        tok = tok_ref[:, part]
        feat += nt(tok, fw_ref[:, part])
        main += nn(tok, jnp.concatenate([ww_ref[part, :], vw_ref[part, :]], axis=1))
    feat = feat.astype(bf16)
    window = main[:, : 2 * dh].astype(bf16)
    values = main[:, 2 * dh :].astype(bf16)
    feat_ref[...] = feat
    small_row, small_col = iotas(2 * nf)
    feat_t = nt((small_row == small_col).astype(bf16), feat).astype(bf16)
    feat_at = 2 * rows
    tail_at = feat_at + 2 * nf

    def put_keys(ref):
        ref[0:rows, :] = window[:, dh:]
        ref[rows : 2 * rows, :] = values
        put_wide(ref, feat_at, feat_t[nf:, :])
        ref[tail_at : tail_at + 16, :] = tail

    def put_query(ref):
        ref[0:rows, :] = window[:, :dh]
        ref[rows : 2 * rows, :] = do_ref[...]
        put_wide(ref, feat_at, feat_t[:nf, :])
        ref[tail_at : tail_at + 16, :] = tail

    put_keys(keys_ref)
    put_query(query_ref)
    for at, ref in enumerate(sends):
        later = jnp.bitwise_xor(me, max(2 * at, 1)) > me
        pl.when(later)(lambda ref=ref: put_keys(ref))
        pl.when(jnp.logical_not(later))(lambda ref=ref: put_query(ref))
    for ref in rest[:packs]:
        pack(me, ww_ref, vw_ref, fw_ref, ref)

def stack_kernel(*refs):
    *parts, out_ref = refs
    for t, ref in enumerate(parts):
        out_ref[t] = ref[...]


def between(totals, low, high):
    at = lax.broadcasted_iota(jnp.int32, totals.shape, 0)
    return jnp.sum(jnp.where((at > low) & (at < high), totals, 0.0), axis=0, keepdims=True)


def over_partners(count, body, carry):
    if count <= 8:
        for d in range(1, count):
            carry = body(d, carry)
        return carry
    return lax.fori_loop(1, count, body, carry)


def query_kernel(ctx, count, recvs, *rest):
    recvs, rest = rest[:recvs], rest[recvs:]
    own_ref, query_ref, feat_ref, cum_ref, *rest = rest
    near_ref, p_ref, cums_ref = rest[-3:]
    me = block_index(ctx)
    if len(rest) > 6:
        *weights, pack_ref = rest[:3] + rest[6:7]
        rest = rest[3:]
        for n in range(pack_ref.shape[0]):
            pack(jnp.bitwise_xor(me, 2 * n), *weights, pack_ref.at[n])
    att_ref, stat_ref, sheet_ref = rest[:3]

    def recv(d):
        return recvs[d - 1] if len(recvs) > 1 else recvs[0].at[d - 1]

    me = block_index(ctx)
    rows, dh = att_ref.shape
    nf = feat_ref.shape[1] // 2
    back = WINDOW // rows
    feat_at = 2 * rows
    tail_at = feat_at + 2 * nf
    scale = dh ** (-0.5)
    feat_scale = nf ** (-0.5)
    wq = query_ref[0:rows, :]
    do = query_ref[rows : 2 * rows, :]
    q = feat_ref[:, :nf]
    at_row, at_col = iotas(rows)
    own_cum = cum_row(own_ref, tail_at)
    cums_ref[pl.ds(me, 1), :] = own_cum
    near_ref[me] = own_ref[0 : 2 * rows, :]

    def gather(d, carry):
        j = partner(me, d, count)
        view = recv(d)
        near_ref[j] = view[0 : 2 * rows, :]
        cums_ref[pl.ds(j, 1), :] = cum_row(view, tail_at)
        return carry

    over_partners(count, gather, 0)

    def near(w):
        return near_ref.at[jnp.maximum(me - back + w, 0)]

    top = jnp.full((rows, LANES), MASKED, f32)
    for w in range(back + 1):
        keys = own_ref[0:rows, :] if w == back else near(w)[0:rows, :]
        s = nt(wq, keys) * scale
        if w == back:
            s = jnp.where(at_col <= at_row, s, MASKED)
        elif w == 0:
            s = jnp.where((at_col > at_row) & (me >= back), s, MASKED)
        else:
            s = jnp.where(me >= back - w, s, MASKED)
        p_ref[w] = s
        for h in range(0, rows, LANES):
            top = jnp.maximum(top, s[:, h : h + LANES])
    top = jnp.max(top, axis=1, keepdims=True)
    total = jnp.zeros((rows, LANES), f32)
    out = jnp.zeros((rows, dh), f32)
    for w in range(back + 1):
        p = jnp.exp(p_ref[w] - top)
        for h in range(0, rows, LANES):
            total += p[:, h : h + LANES]
        vals = own_ref[rows : 2 * rows, :] if w == back else near(w)[rows : 2 * rows, :]
        out += nn(p.astype(bf16), vals)
    total = jnp.sum(total, axis=1, keepdims=True)
    windowed = out * (1.0 / total)

    cum_c = cum_ref[...]
    growth = jnp.exp(cum_c)
    totals = cums_ref[:, rows - 1 : rows]

    def forward(d, carry):
        num, den = carry
        j = partner(me, d, count)
        view = recv(d)
        gap = between(totals, j - 1, me)
        es = jnp.where(j < me, jnp.exp(jnp.minimum(gap - cums_ref[pl.ds(j, 1), :], 0.0)), 0.0)
        x = nn(q, wide(view, feat_at, nf)) * feat_scale
        weight = (1.0 + x + 0.5 * x * x) * es
        for h in range(0, rows, LANES):
            den += weight[:, h : h + LANES]
        num += nn(weight.astype(bf16), view[rows : 2 * rows, :])
        return num, den

    num, den = over_partners(
        count, forward, (jnp.zeros((rows, dh), f32), jnp.zeros((rows, LANES), f32))
    )
    x = nn(q, wide(own_ref, feat_at, nf)) * feat_scale
    e = jnp.where(at_col <= at_row, jnp.exp(jnp.minimum(cum_c - own_cum, 0.0)), 0.0)
    weight = (1.0 + x + 0.5 * x * x) * e
    num = num * growth + nn(weight.astype(bf16), own_ref[rows : 2 * rows, :])
    den = den * growth
    for h in range(0, rows, LANES):
        den += weight[:, h : h + LANES]
    rden = 1.0 / jnp.sum(den, axis=1, keepdims=True)
    linear = num * rden
    att_ref[...] = (linear + windowed).astype(bf16)
    do_f = do.astype(f32)
    delta_w = jnp.sum(do_f * windowed, axis=1, keepdims=True)
    delta_l = jnp.sum(do_f * linear, axis=1, keepdims=True)
    lse = top + jnp.log(total)
    lane = lax.broadcasted_iota(jnp.int32, (rows, LANES), 1)
    sheet = jnp.where(lane == 0, lse, 0.0)
    sheet = jnp.where(lane == 1, delta_w, sheet)
    sheet = jnp.where(lane == 2, rden, sheet)
    sheet = jnp.where(lane == 3, delta_l, sheet)
    sheet = jnp.where(lane == 4, cum_c, sheet)
    sheet_ref[...] = sheet
    stat_ref[...] = jnp.transpose(sheet)[0:8, :]


def gradient_kernel(ctx, count, recvs, stats, *rest):
    recvs, rest = rest[:recvs], rest[recvs:]
    stats, rest = rest[:stats], rest[stats:]
    own_ref, query_ref, feat_ref, sheet_ref, *rest, total_ref = rest

    def recv(d):
        return recvs[d - 1] if len(recvs) > 1 else recvs[0].at[d - 1]

    me = block_index(ctx)
    rows = feat_ref.shape[0]
    dh = LANES
    nf = feat_ref.shape[1] // 2
    feat_at = 2 * rows
    scale = dh ** (-0.5)
    feat_scale = nf ** (-0.5)
    at_row, at_col = iotas(rows)
    apart = at_row - at_col
    wq, wk = query_ref[0:rows, :], own_ref[0:rows, :]
    do, v = query_ref[rows : 2 * rows, :], own_ref[rows : 2 * rows, :]
    q, k = feat_ref[:, :nf], feat_ref[:, nf:]
    lse_c, dw_c = sheet_ref[:, 0:1], sheet_ref[:, 1:2]
    rden_c, dl_c, cum_c = sheet_ref[:, 2:3], sheet_ref[:, 3:4], sheet_ref[:, 4:5]
    def stat(d):
        if len(stats) == 1:
            return stats[0].at[pl.ds(pl.multiple_of(8 * d, 8), 8)]
        at = d.bit_length()
        return stats[at].at[pl.ds(8 * (d - (1 << at >> 1)), 8)]

    mine_ref = stat(0)
    own_cum = mine_ref[4:5, :]
    total_ref[pl.ds(me, 1), :] = own_cum[:, rows - LANES :]

    def place(d, carry):
        total_ref[pl.ds(partner(me, d, count), 1), :] = stat(d)[4:5, rows - LANES :]
        return carry

    over_partners(count, place, 0)
    totals = total_ref[:, LANES - 1 :]
    growth_c = jnp.exp(cum_c) * rden_c
    tail_c = jnp.exp(own_cum[:, rows - 1 : rows] - cum_c)

    def pick(flag, a, b):
        return jnp.where(flag, a, b)

    s = nt(wq, wk) * scale
    causal = at_col <= at_row
    p = jnp.where(causal, jnp.exp(s - lse_c), 0.0)
    dp = nt(do, v)
    dwq = nn((p * (dp - dw_c)).astype(bf16), wk)
    x = nn(q, wide(own_ref, feat_at, nf)) * feat_scale
    e = jnp.where(causal, jnp.exp(jnp.minimum(cum_c - own_cum, 0.0)), 0.0) * rden_c
    dx = (dp - dl_c) * e * (1.0 + x)
    dqt = nt(wide(own_ref, feat_at, nf), dx.astype(bf16))

    s = nt(wk, wq) * scale
    causal = at_row <= at_col
    p = jnp.where(causal, jnp.exp(s - mine_ref[0:1, :]), 0.0)
    dp = nt(v, do)
    dwk = nn((p * (dp - mine_ref[1:2, :])).astype(bf16), wq)
    x = nn(k, wide(query_ref, feat_at, nf)) * feat_scale
    e = jnp.where(causal, jnp.exp(jnp.minimum(own_cum - cum_c, 0.0)), 0.0) * mine_ref[2:3, :]
    dx = (dp - mine_ref[3:4, :]) * e * (1.0 + x)
    dkt = nt(wide(query_ref, feat_at, nf), dx.astype(bf16))
    dv = nn((p + (1.0 + x + 0.5 * x * x) * e).astype(bf16), do)

    def step(d, carry):
        dwq, dqt, dwk, dkt, dv = carry
        j = partner(me, d, count)
        view = recv(d)
        mine = j < me
        sign = pick(mine, 1, -1)
        limit = WINDOW - jnp.abs(me - j) * rows
        rows_w = pick(mine, wq, wk)
        rows_v = pick(mine, do, v)
        rows_f = pick(mine, q, k)
        other_w = view[0:rows, :]
        other_v = view[rows : 2 * rows, :]
        other_f = wide(view, feat_at, nf)
        st = stat(d)
        zero = jnp.zeros((1, rows), f32)
        cum = st[4:5, :]
        gap = between(totals, jnp.minimum(me, j), jnp.maximum(me, j))
        e_r = jnp.exp(jnp.minimum(gap + pick(mine, cum[:, rows - 1 : rows] - cum, cum), 0.0))
        e_r = e_r * pick(mine, 1.0, st[2:3, :])
        e_c = pick(mine, growth_c, tail_c)

        s = nt(rows_w, other_w) * scale
        p = jnp.exp(s - pick(mine, lse_c, 0.0) - pick(mine, zero, st[0:1, :]))
        p = jnp.where(apart * sign < limit, p, 0.0)
        dp = nt(rows_v, other_v)
        ds = p * (dp - pick(mine, dw_c, 0.0) - pick(mine, zero, st[1:2, :]))
        more_w = nn(ds.astype(bf16), other_w)
        x = nn(rows_f, other_f) * feat_scale
        e = e_r * e_c
        dx = (dp - pick(mine, dl_c, 0.0) - pick(mine, zero, st[3:4, :])) * e * (1.0 + x)
        more_f = nt(other_f, dx.astype(bf16))
        more_v = nn((p + (1.0 + x + 0.5 * x * x) * e).astype(bf16), other_v)
        dwq = dwq + pick(mine, more_w, 0.0)
        dwk = dwk + pick(mine, 0.0, more_w)
        dqt = dqt + pick(mine, more_f, 0.0)
        dkt = dkt + pick(mine, 0.0, more_f)
        dv = dv + pick(mine, 0.0, more_v)
        return dwq, dqt, dwk, dkt, dv

    dwq, dqt, dwk, dkt, dv = over_partners(count, step, (dwq, dqt, dwk, dkt, dv))
    dwq, dwk = (dwq * scale).astype(bf16), (dwk * scale).astype(bf16)
    dv = dv.astype(bf16)
    dft = (jnp.concatenate([dqt, dkt], axis=0) * feat_scale).astype(bf16)
    (grad_ref,) = rest
    grad_ref[0:rows, :] = dwq
    grad_ref[rows : 2 * rows, :] = dwk
    grad_ref[2 * rows : 3 * rows, :] = dv
    put_wide(grad_ref, 3 * rows, dft)


def gather_rows(grad_ref, order, cat_ref, feat_ref):
    rows = cat_ref.shape[0]
    nf2 = feat_ref.shape[1] // len(order)
    for at, h in enumerate(order):
        for part in range(3):
            lane = (3 * at + part) * LANES
            cat_ref[:, lane : lane + LANES] = grad_ref[h, part * rows : (part + 1) * rows, :]
    dft = jnp.concatenate([wide(grad_ref.at[h], 3 * rows, nf2) for h in order], axis=0)
    feat_ref[...] = jnp.transpose(dft.astype(f32)).astype(bf16)


def cat_kernel(grad_ref, cat_ref, feat_ref):
    heads = grad_ref.shape[0]
    head = lax.axis_index("tp")
    order = [head] + [jnp.bitwise_xor(head, t) for t in range(1, heads)]
    gather_rows(grad_ref, order, cat_ref, feat_ref)


def columns_kernel(ctx, distances, cat_ref, feat_ref, ww_ref, vw_ref, fw_ref, *rest):
    pieces, firsts = rest[: len(distances)], rest[len(distances) : len(distances) + 2]
    out_ref, tile_ref, sems = rest[-3:]
    nf2 = fw_ref.shape[0]
    heads = feat_ref.shape[1] // nf2
    tile = 2 * LANES
    me = block_index(ctx)
    copies = []
    for n, (e, ref) in enumerate(zip(distances, pieces)):
        part = pl.ds(pl.multiple_of(jnp.bitwise_xor(me, e) * tile, tile), tile)
        views = [firsts[e % 2].at[e // 2]] + [ref.at[t] for t in range(heads - 2)]
        main = [ww_ref[part, :], vw_ref[part, :]]
        main += [v[m * tile : (m + 1) * tile, :] for v in views for m in range(3)]
        feats = [fw_ref[:, part]] + [wide(v, 3 * tile, nf2) for v in views]
        total = nt(cat_ref[...], jnp.concatenate(main, axis=1))
        total += nn(feat_ref[...], jnp.concatenate(feats, axis=0))
        tile_ref[n] = total.astype(bf16)
        copies.append(pltpu.make_async_copy(tile_ref.at[n], out_ref.at[:, part], sems.at[n]))
        copies[-1].start()
    for copy in copies:
        copy.wait()


def merge_kernel(grad_ref, weight_ref, out_ref, cat_ref, feat_ref):
    heads = grad_ref.shape[0]
    tile = out_ref.shape[1]
    lanes = 3 * LANES
    nf2 = feat_ref.shape[1] // heads

    @pl.when(pl.program_id(0) == 0)
    def _():
        gather_rows(grad_ref, range(heads), cat_ref, feat_ref)

    views = [weight_ref.at[h] for h in range(heads)]
    main = jnp.concatenate([v[:, 0:lanes] for v in views], axis=1)
    feats = jnp.concatenate([v[:, lanes:] for v in views], axis=1)
    out_ref[...] = (nt(cat_ref[...], main) + nt(feat_ref[...], feats)).astype(bf16)


VMEM = pl.BlockSpec(memory_space=pltpu.VMEM)
HBM = pl.BlockSpec(memory_space=pltpu.HBM)
ANY = pl.BlockSpec(memory_space=pl.ANY)
params = pltpu.CompilerParams(vmem_limit_bytes=32 * 1024 * 1024)


def in_hbm(*arrays):
    return [pltpu.with_memory_space_constraint(a, pltpu.HBM) for a in arrays]


def cost(flops, nbytes, exps=0):
    return pl.CostEstimate(flops=flops, bytes_accessed=nbytes, transcendentals=exps)


def merge(grads, weights, rows, dim):
    heads, _, columns = weights.shape
    tile = 2 * LANES
    return pl.pallas_call(
        merge_kernel,
        out_shape=jax.ShapeDtypeStruct((rows, dim), bf16),
        grid=(dim // tile,),
        in_specs=[
            pl.BlockSpec(grads.shape, lambda i: (0, 0, 0)),
            pl.BlockSpec((heads, tile, columns), lambda i: (0, i, 0)),
        ],
        out_specs=pl.BlockSpec((rows, tile), lambda i: (0, i)),
        scratch_shapes=[
            pltpu.VMEM((rows, 3 * LANES * heads), bf16),
            pltpu.VMEM((rows, (columns - 3 * LANES) * heads), bf16),
        ],
        compiler_params=params,
        cost_estimate=cost(2 * rows * dim * heads * columns, heads * dim * columns * 2),
        name="head_sum",
    )(grads, weights)


def per_device(ctx, tokens, feature_weight, window_weight, value_weight, log_decay, out_grad):
    rows, dim = tokens.shape
    nf2 = feature_weight.shape[1]
    nf = nf2 // 2
    dh = value_weight.shape[1]
    columns = 3 * dh + nf2
    chips, count, heads = lax.axis_size(ctx[:-1]), lax.axis_size(ctx), lax.axis_size("tp")
    fw_t = feature_weight.T
    tile = 2 * LANES
    spread = heads == 4 and count * tile == dim and count == 8
    packs = []
    if spread:
        packs = [jax.ShapeDtypeStruct((columns * tile // LANES, LANES), bf16)]

    payload = 2 * rows + 2 * nf + 16
    block = jax.ShapeDtypeStruct((payload, LANES), bf16)
    outs = pl.pallas_call(
        partial(project_kernel, ctx, len(packs)),
        out_shape=packs
        + [block] * (chips + 2)
        + [
            jax.ShapeDtypeStruct((rows, nf2), bf16),
            jax.ShapeDtypeStruct((rows, 1), f32),
            jax.ShapeDtypeStruct((dim, 2 * dh), bf16),
            jax.ShapeDtypeStruct((dim, dh), bf16),
            jax.ShapeDtypeStruct((nf2, dim), bf16),
        ],
        in_specs=[HBM] * 6,
        out_specs=[VMEM] * (len(packs) + chips + 7),
        scratch_shapes=[
            pltpu.VMEM((rows, dim), bf16),
            pltpu.VMEM((1, rows), f32),
            pltpu.VMEM((rows, dh), bf16),
            pltpu.SemaphoreType.DMA((CHUNKS, 4)),
            pltpu.SemaphoreType.DMA((2,)),
        ],
        compiler_params=params,
        cost_estimate=cost(1, 1024),
        name="project",
    )(*in_hbm(tokens, fw_t, window_weight, value_weight, log_decay.T, out_grad))
    *sends, own, query, feat, cum, ww, vw, fw = outs[len(packs) :]

    swap = [(0, 1), (1, 0)]
    recv = {}
    for d in range(1, chips):
        recv[2 * d] = lax.ppermute(sends[d], ctx[:-1], [(i, i ^ d) for i in range(chips)])
    recv[1] = lax.ppermute(sends[0], "core", swap)
    if spread:
        across = lax.ppermute(outs[0], "tp", [(z, z ^ 2) for z in range(heads)])
    for d in range(1, chips):
        if spread and d == chips - 1:
            across, recv[2 * d] = lax.optimization_barrier((across, recv[2 * d]))
        recv[2 * d + 1] = lax.ppermute(recv[2 * d], "core", swap)
    recv = [recv[d] for d in range(1, count)]
    if count > 8:
        recv = [jnp.stack(recv)]

    first_pack, first_args = [], []
    if spread:
        across, recv = lax.optimization_barrier((across, recv))
        near = [across, lax.ppermute(across, "tp", [(z, z ^ 1) for z in range(heads)])]
        first_pack = [jax.ShapeDtypeStruct((chips, *packs[0].shape), bf16)]
        first_args = [ww, vw, fw]

    attended, stat, sheet, *first = pl.pallas_call(
        lambda *refs: query_kernel(ctx, count, len(recv), *refs),
        out_shape=[
            jax.ShapeDtypeStruct((rows, dh), bf16),
            jax.ShapeDtypeStruct((8, rows), f32),
            jax.ShapeDtypeStruct((rows, LANES), f32),
            *first_pack,
        ],
        in_specs=[VMEM] * (len(recv) + 4 + len(first_args)),
        out_specs=[VMEM] * (3 + len(first_pack)),
        scratch_shapes=[
            pltpu.VMEM((count, 2 * rows, dh), bf16),
            pltpu.VMEM((WINDOW // rows + 1, rows, rows), f32),
            pltpu.VMEM((count, rows), f32),
        ],
        compiler_params=params,
        cost_estimate=cost(1, 1024),
        name="query_side",
    )(*recv, own, query, feat, cum, *first_args)
    if spread:
        near, stat, first = lax.optimization_barrier((near, stat, first))
    stats = [stat]
    for name in reversed(ctx):
        held = stats[0] if len(stats) == 1 else jnp.concatenate(stats, axis=0)
        stats.append(lax.ppermute(held, name, swap))
    if count > 8:
        stats = [jnp.concatenate(stats, axis=0)]

    if spread:
        first = lax.ppermute(first[0], "tp", [(z, z ^ 1) for z in range(heads)])
        near, stats = lax.optimization_barrier((near, stats))
        pieces = [
            pl.pallas_call(
                stack_kernel,
                out_shape=jax.ShapeDtypeStruct((heads - 2, *packs[0].shape), bf16),
                in_specs=[VMEM] * (heads - 2),
                out_specs=VMEM,
                compiler_params=params,
                cost_estimate=cost(1, 1024),
                name="stack",
            )(*near)
        ]
        for d in range(1, chips):
            pieces.append(
                lax.ppermute(pieces[0], ctx[:-1], [(i, i ^ d) for i in range(chips)])
            )
        pieces[0], sheet = lax.optimization_barrier((pieces[0], sheet))

    grads = pl.pallas_call(
        lambda *refs: gradient_kernel(ctx, count, len(recv), len(stats), *refs),
        out_shape=jax.ShapeDtypeStruct((3 * rows + nf2 * rows // LANES, LANES), bf16),
        in_specs=[VMEM] * (len(recv) + len(stats) + 4),
        out_specs=VMEM,
        scratch_shapes=[pltpu.VMEM((count, LANES), f32)],
        compiler_params=params,
        cost_estimate=cost(1, 1024),
        name="gradients",
    )(*recv, *stats, own, query, feat, sheet)
    if not spread:
        weights = jnp.concatenate([window_weight, value_weight, feature_weight], axis=1)
        weights = lax.all_gather(weights, "tp")
        return (attended, merge(lax.all_gather(grads, "tp"), weights, rows, dim))

    first, grads = lax.optimization_barrier((first, grads))
    swapped = [lax.ppermute(pieces[0], "core", swap)]
    firsts = [first, lax.ppermute(first, "core", swap)]
    grads = lax.all_gather(grads, "tp")
    cat, feats = pl.pallas_call(
        cat_kernel,
        out_shape=[
            jax.ShapeDtypeStruct((rows, 3 * LANES * heads), bf16),
            jax.ShapeDtypeStruct((rows, nf2 * heads), bf16),
        ],
        in_specs=[VMEM],
        out_specs=[VMEM] * 2,
        compiler_params=params,
        cost_estimate=cost(1, 1024),
        name="cat",
    )(grads)
    pieces, _ = lax.optimization_barrier((pieces, cat))
    swapped += [lax.ppermute(p, "core", swap) for p in pieces[1:]]

    total = []
    for distances in ((0, 1, 2, 4, 6), (3, 5, 7)):
        parts = [(swapped if e % 2 else pieces)[e // 2] for e in distances]
        args = [cat, feats, ww, vw, fw, *parts, *firsts, *total]
        total = [
            pl.pallas_call(
                partial(columns_kernel, ctx, distances),
                out_shape=jax.ShapeDtypeStruct((rows, dim), bf16),
                in_specs=[VMEM] * (7 + len(parts)) + [ANY] * len(total),
                out_specs=ANY,
                scratch_shapes=[
                    pltpu.VMEM((len(parts), rows, tile), bf16),
                    pltpu.SemaphoreType.DMA((len(parts),)),
                ],
                input_output_aliases={len(args) - 1: 0} if total else {},
                compiler_params=params,
                cost_estimate=cost(1, 1024),
                name="columns",
            )(*args)
        ]
    return (attended, total[0])


def solution(mesh):
    blocks, tp = mesh.devices.shape
    bits = blocks.bit_length() - 1
    assert blocks == 2**bits
    ctx = tuple(f"half{i}" for i in range(bits - 1)) + ("core",)
    split = Mesh(mesh.devices.reshape((2,) * bits + (tp,)), (*ctx, "tp"))
    in_specs = (
        P(ctx, None),
        P(None, "tp"),
        P(None, "tp"),
        P(None, "tp"),
        P(ctx, "tp"),
        P(ctx, "tp"),
    )
    out_specs = (P(ctx, "tp"), P(ctx, None))
    return jax.shard_map(
        partial(per_device, ctx),
        mesh=split,
        in_specs=in_specs,
        out_specs=out_specs,
        check_vma=False,
    )
```

```python
from functools import partial

import jax
import jax.numpy as jnp
from jax import lax
from jax.experimental import pallas as pl
from jax.experimental.pallas import tpu as pltpu
from jax.sharding import Mesh
from jax.sharding import PartitionSpec as P

WINDOW = 1024
LANES = 128
MASKED = -1e30
CHUNKS = 4
f32 = jnp.float32
bf16 = jnp.bfloat16


def nn(a, b):
    return lax.dot_general(a, b, (((1,), (0,)), ((), ())), preferred_element_type=f32)


def nt(a, b):
    return lax.dot_general(a, b, (((1,), (1,)), ((), ())), preferred_element_type=f32)


def partner(me, d, count):
    assert count & (count - 1) == 0
    return jnp.bitwise_xor(me, d)


def wide(view, start, count):
    return jnp.concatenate(
        [view[start : start + count, :], view[start + count : start + 2 * count, :]], axis=1
    )


def put_wide(ref, start, value):
    count = value.shape[0]
    for half in range(value.shape[1] // LANES):
        ref[start + half * count : start + (half + 1) * count, :] = value[
            :, half * LANES : (half + 1) * LANES
        ]


def cum_row(view, start):
    tail = view[start : start + 16, :].astype(f32)
    first = tail[0:1] + tail[2:3] + tail[4:5]
    second = tail[1:2] + tail[3:4] + tail[5:6]
    return jnp.concatenate([first, second], axis=1)


def iotas(rows):
    return (
        lax.broadcasted_iota(jnp.int32, (rows, rows), 0),
        lax.broadcasted_iota(jnp.int32, (rows, rows), 1),
    )


def block_index(ctx):
    place = 0
    for name in ctx:
        place = place * lax.axis_size(name) + lax.axis_index(name)
    return place


def pack(me, ww_ref, vw_ref, fw_ref, out_ref):
    nf2 = fw_ref.shape[0]
    tile = 2 * LANES
    at = pl.multiple_of(me * tile, tile)
    rows = pl.ds(at, tile)
    out_ref[0:tile, :] = ww_ref[rows, 0:LANES]
    out_ref[tile : 2 * tile, :] = ww_ref[rows, LANES:]
    out_ref[2 * tile : 3 * tile, :] = vw_ref[rows, :]
    put_wide(out_ref, 3 * tile, fw_ref[:, rows])


def project_kernel(ctx, packs, tok_hbm, fw_hbm, ww_hbm, vw_hbm, ld_hbm, do_hbm, *rest):
    *sends, keys_ref, query_ref, feat_ref, cum_ref, ww_ref, vw_ref, fw_ref = rest[packs:-5]
    tok_ref, ld_ref, do_ref, sems, small = rest[-5:]
    me = block_index(ctx)
    rows, dim = tok_ref.shape
    dh = do_ref.shape[1]
    nf = fw_ref.shape[0] // 2
    span = dim // CHUNKS
    copies = []
    for c in range(CHUNKS):
        part = pl.ds(c * span, span)
        copies.append([
            pltpu.make_async_copy(tok_hbm.at[:, part], tok_ref.at[:, part], sems.at[c, 0]),
            pltpu.make_async_copy(ww_hbm.at[part, :], ww_ref.at[part, :], sems.at[c, 1]),
            pltpu.make_async_copy(vw_hbm.at[part, :], vw_ref.at[part, :], sems.at[c, 2]),
            pltpu.make_async_copy(fw_hbm.at[:, part], fw_ref.at[:, part], sems.at[c, 3]),
        ])
    others = [
        pltpu.make_async_copy(ld_hbm, ld_ref, small.at[0]),
        pltpu.make_async_copy(do_hbm, do_ref, small.at[1]),
    ]
    for copy in others:
        copy.start()
    for group in copies:
        for at, copy in enumerate(group):
            copy.start(priority=min(at, 1))
    for copy in others:
        copy.wait()
    at_row, at_col = iotas(rows)
    ld_r = ld_ref[...]
    ld_c = jnp.sum(jnp.where(at_row == at_col, ld_r, 0.0), axis=1, keepdims=True)
    cum_r = jnp.sum(jnp.where(at_row <= at_col, ld_c, 0.0), axis=0, keepdims=True)
    cum_ref[...] = jnp.sum(jnp.where(at_col <= at_row, ld_r, 0.0), axis=1, keepdims=True)
    high = cum_r.astype(bf16)
    left = cum_r - high.astype(f32)
    mid = left.astype(bf16)
    low = (left - mid.astype(f32)).astype(bf16)
    pieces = [t[:, h : h + LANES].astype(f32) for t in (high, mid, low) for h in range(0, rows, LANES)]
    tail = jnp.concatenate(pieces + [jnp.zeros((10, LANES), f32)], axis=0).astype(bf16)

    feat = jnp.zeros((rows, 2 * nf), f32)
    main = jnp.zeros((rows, 3 * dh), f32)
    for c in range(CHUNKS):
        for copy in copies[c]:
            copy.wait()
        part = slice(c * span, (c + 1) * span)
        tok = tok_ref[:, part]
        feat += nt(tok, fw_ref[:, part])
        main += nn(tok, jnp.concatenate([ww_ref[part, :], vw_ref[part, :]], axis=1))
    feat = feat.astype(bf16)
    window = main[:, : 2 * dh].astype(bf16)
    values = main[:, 2 * dh :].astype(bf16)
    feat_ref[...] = feat
    small_row, small_col = iotas(2 * nf)
    feat_t = nt((small_row == small_col).astype(bf16), feat).astype(bf16)
    feat_at = 2 * rows
    tail_at = feat_at + 2 * nf

    def put_keys(ref):
        ref[0:rows, :] = window[:, dh:]
        ref[rows : 2 * rows, :] = values
        put_wide(ref, feat_at, feat_t[nf:, :])
        ref[tail_at : tail_at + 16, :] = tail

    def put_query(ref):
        ref[0:rows, :] = window[:, :dh]
        ref[rows : 2 * rows, :] = do_ref[...]
        put_wide(ref, feat_at, feat_t[:nf, :])
        ref[tail_at : tail_at + 16, :] = tail

    put_keys(keys_ref)
    put_query(query_ref)
    for at, ref in enumerate(sends):
        later = jnp.bitwise_xor(me, max(2 * at, 1)) > me
        pl.when(later)(lambda ref=ref: put_keys(ref))
        pl.when(jnp.logical_not(later))(lambda ref=ref: put_query(ref))
    if packs:
        own_pack, first_pack = rest[:packs]
        pack(me, ww_ref, vw_ref, fw_ref, own_pack)
        for n in range(first_pack.shape[0]):
            pack(jnp.bitwise_xor(me, 2 * n), ww_ref, vw_ref, fw_ref, first_pack.at[n])

def stack_kernel(*refs):
    *parts, out_ref = refs
    for t, ref in enumerate(parts):
        out_ref[t] = ref[...]


def between(totals, low, high):
    at = lax.broadcasted_iota(jnp.int32, totals.shape, 0)
    return jnp.sum(jnp.where((at > low) & (at < high), totals, 0.0), axis=0, keepdims=True)


def over_partners(count, body, carry):
    if count <= 8:
        for d in range(1, count):
            carry = body(d, carry)
        return carry
    return lax.fori_loop(1, count, body, carry)


def query_kernel(ctx, count, recvs, *rest):
    recvs, rest = rest[:recvs], rest[recvs:]
    own_ref, query_ref, feat_ref, cum_ref, *rest = rest
    near_ref, p_ref, cums_ref = rest[-3:]
    att_ref, stat_ref, sheet_ref = rest[:3]

    def recv(d):
        return recvs[d - 1] if len(recvs) > 1 else recvs[0].at[d - 1]

    me = block_index(ctx)
    rows, dh = att_ref.shape
    nf = feat_ref.shape[1] // 2
    back = WINDOW // rows
    feat_at = 2 * rows
    tail_at = feat_at + 2 * nf
    scale = dh ** (-0.5)
    feat_scale = nf ** (-0.5)
    wq = query_ref[0:rows, :]
    do = query_ref[rows : 2 * rows, :]
    q = feat_ref[:, :nf]
    at_row, at_col = iotas(rows)
    own_cum = cum_row(own_ref, tail_at)
    cums_ref[pl.ds(me, 1), :] = own_cum
    near_ref[me] = own_ref[0 : 2 * rows, :]

    def gather(d, carry):
        j = partner(me, d, count)
        view = recv(d)
        near_ref[j] = view[0 : 2 * rows, :]
        cums_ref[pl.ds(j, 1), :] = cum_row(view, tail_at)
        return carry

    over_partners(count, gather, 0)

    def near(w):
        return near_ref.at[jnp.maximum(me - back + w, 0)]

    top = jnp.full((rows, LANES), MASKED, f32)
    for w in range(back + 1):
        keys = own_ref[0:rows, :] if w == back else near(w)[0:rows, :]
        s = nt(wq, keys) * scale
        if w == back:
            s = jnp.where(at_col <= at_row, s, MASKED)
        elif w == 0:
            s = jnp.where((at_col > at_row) & (me >= back), s, MASKED)
        else:
            s = jnp.where(me >= back - w, s, MASKED)
        p_ref[w] = s
        for h in range(0, rows, LANES):
            top = jnp.maximum(top, s[:, h : h + LANES])
    top = jnp.max(top, axis=1, keepdims=True)
    total = jnp.zeros((rows, LANES), f32)
    out = jnp.zeros((rows, dh), f32)
    for w in range(back + 1):
        p = jnp.exp(p_ref[w] - top)
        for h in range(0, rows, LANES):
            total += p[:, h : h + LANES]
        vals = own_ref[rows : 2 * rows, :] if w == back else near(w)[rows : 2 * rows, :]
        out += nn(p.astype(bf16), vals)
    total = jnp.sum(total, axis=1, keepdims=True)
    windowed = out * (1.0 / total)

    cum_c = cum_ref[...]
    growth = jnp.exp(cum_c)
    totals = cums_ref[:, rows - 1 : rows]

    def forward(d, carry):
        num, den = carry
        j = partner(me, d, count)
        view = recv(d)
        gap = between(totals, j - 1, me)
        es = jnp.where(j < me, jnp.exp(jnp.minimum(gap - cums_ref[pl.ds(j, 1), :], 0.0)), 0.0)
        x = nn(q, wide(view, feat_at, nf)) * feat_scale
        weight = (1.0 + x + 0.5 * x * x) * es
        for h in range(0, rows, LANES):
            den += weight[:, h : h + LANES]
        num += nn(weight.astype(bf16), view[rows : 2 * rows, :])
        return num, den

    num, den = over_partners(
        count, forward, (jnp.zeros((rows, dh), f32), jnp.zeros((rows, LANES), f32))
    )
    x = nn(q, wide(own_ref, feat_at, nf)) * feat_scale
    e = jnp.where(at_col <= at_row, jnp.exp(jnp.minimum(cum_c - own_cum, 0.0)), 0.0)
    weight = (1.0 + x + 0.5 * x * x) * e
    num = num * growth + nn(weight.astype(bf16), own_ref[rows : 2 * rows, :])
    den = den * growth
    for h in range(0, rows, LANES):
        den += weight[:, h : h + LANES]
    rden = 1.0 / jnp.sum(den, axis=1, keepdims=True)
    linear = num * rden
    att_ref[...] = (linear + windowed).astype(bf16)
    do_f = do.astype(f32)
    delta_w = jnp.sum(do_f * windowed, axis=1, keepdims=True)
    delta_l = jnp.sum(do_f * linear, axis=1, keepdims=True)
    lse = top + jnp.log(total)
    lane = lax.broadcasted_iota(jnp.int32, (rows, LANES), 1)
    sheet = jnp.where(lane == 0, lse, 0.0)
    sheet = jnp.where(lane == 1, delta_w, sheet)
    sheet = jnp.where(lane == 2, rden, sheet)
    sheet = jnp.where(lane == 3, delta_l, sheet)
    sheet = jnp.where(lane == 4, cum_c, sheet)
    sheet_ref[...] = sheet
    stat_ref[...] = jnp.transpose(sheet)[0:8, :]


def gradient_kernel(ctx, count, recvs, stats, *rest):
    recvs, rest = rest[:recvs], rest[recvs:]
    stats, rest = rest[:stats], rest[stats:]
    own_ref, query_ref, feat_ref, sheet_ref, *rest, total_ref = rest

    def recv(d):
        return recvs[d - 1] if len(recvs) > 1 else recvs[0].at[d - 1]

    me = block_index(ctx)
    rows = feat_ref.shape[0]
    dh = LANES
    nf = feat_ref.shape[1] // 2
    feat_at = 2 * rows
    scale = dh ** (-0.5)
    feat_scale = nf ** (-0.5)
    at_row, at_col = iotas(rows)
    apart = at_row - at_col
    wq, wk = query_ref[0:rows, :], own_ref[0:rows, :]
    do, v = query_ref[rows : 2 * rows, :], own_ref[rows : 2 * rows, :]
    q, k = feat_ref[:, :nf], feat_ref[:, nf:]
    lse_c, dw_c = sheet_ref[:, 0:1], sheet_ref[:, 1:2]
    rden_c, dl_c, cum_c = sheet_ref[:, 2:3], sheet_ref[:, 3:4], sheet_ref[:, 4:5]
    def stat(d):
        if len(stats) == 1:
            return stats[0].at[pl.ds(pl.multiple_of(8 * d, 8), 8)]
        at = d.bit_length()
        return stats[at].at[pl.ds(8 * (d - (1 << at >> 1)), 8)]

    mine_ref = stat(0)
    own_cum = mine_ref[4:5, :]
    total_ref[pl.ds(me, 1), :] = own_cum[:, rows - LANES :]

    def place(d, carry):
        total_ref[pl.ds(partner(me, d, count), 1), :] = stat(d)[4:5, rows - LANES :]
        return carry

    over_partners(count, place, 0)
    totals = total_ref[:, LANES - 1 :]
    growth_c = jnp.exp(cum_c) * rden_c
    tail_c = jnp.exp(own_cum[:, rows - 1 : rows] - cum_c)

    def pick(flag, a, b):
        return jnp.where(flag, a, b)

    s = nt(wq, wk) * scale
    causal = at_col <= at_row
    p = jnp.where(causal, jnp.exp(s - lse_c), 0.0)
    dp = nt(do, v)
    dwq = nn((p * (dp - dw_c)).astype(bf16), wk)
    x = nn(q, wide(own_ref, feat_at, nf)) * feat_scale
    e = jnp.where(causal, jnp.exp(jnp.minimum(cum_c - own_cum, 0.0)), 0.0) * rden_c
    dx = (dp - dl_c) * e * (1.0 + x)
    dqt = nt(wide(own_ref, feat_at, nf), dx.astype(bf16))

    s = nt(wk, wq) * scale
    causal = at_row <= at_col
    p = jnp.where(causal, jnp.exp(s - mine_ref[0:1, :]), 0.0)
    dp = nt(v, do)
    dwk = nn((p * (dp - mine_ref[1:2, :])).astype(bf16), wq)
    x = nn(k, wide(query_ref, feat_at, nf)) * feat_scale
    e = jnp.where(causal, jnp.exp(jnp.minimum(own_cum - cum_c, 0.0)), 0.0) * mine_ref[2:3, :]
    dx = (dp - mine_ref[3:4, :]) * e * (1.0 + x)
    dkt = nt(wide(query_ref, feat_at, nf), dx.astype(bf16))
    dv = nn((p + (1.0 + x + 0.5 * x * x) * e).astype(bf16), do)

    def step(d, carry):
        dwq, dqt, dwk, dkt, dv = carry
        j = partner(me, d, count)
        view = recv(d)
        mine = j < me
        sign = pick(mine, 1, -1)
        limit = WINDOW - jnp.abs(me - j) * rows
        rows_w = pick(mine, wq, wk)
        rows_v = pick(mine, do, v)
        rows_f = pick(mine, q, k)
        other_w = view[0:rows, :]
        other_v = view[rows : 2 * rows, :]
        other_f = wide(view, feat_at, nf)
        st = stat(d)
        zero = jnp.zeros((1, rows), f32)
        cum = st[4:5, :]
        gap = between(totals, jnp.minimum(me, j), jnp.maximum(me, j))
        e_r = jnp.exp(jnp.minimum(gap + pick(mine, cum[:, rows - 1 : rows] - cum, cum), 0.0))
        e_r = e_r * pick(mine, 1.0, st[2:3, :])
        e_c = pick(mine, growth_c, tail_c)

        s = nt(rows_w, other_w) * scale
        p = jnp.exp(s - pick(mine, lse_c, 0.0) - pick(mine, zero, st[0:1, :]))
        p = jnp.where(apart * sign < limit, p, 0.0)
        dp = nt(rows_v, other_v)
        ds = p * (dp - pick(mine, dw_c, 0.0) - pick(mine, zero, st[1:2, :]))
        more_w = nn(ds.astype(bf16), other_w)
        x = nn(rows_f, other_f) * feat_scale
        e = e_r * e_c
        dx = (dp - pick(mine, dl_c, 0.0) - pick(mine, zero, st[3:4, :])) * e * (1.0 + x)
        more_f = nt(other_f, dx.astype(bf16))
        more_v = nn((p + (1.0 + x + 0.5 * x * x) * e).astype(bf16), other_v)
        dwq = dwq + pick(mine, more_w, 0.0)
        dwk = dwk + pick(mine, 0.0, more_w)
        dqt = dqt + pick(mine, more_f, 0.0)
        dkt = dkt + pick(mine, 0.0, more_f)
        dv = dv + pick(mine, 0.0, more_v)
        return dwq, dqt, dwk, dkt, dv

    dwq, dqt, dwk, dkt, dv = over_partners(count, step, (dwq, dqt, dwk, dkt, dv))
    dwq, dwk = (dwq * scale).astype(bf16), (dwk * scale).astype(bf16)
    dv = dv.astype(bf16)
    dft = (jnp.concatenate([dqt, dkt], axis=0) * feat_scale).astype(bf16)
    (grad_ref,) = rest
    grad_ref[0:rows, :] = dwq
    grad_ref[rows : 2 * rows, :] = dwk
    grad_ref[2 * rows : 3 * rows, :] = dv
    put_wide(grad_ref, 3 * rows, dft)


def gather_rows(grad_ref, order, cat_ref, feat_ref):
    rows = cat_ref.shape[0]
    nf2 = feat_ref.shape[1] // len(order)
    for at, h in enumerate(order):
        for part in range(3):
            lane = (3 * at + part) * LANES
            cat_ref[:, lane : lane + LANES] = grad_ref[h, part * rows : (part + 1) * rows, :]
    dft = jnp.concatenate([wide(grad_ref.at[h], 3 * rows, nf2) for h in order], axis=0)
    feat_ref[...] = jnp.transpose(dft.astype(f32)).astype(bf16)


def cat_kernel(grad_ref, cat_ref, feat_ref):
    heads = grad_ref.shape[0]
    head = lax.axis_index("tp")
    order = [head] + [jnp.bitwise_xor(head, t) for t in range(1, heads)]
    gather_rows(grad_ref, order, cat_ref, feat_ref)


def columns_kernel(ctx, distances, cat_ref, feat_ref, ww_ref, vw_ref, fw_ref, *rest):
    pieces, firsts = rest[: len(distances)], rest[len(distances) : len(distances) + 2]
    out_ref, tile_ref, sems = rest[-3:]
    nf2 = fw_ref.shape[0]
    heads = feat_ref.shape[1] // nf2
    tile = 2 * LANES
    me = block_index(ctx)
    copies = []
    for n, (e, ref) in enumerate(zip(distances, pieces)):
        part = pl.ds(pl.multiple_of(jnp.bitwise_xor(me, e) * tile, tile), tile)
        views = [firsts[e % 2].at[e // 2]] + [ref.at[t] for t in range(heads - 2)]
        main = [ww_ref[part, :], vw_ref[part, :]]
        main += [v[m * tile : (m + 1) * tile, :] for v in views for m in range(3)]
        feats = [fw_ref[:, part]] + [wide(v, 3 * tile, nf2) for v in views]
        total = nt(cat_ref[...], jnp.concatenate(main, axis=1))
        total += nn(feat_ref[...], jnp.concatenate(feats, axis=0))
        tile_ref[n] = total.astype(bf16)
        copies.append(pltpu.make_async_copy(tile_ref.at[n], out_ref.at[:, part], sems.at[n]))
        copies[-1].start()
    for copy in copies:
        copy.wait()


def merge_kernel(grad_ref, weight_ref, out_ref, cat_ref, feat_ref):
    heads = grad_ref.shape[0]
    tile = out_ref.shape[1]
    lanes = 3 * LANES
    nf2 = feat_ref.shape[1] // heads

    @pl.when(pl.program_id(0) == 0)
    def _():
        gather_rows(grad_ref, range(heads), cat_ref, feat_ref)

    views = [weight_ref.at[h] for h in range(heads)]
    main = jnp.concatenate([v[:, 0:lanes] for v in views], axis=1)
    feats = jnp.concatenate([v[:, lanes:] for v in views], axis=1)
    out_ref[...] = (nt(cat_ref[...], main) + nt(feat_ref[...], feats)).astype(bf16)


VMEM = pl.BlockSpec(memory_space=pltpu.VMEM)
HBM = pl.BlockSpec(memory_space=pltpu.HBM)
ANY = pl.BlockSpec(memory_space=pl.ANY)
params = pltpu.CompilerParams(vmem_limit_bytes=32 * 1024 * 1024)


def in_hbm(*arrays):
    return [pltpu.with_memory_space_constraint(a, pltpu.HBM) for a in arrays]


def cost(flops, nbytes, exps=0):
    return pl.CostEstimate(flops=flops, bytes_accessed=nbytes, transcendentals=exps)


def merge(grads, weights, rows, dim):
    heads, _, columns = weights.shape
    tile = 2 * LANES
    return pl.pallas_call(
        merge_kernel,
        out_shape=jax.ShapeDtypeStruct((rows, dim), bf16),
        grid=(dim // tile,),
        in_specs=[
            pl.BlockSpec(grads.shape, lambda i: (0, 0, 0)),
            pl.BlockSpec((heads, tile, columns), lambda i: (0, i, 0)),
        ],
        out_specs=pl.BlockSpec((rows, tile), lambda i: (0, i)),
        scratch_shapes=[
            pltpu.VMEM((rows, 3 * LANES * heads), bf16),
            pltpu.VMEM((rows, (columns - 3 * LANES) * heads), bf16),
        ],
        compiler_params=params,
        cost_estimate=cost(2 * rows * dim * heads * columns, heads * dim * columns * 2),
        name="head_sum",
    )(grads, weights)


def per_device(ctx, tokens, feature_weight, window_weight, value_weight, log_decay, out_grad):
    rows, dim = tokens.shape
    nf2 = feature_weight.shape[1]
    nf = nf2 // 2
    dh = value_weight.shape[1]
    columns = 3 * dh + nf2
    chips, count, heads = lax.axis_size(ctx[:-1]), lax.axis_size(ctx), lax.axis_size("tp")
    fw_t = feature_weight.T
    tile = 2 * LANES
    spread = heads == 4 and count * tile == dim and count == 8
    packs = []
    if spread:
        packs = [jax.ShapeDtypeStruct((columns * tile // LANES, LANES), bf16)]
        packs += [jax.ShapeDtypeStruct((chips, *packs[0].shape), bf16)]

    payload = 2 * rows + 2 * nf + 16
    block = jax.ShapeDtypeStruct((payload, LANES), bf16)
    outs = pl.pallas_call(
        partial(project_kernel, ctx, len(packs)),
        out_shape=packs
        + [block] * (chips + 2)
        + [
            jax.ShapeDtypeStruct((rows, nf2), bf16),
            jax.ShapeDtypeStruct((rows, 1), f32),
            jax.ShapeDtypeStruct((dim, 2 * dh), bf16),
            jax.ShapeDtypeStruct((dim, dh), bf16),
            jax.ShapeDtypeStruct((nf2, dim), bf16),
        ],
        in_specs=[HBM] * 6,
        out_specs=[VMEM] * (len(packs) + chips + 7),
        scratch_shapes=[
            pltpu.VMEM((rows, dim), bf16),
            pltpu.VMEM((1, rows), f32),
            pltpu.VMEM((rows, dh), bf16),
            pltpu.SemaphoreType.DMA((CHUNKS, 4)),
            pltpu.SemaphoreType.DMA((2,)),
        ],
        compiler_params=params,
        cost_estimate=cost(1, 1024),
        name="project",
    )(*in_hbm(tokens, fw_t, window_weight, value_weight, log_decay.T, out_grad))
    *sends, own, query, feat, cum, ww, vw, fw = outs[len(packs) :]

    swap = [(0, 1), (1, 0)]
    recv = {}
    for d in range(1, chips):
        recv[2 * d] = lax.ppermute(sends[d], ctx[:-1], [(i, i ^ d) for i in range(chips)])
    recv[1] = lax.ppermute(sends[0], "core", swap)
    if spread:
        across = lax.ppermute(outs[0], "tp", [(z, z ^ 2) for z in range(heads)])
    for d in range(1, chips):
        if spread and d == chips - 1:
            across, recv[2 * d] = lax.optimization_barrier((across, recv[2 * d]))
        recv[2 * d + 1] = lax.ppermute(recv[2 * d], "core", swap)
    recv = [recv[d] for d in range(1, count)]
    if count > 8:
        recv = [jnp.stack(recv)]

    if spread:
        across, recv = lax.optimization_barrier((across, recv))
        near = [across, lax.ppermute(across, "tp", [(z, z ^ 1) for z in range(heads)])]

    attended, stat, sheet = pl.pallas_call(
        lambda *refs: query_kernel(ctx, count, len(recv), *refs),
        out_shape=[
            jax.ShapeDtypeStruct((rows, dh), bf16),
            jax.ShapeDtypeStruct((8, rows), f32),
            jax.ShapeDtypeStruct((rows, LANES), f32),
        ],
        in_specs=[VMEM] * (len(recv) + 4),
        out_specs=[VMEM] * 3,
        scratch_shapes=[
            pltpu.VMEM((count, 2 * rows, dh), bf16),
            pltpu.VMEM((WINDOW // rows + 1, rows, rows), f32),
            pltpu.VMEM((count, rows), f32),
        ],
        compiler_params=params,
        cost_estimate=cost(1, 1024),
        name="query_side",
    )(*recv, own, query, feat, cum)
    stats = [stat]
    for name in reversed(ctx):
        held = stats[0] if len(stats) == 1 else jnp.concatenate(stats, axis=0)
        stats.append(lax.ppermute(held, name, swap))
    if count > 8:
        stats = [jnp.concatenate(stats, axis=0)]

    if spread:
        first = lax.ppermute(outs[1], "tp", [(z, z ^ 1) for z in range(heads)])
        near, stats = lax.optimization_barrier((near, stats))
        pieces = [
            pl.pallas_call(
                stack_kernel,
                out_shape=jax.ShapeDtypeStruct((heads - 2, *packs[0].shape), bf16),
                in_specs=[VMEM] * (heads - 2),
                out_specs=VMEM,
                compiler_params=params,
                cost_estimate=cost(1, 1024),
                name="stack",
            )(*near)
        ]
        for d in range(1, chips):
            pieces.append(
                lax.ppermute(pieces[0], ctx[:-1], [(i, i ^ d) for i in range(chips)])
            )
        pieces[0], sheet = lax.optimization_barrier((pieces[0], sheet))

    grads = pl.pallas_call(
        lambda *refs: gradient_kernel(ctx, count, len(recv), len(stats), *refs),
        out_shape=jax.ShapeDtypeStruct((3 * rows + nf2 * rows // LANES, LANES), bf16),
        in_specs=[VMEM] * (len(recv) + len(stats) + 4),
        out_specs=VMEM,
        scratch_shapes=[pltpu.VMEM((count, LANES), f32)],
        compiler_params=params,
        cost_estimate=cost(1, 1024),
        name="gradients",
    )(*recv, *stats, own, query, feat, sheet)
    if not spread:
        weights = jnp.concatenate([window_weight, value_weight, feature_weight], axis=1)
        weights = lax.all_gather(weights, "tp")
        return (attended, merge(lax.all_gather(grads, "tp"), weights, rows, dim))

    first, grads = lax.optimization_barrier((first, grads))
    swapped = [lax.ppermute(pieces[0], "core", swap)]
    firsts = [first, lax.ppermute(first, "core", swap)]
    grads = lax.all_gather(grads, "tp")
    cat, feats = pl.pallas_call(
        cat_kernel,
        out_shape=[
            jax.ShapeDtypeStruct((rows, 3 * LANES * heads), bf16),
            jax.ShapeDtypeStruct((rows, nf2 * heads), bf16),
        ],
        in_specs=[VMEM],
        out_specs=[VMEM] * 2,
        compiler_params=params,
        cost_estimate=cost(1, 1024),
        name="cat",
    )(grads)
    pieces, _ = lax.optimization_barrier((pieces, cat))
    swapped += [lax.ppermute(p, "core", swap) for p in pieces[1:]]

    total = []
    for distances in ((0, 1, 2, 4, 6), (3, 5, 7)):
        parts = [(swapped if e % 2 else pieces)[e // 2] for e in distances]
        args = [cat, feats, ww, vw, fw, *parts, *firsts, *total]
        total = [
            pl.pallas_call(
                partial(columns_kernel, ctx, distances),
                out_shape=jax.ShapeDtypeStruct((rows, dim), bf16),
                in_specs=[VMEM] * (7 + len(parts)) + [ANY] * len(total),
                out_specs=ANY,
                scratch_shapes=[
                    pltpu.VMEM((len(parts), rows, tile), bf16),
                    pltpu.SemaphoreType.DMA((len(parts),)),
                ],
                input_output_aliases={len(args) - 1: 0} if total else {},
                compiler_params=params,
                cost_estimate=cost(1, 1024),
                name="columns",
            )(*args)
        ]
    return (attended, total[0])


def solution(mesh):
    blocks, tp = mesh.devices.shape
    bits = blocks.bit_length() - 1
    assert blocks == 2**bits
    ctx = tuple(f"half{i}" for i in range(bits - 1)) + ("core",)
    split = Mesh(mesh.devices.reshape((2,) * bits + (tp,)), (*ctx, "tp"))
    in_specs = (
        P(ctx, None),
        P(None, "tp"),
        P(None, "tp"),
        P(None, "tp"),
        P(ctx, "tp"),
        P(ctx, "tp"),
    )
    out_specs = (P(ctx, "tp"), P(ctx, None))
    return jax.shard_map(
        partial(per_device, ctx),
        mesh=split,
        in_specs=in_specs,
        out_specs=out_specs,
        check_vma=False,
    )
```

```python
from functools import partial

import jax
import jax.numpy as jnp
from jax import lax
from jax.experimental import pallas as pl
from jax.experimental.pallas import tpu as pltpu
from jax.sharding import Mesh
from jax.sharding import PartitionSpec as P

WINDOW = 1024
LANES = 128
MASKED = -1e30
CHUNKS = 4
f32 = jnp.float32
bf16 = jnp.bfloat16


def nn(a, b):
    return lax.dot_general(a, b, (((1,), (0,)), ((), ())), preferred_element_type=f32)


def nt(a, b):
    return lax.dot_general(a, b, (((1,), (1,)), ((), ())), preferred_element_type=f32)


def partner(me, d, count):
    assert count & (count - 1) == 0
    return jnp.bitwise_xor(me, d)


def wide(view, start, count):
    return jnp.concatenate(
        [view[start : start + count, :], view[start + count : start + 2 * count, :]], axis=1
    )


def put_wide(ref, start, value):
    count = value.shape[0]
    for half in range(value.shape[1] // LANES):
        ref[start + half * count : start + (half + 1) * count, :] = value[
            :, half * LANES : (half + 1) * LANES
        ]


def cum_row(view, start):
    tail = view[start : start + 16, :].astype(f32)
    first = tail[0:1] + tail[2:3] + tail[4:5]
    second = tail[1:2] + tail[3:4] + tail[5:6]
    return jnp.concatenate([first, second], axis=1)


def iotas(rows):
    return (
        lax.broadcasted_iota(jnp.int32, (rows, rows), 0),
        lax.broadcasted_iota(jnp.int32, (rows, rows), 1),
    )


def block_index(ctx):
    place = 0
    for name in ctx:
        place = place * lax.axis_size(name) + lax.axis_index(name)
    return place


def pack(me, ww_ref, vw_ref, fw_ref, out_ref):
    nf2 = fw_ref.shape[0]
    tile = 2 * LANES
    at = pl.multiple_of(me * tile, tile)
    rows = pl.ds(at, tile)
    out_ref[0:tile, :] = ww_ref[rows, 0:LANES]
    out_ref[tile : 2 * tile, :] = ww_ref[rows, LANES:]
    out_ref[2 * tile : 3 * tile, :] = vw_ref[rows, :]
    put_wide(out_ref, 3 * tile, fw_ref[:, rows])


def project_kernel(ctx, packs, tok_hbm, fw_hbm, ww_hbm, vw_hbm, ld_hbm, do_hbm, *rest):
    *sends, keys_ref, query_ref, feat_ref, cum_ref, ww_ref, vw_ref, fw_ref = rest[packs:-5]
    tok_ref, ld_ref, do_ref, sems, small = rest[-5:]
    me = block_index(ctx)
    rows, dim = tok_ref.shape
    dh = do_ref.shape[1]
    nf = fw_ref.shape[0] // 2
    span = dim // CHUNKS
    copies = []
    for c in range(CHUNKS):
        part = pl.ds(c * span, span)
        copies.append([
            pltpu.make_async_copy(tok_hbm.at[:, part], tok_ref.at[:, part], sems.at[c, 0]),
            pltpu.make_async_copy(ww_hbm.at[part, :], ww_ref.at[part, :], sems.at[c, 1]),
            pltpu.make_async_copy(vw_hbm.at[part, :], vw_ref.at[part, :], sems.at[c, 2]),
            pltpu.make_async_copy(fw_hbm.at[:, part], fw_ref.at[:, part], sems.at[c, 3]),
        ])
    others = [
        pltpu.make_async_copy(ld_hbm, ld_ref, small.at[0]),
        pltpu.make_async_copy(do_hbm, do_ref, small.at[1]),
    ]
    for copy in others:
        copy.start()
    for group in copies:
        for at, copy in enumerate(group):
            copy.start(priority=min(at, 1))
    for copy in others:
        copy.wait()
    at_row, at_col = iotas(rows)
    ld_r = ld_ref[...]
    ld_c = jnp.sum(jnp.where(at_row == at_col, ld_r, 0.0), axis=1, keepdims=True)
    cum_r = jnp.sum(jnp.where(at_row <= at_col, ld_c, 0.0), axis=0, keepdims=True)
    cum_ref[...] = jnp.sum(jnp.where(at_col <= at_row, ld_r, 0.0), axis=1, keepdims=True)
    high = cum_r.astype(bf16)
    left = cum_r - high.astype(f32)
    mid = left.astype(bf16)
    low = (left - mid.astype(f32)).astype(bf16)
    pieces = [t[:, h : h + LANES].astype(f32) for t in (high, mid, low) for h in range(0, rows, LANES)]
    tail = jnp.concatenate(pieces + [jnp.zeros((10, LANES), f32)], axis=0).astype(bf16)

    feat = jnp.zeros((rows, 2 * nf), f32)
    main = jnp.zeros((rows, 3 * dh), f32)
    for c in range(CHUNKS):
        for copy in copies[c]:
            copy.wait()
        part = slice(c * span, (c + 1) * span)
        tok = tok_ref[:, part]
        feat += nt(tok, fw_ref[:, part])
        main += nn(tok, jnp.concatenate([ww_ref[part, :], vw_ref[part, :]], axis=1))
    feat = feat.astype(bf16)
    window = main[:, : 2 * dh].astype(bf16)
    values = main[:, 2 * dh :].astype(bf16)
    feat_ref[...] = feat
    small_row, small_col = iotas(2 * nf)
    feat_t = nt((small_row == small_col).astype(bf16), feat).astype(bf16)
    feat_at = 2 * rows
    tail_at = feat_at + 2 * nf

    def put_keys(ref):
        ref[0:rows, :] = window[:, dh:]
        ref[rows : 2 * rows, :] = values
        put_wide(ref, feat_at, feat_t[nf:, :])
        ref[tail_at : tail_at + 16, :] = tail

    def put_query(ref):
        ref[0:rows, :] = window[:, :dh]
        ref[rows : 2 * rows, :] = do_ref[...]
        put_wide(ref, feat_at, feat_t[:nf, :])
        ref[tail_at : tail_at + 16, :] = tail

    put_keys(keys_ref)
    put_query(query_ref)
    for at, ref in enumerate(sends):
        later = jnp.bitwise_xor(me, max(2 * at, 1)) > me
        pl.when(later)(lambda ref=ref: put_keys(ref))
        pl.when(jnp.logical_not(later))(lambda ref=ref: put_query(ref))
    if packs:
        own_pack, *first_packs = rest[:packs]
        pack(me, ww_ref, vw_ref, fw_ref, own_pack)
        for n, ref in enumerate(first_packs):
            for d in range(2):
                piece = jnp.bitwise_xor(me, 4 * n + 2 * d)
                pack(piece, ww_ref, vw_ref, fw_ref, ref.at[d])

def stack_kernel(*refs):
    *parts, out_ref = refs
    for t, ref in enumerate(parts):
        out_ref[t] = ref[...]


def between(totals, low, high):
    at = lax.broadcasted_iota(jnp.int32, totals.shape, 0)
    return jnp.sum(jnp.where((at > low) & (at < high), totals, 0.0), axis=0, keepdims=True)


def over_partners(count, body, carry):
    if count <= 8:
        for d in range(1, count):
            carry = body(d, carry)
        return carry
    return lax.fori_loop(1, count, body, carry)


def query_kernel(ctx, count, recvs, *rest):
    recvs, rest = rest[:recvs], rest[recvs:]
    own_ref, query_ref, feat_ref, cum_ref, *rest = rest
    near_ref, p_ref, cums_ref = rest[-3:]
    att_ref, stat_ref, sheet_ref = rest[:3]

    def recv(d):
        return recvs[d - 1] if len(recvs) > 1 else recvs[0].at[d - 1]

    me = block_index(ctx)
    rows, dh = att_ref.shape
    nf = feat_ref.shape[1] // 2
    back = WINDOW // rows
    feat_at = 2 * rows
    tail_at = feat_at + 2 * nf
    scale = dh ** (-0.5)
    feat_scale = nf ** (-0.5)
    wq = query_ref[0:rows, :]
    do = query_ref[rows : 2 * rows, :]
    q = feat_ref[:, :nf]
    at_row, at_col = iotas(rows)
    own_cum = cum_row(own_ref, tail_at)
    cums_ref[pl.ds(me, 1), :] = own_cum
    near_ref[me] = own_ref[0 : 2 * rows, :]

    def gather(d, carry):
        j = partner(me, d, count)
        view = recv(d)
        near_ref[j] = view[0 : 2 * rows, :]
        cums_ref[pl.ds(j, 1), :] = cum_row(view, tail_at)
        return carry

    over_partners(count, gather, 0)

    def near(w):
        return near_ref.at[jnp.maximum(me - back + w, 0)]

    top = jnp.full((rows, LANES), MASKED, f32)
    for w in range(back + 1):
        keys = own_ref[0:rows, :] if w == back else near(w)[0:rows, :]
        s = nt(wq, keys) * scale
        if w == back:
            s = jnp.where(at_col <= at_row, s, MASKED)
        elif w == 0:
            s = jnp.where((at_col > at_row) & (me >= back), s, MASKED)
        else:
            s = jnp.where(me >= back - w, s, MASKED)
        p_ref[w] = s
        for h in range(0, rows, LANES):
            top = jnp.maximum(top, s[:, h : h + LANES])
    top = jnp.max(top, axis=1, keepdims=True)
    total = jnp.zeros((rows, LANES), f32)
    out = jnp.zeros((rows, dh), f32)
    for w in range(back + 1):
        p = jnp.exp(p_ref[w] - top)
        for h in range(0, rows, LANES):
            total += p[:, h : h + LANES]
        vals = own_ref[rows : 2 * rows, :] if w == back else near(w)[rows : 2 * rows, :]
        out += nn(p.astype(bf16), vals)
    total = jnp.sum(total, axis=1, keepdims=True)
    windowed = out * (1.0 / total)

    cum_c = cum_ref[...]
    growth = jnp.exp(cum_c)
    totals = cums_ref[:, rows - 1 : rows]

    def forward(d, carry):
        num, den = carry
        j = partner(me, d, count)
        view = recv(d)
        gap = between(totals, j - 1, me)
        es = jnp.where(j < me, jnp.exp(jnp.minimum(gap - cums_ref[pl.ds(j, 1), :], 0.0)), 0.0)
        x = nn(q, wide(view, feat_at, nf)) * feat_scale
        weight = (1.0 + x + 0.5 * x * x) * es
        for h in range(0, rows, LANES):
            den += weight[:, h : h + LANES]
        num += nn(weight.astype(bf16), view[rows : 2 * rows, :])
        return num, den

    num, den = over_partners(
        count, forward, (jnp.zeros((rows, dh), f32), jnp.zeros((rows, LANES), f32))
    )
    x = nn(q, wide(own_ref, feat_at, nf)) * feat_scale
    e = jnp.where(at_col <= at_row, jnp.exp(jnp.minimum(cum_c - own_cum, 0.0)), 0.0)
    weight = (1.0 + x + 0.5 * x * x) * e
    num = num * growth + nn(weight.astype(bf16), own_ref[rows : 2 * rows, :])
    den = den * growth
    for h in range(0, rows, LANES):
        den += weight[:, h : h + LANES]
    rden = 1.0 / jnp.sum(den, axis=1, keepdims=True)
    linear = num * rden
    att_ref[...] = (linear + windowed).astype(bf16)
    do_f = do.astype(f32)
    delta_w = jnp.sum(do_f * windowed, axis=1, keepdims=True)
    delta_l = jnp.sum(do_f * linear, axis=1, keepdims=True)
    lse = top + jnp.log(total)
    lane = lax.broadcasted_iota(jnp.int32, (rows, LANES), 1)
    sheet = jnp.where(lane == 0, lse, 0.0)
    sheet = jnp.where(lane == 1, delta_w, sheet)
    sheet = jnp.where(lane == 2, rden, sheet)
    sheet = jnp.where(lane == 3, delta_l, sheet)
    sheet = jnp.where(lane == 4, cum_c, sheet)
    sheet_ref[...] = sheet
    stat_ref[...] = jnp.transpose(sheet)[0:8, :]


def gradient_kernel(ctx, count, recvs, stats, *rest):
    recvs, rest = rest[:recvs], rest[recvs:]
    stats, rest = rest[:stats], rest[stats:]
    own_ref, query_ref, feat_ref, sheet_ref, *rest, total_ref = rest

    def recv(d):
        return recvs[d - 1] if len(recvs) > 1 else recvs[0].at[d - 1]

    me = block_index(ctx)
    rows = feat_ref.shape[0]
    dh = LANES
    nf = feat_ref.shape[1] // 2
    feat_at = 2 * rows
    scale = dh ** (-0.5)
    feat_scale = nf ** (-0.5)
    at_row, at_col = iotas(rows)
    apart = at_row - at_col
    wq, wk = query_ref[0:rows, :], own_ref[0:rows, :]
    do, v = query_ref[rows : 2 * rows, :], own_ref[rows : 2 * rows, :]
    q, k = feat_ref[:, :nf], feat_ref[:, nf:]
    lse_c, dw_c = sheet_ref[:, 0:1], sheet_ref[:, 1:2]
    rden_c, dl_c, cum_c = sheet_ref[:, 2:3], sheet_ref[:, 3:4], sheet_ref[:, 4:5]
    def stat(d):
        if len(stats) == 1:
            return stats[0].at[pl.ds(pl.multiple_of(8 * d, 8), 8)]
        at = d.bit_length()
        return stats[at].at[pl.ds(8 * (d - (1 << at >> 1)), 8)]

    mine_ref = stat(0)
    own_cum = mine_ref[4:5, :]
    total_ref[pl.ds(me, 1), :] = own_cum[:, rows - LANES :]

    def place(d, carry):
        total_ref[pl.ds(partner(me, d, count), 1), :] = stat(d)[4:5, rows - LANES :]
        return carry

    over_partners(count, place, 0)
    totals = total_ref[:, LANES - 1 :]
    growth_c = jnp.exp(cum_c) * rden_c
    tail_c = jnp.exp(own_cum[:, rows - 1 : rows] - cum_c)

    def pick(flag, a, b):
        return jnp.where(flag, a, b)

    s = nt(wq, wk) * scale
    causal = at_col <= at_row
    p = jnp.where(causal, jnp.exp(s - lse_c), 0.0)
    dp = nt(do, v)
    dwq = nn((p * (dp - dw_c)).astype(bf16), wk)
    x = nn(q, wide(own_ref, feat_at, nf)) * feat_scale
    e = jnp.where(causal, jnp.exp(jnp.minimum(cum_c - own_cum, 0.0)), 0.0) * rden_c
    dx = (dp - dl_c) * e * (1.0 + x)
    dqt = nt(wide(own_ref, feat_at, nf), dx.astype(bf16))

    s = nt(wk, wq) * scale
    causal = at_row <= at_col
    p = jnp.where(causal, jnp.exp(s - mine_ref[0:1, :]), 0.0)
    dp = nt(v, do)
    dwk = nn((p * (dp - mine_ref[1:2, :])).astype(bf16), wq)
    x = nn(k, wide(query_ref, feat_at, nf)) * feat_scale
    e = jnp.where(causal, jnp.exp(jnp.minimum(own_cum - cum_c, 0.0)), 0.0) * mine_ref[2:3, :]
    dx = (dp - mine_ref[3:4, :]) * e * (1.0 + x)
    dkt = nt(wide(query_ref, feat_at, nf), dx.astype(bf16))
    dv = nn((p + (1.0 + x + 0.5 * x * x) * e).astype(bf16), do)

    def step(d, carry):
        dwq, dqt, dwk, dkt, dv = carry
        j = partner(me, d, count)
        view = recv(d)
        mine = j < me
        sign = pick(mine, 1, -1)
        limit = WINDOW - jnp.abs(me - j) * rows
        rows_w = pick(mine, wq, wk)
        rows_v = pick(mine, do, v)
        rows_f = pick(mine, q, k)
        other_w = view[0:rows, :]
        other_v = view[rows : 2 * rows, :]
        other_f = wide(view, feat_at, nf)
        st = stat(d)
        zero = jnp.zeros((1, rows), f32)
        cum = st[4:5, :]
        gap = between(totals, jnp.minimum(me, j), jnp.maximum(me, j))
        e_r = jnp.exp(jnp.minimum(gap + pick(mine, cum[:, rows - 1 : rows] - cum, cum), 0.0))
        e_r = e_r * pick(mine, 1.0, st[2:3, :])
        e_c = pick(mine, growth_c, tail_c)

        s = nt(rows_w, other_w) * scale
        p = jnp.exp(s - pick(mine, lse_c, 0.0) - pick(mine, zero, st[0:1, :]))
        p = jnp.where(apart * sign < limit, p, 0.0)
        dp = nt(rows_v, other_v)
        ds = p * (dp - pick(mine, dw_c, 0.0) - pick(mine, zero, st[1:2, :]))
        more_w = nn(ds.astype(bf16), other_w)
        x = nn(rows_f, other_f) * feat_scale
        e = e_r * e_c
        dx = (dp - pick(mine, dl_c, 0.0) - pick(mine, zero, st[3:4, :])) * e * (1.0 + x)
        more_f = nt(other_f, dx.astype(bf16))
        more_v = nn((p + (1.0 + x + 0.5 * x * x) * e).astype(bf16), other_v)
        dwq = dwq + pick(mine, more_w, 0.0)
        dwk = dwk + pick(mine, 0.0, more_w)
        dqt = dqt + pick(mine, more_f, 0.0)
        dkt = dkt + pick(mine, 0.0, more_f)
        dv = dv + pick(mine, 0.0, more_v)
        return dwq, dqt, dwk, dkt, dv

    dwq, dqt, dwk, dkt, dv = over_partners(count, step, (dwq, dqt, dwk, dkt, dv))
    dwq, dwk = (dwq * scale).astype(bf16), (dwk * scale).astype(bf16)
    dv = dv.astype(bf16)
    dft = (jnp.concatenate([dqt, dkt], axis=0) * feat_scale).astype(bf16)
    (grad_ref,) = rest
    grad_ref[0:rows, :] = dwq
    grad_ref[rows : 2 * rows, :] = dwk
    grad_ref[2 * rows : 3 * rows, :] = dv
    put_wide(grad_ref, 3 * rows, dft)


def gather_rows(grad_ref, order, cat_ref, feat_ref):
    rows = cat_ref.shape[0]
    nf2 = feat_ref.shape[1] // len(order)
    for at, h in enumerate(order):
        for part in range(3):
            lane = (3 * at + part) * LANES
            cat_ref[:, lane : lane + LANES] = grad_ref[h, part * rows : (part + 1) * rows, :]
    dft = jnp.concatenate([wide(grad_ref.at[h], 3 * rows, nf2) for h in order], axis=0)
    feat_ref[...] = jnp.transpose(dft.astype(f32)).astype(bf16)


def cat_kernel(grad_ref, cat_ref, feat_ref):
    heads = grad_ref.shape[0]
    head = lax.axis_index("tp")
    order = [head] + [jnp.bitwise_xor(head, t) for t in range(1, heads)]
    gather_rows(grad_ref, order, cat_ref, feat_ref)


def columns_kernel(ctx, distances, cat_ref, feat_ref, ww_ref, vw_ref, fw_ref, *rest):
    pieces, firsts = rest[: len(distances)], rest[len(distances) : len(distances) + 4]
    out_ref, tile_ref, sems = rest[-3:]
    nf2 = fw_ref.shape[0]
    heads = feat_ref.shape[1] // nf2
    tile = 2 * LANES
    me = block_index(ctx)
    copies = []
    for n, (e, ref) in enumerate(zip(distances, pieces)):
        part = pl.ds(pl.multiple_of(jnp.bitwise_xor(me, e) * tile, tile), tile)
        views = [firsts[2 * (e % 2) + e // 4].at[e // 2 % 2]]
        views += [ref.at[t] for t in range(heads - 2)]
        main = [ww_ref[part, :], vw_ref[part, :]]
        main += [v[m * tile : (m + 1) * tile, :] for v in views for m in range(3)]
        feats = [fw_ref[:, part]] + [wide(v, 3 * tile, nf2) for v in views]
        total = nt(cat_ref[...], jnp.concatenate(main, axis=1))
        total += nn(feat_ref[...], jnp.concatenate(feats, axis=0))
        tile_ref[n] = total.astype(bf16)
        copies.append(pltpu.make_async_copy(tile_ref.at[n], out_ref.at[:, part], sems.at[n]))
        copies[-1].start()
    for copy in copies:
        copy.wait()


def merge_kernel(grad_ref, weight_ref, out_ref, cat_ref, feat_ref):
    heads = grad_ref.shape[0]
    tile = out_ref.shape[1]
    lanes = 3 * LANES
    nf2 = feat_ref.shape[1] // heads

    @pl.when(pl.program_id(0) == 0)
    def _():
        gather_rows(grad_ref, range(heads), cat_ref, feat_ref)

    views = [weight_ref.at[h] for h in range(heads)]
    main = jnp.concatenate([v[:, 0:lanes] for v in views], axis=1)
    feats = jnp.concatenate([v[:, lanes:] for v in views], axis=1)
    out_ref[...] = (nt(cat_ref[...], main) + nt(feat_ref[...], feats)).astype(bf16)


VMEM = pl.BlockSpec(memory_space=pltpu.VMEM)
HBM = pl.BlockSpec(memory_space=pltpu.HBM)
ANY = pl.BlockSpec(memory_space=pl.ANY)
params = pltpu.CompilerParams(vmem_limit_bytes=32 * 1024 * 1024)


def in_hbm(*arrays):
    return [pltpu.with_memory_space_constraint(a, pltpu.HBM) for a in arrays]


def cost(flops, nbytes, exps=0):
    return pl.CostEstimate(flops=flops, bytes_accessed=nbytes, transcendentals=exps)


def merge(grads, weights, rows, dim):
    heads, _, columns = weights.shape
    tile = 2 * LANES
    return pl.pallas_call(
        merge_kernel,
        out_shape=jax.ShapeDtypeStruct((rows, dim), bf16),
        grid=(dim // tile,),
        in_specs=[
            pl.BlockSpec(grads.shape, lambda i: (0, 0, 0)),
            pl.BlockSpec((heads, tile, columns), lambda i: (0, i, 0)),
        ],
        out_specs=pl.BlockSpec((rows, tile), lambda i: (0, i)),
        scratch_shapes=[
            pltpu.VMEM((rows, 3 * LANES * heads), bf16),
            pltpu.VMEM((rows, (columns - 3 * LANES) * heads), bf16),
        ],
        compiler_params=params,
        cost_estimate=cost(2 * rows * dim * heads * columns, heads * dim * columns * 2),
        name="head_sum",
    )(grads, weights)


def per_device(ctx, tokens, feature_weight, window_weight, value_weight, log_decay, out_grad):
    rows, dim = tokens.shape
    nf2 = feature_weight.shape[1]
    nf = nf2 // 2
    dh = value_weight.shape[1]
    columns = 3 * dh + nf2
    chips, count, heads = lax.axis_size(ctx[:-1]), lax.axis_size(ctx), lax.axis_size("tp")
    fw_t = feature_weight.T
    tile = 2 * LANES
    spread = heads == 4 and count * tile == dim and count == 8
    packs = []
    if spread:
        packs = [jax.ShapeDtypeStruct((columns * tile // LANES, LANES), bf16)]
        packs += [jax.ShapeDtypeStruct((2, *packs[0].shape), bf16)] * (chips // 2)

    payload = 2 * rows + 2 * nf + 16
    block = jax.ShapeDtypeStruct((payload, LANES), bf16)
    outs = pl.pallas_call(
        partial(project_kernel, ctx, len(packs)),
        out_shape=packs
        + [block] * (chips + 2)
        + [
            jax.ShapeDtypeStruct((rows, nf2), bf16),
            jax.ShapeDtypeStruct((rows, 1), f32),
            jax.ShapeDtypeStruct((dim, 2 * dh), bf16),
            jax.ShapeDtypeStruct((dim, dh), bf16),
            jax.ShapeDtypeStruct((nf2, dim), bf16),
        ],
        in_specs=[HBM] * 6,
        out_specs=[VMEM] * (len(packs) + chips + 7),
        scratch_shapes=[
            pltpu.VMEM((rows, dim), bf16),
            pltpu.VMEM((1, rows), f32),
            pltpu.VMEM((rows, dh), bf16),
            pltpu.SemaphoreType.DMA((CHUNKS, 4)),
            pltpu.SemaphoreType.DMA((2,)),
        ],
        compiler_params=params,
        cost_estimate=cost(1, 1024),
        name="project",
    )(*in_hbm(tokens, fw_t, window_weight, value_weight, log_decay.T, out_grad))
    *sends, own, query, feat, cum, ww, vw, fw = outs[len(packs) :]

    swap = [(0, 1), (1, 0)]
    recv = {}
    for d in range(1, chips):
        recv[2 * d] = lax.ppermute(sends[d], ctx[:-1], [(i, i ^ d) for i in range(chips)])
    recv[1] = lax.ppermute(sends[0], "core", swap)
    if spread:
        across = lax.ppermute(outs[0], "tp", [(z, z ^ 2) for z in range(heads)])
    for d in range(1, chips):
        if spread and d == chips - 1:
            across, recv[2 * d] = lax.optimization_barrier((across, recv[2 * d]))
        recv[2 * d + 1] = lax.ppermute(recv[2 * d], "core", swap)
    recv = [recv[d] for d in range(1, count)]
    if count > 8:
        recv = [jnp.stack(recv)]

    if spread:
        across, recv, sent = lax.optimization_barrier((across, recv, outs[1]))
        near = [across, lax.ppermute(across, "tp", [(z, z ^ 1) for z in range(heads)])]

    attended, stat, sheet = pl.pallas_call(
        lambda *refs: query_kernel(ctx, count, len(recv), *refs),
        out_shape=[
            jax.ShapeDtypeStruct((rows, dh), bf16),
            jax.ShapeDtypeStruct((8, rows), f32),
            jax.ShapeDtypeStruct((rows, LANES), f32),
        ],
        in_specs=[VMEM] * (len(recv) + 4),
        out_specs=[VMEM] * 3,
        scratch_shapes=[
            pltpu.VMEM((count, 2 * rows, dh), bf16),
            pltpu.VMEM((WINDOW // rows + 1, rows, rows), f32),
            pltpu.VMEM((count, rows), f32),
        ],
        compiler_params=params,
        cost_estimate=cost(1, 1024),
        name="query_side",
    )(*recv, own, query, feat, cum)
    stats = [stat]
    for name in reversed(ctx):
        held = stats[0] if len(stats) == 1 else jnp.concatenate(stats, axis=0)
        stats.append(lax.ppermute(held, name, swap))
    if count > 8:
        stats = [jnp.concatenate(stats, axis=0)]

    if spread:
        later, stats = lax.optimization_barrier((outs[2], stats))
        first = [lax.ppermute(p, "tp", [(z, z ^ 1) for z in range(heads)]) for p in (sent, later)]
        near, stats = lax.optimization_barrier((near, stats))
        pieces = [
            pl.pallas_call(
                stack_kernel,
                out_shape=jax.ShapeDtypeStruct((heads - 2, *packs[0].shape), bf16),
                in_specs=[VMEM] * (heads - 2),
                out_specs=VMEM,
                compiler_params=params,
                cost_estimate=cost(1, 1024),
                name="stack",
            )(*near)
        ]
        for d in range(1, chips):
            pieces.append(
                lax.ppermute(pieces[0], ctx[:-1], [(i, i ^ d) for i in range(chips)])
            )
        pieces[0], sheet = lax.optimization_barrier((pieces[0], sheet))

    grads = pl.pallas_call(
        lambda *refs: gradient_kernel(ctx, count, len(recv), len(stats), *refs),
        out_shape=jax.ShapeDtypeStruct((3 * rows + nf2 * rows // LANES, LANES), bf16),
        in_specs=[VMEM] * (len(recv) + len(stats) + 4),
        out_specs=VMEM,
        scratch_shapes=[pltpu.VMEM((count, LANES), f32)],
        compiler_params=params,
        cost_estimate=cost(1, 1024),
        name="gradients",
    )(*recv, *stats, own, query, feat, sheet)
    if not spread:
        weights = jnp.concatenate([window_weight, value_weight, feature_weight], axis=1)
        weights = lax.all_gather(weights, "tp")
        return (attended, merge(lax.all_gather(grads, "tp"), weights, rows, dim))

    first[0], grads = lax.optimization_barrier((first[0], grads))
    swapped = [lax.ppermute(pieces[0], "core", swap)]
    firsts = [lax.ppermute(first[0], "core", swap)]
    grads = lax.all_gather(grads, "tp")
    cat, feats = pl.pallas_call(
        cat_kernel,
        out_shape=[
            jax.ShapeDtypeStruct((rows, 3 * LANES * heads), bf16),
            jax.ShapeDtypeStruct((rows, nf2 * heads), bf16),
        ],
        in_specs=[VMEM],
        out_specs=[VMEM] * 2,
        compiler_params=params,
        cost_estimate=cost(1, 1024),
        name="cat",
    )(grads)
    pieces, first[1], _ = lax.optimization_barrier((pieces, first[1], cat))
    firsts = [*first, *firsts, lax.ppermute(first[1], "core", swap)]
    swapped += [lax.ppermute(p, "core", swap) for p in pieces[1:]]

    total = []
    for distances in ((0, 1, 2, 4, 6), (3, 5, 7)):
        parts = [(swapped if e % 2 else pieces)[e // 2] for e in distances]
        args = [cat, feats, ww, vw, fw, *parts, *firsts[:3], firsts[3 if total else 2], *total]
        total = [
            pl.pallas_call(
                partial(columns_kernel, ctx, distances),
                out_shape=jax.ShapeDtypeStruct((rows, dim), bf16),
                in_specs=[VMEM] * (9 + len(parts)) + [ANY] * len(total),
                out_specs=ANY,
                scratch_shapes=[
                    pltpu.VMEM((len(parts), rows, tile), bf16),
                    pltpu.SemaphoreType.DMA((len(parts),)),
                ],
                input_output_aliases={len(args) - 1: 0} if total else {},
                compiler_params=params,
                cost_estimate=cost(1, 1024),
                name="columns",
            )(*args)
        ]
    return (attended, total[0])


def solution(mesh):
    blocks, tp = mesh.devices.shape
    bits = blocks.bit_length() - 1
    assert blocks == 2**bits
    ctx = tuple(f"half{i}" for i in range(bits - 1)) + ("core",)
    split = Mesh(mesh.devices.reshape((2,) * bits + (tp,)), (*ctx, "tp"))
    in_specs = (
        P(ctx, None),
        P(None, "tp"),
        P(None, "tp"),
        P(None, "tp"),
        P(ctx, "tp"),
        P(ctx, "tp"),
    )
    out_specs = (P(ctx, "tp"), P(ctx, None))
    return jax.shard_map(
        partial(per_device, ctx),
        mesh=split,
        in_specs=in_specs,
        out_specs=out_specs,
        check_vma=False,
    )
```

```python
from functools import partial

import jax
import jax.numpy as jnp
from jax import lax
from jax.experimental import pallas as pl
from jax.experimental.pallas import tpu as pltpu
from jax.sharding import Mesh
from jax.sharding import PartitionSpec as P

WINDOW = 1024
LANES = 128
MASKED = -1e30
CHUNKS = 4
f32 = jnp.float32
bf16 = jnp.bfloat16


def nn(a, b):
    return lax.dot_general(a, b, (((1,), (0,)), ((), ())), preferred_element_type=f32)


def nt(a, b):
    return lax.dot_general(a, b, (((1,), (1,)), ((), ())), preferred_element_type=f32)


def partner(me, d, count):
    assert count & (count - 1) == 0
    return jnp.bitwise_xor(me, d)


def wide(view, start, count):
    return jnp.concatenate(
        [view[start : start + count, :], view[start + count : start + 2 * count, :]], axis=1
    )


def put_wide(ref, start, value):
    count = value.shape[0]
    for half in range(value.shape[1] // LANES):
        ref[start + half * count : start + (half + 1) * count, :] = value[
            :, half * LANES : (half + 1) * LANES
        ]


def cum_row(view, start):
    tail = view[start : start + 16, :].astype(f32)
    first = tail[0:1] + tail[2:3] + tail[4:5]
    second = tail[1:2] + tail[3:4] + tail[5:6]
    return jnp.concatenate([first, second], axis=1)


def iotas(rows):
    return (
        lax.broadcasted_iota(jnp.int32, (rows, rows), 0),
        lax.broadcasted_iota(jnp.int32, (rows, rows), 1),
    )


def block_index(ctx):
    place = 0
    for name in ctx:
        place = place * lax.axis_size(name) + lax.axis_index(name)
    return place


def pack(me, ww_ref, vw_ref, fw_ref, out_ref):
    nf2 = fw_ref.shape[0]
    tile = 2 * LANES
    at = pl.multiple_of(me * tile, tile)
    rows = pl.ds(at, tile)
    out_ref[0:tile, :] = ww_ref[rows, 0:LANES]
    out_ref[tile : 2 * tile, :] = ww_ref[rows, LANES:]
    out_ref[2 * tile : 3 * tile, :] = vw_ref[rows, :]
    put_wide(out_ref, 3 * tile, fw_ref[:, rows])


def project_kernel(ctx, packs, tok_hbm, fw_hbm, ww_hbm, vw_hbm, ld_hbm, do_hbm, *rest):
    *sends, keys_ref, query_ref, feat_ref, cum_ref, ww_ref, vw_ref, fw_ref = rest[packs:-5]
    tok_ref, ld_ref, do_ref, sems, small = rest[-5:]
    me = block_index(ctx)
    rows, dim = tok_ref.shape
    dh = do_ref.shape[1]
    nf = fw_ref.shape[0] // 2
    span = dim // CHUNKS
    copies = []
    for c in range(CHUNKS):
        part = pl.ds(c * span, span)
        copies.append([
            pltpu.make_async_copy(tok_hbm.at[:, part], tok_ref.at[:, part], sems.at[c, 0]),
            pltpu.make_async_copy(ww_hbm.at[part, :], ww_ref.at[part, :], sems.at[c, 1]),
            pltpu.make_async_copy(vw_hbm.at[part, :], vw_ref.at[part, :], sems.at[c, 2]),
            pltpu.make_async_copy(fw_hbm.at[:, part], fw_ref.at[:, part], sems.at[c, 3]),
        ])
    others = [
        pltpu.make_async_copy(ld_hbm, ld_ref, small.at[0]),
        pltpu.make_async_copy(do_hbm, do_ref, small.at[1]),
    ]
    for copy in others:
        copy.start()
    for group in copies:
        for at, copy in enumerate(group):
            copy.start(priority=min(at, 1))
    for copy in others:
        copy.wait()
    at_row, at_col = iotas(rows)
    ld_r = ld_ref[...]
    ld_c = jnp.sum(jnp.where(at_row == at_col, ld_r, 0.0), axis=1, keepdims=True)
    cum_r = jnp.sum(jnp.where(at_row <= at_col, ld_c, 0.0), axis=0, keepdims=True)
    cum_ref[...] = jnp.sum(jnp.where(at_col <= at_row, ld_r, 0.0), axis=1, keepdims=True)
    high = cum_r.astype(bf16)
    left = cum_r - high.astype(f32)
    mid = left.astype(bf16)
    low = (left - mid.astype(f32)).astype(bf16)
    pieces = [t[:, h : h + LANES].astype(f32) for t in (high, mid, low) for h in range(0, rows, LANES)]
    tail = jnp.concatenate(pieces + [jnp.zeros((10, LANES), f32)], axis=0).astype(bf16)

    feat = jnp.zeros((rows, 2 * nf), f32)
    main = jnp.zeros((rows, 3 * dh), f32)
    for c in range(CHUNKS):
        for copy in copies[c]:
            copy.wait()
        part = slice(c * span, (c + 1) * span)
        tok = tok_ref[:, part]
        feat += nt(tok, fw_ref[:, part])
        main += nn(tok, jnp.concatenate([ww_ref[part, :], vw_ref[part, :]], axis=1))
    feat = feat.astype(bf16)
    window = main[:, : 2 * dh].astype(bf16)
    values = main[:, 2 * dh :].astype(bf16)
    feat_ref[...] = feat
    small_row, small_col = iotas(2 * nf)
    feat_t = nt((small_row == small_col).astype(bf16), feat).astype(bf16)
    feat_at = 2 * rows
    tail_at = feat_at + 2 * nf

    def put_keys(ref):
        ref[0:rows, :] = window[:, dh:]
        ref[rows : 2 * rows, :] = values
        put_wide(ref, feat_at, feat_t[nf:, :])
        ref[tail_at : tail_at + 16, :] = tail

    def put_query(ref):
        ref[0:rows, :] = window[:, :dh]
        ref[rows : 2 * rows, :] = do_ref[...]
        put_wide(ref, feat_at, feat_t[:nf, :])
        ref[tail_at : tail_at + 16, :] = tail

    put_keys(keys_ref)
    put_query(query_ref)
    for at, ref in enumerate(sends):
        later = jnp.bitwise_xor(me, max(2 * at, 1)) > me
        pl.when(later)(lambda ref=ref: put_keys(ref))
        pl.when(jnp.logical_not(later))(lambda ref=ref: put_query(ref))
    if packs:
        own_pack, *first_packs = rest[:packs]
        pack(me, ww_ref, vw_ref, fw_ref, own_pack)
        for n, ref in enumerate(first_packs):
            for d in range(2):
                piece = jnp.bitwise_xor(me, 4 * n + 2 * d)
                pack(piece, ww_ref, vw_ref, fw_ref, ref.at[d])

def stack_kernel(*refs):
    *parts, out_ref = refs
    for t, ref in enumerate(parts):
        out_ref[t] = ref[...]


def between(totals, low, high):
    at = lax.broadcasted_iota(jnp.int32, totals.shape, 0)
    return jnp.sum(jnp.where((at > low) & (at < high), totals, 0.0), axis=0, keepdims=True)


def over_partners(count, body, carry):
    if count <= 8:
        for d in range(1, count):
            carry = body(d, carry)
        return carry
    return lax.fori_loop(1, count, body, carry)


def query_kernel(ctx, count, recvs, *rest):
    recvs, rest = rest[:recvs], rest[recvs:]
    own_ref, query_ref, feat_ref, cum_ref, *rest = rest
    near_ref, p_ref, cums_ref = rest[-3:]
    att_ref, stat_ref, sheet_ref = rest[:3]

    def recv(d):
        return recvs[d - 1] if len(recvs) > 1 else recvs[0].at[d - 1]

    me = block_index(ctx)
    rows, dh = att_ref.shape
    nf = feat_ref.shape[1] // 2
    back = WINDOW // rows
    feat_at = 2 * rows
    tail_at = feat_at + 2 * nf
    scale = dh ** (-0.5)
    feat_scale = nf ** (-0.5)
    wq = query_ref[0:rows, :]
    do = query_ref[rows : 2 * rows, :]
    q = feat_ref[:, :nf]
    at_row, at_col = iotas(rows)
    own_cum = cum_row(own_ref, tail_at)
    cums_ref[pl.ds(me, 1), :] = own_cum
    near_ref[me] = own_ref[0 : 2 * rows, :]

    def gather(d, carry):
        j = partner(me, d, count)
        view = recv(d)
        near_ref[j] = view[0 : 2 * rows, :]
        cums_ref[pl.ds(j, 1), :] = cum_row(view, tail_at)
        return carry

    over_partners(count, gather, 0)

    def near(w):
        return near_ref.at[jnp.maximum(me - back + w, 0)]

    top = jnp.full((rows, LANES), MASKED, f32)
    for w in range(back + 1):
        keys = own_ref[0:rows, :] if w == back else near(w)[0:rows, :]
        s = nt(wq, keys) * scale
        if w == back:
            s = jnp.where(at_col <= at_row, s, MASKED)
        elif w == 0:
            s = jnp.where((at_col > at_row) & (me >= back), s, MASKED)
        else:
            s = jnp.where(me >= back - w, s, MASKED)
        p_ref[w] = s
        for h in range(0, rows, LANES):
            top = jnp.maximum(top, s[:, h : h + LANES])
    top = jnp.max(top, axis=1, keepdims=True)
    total = jnp.zeros((rows, LANES), f32)
    out = jnp.zeros((rows, dh), f32)
    for w in range(back + 1):
        p = jnp.exp(p_ref[w] - top)
        for h in range(0, rows, LANES):
            total += p[:, h : h + LANES]
        vals = own_ref[rows : 2 * rows, :] if w == back else near(w)[rows : 2 * rows, :]
        out += nn(p.astype(bf16), vals)
    total = jnp.sum(total, axis=1, keepdims=True)
    windowed = out * (1.0 / total)

    cum_c = cum_ref[...]
    growth = jnp.exp(cum_c)
    totals = cums_ref[:, rows - 1 : rows]

    def forward(d, carry):
        num, den = carry
        j = partner(me, d, count)
        view = recv(d)
        gap = between(totals, j - 1, me)
        es = jnp.where(j < me, jnp.exp(jnp.minimum(gap - cums_ref[pl.ds(j, 1), :], 0.0)), 0.0)
        x = nn(q, wide(view, feat_at, nf)) * feat_scale
        weight = (1.0 + x + 0.5 * x * x) * es
        for h in range(0, rows, LANES):
            den += weight[:, h : h + LANES]
        num += nn(weight.astype(bf16), view[rows : 2 * rows, :])
        return num, den

    num, den = over_partners(
        count, forward, (jnp.zeros((rows, dh), f32), jnp.zeros((rows, LANES), f32))
    )
    x = nn(q, wide(own_ref, feat_at, nf)) * feat_scale
    e = jnp.where(at_col <= at_row, jnp.exp(jnp.minimum(cum_c - own_cum, 0.0)), 0.0)
    weight = (1.0 + x + 0.5 * x * x) * e
    num = num * growth + nn(weight.astype(bf16), own_ref[rows : 2 * rows, :])
    den = den * growth
    for h in range(0, rows, LANES):
        den += weight[:, h : h + LANES]
    rden = 1.0 / jnp.sum(den, axis=1, keepdims=True)
    linear = num * rden
    att_ref[...] = (linear + windowed).astype(bf16)
    do_f = do.astype(f32)
    delta_w = jnp.sum(do_f * windowed, axis=1, keepdims=True)
    delta_l = jnp.sum(do_f * linear, axis=1, keepdims=True)
    lse = top + jnp.log(total)
    lane = lax.broadcasted_iota(jnp.int32, (rows, LANES), 1)
    sheet = jnp.where(lane == 0, lse, 0.0)
    sheet = jnp.where(lane == 1, delta_w, sheet)
    sheet = jnp.where(lane == 2, rden, sheet)
    sheet = jnp.where(lane == 3, delta_l, sheet)
    sheet = jnp.where(lane == 4, cum_c, sheet)
    sheet_ref[...] = sheet
    stat_ref[...] = jnp.transpose(sheet)[0:8, :]


def gradient_kernel(ctx, count, recvs, stats, *rest):
    recvs, rest = rest[:recvs], rest[recvs:]
    stats, rest = rest[:stats], rest[stats:]
    own_ref, query_ref, feat_ref, sheet_ref, *rest, total_ref = rest

    def recv(d):
        return recvs[d - 1] if len(recvs) > 1 else recvs[0].at[d - 1]

    me = block_index(ctx)
    rows = feat_ref.shape[0]
    dh = LANES
    nf = feat_ref.shape[1] // 2
    feat_at = 2 * rows
    scale = dh ** (-0.5)
    feat_scale = nf ** (-0.5)
    at_row, at_col = iotas(rows)
    apart = at_row - at_col
    wq, wk = query_ref[0:rows, :], own_ref[0:rows, :]
    do, v = query_ref[rows : 2 * rows, :], own_ref[rows : 2 * rows, :]
    q, k = feat_ref[:, :nf], feat_ref[:, nf:]
    lse_c, dw_c = sheet_ref[:, 0:1], sheet_ref[:, 1:2]
    rden_c, dl_c, cum_c = sheet_ref[:, 2:3], sheet_ref[:, 3:4], sheet_ref[:, 4:5]
    def stat(d):
        if len(stats) == 1:
            return stats[0].at[pl.ds(pl.multiple_of(8 * d, 8), 8)]
        at = d.bit_length()
        return stats[at].at[pl.ds(8 * (d - (1 << at >> 1)), 8)]

    mine_ref = stat(0)
    own_cum = mine_ref[4:5, :]
    total_ref[pl.ds(me, 1), :] = own_cum[:, rows - LANES :]

    def place(d, carry):
        total_ref[pl.ds(partner(me, d, count), 1), :] = stat(d)[4:5, rows - LANES :]
        return carry

    over_partners(count, place, 0)
    totals = total_ref[:, LANES - 1 :]
    growth_c = jnp.exp(cum_c) * rden_c
    tail_c = jnp.exp(own_cum[:, rows - 1 : rows] - cum_c)

    def pick(flag, a, b):
        return jnp.where(flag, a, b)

    s = nt(wq, wk) * scale
    causal = at_col <= at_row
    p = jnp.where(causal, jnp.exp(s - lse_c), 0.0)
    dp = nt(do, v)
    dwq = nn((p * (dp - dw_c)).astype(bf16), wk)
    x = nn(q, wide(own_ref, feat_at, nf)) * feat_scale
    e = jnp.where(causal, jnp.exp(jnp.minimum(cum_c - own_cum, 0.0)), 0.0) * rden_c
    dx = (dp - dl_c) * e * (1.0 + x)
    dqt = nt(wide(own_ref, feat_at, nf), dx.astype(bf16))

    s = nt(wk, wq) * scale
    causal = at_row <= at_col
    p = jnp.where(causal, jnp.exp(s - mine_ref[0:1, :]), 0.0)
    dp = nt(v, do)
    dwk = nn((p * (dp - mine_ref[1:2, :])).astype(bf16), wq)
    x = nn(k, wide(query_ref, feat_at, nf)) * feat_scale
    e = jnp.where(causal, jnp.exp(jnp.minimum(own_cum - cum_c, 0.0)), 0.0) * mine_ref[2:3, :]
    dx = (dp - mine_ref[3:4, :]) * e * (1.0 + x)
    dkt = nt(wide(query_ref, feat_at, nf), dx.astype(bf16))
    dv = nn((p + (1.0 + x + 0.5 * x * x) * e).astype(bf16), do)

    def step(d, carry):
        dwq, dqt, dwk, dkt, dv = carry
        j = partner(me, d, count)
        view = recv(d)
        mine = j < me
        sign = pick(mine, 1, -1)
        limit = WINDOW - jnp.abs(me - j) * rows
        rows_w = pick(mine, wq, wk)
        rows_v = pick(mine, do, v)
        rows_f = pick(mine, q, k)
        other_w = view[0:rows, :]
        other_v = view[rows : 2 * rows, :]
        other_f = wide(view, feat_at, nf)
        st = stat(d)
        zero = jnp.zeros((1, rows), f32)
        cum = st[4:5, :]
        gap = between(totals, jnp.minimum(me, j), jnp.maximum(me, j))
        e_r = jnp.exp(jnp.minimum(gap + pick(mine, cum[:, rows - 1 : rows] - cum, cum), 0.0))
        e_r = e_r * pick(mine, 1.0, st[2:3, :])
        e_c = pick(mine, growth_c, tail_c)

        s = nt(rows_w, other_w) * scale
        p = jnp.exp(s - pick(mine, lse_c, 0.0) - pick(mine, zero, st[0:1, :]))
        p = jnp.where(apart * sign < limit, p, 0.0)
        dp = nt(rows_v, other_v)
        ds = p * (dp - pick(mine, dw_c, 0.0) - pick(mine, zero, st[1:2, :]))
        more_w = nn(ds.astype(bf16), other_w)
        x = nn(rows_f, other_f) * feat_scale
        e = e_r * e_c
        dx = (dp - pick(mine, dl_c, 0.0) - pick(mine, zero, st[3:4, :])) * e * (1.0 + x)
        more_f = nt(other_f, dx.astype(bf16))
        more_v = nn((p + (1.0 + x + 0.5 * x * x) * e).astype(bf16), other_v)
        dwq = dwq + pick(mine, more_w, 0.0)
        dwk = dwk + pick(mine, 0.0, more_w)
        dqt = dqt + pick(mine, more_f, 0.0)
        dkt = dkt + pick(mine, 0.0, more_f)
        dv = dv + pick(mine, 0.0, more_v)
        return dwq, dqt, dwk, dkt, dv

    dwq, dqt, dwk, dkt, dv = over_partners(count, step, (dwq, dqt, dwk, dkt, dv))
    dwq, dwk = (dwq * scale).astype(bf16), (dwk * scale).astype(bf16)
    dv = dv.astype(bf16)
    dft = (jnp.concatenate([dqt, dkt], axis=0) * feat_scale).astype(bf16)
    (grad_ref,) = rest
    grad_ref[0:rows, :] = dwq
    grad_ref[rows : 2 * rows, :] = dwk
    grad_ref[2 * rows : 3 * rows, :] = dv
    put_wide(grad_ref, 3 * rows, dft)


def gather_rows(grad_ref, order, cat_ref, feat_ref):
    rows = cat_ref.shape[0]
    nf2 = feat_ref.shape[1] // len(order)
    for at, h in enumerate(order):
        for part in range(3):
            lane = (3 * at + part) * LANES
            cat_ref[:, lane : lane + LANES] = grad_ref[h, part * rows : (part + 1) * rows, :]
    dft = jnp.concatenate([wide(grad_ref.at[h], 3 * rows, nf2) for h in order], axis=0)
    feat_ref[...] = jnp.transpose(dft.astype(f32)).astype(bf16)


def cat_kernel(grad_ref, cat_ref, feat_ref):
    heads = grad_ref.shape[0]
    head = lax.axis_index("tp")
    order = [head] + [jnp.bitwise_xor(head, t) for t in range(1, heads)]
    gather_rows(grad_ref, order, cat_ref, feat_ref)


def columns_kernel(ctx, distances, cat_ref, feat_ref, ww_ref, vw_ref, fw_ref, *rest):
    pieces, firsts = rest[: len(distances)], rest[len(distances) : len(distances) + 4]
    out_ref, tile_ref, sems = rest[-3:]
    nf2 = fw_ref.shape[0]
    heads = feat_ref.shape[1] // nf2
    tile = 2 * LANES
    me = block_index(ctx)
    copies = []
    for n, (e, ref) in enumerate(zip(distances, pieces)):
        part = pl.ds(pl.multiple_of(jnp.bitwise_xor(me, e) * tile, tile), tile)
        views = [firsts[2 * (e % 2) + e // 4].at[e // 2 % 2]]
        views += [ref.at[t] for t in range(heads - 2)]
        main = [ww_ref[part, :], vw_ref[part, :]]
        main += [v[m * tile : (m + 1) * tile, :] for v in views for m in range(3)]
        feats = [fw_ref[:, part]] + [wide(v, 3 * tile, nf2) for v in views]
        total = nt(cat_ref[...], jnp.concatenate(main, axis=1))
        total += nn(feat_ref[...], jnp.concatenate(feats, axis=0))
        tile_ref[n] = total.astype(bf16)
        copies.append(pltpu.make_async_copy(tile_ref.at[n], out_ref.at[:, part], sems.at[n]))
        copies[-1].start()
    for copy in copies:
        copy.wait()


def merge_kernel(grad_ref, weight_ref, out_ref, cat_ref, feat_ref):
    heads = grad_ref.shape[0]
    tile = out_ref.shape[1]
    lanes = 3 * LANES
    nf2 = feat_ref.shape[1] // heads

    @pl.when(pl.program_id(0) == 0)
    def _():
        gather_rows(grad_ref, range(heads), cat_ref, feat_ref)

    views = [weight_ref.at[h] for h in range(heads)]
    main = jnp.concatenate([v[:, 0:lanes] for v in views], axis=1)
    feats = jnp.concatenate([v[:, lanes:] for v in views], axis=1)
    out_ref[...] = (nt(cat_ref[...], main) + nt(feat_ref[...], feats)).astype(bf16)


VMEM = pl.BlockSpec(memory_space=pltpu.VMEM)
HBM = pl.BlockSpec(memory_space=pltpu.HBM)
ANY = pl.BlockSpec(memory_space=pl.ANY)
params = pltpu.CompilerParams(vmem_limit_bytes=32 * 1024 * 1024)


def in_hbm(*arrays):
    return [pltpu.with_memory_space_constraint(a, pltpu.HBM) for a in arrays]


def cost(flops, nbytes, exps=0):
    return pl.CostEstimate(flops=flops, bytes_accessed=nbytes, transcendentals=exps)


def merge(grads, weights, rows, dim):
    heads, _, columns = weights.shape
    tile = 2 * LANES
    return pl.pallas_call(
        merge_kernel,
        out_shape=jax.ShapeDtypeStruct((rows, dim), bf16),
        grid=(dim // tile,),
        in_specs=[
            pl.BlockSpec(grads.shape, lambda i: (0, 0, 0)),
            pl.BlockSpec((heads, tile, columns), lambda i: (0, i, 0)),
        ],
        out_specs=pl.BlockSpec((rows, tile), lambda i: (0, i)),
        scratch_shapes=[
            pltpu.VMEM((rows, 3 * LANES * heads), bf16),
            pltpu.VMEM((rows, (columns - 3 * LANES) * heads), bf16),
        ],
        compiler_params=params,
        cost_estimate=cost(2 * rows * dim * heads * columns, heads * dim * columns * 2),
        name="head_sum",
    )(grads, weights)


def per_device(ctx, tokens, feature_weight, window_weight, value_weight, log_decay, out_grad):
    rows, dim = tokens.shape
    nf2 = feature_weight.shape[1]
    nf = nf2 // 2
    dh = value_weight.shape[1]
    columns = 3 * dh + nf2
    chips, count, heads = lax.axis_size(ctx[:-1]), lax.axis_size(ctx), lax.axis_size("tp")
    fw_t = feature_weight.T
    tile = 2 * LANES
    spread = heads == 4 and count * tile == dim and count == 8
    packs = []
    if spread:
        packs = [jax.ShapeDtypeStruct((columns * tile // LANES, LANES), bf16)]
        packs += [jax.ShapeDtypeStruct((2, *packs[0].shape), bf16)] * (chips // 2)

    payload = 2 * rows + 2 * nf + 16
    block = jax.ShapeDtypeStruct((payload, LANES), bf16)
    outs = pl.pallas_call(
        partial(project_kernel, ctx, len(packs)),
        out_shape=packs
        + [block] * (chips + 2)
        + [
            jax.ShapeDtypeStruct((rows, nf2), bf16),
            jax.ShapeDtypeStruct((rows, 1), f32),
            jax.ShapeDtypeStruct((dim, 2 * dh), bf16),
            jax.ShapeDtypeStruct((dim, dh), bf16),
            jax.ShapeDtypeStruct((nf2, dim), bf16),
        ],
        in_specs=[HBM] * 6,
        out_specs=[VMEM] * (len(packs) + chips + 7),
        scratch_shapes=[
            pltpu.VMEM((rows, dim), bf16),
            pltpu.VMEM((1, rows), f32),
            pltpu.VMEM((rows, dh), bf16),
            pltpu.SemaphoreType.DMA((CHUNKS, 4)),
            pltpu.SemaphoreType.DMA((2,)),
        ],
        compiler_params=params,
        cost_estimate=cost(1, 1024),
        name="project",
    )(*in_hbm(tokens, fw_t, window_weight, value_weight, log_decay.T, out_grad))
    *sends, own, query, feat, cum, ww, vw, fw = outs[len(packs) :]

    swap = [(0, 1), (1, 0)]
    recv = {}
    for d in range(1, chips):
        recv[2 * d] = lax.ppermute(sends[d], ctx[:-1], [(i, i ^ d) for i in range(chips)])
    recv[1] = lax.ppermute(sends[0], "core", swap)
    if spread:
        across = lax.ppermute(outs[0], "tp", [(z, z ^ 2) for z in range(heads)])
    for d in range(1, chips):
        if spread and d == chips - 1:
            across, recv = lax.optimization_barrier((across, recv))
        recv[2 * d + 1] = lax.ppermute(recv[2 * d], "core", swap)
    recv = [recv[d] for d in range(1, count)]
    if count > 8:
        recv = [jnp.stack(recv)]

    if spread:
        near = [across, lax.ppermute(across, "tp", [(z, z ^ 1) for z in range(heads)])]

    attended, stat, sheet = pl.pallas_call(
        lambda *refs: query_kernel(ctx, count, len(recv), *refs),
        out_shape=[
            jax.ShapeDtypeStruct((rows, dh), bf16),
            jax.ShapeDtypeStruct((8, rows), f32),
            jax.ShapeDtypeStruct((rows, LANES), f32),
        ],
        in_specs=[VMEM] * (len(recv) + 4),
        out_specs=[VMEM] * 3,
        scratch_shapes=[
            pltpu.VMEM((count, 2 * rows, dh), bf16),
            pltpu.VMEM((WINDOW // rows + 1, rows, rows), f32),
            pltpu.VMEM((count, rows), f32),
        ],
        compiler_params=params,
        cost_estimate=cost(1, 1024),
        name="query_side",
    )(*recv, own, query, feat, cum)
    stats = [stat]
    for name in reversed(ctx):
        if spread and len(stats) == 2:
            near, sent, stats = lax.optimization_barrier((near, outs[1], stats))
        held = stats[0] if len(stats) == 1 else jnp.concatenate(stats, axis=0)
        stats.append(lax.ppermute(held, name, swap))
    if count > 8:
        stats = [jnp.concatenate(stats, axis=0)]

    if spread:
        later, stats = lax.optimization_barrier((outs[2], stats))
        first = [lax.ppermute(p, "tp", [(z, z ^ 1) for z in range(heads)]) for p in (sent, later)]
        near, stats = lax.optimization_barrier((near, stats))
        pieces = [
            pl.pallas_call(
                stack_kernel,
                out_shape=jax.ShapeDtypeStruct((heads - 2, *packs[0].shape), bf16),
                in_specs=[VMEM] * (heads - 2),
                out_specs=VMEM,
                compiler_params=params,
                cost_estimate=cost(1, 1024),
                name="stack",
            )(*near)
        ]
        for d in range(1, chips):
            pieces.append(
                lax.ppermute(pieces[0], ctx[:-1], [(i, i ^ d) for i in range(chips)])
            )
        pieces[0], sheet = lax.optimization_barrier((pieces[0], sheet))

    grads = pl.pallas_call(
        lambda *refs: gradient_kernel(ctx, count, len(recv), len(stats), *refs),
        out_shape=jax.ShapeDtypeStruct((3 * rows + nf2 * rows // LANES, LANES), bf16),
        in_specs=[VMEM] * (len(recv) + len(stats) + 4),
        out_specs=VMEM,
        scratch_shapes=[pltpu.VMEM((count, LANES), f32)],
        compiler_params=params,
        cost_estimate=cost(1, 1024),
        name="gradients",
    )(*recv, *stats, own, query, feat, sheet)
    if not spread:
        weights = jnp.concatenate([window_weight, value_weight, feature_weight], axis=1)
        weights = lax.all_gather(weights, "tp")
        return (attended, merge(lax.all_gather(grads, "tp"), weights, rows, dim))

    first[0], grads = lax.optimization_barrier((first[0], grads))
    swapped = [lax.ppermute(pieces[0], "core", swap)]
    firsts = [lax.ppermute(first[0], "core", swap)]
    grads = lax.all_gather(grads, "tp")
    cat, feats = pl.pallas_call(
        cat_kernel,
        out_shape=[
            jax.ShapeDtypeStruct((rows, 3 * LANES * heads), bf16),
            jax.ShapeDtypeStruct((rows, nf2 * heads), bf16),
        ],
        in_specs=[VMEM],
        out_specs=[VMEM] * 2,
        compiler_params=params,
        cost_estimate=cost(1, 1024),
        name="cat",
    )(grads)
    pieces, first[1], _ = lax.optimization_barrier((pieces, first[1], cat))
    firsts = [*first, *firsts, lax.ppermute(first[1], "core", swap)]
    swapped += [lax.ppermute(p, "core", swap) for p in pieces[1:]]

    total = []
    for distances in ((0, 1, 2, 4, 6), (3, 5, 7)):
        parts = [(swapped if e % 2 else pieces)[e // 2] for e in distances]
        args = [cat, feats, ww, vw, fw, *parts, *firsts[:3], firsts[3 if total else 2], *total]
        total = [
            pl.pallas_call(
                partial(columns_kernel, ctx, distances),
                out_shape=jax.ShapeDtypeStruct((rows, dim), bf16),
                in_specs=[VMEM] * (9 + len(parts)) + [ANY] * len(total),
                out_specs=ANY,
                scratch_shapes=[
                    pltpu.VMEM((len(parts), rows, tile), bf16),
                    pltpu.SemaphoreType.DMA((len(parts),)),
                ],
                input_output_aliases={len(args) - 1: 0} if total else {},
                compiler_params=params,
                cost_estimate=cost(1, 1024),
                name="columns",
            )(*args)
        ]
    return (attended, total[0])


def solution(mesh):
    blocks, tp = mesh.devices.shape
    bits = blocks.bit_length() - 1
    assert blocks == 2**bits
    ctx = tuple(f"half{i}" for i in range(bits - 1)) + ("core",)
    split = Mesh(mesh.devices.reshape((2,) * bits + (tp,)), (*ctx, "tp"))
    in_specs = (
        P(ctx, None),
        P(None, "tp"),
        P(None, "tp"),
        P(None, "tp"),
        P(ctx, "tp"),
        P(ctx, "tp"),
    )
    out_specs = (P(ctx, "tp"), P(ctx, None))
    return jax.shard_map(
        partial(per_device, ctx),
        mesh=split,
        in_specs=in_specs,
        out_specs=out_specs,
        check_vma=False,
    )
```

```python
from functools import partial

import jax
import jax.numpy as jnp
from jax import lax
from jax.experimental import pallas as pl
from jax.experimental.pallas import tpu as pltpu
from jax.sharding import Mesh
from jax.sharding import PartitionSpec as P

WINDOW = 1024
LANES = 128
MASKED = -1e30
CHUNKS = 4
f32 = jnp.float32
bf16 = jnp.bfloat16


def nn(a, b):
    return lax.dot_general(a, b, (((1,), (0,)), ((), ())), preferred_element_type=f32)


def nt(a, b):
    return lax.dot_general(a, b, (((1,), (1,)), ((), ())), preferred_element_type=f32)


def partner(me, d, count):
    assert count & (count - 1) == 0
    return jnp.bitwise_xor(me, d)


def wide(view, start, count):
    return jnp.concatenate(
        [view[start : start + count, :], view[start + count : start + 2 * count, :]], axis=1
    )


def put_wide(ref, start, value):
    count = value.shape[0]
    for half in range(value.shape[1] // LANES):
        ref[start + half * count : start + (half + 1) * count, :] = value[
            :, half * LANES : (half + 1) * LANES
        ]


def cum_row(view, start):
    tail = view[start : start + 16, :].astype(f32)
    first = tail[0:1] + tail[2:3] + tail[4:5]
    second = tail[1:2] + tail[3:4] + tail[5:6]
    return jnp.concatenate([first, second], axis=1)


def iotas(rows):
    return (
        lax.broadcasted_iota(jnp.int32, (rows, rows), 0),
        lax.broadcasted_iota(jnp.int32, (rows, rows), 1),
    )


def block_index(ctx):
    place = 0
    for name in ctx:
        place = place * lax.axis_size(name) + lax.axis_index(name)
    return place


def pack(me, ww_ref, vw_ref, fw_ref, out_ref):
    nf2 = fw_ref.shape[0]
    tile = 2 * LANES
    at = pl.multiple_of(me * tile, tile)
    rows = pl.ds(at, tile)
    out_ref[0:tile, :] = ww_ref[rows, 0:LANES]
    out_ref[tile : 2 * tile, :] = ww_ref[rows, LANES:]
    out_ref[2 * tile : 3 * tile, :] = vw_ref[rows, :]
    put_wide(out_ref, 3 * tile, fw_ref[:, rows])


def project_kernel(ctx, packs, tok_hbm, fw_hbm, ww_hbm, vw_hbm, ld_hbm, do_hbm, *rest):
    *sends, keys_ref, query_ref, feat_ref, cum_ref, ww_ref, vw_ref, fw_ref = rest[packs:-5]
    tok_ref, ld_ref, do_ref, sems, small = rest[-5:]
    me = block_index(ctx)
    rows, dim = tok_ref.shape
    dh = do_ref.shape[1]
    nf = fw_ref.shape[0] // 2
    span = dim // CHUNKS
    copies = []
    for c in range(CHUNKS):
        part = pl.ds(c * span, span)
        copies.append([
            pltpu.make_async_copy(tok_hbm.at[:, part], tok_ref.at[:, part], sems.at[c, 0]),
            pltpu.make_async_copy(ww_hbm.at[part, :], ww_ref.at[part, :], sems.at[c, 1]),
            pltpu.make_async_copy(vw_hbm.at[part, :], vw_ref.at[part, :], sems.at[c, 2]),
            pltpu.make_async_copy(fw_hbm.at[:, part], fw_ref.at[:, part], sems.at[c, 3]),
        ])
    others = [
        pltpu.make_async_copy(ld_hbm, ld_ref, small.at[0]),
        pltpu.make_async_copy(do_hbm, do_ref, small.at[1]),
    ]
    for copy in others:
        copy.start()
    for group in copies:
        for at, copy in enumerate(group):
            copy.start(priority=min(at, 1))
    for copy in others:
        copy.wait()
    at_row, at_col = iotas(rows)
    ld_r = ld_ref[...]
    ld_c = jnp.sum(jnp.where(at_row == at_col, ld_r, 0.0), axis=1, keepdims=True)
    cum_r = jnp.sum(jnp.where(at_row <= at_col, ld_c, 0.0), axis=0, keepdims=True)
    cum_ref[...] = jnp.sum(jnp.where(at_col <= at_row, ld_r, 0.0), axis=1, keepdims=True)
    high = cum_r.astype(bf16)
    left = cum_r - high.astype(f32)
    mid = left.astype(bf16)
    low = (left - mid.astype(f32)).astype(bf16)
    pieces = [t[:, h : h + LANES].astype(f32) for t in (high, mid, low) for h in range(0, rows, LANES)]
    tail = jnp.concatenate(pieces + [jnp.zeros((10, LANES), f32)], axis=0).astype(bf16)

    feat = jnp.zeros((rows, 2 * nf), f32)
    main = jnp.zeros((rows, 3 * dh), f32)
    for c in range(CHUNKS):
        for copy in copies[c]:
            copy.wait()
        part = slice(c * span, (c + 1) * span)
        tok = tok_ref[:, part]
        feat += nt(tok, fw_ref[:, part])
        main += nn(tok, jnp.concatenate([ww_ref[part, :], vw_ref[part, :]], axis=1))
    feat = feat.astype(bf16)
    window = main[:, : 2 * dh].astype(bf16)
    values = main[:, 2 * dh :].astype(bf16)
    feat_ref[...] = feat
    small_row, small_col = iotas(2 * nf)
    feat_t = nt((small_row == small_col).astype(bf16), feat).astype(bf16)
    feat_at = 2 * rows
    tail_at = feat_at + 2 * nf

    def put_keys(ref):
        ref[0:rows, :] = window[:, dh:]
        ref[rows : 2 * rows, :] = values
        put_wide(ref, feat_at, feat_t[nf:, :])
        ref[tail_at : tail_at + 16, :] = tail

    def put_query(ref):
        ref[0:rows, :] = window[:, :dh]
        ref[rows : 2 * rows, :] = do_ref[...]
        put_wide(ref, feat_at, feat_t[:nf, :])
        ref[tail_at : tail_at + 16, :] = tail

    put_keys(keys_ref)
    put_query(query_ref)
    for at, ref in enumerate(sends):
        later = jnp.bitwise_xor(me, max(2 * at, 1)) > me
        pl.when(later)(lambda ref=ref: put_keys(ref))
        pl.when(jnp.logical_not(later))(lambda ref=ref: put_query(ref))
    if packs:
        own_pack, *first_packs = rest[:packs]
        pack(me, ww_ref, vw_ref, fw_ref, own_pack)
        for n, ref in enumerate(first_packs):
            for d in range(2):
                piece = jnp.bitwise_xor(me, 4 * n + 2 * d)
                pack(piece, ww_ref, vw_ref, fw_ref, ref.at[d])

def stack_kernel(*refs):
    *parts, out_ref = refs
    for t, ref in enumerate(parts):
        out_ref[t] = ref[...]


def between(totals, low, high):
    at = lax.broadcasted_iota(jnp.int32, totals.shape, 0)
    return jnp.sum(jnp.where((at > low) & (at < high), totals, 0.0), axis=0, keepdims=True)


def over_partners(count, body, carry):
    if count <= 8:
        for d in range(1, count):
            carry = body(d, carry)
        return carry
    return lax.fori_loop(1, count, body, carry)


def query_kernel(ctx, count, recvs, *rest):
    recvs, rest = rest[:recvs], rest[recvs:]
    own_ref, query_ref, feat_ref, cum_ref, *rest = rest
    near_ref, p_ref, cums_ref = rest[-3:]
    att_ref, stat_ref, sheet_ref = rest[:3]

    def recv(d):
        return recvs[d - 1] if len(recvs) > 1 else recvs[0].at[d - 1]

    me = block_index(ctx)
    rows, dh = att_ref.shape
    nf = feat_ref.shape[1] // 2
    back = WINDOW // rows
    feat_at = 2 * rows
    tail_at = feat_at + 2 * nf
    scale = dh ** (-0.5)
    feat_scale = nf ** (-0.5)
    wq = query_ref[0:rows, :]
    do = query_ref[rows : 2 * rows, :]
    q = feat_ref[:, :nf]
    at_row, at_col = iotas(rows)
    own_cum = cum_row(own_ref, tail_at)
    cums_ref[pl.ds(me, 1), :] = own_cum
    near_ref[me] = own_ref[0 : 2 * rows, :]

    def gather(d, carry):
        j = partner(me, d, count)
        view = recv(d)
        near_ref[j] = view[0 : 2 * rows, :]
        cums_ref[pl.ds(j, 1), :] = cum_row(view, tail_at)
        return carry

    over_partners(count, gather, 0)

    def near(w):
        return near_ref.at[jnp.maximum(me - back + w, 0)]

    top = jnp.full((rows, LANES), MASKED, f32)
    for w in range(back + 1):
        keys = own_ref[0:rows, :] if w == back else near(w)[0:rows, :]
        s = nt(wq, keys) * scale
        if w == back:
            s = jnp.where(at_col <= at_row, s, MASKED)
        elif w == 0:
            s = jnp.where((at_col > at_row) & (me >= back), s, MASKED)
        else:
            s = jnp.where(me >= back - w, s, MASKED)
        p_ref[w] = s
        for h in range(0, rows, LANES):
            top = jnp.maximum(top, s[:, h : h + LANES])
    top = jnp.max(top, axis=1, keepdims=True)
    total = jnp.zeros((rows, LANES), f32)
    out = jnp.zeros((rows, dh), f32)
    for w in range(back + 1):
        p = jnp.exp(p_ref[w] - top)
        for h in range(0, rows, LANES):
            total += p[:, h : h + LANES]
        vals = own_ref[rows : 2 * rows, :] if w == back else near(w)[rows : 2 * rows, :]
        out += nn(p.astype(bf16), vals)
    total = jnp.sum(total, axis=1, keepdims=True)
    windowed = out * (1.0 / total)

    cum_c = cum_ref[...]
    growth = jnp.exp(cum_c)
    totals = cums_ref[:, rows - 1 : rows]

    def forward(d, carry):
        num, den = carry
        j = partner(me, d, count)
        view = recv(d)
        gap = between(totals, j - 1, me)
        es = jnp.where(j < me, jnp.exp(jnp.minimum(gap - cums_ref[pl.ds(j, 1), :], 0.0)), 0.0)
        x = nn(q, wide(view, feat_at, nf)) * feat_scale
        weight = (1.0 + x + 0.5 * x * x) * es
        for h in range(0, rows, LANES):
            den += weight[:, h : h + LANES]
        num += nn(weight.astype(bf16), view[rows : 2 * rows, :])
        return num, den

    num, den = over_partners(
        count, forward, (jnp.zeros((rows, dh), f32), jnp.zeros((rows, LANES), f32))
    )
    x = nn(q, wide(own_ref, feat_at, nf)) * feat_scale
    e = jnp.where(at_col <= at_row, jnp.exp(jnp.minimum(cum_c - own_cum, 0.0)), 0.0)
    weight = (1.0 + x + 0.5 * x * x) * e
    num = num * growth + nn(weight.astype(bf16), own_ref[rows : 2 * rows, :])
    den = den * growth
    for h in range(0, rows, LANES):
        den += weight[:, h : h + LANES]
    rden = 1.0 / jnp.sum(den, axis=1, keepdims=True)
    linear = num * rden
    att_ref[...] = (linear + windowed).astype(bf16)
    do_f = do.astype(f32)
    delta_w = jnp.sum(do_f * windowed, axis=1, keepdims=True)
    delta_l = jnp.sum(do_f * linear, axis=1, keepdims=True)
    lse = top + jnp.log(total)
    lane = lax.broadcasted_iota(jnp.int32, (rows, LANES), 1)
    sheet = jnp.where(lane == 0, lse, 0.0)
    sheet = jnp.where(lane == 1, delta_w, sheet)
    sheet = jnp.where(lane == 2, rden, sheet)
    sheet = jnp.where(lane == 3, delta_l, sheet)
    sheet = jnp.where(lane == 4, cum_c, sheet)
    sheet_ref[...] = sheet
    stat_ref[...] = jnp.transpose(sheet)[0:8, :]


def gradient_kernel(ctx, count, recvs, stats, *rest):
    recvs, rest = rest[:recvs], rest[recvs:]
    stats, rest = rest[:stats], rest[stats:]
    own_ref, query_ref, feat_ref, sheet_ref, *rest, total_ref = rest

    def recv(d):
        return recvs[d - 1] if len(recvs) > 1 else recvs[0].at[d - 1]

    me = block_index(ctx)
    rows = feat_ref.shape[0]
    dh = LANES
    nf = feat_ref.shape[1] // 2
    feat_at = 2 * rows
    scale = dh ** (-0.5)
    feat_scale = nf ** (-0.5)
    at_row, at_col = iotas(rows)
    apart = at_row - at_col
    wq, wk = query_ref[0:rows, :], own_ref[0:rows, :]
    do, v = query_ref[rows : 2 * rows, :], own_ref[rows : 2 * rows, :]
    q, k = feat_ref[:, :nf], feat_ref[:, nf:]
    lse_c, dw_c = sheet_ref[:, 0:1], sheet_ref[:, 1:2]
    rden_c, dl_c, cum_c = sheet_ref[:, 2:3], sheet_ref[:, 3:4], sheet_ref[:, 4:5]
    def stat(d):
        if len(stats) == 1:
            return stats[0].at[pl.ds(pl.multiple_of(8 * d, 8), 8)]
        at = d.bit_length()
        return stats[at].at[pl.ds(8 * (d - (1 << at >> 1)), 8)]

    mine_ref = stat(0)
    own_cum = mine_ref[4:5, :]
    total_ref[pl.ds(me, 1), :] = own_cum[:, rows - LANES :]

    def place(d, carry):
        total_ref[pl.ds(partner(me, d, count), 1), :] = stat(d)[4:5, rows - LANES :]
        return carry

    over_partners(count, place, 0)
    totals = total_ref[:, LANES - 1 :]
    growth_c = jnp.exp(cum_c) * rden_c
    tail_c = jnp.exp(own_cum[:, rows - 1 : rows] - cum_c)

    def pick(flag, a, b):
        return jnp.where(flag, a, b)

    s = nt(wq, wk) * scale
    causal = at_col <= at_row
    p = jnp.where(causal, jnp.exp(s - lse_c), 0.0)
    dp = nt(do, v)
    dwq = nn((p * (dp - dw_c)).astype(bf16), wk)
    x = nn(q, wide(own_ref, feat_at, nf)) * feat_scale
    e = jnp.where(causal, jnp.exp(jnp.minimum(cum_c - own_cum, 0.0)), 0.0) * rden_c
    dx = (dp - dl_c) * e * (1.0 + x)
    dqt = nt(wide(own_ref, feat_at, nf), dx.astype(bf16))

    s = nt(wk, wq) * scale
    causal = at_row <= at_col
    p = jnp.where(causal, jnp.exp(s - mine_ref[0:1, :]), 0.0)
    dp = nt(v, do)
    dwk = nn((p * (dp - mine_ref[1:2, :])).astype(bf16), wq)
    x = nn(k, wide(query_ref, feat_at, nf)) * feat_scale
    e = jnp.where(causal, jnp.exp(jnp.minimum(own_cum - cum_c, 0.0)), 0.0) * mine_ref[2:3, :]
    dx = (dp - mine_ref[3:4, :]) * e * (1.0 + x)
    dkt = nt(wide(query_ref, feat_at, nf), dx.astype(bf16))
    dv = nn((p + (1.0 + x + 0.5 * x * x) * e).astype(bf16), do)

    def step(d, carry):
        dwq, dqt, dwk, dkt, dv = carry
        j = partner(me, d, count)
        view = recv(d)
        mine = j < me
        sign = pick(mine, 1, -1)
        limit = WINDOW - jnp.abs(me - j) * rows
        rows_w = pick(mine, wq, wk)
        rows_v = pick(mine, do, v)
        rows_f = pick(mine, q, k)
        other_w = view[0:rows, :]
        other_v = view[rows : 2 * rows, :]
        other_f = wide(view, feat_at, nf)
        st = stat(d)
        zero = jnp.zeros((1, rows), f32)
        cum = st[4:5, :]
        gap = between(totals, jnp.minimum(me, j), jnp.maximum(me, j))
        e_r = jnp.exp(jnp.minimum(gap + pick(mine, cum[:, rows - 1 : rows] - cum, cum), 0.0))
        e_r = e_r * pick(mine, 1.0, st[2:3, :])
        e_c = pick(mine, growth_c, tail_c)

        s = nt(rows_w, other_w) * scale
        p = jnp.exp(s - pick(mine, lse_c, 0.0) - pick(mine, zero, st[0:1, :]))
        p = jnp.where(apart * sign < limit, p, 0.0)
        dp = nt(rows_v, other_v)
        ds = p * (dp - pick(mine, dw_c, 0.0) - pick(mine, zero, st[1:2, :]))
        more_w = nn(ds.astype(bf16), other_w)
        x = nn(rows_f, other_f) * feat_scale
        e = e_r * e_c
        dx = (dp - pick(mine, dl_c, 0.0) - pick(mine, zero, st[3:4, :])) * e * (1.0 + x)
        more_f = nt(other_f, dx.astype(bf16))
        more_v = nn((p + (1.0 + x + 0.5 * x * x) * e).astype(bf16), other_v)
        dwq = dwq + pick(mine, more_w, 0.0)
        dwk = dwk + pick(mine, 0.0, more_w)
        dqt = dqt + pick(mine, more_f, 0.0)
        dkt = dkt + pick(mine, 0.0, more_f)
        dv = dv + pick(mine, 0.0, more_v)
        return dwq, dqt, dwk, dkt, dv

    dwq, dqt, dwk, dkt, dv = over_partners(count, step, (dwq, dqt, dwk, dkt, dv))
    dwq, dwk = (dwq * scale).astype(bf16), (dwk * scale).astype(bf16)
    dv = dv.astype(bf16)
    dft = (jnp.concatenate([dqt, dkt], axis=0) * feat_scale).astype(bf16)
    (grad_ref,) = rest
    grad_ref[0:rows, :] = dwq
    grad_ref[rows : 2 * rows, :] = dwk
    grad_ref[2 * rows : 3 * rows, :] = dv
    put_wide(grad_ref, 3 * rows, dft)


def gather_rows(grad_ref, order, cat_ref, feat_ref):
    rows = cat_ref.shape[0]
    nf2 = feat_ref.shape[1] // len(order)
    for at, h in enumerate(order):
        for part in range(3):
            lane = (3 * at + part) * LANES
            cat_ref[:, lane : lane + LANES] = grad_ref[h, part * rows : (part + 1) * rows, :]
    dft = jnp.concatenate([wide(grad_ref.at[h], 3 * rows, nf2) for h in order], axis=0)
    feat_ref[...] = jnp.transpose(dft.astype(f32)).astype(bf16)


def cat_kernel(grad_ref, cat_ref, feat_ref):
    heads = grad_ref.shape[0]
    head = lax.axis_index("tp")
    order = [head] + [jnp.bitwise_xor(head, t) for t in range(1, heads)]
    gather_rows(grad_ref, order, cat_ref, feat_ref)


def columns_kernel(ctx, distances, cat_ref, feat_ref, ww_ref, vw_ref, fw_ref, *rest):
    pieces, firsts = rest[: len(distances)], rest[len(distances) : len(distances) + 2]
    out_ref, tile_ref, sems = rest[-3:]
    nf2 = fw_ref.shape[0]
    heads = feat_ref.shape[1] // nf2
    tile = 2 * LANES
    me = block_index(ctx)
    copies = []
    for n, (e, ref) in enumerate(zip(distances, pieces)):
        part = pl.ds(pl.multiple_of(jnp.bitwise_xor(me, e) * tile, tile), tile)
        views = [firsts[e // 4].at[e // 2 % 2]]
        views += [ref.at[t] for t in range(heads - 2)]
        main = [ww_ref[part, :], vw_ref[part, :]]
        main += [v[m * tile : (m + 1) * tile, :] for v in views for m in range(3)]
        feats = [fw_ref[:, part]] + [wide(v, 3 * tile, nf2) for v in views]
        total = nt(cat_ref[...], jnp.concatenate(main, axis=1))
        total += nn(feat_ref[...], jnp.concatenate(feats, axis=0))
        tile_ref[n] = total.astype(bf16)
        copies.append(pltpu.make_async_copy(tile_ref.at[n], out_ref.at[:, part], sems.at[n]))
        copies[-1].start()
    for copy in copies:
        copy.wait()


def merge_kernel(grad_ref, weight_ref, out_ref, cat_ref, feat_ref):
    heads = grad_ref.shape[0]
    tile = out_ref.shape[1]
    lanes = 3 * LANES
    nf2 = feat_ref.shape[1] // heads

    @pl.when(pl.program_id(0) == 0)
    def _():
        gather_rows(grad_ref, range(heads), cat_ref, feat_ref)

    views = [weight_ref.at[h] for h in range(heads)]
    main = jnp.concatenate([v[:, 0:lanes] for v in views], axis=1)
    feats = jnp.concatenate([v[:, lanes:] for v in views], axis=1)
    out_ref[...] = (nt(cat_ref[...], main) + nt(feat_ref[...], feats)).astype(bf16)


VMEM = pl.BlockSpec(memory_space=pltpu.VMEM)
HBM = pl.BlockSpec(memory_space=pltpu.HBM)
ANY = pl.BlockSpec(memory_space=pl.ANY)
params = pltpu.CompilerParams(vmem_limit_bytes=32 * 1024 * 1024)


def in_hbm(*arrays):
    return [pltpu.with_memory_space_constraint(a, pltpu.HBM) for a in arrays]


def cost(flops, nbytes, exps=0):
    return pl.CostEstimate(flops=flops, bytes_accessed=nbytes, transcendentals=exps)


def merge(grads, weights, rows, dim):
    heads, _, columns = weights.shape
    tile = 2 * LANES
    return pl.pallas_call(
        merge_kernel,
        out_shape=jax.ShapeDtypeStruct((rows, dim), bf16),
        grid=(dim // tile,),
        in_specs=[
            pl.BlockSpec(grads.shape, lambda i: (0, 0, 0)),
            pl.BlockSpec((heads, tile, columns), lambda i: (0, i, 0)),
        ],
        out_specs=pl.BlockSpec((rows, tile), lambda i: (0, i)),
        scratch_shapes=[
            pltpu.VMEM((rows, 3 * LANES * heads), bf16),
            pltpu.VMEM((rows, (columns - 3 * LANES) * heads), bf16),
        ],
        compiler_params=params,
        cost_estimate=cost(2 * rows * dim * heads * columns, heads * dim * columns * 2),
        name="head_sum",
    )(grads, weights)


def per_device(ctx, tokens, feature_weight, window_weight, value_weight, log_decay, out_grad):
    rows, dim = tokens.shape
    nf2 = feature_weight.shape[1]
    nf = nf2 // 2
    dh = value_weight.shape[1]
    columns = 3 * dh + nf2
    chips, count, heads = lax.axis_size(ctx[:-1]), lax.axis_size(ctx), lax.axis_size("tp")
    fw_t = feature_weight.T
    tile = 2 * LANES
    spread = heads == 4 and count * tile == dim and count == 8
    packs = []
    if spread:
        packs = [jax.ShapeDtypeStruct((columns * tile // LANES, LANES), bf16)]
        packs += [jax.ShapeDtypeStruct((2, *packs[0].shape), bf16)] * (chips // 2)

    payload = 2 * rows + 2 * nf + 16
    block = jax.ShapeDtypeStruct((payload, LANES), bf16)
    outs = pl.pallas_call(
        partial(project_kernel, ctx, len(packs)),
        out_shape=packs
        + [block] * (chips + 2)
        + [
            jax.ShapeDtypeStruct((rows, nf2), bf16),
            jax.ShapeDtypeStruct((rows, 1), f32),
            jax.ShapeDtypeStruct((dim, 2 * dh), bf16),
            jax.ShapeDtypeStruct((dim, dh), bf16),
            jax.ShapeDtypeStruct((nf2, dim), bf16),
        ],
        in_specs=[HBM] * 6,
        out_specs=[VMEM] * (len(packs) + chips + 7),
        scratch_shapes=[
            pltpu.VMEM((rows, dim), bf16),
            pltpu.VMEM((1, rows), f32),
            pltpu.VMEM((rows, dh), bf16),
            pltpu.SemaphoreType.DMA((CHUNKS, 4)),
            pltpu.SemaphoreType.DMA((2,)),
        ],
        compiler_params=params,
        cost_estimate=cost(1, 1024),
        name="project",
    )(*in_hbm(tokens, fw_t, window_weight, value_weight, log_decay.T, out_grad))
    *sends, own, query, feat, cum, ww, vw, fw = outs[len(packs) :]

    swap = [(0, 1), (1, 0)]
    recv = {}
    for d in range(1, chips):
        recv[2 * d] = lax.ppermute(sends[d], ctx[:-1], [(i, i ^ d) for i in range(chips)])
    recv[1] = lax.ppermute(sends[0], "core", swap)
    if spread:
        across = lax.ppermute(outs[0], "tp", [(z, z ^ 2) for z in range(heads)])
    for d in range(1, chips):
        if spread and d == chips - 1:
            across, recv[2 * d] = lax.optimization_barrier((across, recv[2 * d]))
        recv[2 * d + 1] = lax.ppermute(recv[2 * d], "core", swap)
    recv = [recv[d] for d in range(1, count)]
    if count > 8:
        recv = [jnp.stack(recv)]

    if spread:
        across, recv = lax.optimization_barrier((across, recv))
        near = [across, lax.ppermute(across, "tp", [(z, z ^ 1) for z in range(heads)])]

    attended, stat, sheet = pl.pallas_call(
        lambda *refs: query_kernel(ctx, count, len(recv), *refs),
        out_shape=[
            jax.ShapeDtypeStruct((rows, dh), bf16),
            jax.ShapeDtypeStruct((8, rows), f32),
            jax.ShapeDtypeStruct((rows, LANES), f32),
        ],
        in_specs=[VMEM] * (len(recv) + 4),
        out_specs=[VMEM] * 3,
        scratch_shapes=[
            pltpu.VMEM((count, 2 * rows, dh), bf16),
            pltpu.VMEM((WINDOW // rows + 1, rows, rows), f32),
            pltpu.VMEM((count, rows), f32),
        ],
        compiler_params=params,
        cost_estimate=cost(1, 1024),
        name="query_side",
    )(*recv, own, query, feat, cum)
    stats = [stat]
    for name in reversed(ctx):
        if spread and len(stats) == 2:
            near, sent, stats = lax.optimization_barrier((near, outs[1], stats))
        held = stats[0] if len(stats) == 1 else jnp.concatenate(stats, axis=0)
        stats.append(lax.ppermute(held, name, swap))
    if count > 8:
        stats = [jnp.concatenate(stats, axis=0)]

    if spread:
        later, stats = lax.optimization_barrier((outs[2], stats))
        first = [lax.ppermute(p, "tp", [(z, z ^ 1) for z in range(heads)]) for p in (sent, later)]
        near, stats = lax.optimization_barrier((near, stats))
        pieces = [
            pl.pallas_call(
                stack_kernel,
                out_shape=jax.ShapeDtypeStruct((heads - 2, *packs[0].shape), bf16),
                in_specs=[VMEM] * (heads - 2),
                out_specs=VMEM,
                compiler_params=params,
                cost_estimate=cost(1, 1024),
                name="stack",
            )(*near)
        ]
        for d in range(1, chips):
            pieces.append(
                lax.ppermute(pieces[0], ctx[:-1], [(i, i ^ d) for i in range(chips)])
            )
        pieces[0], sheet = lax.optimization_barrier((pieces[0], sheet))

    grads = pl.pallas_call(
        lambda *refs: gradient_kernel(ctx, count, len(recv), len(stats), *refs),
        out_shape=jax.ShapeDtypeStruct((3 * rows + nf2 * rows // LANES, LANES), bf16),
        in_specs=[VMEM] * (len(recv) + len(stats) + 4),
        out_specs=VMEM,
        scratch_shapes=[pltpu.VMEM((count, LANES), f32)],
        compiler_params=params,
        cost_estimate=cost(1, 1024),
        name="gradients",
    )(*recv, *stats, own, query, feat, sheet)
    if not spread:
        weights = jnp.concatenate([window_weight, value_weight, feature_weight], axis=1)
        weights = lax.all_gather(weights, "tp")
        return (attended, merge(lax.all_gather(grads, "tp"), weights, rows, dim))

    first[0], grads = lax.optimization_barrier((first[0], grads))
    grads = lax.all_gather(grads, "tp")
    cat, feats = pl.pallas_call(
        cat_kernel,
        out_shape=[
            jax.ShapeDtypeStruct((rows, 3 * LANES * heads), bf16),
            jax.ShapeDtypeStruct((rows, nf2 * heads), bf16),
        ],
        in_specs=[VMEM],
        out_specs=[VMEM] * 2,
        compiler_params=params,
        cost_estimate=cost(1, 1024),
        name="cat",
    )(grads)
    pieces, first, _ = lax.optimization_barrier((pieces, first, cat))
    other_first = [lax.ppermute(p, "core", swap) for p in first]
    swapped = [lax.ppermute(p, "core", swap) for p in pieces]

    total = []
    for distances in ((0, 2, 4, 6), (1, 3, 5, 7)):
        parts = [(swapped if e % 2 else pieces)[e // 2] for e in distances]
        args = [cat, feats, ww, vw, fw, *parts, *(other_first if total else first), *total]
        total = [
            pl.pallas_call(
                partial(columns_kernel, ctx, distances),
                out_shape=jax.ShapeDtypeStruct((rows, dim), bf16),
                in_specs=[VMEM] * (7 + len(parts)) + [ANY] * len(total),
                out_specs=ANY,
                scratch_shapes=[
                    pltpu.VMEM((len(parts), rows, tile), bf16),
                    pltpu.SemaphoreType.DMA((len(parts),)),
                ],
                input_output_aliases={len(args) - 1: 0} if total else {},
                compiler_params=params,
                cost_estimate=cost(1, 1024),
                name="columns",
            )(*args)
        ]
    return (attended, total[0])


def solution(mesh):
    blocks, tp = mesh.devices.shape
    bits = blocks.bit_length() - 1
    assert blocks == 2**bits
    ctx = tuple(f"half{i}" for i in range(bits - 1)) + ("core",)
    split = Mesh(mesh.devices.reshape((2,) * bits + (tp,)), (*ctx, "tp"))
    in_specs = (
        P(ctx, None),
        P(None, "tp"),
        P(None, "tp"),
        P(None, "tp"),
        P(ctx, "tp"),
        P(ctx, "tp"),
    )
    out_specs = (P(ctx, "tp"), P(ctx, None))
    return jax.shard_map(
        partial(per_device, ctx),
        mesh=split,
        in_specs=in_specs,
        out_specs=out_specs,
        check_vma=False,
    )
```

```python
from functools import partial

import jax
import jax.numpy as jnp
from jax import lax
from jax.experimental import pallas as pl
from jax.experimental.pallas import tpu as pltpu
from jax.sharding import Mesh
from jax.sharding import PartitionSpec as P

WINDOW = 1024
LANES = 128
MASKED = -1e30
CHUNKS = 4
f32 = jnp.float32
bf16 = jnp.bfloat16


def nn(a, b):
    return lax.dot_general(a, b, (((1,), (0,)), ((), ())), preferred_element_type=f32)


def nt(a, b):
    return lax.dot_general(a, b, (((1,), (1,)), ((), ())), preferred_element_type=f32)


def partner(me, d, count):
    assert count & (count - 1) == 0
    return jnp.bitwise_xor(me, d)


def wide(view, start, count):
    return jnp.concatenate(
        [view[start : start + count, :], view[start + count : start + 2 * count, :]], axis=1
    )


def put_wide(ref, start, value):
    count = value.shape[0]
    for half in range(value.shape[1] // LANES):
        ref[start + half * count : start + (half + 1) * count, :] = value[
            :, half * LANES : (half + 1) * LANES
        ]


def cum_row(view, start):
    tail = view[start : start + 16, :].astype(f32)
    first = tail[0:1] + tail[2:3] + tail[4:5]
    second = tail[1:2] + tail[3:4] + tail[5:6]
    return jnp.concatenate([first, second], axis=1)


def iotas(rows):
    return (
        lax.broadcasted_iota(jnp.int32, (rows, rows), 0),
        lax.broadcasted_iota(jnp.int32, (rows, rows), 1),
    )


def block_index(ctx):
    place = 0
    for name in ctx:
        place = place * lax.axis_size(name) + lax.axis_index(name)
    return place


def pack(me, ww_ref, vw_ref, fw_ref, out_ref):
    nf2 = fw_ref.shape[0]
    tile = 2 * LANES
    at = pl.multiple_of(me * tile, tile)
    rows = pl.ds(at, tile)
    out_ref[0:tile, :] = ww_ref[rows, 0:LANES]
    out_ref[tile : 2 * tile, :] = ww_ref[rows, LANES:]
    out_ref[2 * tile : 3 * tile, :] = vw_ref[rows, :]
    put_wide(out_ref, 3 * tile, fw_ref[:, rows])


def project_kernel(ctx, packs, tok_hbm, fw_hbm, ww_hbm, vw_hbm, ld_hbm, do_hbm, *rest):
    *sends, keys_ref, query_ref, feat_ref, cum_ref, ww_ref, vw_ref, fw_ref = rest[packs:-5]
    tok_ref, ld_ref, do_ref, sems, small = rest[-5:]
    me = block_index(ctx)
    rows, dim = tok_ref.shape
    dh = do_ref.shape[1]
    nf = fw_ref.shape[0] // 2
    span = dim // CHUNKS
    copies = []
    for c in range(CHUNKS):
        part = pl.ds(c * span, span)
        copies.append([
            pltpu.make_async_copy(tok_hbm.at[:, part], tok_ref.at[:, part], sems.at[c, 0]),
            pltpu.make_async_copy(ww_hbm.at[part, :], ww_ref.at[part, :], sems.at[c, 1]),
            pltpu.make_async_copy(vw_hbm.at[part, :], vw_ref.at[part, :], sems.at[c, 2]),
            pltpu.make_async_copy(fw_hbm.at[:, part], fw_ref.at[:, part], sems.at[c, 3]),
        ])
    others = [
        pltpu.make_async_copy(ld_hbm, ld_ref, small.at[0]),
        pltpu.make_async_copy(do_hbm, do_ref, small.at[1]),
    ]
    for copy in others:
        copy.start()
    for group in copies:
        for at, copy in enumerate(group):
            copy.start(priority=min(at, 1))
    for copy in others:
        copy.wait()
    at_row, at_col = iotas(rows)
    ld_r = ld_ref[...]
    ld_c = jnp.sum(jnp.where(at_row == at_col, ld_r, 0.0), axis=1, keepdims=True)
    cum_r = jnp.sum(jnp.where(at_row <= at_col, ld_c, 0.0), axis=0, keepdims=True)
    cum_ref[...] = jnp.sum(jnp.where(at_col <= at_row, ld_r, 0.0), axis=1, keepdims=True)
    high = cum_r.astype(bf16)
    left = cum_r - high.astype(f32)
    mid = left.astype(bf16)
    low = (left - mid.astype(f32)).astype(bf16)
    pieces = [t[:, h : h + LANES].astype(f32) for t in (high, mid, low) for h in range(0, rows, LANES)]
    tail = jnp.concatenate(pieces + [jnp.zeros((10, LANES), f32)], axis=0).astype(bf16)

    feat = jnp.zeros((rows, 2 * nf), f32)
    main = jnp.zeros((rows, 3 * dh), f32)
    for c in range(CHUNKS):
        for copy in copies[c]:
            copy.wait()
        part = slice(c * span, (c + 1) * span)
        tok = tok_ref[:, part]
        feat += nt(tok, fw_ref[:, part])
        main += nn(tok, jnp.concatenate([ww_ref[part, :], vw_ref[part, :]], axis=1))
    feat = feat.astype(bf16)
    window = main[:, : 2 * dh].astype(bf16)
    values = main[:, 2 * dh :].astype(bf16)
    feat_ref[...] = feat
    small_row, small_col = iotas(2 * nf)
    feat_t = nt((small_row == small_col).astype(bf16), feat).astype(bf16)
    feat_at = 2 * rows
    tail_at = feat_at + 2 * nf

    def put_keys(ref):
        ref[0:rows, :] = window[:, dh:]
        ref[rows : 2 * rows, :] = values
        put_wide(ref, feat_at, feat_t[nf:, :])
        ref[tail_at : tail_at + 16, :] = tail

    def put_query(ref):
        ref[0:rows, :] = window[:, :dh]
        ref[rows : 2 * rows, :] = do_ref[...]
        put_wide(ref, feat_at, feat_t[:nf, :])
        ref[tail_at : tail_at + 16, :] = tail

    put_keys(keys_ref)
    put_query(query_ref)
    for at, ref in enumerate(sends):
        later = jnp.bitwise_xor(me, max(2 * at, 1)) > me
        pl.when(later)(lambda ref=ref: put_keys(ref))
        pl.when(jnp.logical_not(later))(lambda ref=ref: put_query(ref))
    if packs:
        own_pack, other_pack = rest[:packs]
        pack(me, ww_ref, vw_ref, fw_ref, own_pack)
        for d in range(other_pack.shape[0]):
            piece = jnp.bitwise_xor(me, 2 * d + 2)
            pack(piece, ww_ref, vw_ref, fw_ref, other_pack.at[d])

def stack_kernel(*refs):
    *parts, out_ref = refs
    for t, ref in enumerate(parts):
        out_ref[t] = ref[...]


def between(totals, low, high):
    at = lax.broadcasted_iota(jnp.int32, totals.shape, 0)
    return jnp.sum(jnp.where((at > low) & (at < high), totals, 0.0), axis=0, keepdims=True)


def over_partners(count, body, carry):
    if count <= 8:
        for d in range(1, count):
            carry = body(d, carry)
        return carry
    return lax.fori_loop(1, count, body, carry)


def query_kernel(ctx, count, recvs, *rest):
    recvs, rest = rest[:recvs], rest[recvs:]
    own_ref, query_ref, feat_ref, cum_ref, *rest = rest
    near_ref, p_ref, cums_ref = rest[-3:]
    att_ref, stat_ref, sheet_ref = rest[:3]

    def recv(d):
        return recvs[d - 1] if len(recvs) > 1 else recvs[0].at[d - 1]

    me = block_index(ctx)
    rows, dh = att_ref.shape
    nf = feat_ref.shape[1] // 2
    back = WINDOW // rows
    feat_at = 2 * rows
    tail_at = feat_at + 2 * nf
    scale = dh ** (-0.5)
    feat_scale = nf ** (-0.5)
    wq = query_ref[0:rows, :]
    do = query_ref[rows : 2 * rows, :]
    q = feat_ref[:, :nf]
    at_row, at_col = iotas(rows)
    own_cum = cum_row(own_ref, tail_at)
    cums_ref[pl.ds(me, 1), :] = own_cum
    near_ref[me] = own_ref[0 : 2 * rows, :]

    def gather(d, carry):
        j = partner(me, d, count)
        view = recv(d)
        near_ref[j] = view[0 : 2 * rows, :]
        cums_ref[pl.ds(j, 1), :] = cum_row(view, tail_at)
        return carry

    over_partners(count, gather, 0)

    def near(w):
        return near_ref.at[jnp.maximum(me - back + w, 0)]

    top = jnp.full((rows, LANES), MASKED, f32)
    for w in range(back + 1):
        keys = own_ref[0:rows, :] if w == back else near(w)[0:rows, :]
        s = nt(wq, keys) * scale
        if w == back:
            s = jnp.where(at_col <= at_row, s, MASKED)
        elif w == 0:
            s = jnp.where((at_col > at_row) & (me >= back), s, MASKED)
        else:
            s = jnp.where(me >= back - w, s, MASKED)
        p_ref[w] = s
        for h in range(0, rows, LANES):
            top = jnp.maximum(top, s[:, h : h + LANES])
    top = jnp.max(top, axis=1, keepdims=True)
    total = jnp.zeros((rows, LANES), f32)
    out = jnp.zeros((rows, dh), f32)
    for w in range(back + 1):
        p = jnp.exp(p_ref[w] - top)
        for h in range(0, rows, LANES):
            total += p[:, h : h + LANES]
        vals = own_ref[rows : 2 * rows, :] if w == back else near(w)[rows : 2 * rows, :]
        out += nn(p.astype(bf16), vals)
    total = jnp.sum(total, axis=1, keepdims=True)
    windowed = out * (1.0 / total)

    cum_c = cum_ref[...]
    growth = jnp.exp(cum_c)
    totals = cums_ref[:, rows - 1 : rows]

    def forward(d, carry):
        num, den = carry
        j = partner(me, d, count)
        view = recv(d)
        gap = between(totals, j - 1, me)
        es = jnp.where(j < me, jnp.exp(jnp.minimum(gap - cums_ref[pl.ds(j, 1), :], 0.0)), 0.0)
        x = nn(q, wide(view, feat_at, nf)) * feat_scale
        weight = (1.0 + x + 0.5 * x * x) * es
        for h in range(0, rows, LANES):
            den += weight[:, h : h + LANES]
        num += nn(weight.astype(bf16), view[rows : 2 * rows, :])
        return num, den

    num, den = over_partners(
        count, forward, (jnp.zeros((rows, dh), f32), jnp.zeros((rows, LANES), f32))
    )
    x = nn(q, wide(own_ref, feat_at, nf)) * feat_scale
    e = jnp.where(at_col <= at_row, jnp.exp(jnp.minimum(cum_c - own_cum, 0.0)), 0.0)
    weight = (1.0 + x + 0.5 * x * x) * e
    num = num * growth + nn(weight.astype(bf16), own_ref[rows : 2 * rows, :])
    den = den * growth
    for h in range(0, rows, LANES):
        den += weight[:, h : h + LANES]
    rden = 1.0 / jnp.sum(den, axis=1, keepdims=True)
    linear = num * rden
    att_ref[...] = (linear + windowed).astype(bf16)
    do_f = do.astype(f32)
    delta_w = jnp.sum(do_f * windowed, axis=1, keepdims=True)
    delta_l = jnp.sum(do_f * linear, axis=1, keepdims=True)
    lse = top + jnp.log(total)
    lane = lax.broadcasted_iota(jnp.int32, (rows, LANES), 1)
    sheet = jnp.where(lane == 0, lse, 0.0)
    sheet = jnp.where(lane == 1, delta_w, sheet)
    sheet = jnp.where(lane == 2, rden, sheet)
    sheet = jnp.where(lane == 3, delta_l, sheet)
    sheet = jnp.where(lane == 4, cum_c, sheet)
    sheet_ref[...] = sheet
    stat_ref[...] = jnp.transpose(sheet)[0:8, :]


def gradient_kernel(ctx, count, recvs, stats, *rest):
    recvs, rest = rest[:recvs], rest[recvs:]
    stats, rest = rest[:stats], rest[stats:]
    own_ref, query_ref, feat_ref, sheet_ref, *rest, total_ref = rest

    def recv(d):
        return recvs[d - 1] if len(recvs) > 1 else recvs[0].at[d - 1]

    me = block_index(ctx)
    rows = feat_ref.shape[0]
    dh = LANES
    nf = feat_ref.shape[1] // 2
    feat_at = 2 * rows
    scale = dh ** (-0.5)
    feat_scale = nf ** (-0.5)
    at_row, at_col = iotas(rows)
    apart = at_row - at_col
    wq, wk = query_ref[0:rows, :], own_ref[0:rows, :]
    do, v = query_ref[rows : 2 * rows, :], own_ref[rows : 2 * rows, :]
    q, k = feat_ref[:, :nf], feat_ref[:, nf:]
    lse_c, dw_c = sheet_ref[:, 0:1], sheet_ref[:, 1:2]
    rden_c, dl_c, cum_c = sheet_ref[:, 2:3], sheet_ref[:, 3:4], sheet_ref[:, 4:5]
    def stat(d):
        if len(stats) == 1:
            return stats[0].at[pl.ds(pl.multiple_of(8 * d, 8), 8)]
        at = d.bit_length()
        return stats[at].at[pl.ds(8 * (d - (1 << at >> 1)), 8)]

    mine_ref = stat(0)
    own_cum = mine_ref[4:5, :]
    total_ref[pl.ds(me, 1), :] = own_cum[:, rows - LANES :]

    def place(d, carry):
        total_ref[pl.ds(partner(me, d, count), 1), :] = stat(d)[4:5, rows - LANES :]
        return carry

    over_partners(count, place, 0)
    totals = total_ref[:, LANES - 1 :]
    growth_c = jnp.exp(cum_c) * rden_c
    tail_c = jnp.exp(own_cum[:, rows - 1 : rows] - cum_c)

    def pick(flag, a, b):
        return jnp.where(flag, a, b)

    s = nt(wq, wk) * scale
    causal = at_col <= at_row
    p = jnp.where(causal, jnp.exp(s - lse_c), 0.0)
    dp = nt(do, v)
    dwq = nn((p * (dp - dw_c)).astype(bf16), wk)
    x = nn(q, wide(own_ref, feat_at, nf)) * feat_scale
    e = jnp.where(causal, jnp.exp(jnp.minimum(cum_c - own_cum, 0.0)), 0.0) * rden_c
    dx = (dp - dl_c) * e * (1.0 + x)
    dqt = nt(wide(own_ref, feat_at, nf), dx.astype(bf16))

    s = nt(wk, wq) * scale
    causal = at_row <= at_col
    p = jnp.where(causal, jnp.exp(s - mine_ref[0:1, :]), 0.0)
    dp = nt(v, do)
    dwk = nn((p * (dp - mine_ref[1:2, :])).astype(bf16), wq)
    x = nn(k, wide(query_ref, feat_at, nf)) * feat_scale
    e = jnp.where(causal, jnp.exp(jnp.minimum(own_cum - cum_c, 0.0)), 0.0) * mine_ref[2:3, :]
    dx = (dp - mine_ref[3:4, :]) * e * (1.0 + x)
    dkt = nt(wide(query_ref, feat_at, nf), dx.astype(bf16))
    dv = nn((p + (1.0 + x + 0.5 * x * x) * e).astype(bf16), do)

    def step(d, carry):
        dwq, dqt, dwk, dkt, dv = carry
        j = partner(me, d, count)
        view = recv(d)
        mine = j < me
        sign = pick(mine, 1, -1)
        limit = WINDOW - jnp.abs(me - j) * rows
        rows_w = pick(mine, wq, wk)
        rows_v = pick(mine, do, v)
        rows_f = pick(mine, q, k)
        other_w = view[0:rows, :]
        other_v = view[rows : 2 * rows, :]
        other_f = wide(view, feat_at, nf)
        st = stat(d)
        zero = jnp.zeros((1, rows), f32)
        cum = st[4:5, :]
        gap = between(totals, jnp.minimum(me, j), jnp.maximum(me, j))
        e_r = jnp.exp(jnp.minimum(gap + pick(mine, cum[:, rows - 1 : rows] - cum, cum), 0.0))
        e_r = e_r * pick(mine, 1.0, st[2:3, :])
        e_c = pick(mine, growth_c, tail_c)

        s = nt(rows_w, other_w) * scale
        p = jnp.exp(s - pick(mine, lse_c, 0.0) - pick(mine, zero, st[0:1, :]))
        p = jnp.where(apart * sign < limit, p, 0.0)
        dp = nt(rows_v, other_v)
        ds = p * (dp - pick(mine, dw_c, 0.0) - pick(mine, zero, st[1:2, :]))
        more_w = nn(ds.astype(bf16), other_w)
        x = nn(rows_f, other_f) * feat_scale
        e = e_r * e_c
        dx = (dp - pick(mine, dl_c, 0.0) - pick(mine, zero, st[3:4, :])) * e * (1.0 + x)
        more_f = nt(other_f, dx.astype(bf16))
        more_v = nn((p + (1.0 + x + 0.5 * x * x) * e).astype(bf16), other_v)
        dwq = dwq + pick(mine, more_w, 0.0)
        dwk = dwk + pick(mine, 0.0, more_w)
        dqt = dqt + pick(mine, more_f, 0.0)
        dkt = dkt + pick(mine, 0.0, more_f)
        dv = dv + pick(mine, 0.0, more_v)
        return dwq, dqt, dwk, dkt, dv

    dwq, dqt, dwk, dkt, dv = over_partners(count, step, (dwq, dqt, dwk, dkt, dv))
    dwq, dwk = (dwq * scale).astype(bf16), (dwk * scale).astype(bf16)
    dv = dv.astype(bf16)
    dft = (jnp.concatenate([dqt, dkt], axis=0) * feat_scale).astype(bf16)
    (grad_ref,) = rest
    grad_ref[0:rows, :] = dwq
    grad_ref[rows : 2 * rows, :] = dwk
    grad_ref[2 * rows : 3 * rows, :] = dv
    put_wide(grad_ref, 3 * rows, dft)


def gather_rows(grad_ref, order, cat_ref, feat_ref):
    rows = cat_ref.shape[0]
    nf2 = feat_ref.shape[1] // len(order)
    for at, h in enumerate(order):
        for part in range(3):
            lane = (3 * at + part) * LANES
            cat_ref[:, lane : lane + LANES] = grad_ref[h, part * rows : (part + 1) * rows, :]
    dft = jnp.concatenate([wide(grad_ref.at[h], 3 * rows, nf2) for h in order], axis=0)
    feat_ref[...] = jnp.transpose(dft.astype(f32)).astype(bf16)


def cat_kernel(grad_ref, cat_ref, feat_ref):
    heads = grad_ref.shape[0]
    head = lax.axis_index("tp")
    order = [head] + [jnp.bitwise_xor(head, t) for t in range(1, heads)]
    gather_rows(grad_ref, order, cat_ref, feat_ref)


def columns_kernel(ctx, distances, cat_ref, feat_ref, ww_ref, vw_ref, fw_ref, *rest):
    pieces, firsts = rest[: len(distances)], rest[len(distances) : len(distances) + 2]
    out_ref, tile_ref, sems = rest[-3:]
    nf2 = fw_ref.shape[0]
    heads = feat_ref.shape[1] // nf2
    tile = 2 * LANES
    me = block_index(ctx)
    copies = []
    for n, (e, ref) in enumerate(zip(distances, pieces)):
        part = pl.ds(pl.multiple_of(jnp.bitwise_xor(me, e) * tile, tile), tile)
        views = [firsts[1].at[e // 2 - 1] if e > 1 else firsts[0]]
        views += [ref.at[t] for t in range(heads - 2)]
        main = [ww_ref[part, :], vw_ref[part, :]]
        main += [v[m * tile : (m + 1) * tile, :] for v in views for m in range(3)]
        feats = [fw_ref[:, part]] + [wide(v, 3 * tile, nf2) for v in views]
        total = nt(cat_ref[...], jnp.concatenate(main, axis=1))
        total += nn(feat_ref[...], jnp.concatenate(feats, axis=0))
        tile_ref[n] = total.astype(bf16)
        copies.append(pltpu.make_async_copy(tile_ref.at[n], out_ref.at[:, part], sems.at[n]))
        copies[-1].start()
    for copy in copies:
        copy.wait()


def merge_kernel(grad_ref, weight_ref, out_ref, cat_ref, feat_ref):
    heads = grad_ref.shape[0]
    tile = out_ref.shape[1]
    lanes = 3 * LANES
    nf2 = feat_ref.shape[1] // heads

    @pl.when(pl.program_id(0) == 0)
    def _():
        gather_rows(grad_ref, range(heads), cat_ref, feat_ref)

    views = [weight_ref.at[h] for h in range(heads)]
    main = jnp.concatenate([v[:, 0:lanes] for v in views], axis=1)
    feats = jnp.concatenate([v[:, lanes:] for v in views], axis=1)
    out_ref[...] = (nt(cat_ref[...], main) + nt(feat_ref[...], feats)).astype(bf16)


VMEM = pl.BlockSpec(memory_space=pltpu.VMEM)
HBM = pl.BlockSpec(memory_space=pltpu.HBM)
ANY = pl.BlockSpec(memory_space=pl.ANY)
params = pltpu.CompilerParams(vmem_limit_bytes=32 * 1024 * 1024)


def in_hbm(*arrays):
    return [pltpu.with_memory_space_constraint(a, pltpu.HBM) for a in arrays]


def cost(flops, nbytes, exps=0):
    return pl.CostEstimate(flops=flops, bytes_accessed=nbytes, transcendentals=exps)


def merge(grads, weights, rows, dim):
    heads, _, columns = weights.shape
    tile = 2 * LANES
    return pl.pallas_call(
        merge_kernel,
        out_shape=jax.ShapeDtypeStruct((rows, dim), bf16),
        grid=(dim // tile,),
        in_specs=[
            pl.BlockSpec(grads.shape, lambda i: (0, 0, 0)),
            pl.BlockSpec((heads, tile, columns), lambda i: (0, i, 0)),
        ],
        out_specs=pl.BlockSpec((rows, tile), lambda i: (0, i)),
        scratch_shapes=[
            pltpu.VMEM((rows, 3 * LANES * heads), bf16),
            pltpu.VMEM((rows, (columns - 3 * LANES) * heads), bf16),
        ],
        compiler_params=params,
        cost_estimate=cost(2 * rows * dim * heads * columns, heads * dim * columns * 2),
        name="head_sum",
    )(grads, weights)


def per_device(ctx, tokens, feature_weight, window_weight, value_weight, log_decay, out_grad):
    rows, dim = tokens.shape
    nf2 = feature_weight.shape[1]
    nf = nf2 // 2
    dh = value_weight.shape[1]
    columns = 3 * dh + nf2
    chips, count, heads = lax.axis_size(ctx[:-1]), lax.axis_size(ctx), lax.axis_size("tp")
    fw_t = feature_weight.T
    tile = 2 * LANES
    spread = heads == 4 and count * tile == dim and count == 8
    packs = []
    if spread:
        packs = [jax.ShapeDtypeStruct((columns * tile // LANES, LANES), bf16)]
        packs += [jax.ShapeDtypeStruct((chips - 1, *packs[0].shape), bf16)]

    payload = 2 * rows + 2 * nf + 16
    block = jax.ShapeDtypeStruct((payload, LANES), bf16)
    outs = pl.pallas_call(
        partial(project_kernel, ctx, len(packs)),
        out_shape=packs
        + [block] * (chips + 2)
        + [
            jax.ShapeDtypeStruct((rows, nf2), bf16),
            jax.ShapeDtypeStruct((rows, 1), f32),
            jax.ShapeDtypeStruct((dim, 2 * dh), bf16),
            jax.ShapeDtypeStruct((dim, dh), bf16),
            jax.ShapeDtypeStruct((nf2, dim), bf16),
        ],
        in_specs=[HBM] * 6,
        out_specs=[VMEM] * (len(packs) + chips + 7),
        scratch_shapes=[
            pltpu.VMEM((rows, dim), bf16),
            pltpu.VMEM((1, rows), f32),
            pltpu.VMEM((rows, dh), bf16),
            pltpu.SemaphoreType.DMA((CHUNKS, 4)),
            pltpu.SemaphoreType.DMA((2,)),
        ],
        compiler_params=params,
        cost_estimate=cost(1, 1024),
        name="project",
    )(*in_hbm(tokens, fw_t, window_weight, value_weight, log_decay.T, out_grad))
    *sends, own, query, feat, cum, ww, vw, fw = outs[len(packs) :]

    swap = [(0, 1), (1, 0)]
    recv = {}
    for d in range(1, chips):
        recv[2 * d] = lax.ppermute(sends[d], ctx[:-1], [(i, i ^ d) for i in range(chips)])
    recv[1] = lax.ppermute(sends[0], "core", swap)
    if spread:
        across = lax.ppermute(outs[0], "tp", [(z, z ^ 2) for z in range(heads)])
    for d in range(1, chips):
        if spread and d == chips - 1:
            across, recv[2 * d] = lax.optimization_barrier((across, recv[2 * d]))
        recv[2 * d + 1] = lax.ppermute(recv[2 * d], "core", swap)
    recv = [recv[d] for d in range(1, count)]
    if count > 8:
        recv = [jnp.stack(recv)]

    if spread:
        early = lax.ppermute(outs[0], "tp", [(z, z ^ 1) for z in range(heads)])
        across, early, recv = lax.optimization_barrier((across, early, recv))
        near = [across, lax.ppermute(across, "tp", [(z, z ^ 1) for z in range(heads)])]

    attended, stat, sheet = pl.pallas_call(
        lambda *refs: query_kernel(ctx, count, len(recv), *refs),
        out_shape=[
            jax.ShapeDtypeStruct((rows, dh), bf16),
            jax.ShapeDtypeStruct((8, rows), f32),
            jax.ShapeDtypeStruct((rows, LANES), f32),
        ],
        in_specs=[VMEM] * (len(recv) + 4),
        out_specs=[VMEM] * 3,
        scratch_shapes=[
            pltpu.VMEM((count, 2 * rows, dh), bf16),
            pltpu.VMEM((WINDOW // rows + 1, rows, rows), f32),
            pltpu.VMEM((count, rows), f32),
        ],
        compiler_params=params,
        cost_estimate=cost(1, 1024),
        name="query_side",
    )(*recv, own, query, feat, cum)
    stats = [stat]
    for name in reversed(ctx):
        if spread and len(stats) == 2:
            near, sent, stats = lax.optimization_barrier((near, outs[1], stats))
        held = stats[0] if len(stats) == 1 else jnp.concatenate(stats, axis=0)
        stats.append(lax.ppermute(held, name, swap))
    if count > 8:
        stats = [jnp.concatenate(stats, axis=0)]

    if spread:
        first = [early, lax.ppermute(sent, "tp", [(z, z ^ 1) for z in range(heads)])]
        near, stats = lax.optimization_barrier((near, stats))
        pieces = [
            pl.pallas_call(
                stack_kernel,
                out_shape=jax.ShapeDtypeStruct((heads - 2, *packs[0].shape), bf16),
                in_specs=[VMEM] * (heads - 2),
                out_specs=VMEM,
                compiler_params=params,
                cost_estimate=cost(1, 1024),
                name="stack",
            )(*near)
        ]
        for d in range(1, chips):
            pieces.append(
                lax.ppermute(pieces[0], ctx[:-1], [(i, i ^ d) for i in range(chips)])
            )
        pieces[0], sheet = lax.optimization_barrier((pieces[0], sheet))

    grads = pl.pallas_call(
        lambda *refs: gradient_kernel(ctx, count, len(recv), len(stats), *refs),
        out_shape=jax.ShapeDtypeStruct((3 * rows + nf2 * rows // LANES, LANES), bf16),
        in_specs=[VMEM] * (len(recv) + len(stats) + 4),
        out_specs=VMEM,
        scratch_shapes=[pltpu.VMEM((count, LANES), f32)],
        compiler_params=params,
        cost_estimate=cost(1, 1024),
        name="gradients",
    )(*recv, *stats, own, query, feat, sheet)
    if not spread:
        weights = jnp.concatenate([window_weight, value_weight, feature_weight], axis=1)
        weights = lax.all_gather(weights, "tp")
        return (attended, merge(lax.all_gather(grads, "tp"), weights, rows, dim))

    first[1], grads = lax.optimization_barrier((first[1], grads))
    grads = lax.all_gather(grads, "tp")
    cat, feats = pl.pallas_call(
        cat_kernel,
        out_shape=[
            jax.ShapeDtypeStruct((rows, 3 * LANES * heads), bf16),
            jax.ShapeDtypeStruct((rows, nf2 * heads), bf16),
        ],
        in_specs=[VMEM],
        out_specs=[VMEM] * 2,
        compiler_params=params,
        cost_estimate=cost(1, 1024),
        name="cat",
    )(grads)
    pieces, first, _ = lax.optimization_barrier((pieces, first, cat))
    other_first = [lax.ppermute(p, "core", swap) for p in first]
    swapped = [lax.ppermute(p, "core", swap) for p in pieces]

    total = []
    for distances in ((0, 2, 4, 6), (1, 3, 5, 7)):
        parts = [(swapped if e % 2 else pieces)[e // 2] for e in distances]
        args = [cat, feats, ww, vw, fw, *parts, *(other_first if total else first), *total]
        total = [
            pl.pallas_call(
                partial(columns_kernel, ctx, distances),
                out_shape=jax.ShapeDtypeStruct((rows, dim), bf16),
                in_specs=[VMEM] * (7 + len(parts)) + [ANY] * len(total),
                out_specs=ANY,
                scratch_shapes=[
                    pltpu.VMEM((len(parts), rows, tile), bf16),
                    pltpu.SemaphoreType.DMA((len(parts),)),
                ],
                input_output_aliases={len(args) - 1: 0} if total else {},
                compiler_params=params,
                cost_estimate=cost(1, 1024),
                name="columns",
            )(*args)
        ]
    return (attended, total[0])


def solution(mesh):
    blocks, tp = mesh.devices.shape
    bits = blocks.bit_length() - 1
    assert blocks == 2**bits
    ctx = tuple(f"half{i}" for i in range(bits - 1)) + ("core",)
    split = Mesh(mesh.devices.reshape((2,) * bits + (tp,)), (*ctx, "tp"))
    in_specs = (
        P(ctx, None),
        P(None, "tp"),
        P(None, "tp"),
        P(None, "tp"),
        P(ctx, "tp"),
        P(ctx, "tp"),
    )
    out_specs = (P(ctx, "tp"), P(ctx, None))
    return jax.shard_map(
        partial(per_device, ctx),
        mesh=split,
        in_specs=in_specs,
        out_specs=out_specs,
        check_vma=False,
    )
```

```python
from functools import partial

import jax
import jax.numpy as jnp
from jax import lax
from jax.experimental import pallas as pl
from jax.experimental.pallas import tpu as pltpu
from jax.sharding import Mesh
from jax.sharding import PartitionSpec as P

WINDOW = 1024
LANES = 128
MASKED = -1e30
CHUNKS = 4
f32 = jnp.float32
bf16 = jnp.bfloat16


def nn(a, b):
    return lax.dot_general(a, b, (((1,), (0,)), ((), ())), preferred_element_type=f32)


def nt(a, b):
    return lax.dot_general(a, b, (((1,), (1,)), ((), ())), preferred_element_type=f32)


def partner(me, d, count):
    assert count & (count - 1) == 0
    return jnp.bitwise_xor(me, d)


def wide(view, start, count):
    return jnp.concatenate(
        [view[start : start + count, :], view[start + count : start + 2 * count, :]], axis=1
    )


def put_wide(ref, start, value):
    count = value.shape[0]
    for half in range(value.shape[1] // LANES):
        ref[start + half * count : start + (half + 1) * count, :] = value[
            :, half * LANES : (half + 1) * LANES
        ]


def cum_row(view, start):
    tail = view[start : start + 16, :].astype(f32)
    first = tail[0:1] + tail[2:3] + tail[4:5]
    second = tail[1:2] + tail[3:4] + tail[5:6]
    return jnp.concatenate([first, second], axis=1)


def iotas(rows):
    return (
        lax.broadcasted_iota(jnp.int32, (rows, rows), 0),
        lax.broadcasted_iota(jnp.int32, (rows, rows), 1),
    )


def block_index(ctx):
    place = 0
    for name in ctx:
        place = place * lax.axis_size(name) + lax.axis_index(name)
    return place


def pack(me, ww_ref, vw_ref, fw_ref, out_ref):
    nf2 = fw_ref.shape[0]
    tile = 2 * LANES
    at = pl.multiple_of(me * tile, tile)
    rows = pl.ds(at, tile)
    out_ref[0:tile, :] = ww_ref[rows, 0:LANES]
    out_ref[tile : 2 * tile, :] = ww_ref[rows, LANES:]
    out_ref[2 * tile : 3 * tile, :] = vw_ref[rows, :]
    put_wide(out_ref, 3 * tile, fw_ref[:, rows])


def project_kernel(ctx, packs, tok_hbm, fw_hbm, ww_hbm, vw_hbm, ld_hbm, do_hbm, *rest):
    *sends, keys_ref, query_ref, feat_ref, cum_ref, ww_ref, vw_ref, fw_ref = rest[packs:-5]
    tok_ref, ld_ref, do_ref, sems, small = rest[-5:]
    me = block_index(ctx)
    rows, dim = tok_ref.shape
    dh = do_ref.shape[1]
    nf = fw_ref.shape[0] // 2
    span = dim // CHUNKS
    copies = []
    for c in range(CHUNKS):
        part = pl.ds(c * span, span)
        copies.append([
            pltpu.make_async_copy(tok_hbm.at[:, part], tok_ref.at[:, part], sems.at[c, 0]),
            pltpu.make_async_copy(ww_hbm.at[part, :], ww_ref.at[part, :], sems.at[c, 1]),
            pltpu.make_async_copy(vw_hbm.at[part, :], vw_ref.at[part, :], sems.at[c, 2]),
            pltpu.make_async_copy(fw_hbm.at[:, part], fw_ref.at[:, part], sems.at[c, 3]),
        ])
    others = [
        pltpu.make_async_copy(ld_hbm, ld_ref, small.at[0]),
        pltpu.make_async_copy(do_hbm, do_ref, small.at[1]),
    ]
    for copy in others:
        copy.start()
    for group in copies:
        for at, copy in enumerate(group):
            copy.start(priority=min(at, 1))
    for copy in others:
        copy.wait()
    at_row, at_col = iotas(rows)
    ld_r = ld_ref[...]
    ld_c = jnp.sum(jnp.where(at_row == at_col, ld_r, 0.0), axis=1, keepdims=True)
    cum_r = jnp.sum(jnp.where(at_row <= at_col, ld_c, 0.0), axis=0, keepdims=True)
    cum_ref[...] = jnp.sum(jnp.where(at_col <= at_row, ld_r, 0.0), axis=1, keepdims=True)
    high = cum_r.astype(bf16)
    left = cum_r - high.astype(f32)
    mid = left.astype(bf16)
    low = (left - mid.astype(f32)).astype(bf16)
    pieces = [t[:, h : h + LANES].astype(f32) for t in (high, mid, low) for h in range(0, rows, LANES)]
    tail = jnp.concatenate(pieces + [jnp.zeros((10, LANES), f32)], axis=0).astype(bf16)

    feat = jnp.zeros((rows, 2 * nf), f32)
    main = jnp.zeros((rows, 3 * dh), f32)
    for c in range(CHUNKS):
        for copy in copies[c]:
            copy.wait()
        part = slice(c * span, (c + 1) * span)
        tok = tok_ref[:, part]
        feat += nt(tok, fw_ref[:, part])
        main += nn(tok, jnp.concatenate([ww_ref[part, :], vw_ref[part, :]], axis=1))
    feat = feat.astype(bf16)
    window = main[:, : 2 * dh].astype(bf16)
    values = main[:, 2 * dh :].astype(bf16)
    feat_ref[...] = feat
    small_row, small_col = iotas(2 * nf)
    feat_t = nt((small_row == small_col).astype(bf16), feat).astype(bf16)
    feat_at = 2 * rows
    tail_at = feat_at + 2 * nf

    def put_keys(ref):
        ref[0:rows, :] = window[:, dh:]
        ref[rows : 2 * rows, :] = values
        put_wide(ref, feat_at, feat_t[nf:, :])
        ref[tail_at : tail_at + 16, :] = tail

    def put_query(ref):
        ref[0:rows, :] = window[:, :dh]
        ref[rows : 2 * rows, :] = do_ref[...]
        put_wide(ref, feat_at, feat_t[:nf, :])
        ref[tail_at : tail_at + 16, :] = tail

    put_keys(keys_ref)
    put_query(query_ref)
    for at, ref in enumerate(sends):
        later = jnp.bitwise_xor(me, max(2 * at, 1)) > me
        pl.when(later)(lambda ref=ref: put_keys(ref))
        pl.when(jnp.logical_not(later))(lambda ref=ref: put_query(ref))
    if packs:
        own_pack, other_pack = rest[:packs]
        pack(me, ww_ref, vw_ref, fw_ref, own_pack)
        for d in range(other_pack.shape[0]):
            piece = jnp.bitwise_xor(me, 2 * d + 2)
            pack(piece, ww_ref, vw_ref, fw_ref, other_pack.at[d])

def stack_kernel(*refs):
    *parts, out_ref = refs
    for t, ref in enumerate(parts):
        out_ref[t] = ref[...]


def between(totals, low, high):
    at = lax.broadcasted_iota(jnp.int32, totals.shape, 0)
    return jnp.sum(jnp.where((at > low) & (at < high), totals, 0.0), axis=0, keepdims=True)


def over_partners(count, body, carry):
    if count <= 8:
        for d in range(1, count):
            carry = body(d, carry)
        return carry
    return lax.fori_loop(1, count, body, carry)


def query_kernel(ctx, count, recvs, *rest):
    recvs, rest = rest[:recvs], rest[recvs:]
    own_ref, query_ref, feat_ref, cum_ref, *rest = rest
    near_ref, p_ref, cums_ref = rest[-3:]
    att_ref, stat_ref, sheet_ref = rest[:3]

    def recv(d):
        return recvs[d - 1] if len(recvs) > 1 else recvs[0].at[d - 1]

    me = block_index(ctx)
    rows, dh = att_ref.shape
    nf = feat_ref.shape[1] // 2
    back = WINDOW // rows
    feat_at = 2 * rows
    tail_at = feat_at + 2 * nf
    scale = dh ** (-0.5)
    feat_scale = nf ** (-0.5)
    wq = query_ref[0:rows, :]
    do = query_ref[rows : 2 * rows, :]
    q = feat_ref[:, :nf]
    at_row, at_col = iotas(rows)
    own_cum = cum_row(own_ref, tail_at)
    cums_ref[pl.ds(me, 1), :] = own_cum
    near_ref[me] = own_ref[0 : 2 * rows, :]

    def gather(d, carry):
        j = partner(me, d, count)
        view = recv(d)
        near_ref[j] = view[0 : 2 * rows, :]
        cums_ref[pl.ds(j, 1), :] = cum_row(view, tail_at)
        return carry

    over_partners(count, gather, 0)

    def near(w):
        return near_ref.at[jnp.maximum(me - back + w, 0)]

    top = jnp.full((rows, LANES), MASKED, f32)
    for w in range(back + 1):
        keys = own_ref[0:rows, :] if w == back else near(w)[0:rows, :]
        s = nt(wq, keys) * scale
        if w == back:
            s = jnp.where(at_col <= at_row, s, MASKED)
        elif w == 0:
            s = jnp.where((at_col > at_row) & (me >= back), s, MASKED)
        else:
            s = jnp.where(me >= back - w, s, MASKED)
        p_ref[w] = s
        for h in range(0, rows, LANES):
            top = jnp.maximum(top, s[:, h : h + LANES])
    top = jnp.max(top, axis=1, keepdims=True)
    total = jnp.zeros((rows, LANES), f32)
    out = jnp.zeros((rows, dh), f32)
    for w in range(back + 1):
        p = jnp.exp(p_ref[w] - top)
        for h in range(0, rows, LANES):
            total += p[:, h : h + LANES]
        vals = own_ref[rows : 2 * rows, :] if w == back else near(w)[rows : 2 * rows, :]
        out += nn(p.astype(bf16), vals)
    total = jnp.sum(total, axis=1, keepdims=True)
    windowed = out * (1.0 / total)

    cum_c = cum_ref[...]
    growth = jnp.exp(cum_c)
    totals = cums_ref[:, rows - 1 : rows]

    def forward(d, carry):
        num, den = carry
        j = partner(me, d, count)
        view = recv(d)
        gap = between(totals, j - 1, me)
        es = jnp.where(j < me, jnp.exp(jnp.minimum(gap - cums_ref[pl.ds(j, 1), :], 0.0)), 0.0)
        x = nn(q, wide(view, feat_at, nf)) * feat_scale
        weight = (1.0 + x + 0.5 * x * x) * es
        for h in range(0, rows, LANES):
            den += weight[:, h : h + LANES]
        num += nn(weight.astype(bf16), view[rows : 2 * rows, :])
        return num, den

    num, den = over_partners(
        count, forward, (jnp.zeros((rows, dh), f32), jnp.zeros((rows, LANES), f32))
    )
    x = nn(q, wide(own_ref, feat_at, nf)) * feat_scale
    e = jnp.where(at_col <= at_row, jnp.exp(jnp.minimum(cum_c - own_cum, 0.0)), 0.0)
    weight = (1.0 + x + 0.5 * x * x) * e
    num = num * growth + nn(weight.astype(bf16), own_ref[rows : 2 * rows, :])
    den = den * growth
    for h in range(0, rows, LANES):
        den += weight[:, h : h + LANES]
    rden = 1.0 / jnp.sum(den, axis=1, keepdims=True)
    linear = num * rden
    att_ref[...] = (linear + windowed).astype(bf16)
    do_f = do.astype(f32)
    delta_w = jnp.sum(do_f * windowed, axis=1, keepdims=True)
    delta_l = jnp.sum(do_f * linear, axis=1, keepdims=True)
    lse = top + jnp.log(total)
    lane = lax.broadcasted_iota(jnp.int32, (rows, LANES), 1)
    sheet = jnp.where(lane == 0, lse, 0.0)
    sheet = jnp.where(lane == 1, delta_w, sheet)
    sheet = jnp.where(lane == 2, rden, sheet)
    sheet = jnp.where(lane == 3, delta_l, sheet)
    sheet = jnp.where(lane == 4, cum_c, sheet)
    sheet_ref[...] = sheet
    stat_ref[...] = jnp.transpose(sheet)[0:8, :]


def gradient_kernel(ctx, count, recvs, stats, *rest):
    recvs, rest = rest[:recvs], rest[recvs:]
    stats, rest = rest[:stats], rest[stats:]
    own_ref, query_ref, feat_ref, sheet_ref, *rest, total_ref = rest

    def recv(d):
        return recvs[d - 1] if len(recvs) > 1 else recvs[0].at[d - 1]

    me = block_index(ctx)
    rows = feat_ref.shape[0]
    dh = LANES
    nf = feat_ref.shape[1] // 2
    feat_at = 2 * rows
    scale = dh ** (-0.5)
    feat_scale = nf ** (-0.5)
    at_row, at_col = iotas(rows)
    apart = at_row - at_col
    wq, wk = query_ref[0:rows, :], own_ref[0:rows, :]
    do, v = query_ref[rows : 2 * rows, :], own_ref[rows : 2 * rows, :]
    q, k = feat_ref[:, :nf], feat_ref[:, nf:]
    lse_c, dw_c = sheet_ref[:, 0:1], sheet_ref[:, 1:2]
    rden_c, dl_c, cum_c = sheet_ref[:, 2:3], sheet_ref[:, 3:4], sheet_ref[:, 4:5]
    def stat(d):
        if len(stats) == 1:
            return stats[0].at[pl.ds(pl.multiple_of(8 * d, 8), 8)]
        at = d.bit_length()
        return stats[at].at[pl.ds(8 * (d - (1 << at >> 1)), 8)]

    mine_ref = stat(0)
    own_cum = mine_ref[4:5, :]
    total_ref[pl.ds(me, 1), :] = own_cum[:, rows - LANES :]

    def place(d, carry):
        total_ref[pl.ds(partner(me, d, count), 1), :] = stat(d)[4:5, rows - LANES :]
        return carry

    over_partners(count, place, 0)
    totals = total_ref[:, LANES - 1 :]
    growth_c = jnp.exp(cum_c) * rden_c
    tail_c = jnp.exp(own_cum[:, rows - 1 : rows] - cum_c)

    def pick(flag, a, b):
        return jnp.where(flag, a, b)

    s = nt(wq, wk) * scale
    causal = at_col <= at_row
    p = jnp.where(causal, jnp.exp(s - lse_c), 0.0)
    dp = nt(do, v)
    dwq = nn((p * (dp - dw_c)).astype(bf16), wk)
    x = nn(q, wide(own_ref, feat_at, nf)) * feat_scale
    e = jnp.where(causal, jnp.exp(jnp.minimum(cum_c - own_cum, 0.0)), 0.0) * rden_c
    dx = (dp - dl_c) * e * (1.0 + x)
    dq_f = nt(dx.astype(bf16), wide(own_ref, feat_at, nf))

    s = nt(wk, wq) * scale
    causal = at_row <= at_col
    p = jnp.where(causal, jnp.exp(s - mine_ref[0:1, :]), 0.0)
    dp = nt(v, do)
    dwk = nn((p * (dp - mine_ref[1:2, :])).astype(bf16), wq)
    x = nn(k, wide(query_ref, feat_at, nf)) * feat_scale
    e = jnp.where(causal, jnp.exp(jnp.minimum(own_cum - cum_c, 0.0)), 0.0) * mine_ref[2:3, :]
    dx = (dp - mine_ref[3:4, :]) * e * (1.0 + x)
    dk_f = nt(dx.astype(bf16), wide(query_ref, feat_at, nf))
    dv = nn((p + (1.0 + x + 0.5 * x * x) * e).astype(bf16), do)

    def step(d, carry):
        dwq, dq_f, dwk, dk_f, dv = carry
        j = partner(me, d, count)
        view = recv(d)
        mine = j < me
        sign = pick(mine, 1, -1)
        limit = WINDOW - jnp.abs(me - j) * rows
        rows_w = pick(mine, wq, wk)
        rows_v = pick(mine, do, v)
        rows_f = pick(mine, q, k)
        other_w = view[0:rows, :]
        other_v = view[rows : 2 * rows, :]
        other_f = wide(view, feat_at, nf)
        st = stat(d)
        zero = jnp.zeros((1, rows), f32)
        cum = st[4:5, :]
        gap = between(totals, jnp.minimum(me, j), jnp.maximum(me, j))
        e_r = jnp.exp(jnp.minimum(gap + pick(mine, cum[:, rows - 1 : rows] - cum, cum), 0.0))
        e_r = e_r * pick(mine, 1.0, st[2:3, :])
        e_c = pick(mine, growth_c, tail_c)

        s = nt(rows_w, other_w) * scale
        p = jnp.exp(s - pick(mine, lse_c, 0.0) - pick(mine, zero, st[0:1, :]))
        p = jnp.where(apart * sign < limit, p, 0.0)
        dp = nt(rows_v, other_v)
        ds = p * (dp - pick(mine, dw_c, 0.0) - pick(mine, zero, st[1:2, :]))
        more_w = nn(ds.astype(bf16), other_w)
        x = nn(rows_f, other_f) * feat_scale
        e = e_r * e_c
        dx = (dp - pick(mine, dl_c, 0.0) - pick(mine, zero, st[3:4, :])) * e * (1.0 + x)
        more_f = nt(dx.astype(bf16), other_f)
        more_v = nn((p + (1.0 + x + 0.5 * x * x) * e).astype(bf16), other_v)
        dwq = dwq + pick(mine, more_w, 0.0)
        dwk = dwk + pick(mine, 0.0, more_w)
        dq_f = dq_f + pick(mine, more_f, 0.0)
        dk_f = dk_f + pick(mine, 0.0, more_f)
        dv = dv + pick(mine, 0.0, more_v)
        return dwq, dq_f, dwk, dk_f, dv

    dwq, dq_f, dwk, dk_f, dv = over_partners(count, step, (dwq, dq_f, dwk, dk_f, dv))
    dwq, dwk = (dwq * scale).astype(bf16), (dwk * scale).astype(bf16)
    dv = dv.astype(bf16)
    padded = jnp.concatenate([dq_f, dk_f, jnp.zeros((rows, LANES - 2 * nf), f32)], axis=1)
    dft = (jnp.transpose(padded)[: 2 * nf] * feat_scale).astype(bf16)
    (grad_ref,) = rest
    grad_ref[0:rows, :] = dwq
    grad_ref[rows : 2 * rows, :] = dwk
    grad_ref[2 * rows : 3 * rows, :] = dv
    put_wide(grad_ref, 3 * rows, dft)


def gather_rows(grad_ref, order, cat_ref, feat_ref):
    rows = cat_ref.shape[0]
    nf2 = feat_ref.shape[1] // len(order)
    for at, h in enumerate(order):
        for part in range(3):
            lane = (3 * at + part) * LANES
            cat_ref[:, lane : lane + LANES] = grad_ref[h, part * rows : (part + 1) * rows, :]
    dft = jnp.concatenate([wide(grad_ref.at[h], 3 * rows, nf2) for h in order], axis=0)
    feat_ref[...] = jnp.transpose(dft.astype(f32)).astype(bf16)


def cat_kernel(grad_ref, cat_ref, feat_ref):
    heads = grad_ref.shape[0]
    head = lax.axis_index("tp")
    order = [head] + [jnp.bitwise_xor(head, t) for t in range(1, heads)]
    gather_rows(grad_ref, order, cat_ref, feat_ref)


def column_sums(ctx, e, cat_ref, feat_ref, ww_ref, vw_ref, fw_ref, piece_ref, firsts):
    nf2 = fw_ref.shape[0]
    heads = feat_ref.shape[1] // nf2
    tile = 2 * LANES
    part = pl.ds(pl.multiple_of(jnp.bitwise_xor(block_index(ctx), e) * tile, tile), tile)
    views = [firsts[1].at[e // 2 - 1] if e > 1 else firsts[0]]
    views += [piece_ref.at[t] for t in range(heads - 2)]
    main = [ww_ref[part, :], vw_ref[part, :]]
    main += [v[m * tile : (m + 1) * tile, :] for v in views for m in range(3)]
    feats = [fw_ref[:, part]] + [wide(v, 3 * tile, nf2) for v in views]
    total = nt(cat_ref[...], jnp.concatenate(main, axis=1))
    total += nn(feat_ref[...], jnp.concatenate(feats, axis=0))
    return total.astype(bf16), part


def columns_kernel(ctx, distances, *rest):
    operands, rest = rest[:5], rest[5:]
    pieces, firsts = rest[: len(distances)], rest[len(distances) : len(distances) + 2]
    out_ref, tile_ref, sems = rest[-3:]
    copies = []
    for n, (e, ref) in enumerate(zip(distances, pieces)):
        tile_ref[n], part = column_sums(ctx, e, *operands, ref, firsts)
        copies.append(pltpu.make_async_copy(tile_ref.at[n], out_ref.at[:, part], sems.at[n]))
        copies[-1].start()
    for copy in copies:
        copy.wait()


def passed_kernel(ctx, distances, *rest):
    operands, rest = rest[:5], rest[5:]
    pieces, firsts = rest[: len(distances)], rest[len(distances) : len(distances) + 2]
    for n, (e, ref) in enumerate(zip(distances, pieces)):
        rest[-1][n], _ = column_sums(ctx, e, *operands, ref, firsts)


def lay_kernel(ctx, tiles_ref, before_hbm, out_ref, sems):
    del before_hbm
    count, _, tile = tiles_ref.shape
    copies = []
    for d in range(count):
        at = jnp.bitwise_xor(block_index(ctx), 2 * d + 1) * tile
        part = pl.ds(pl.multiple_of(at, tile), tile)
        copies.append(pltpu.make_async_copy(tiles_ref.at[d], out_ref.at[:, part], sems.at[d]))
        copies[-1].start()
    for copy in copies:
        copy.wait()


def merge_kernel(grad_ref, weight_ref, out_ref, cat_ref, feat_ref):
    heads = grad_ref.shape[0]
    tile = out_ref.shape[1]
    lanes = 3 * LANES
    nf2 = feat_ref.shape[1] // heads

    @pl.when(pl.program_id(0) == 0)
    def _():
        gather_rows(grad_ref, range(heads), cat_ref, feat_ref)

    views = [weight_ref.at[h] for h in range(heads)]
    main = jnp.concatenate([v[:, 0:lanes] for v in views], axis=1)
    feats = jnp.concatenate([v[:, lanes:] for v in views], axis=1)
    out_ref[...] = (nt(cat_ref[...], main) + nt(feat_ref[...], feats)).astype(bf16)


VMEM = pl.BlockSpec(memory_space=pltpu.VMEM)
HBM = pl.BlockSpec(memory_space=pltpu.HBM)
ANY = pl.BlockSpec(memory_space=pl.ANY)
params = pltpu.CompilerParams(vmem_limit_bytes=32 * 1024 * 1024)


def in_hbm(*arrays):
    return [pltpu.with_memory_space_constraint(a, pltpu.HBM) for a in arrays]


def cost(flops, nbytes, exps=0):
    return pl.CostEstimate(flops=flops, bytes_accessed=nbytes, transcendentals=exps)


def merge(grads, weights, rows, dim):
    heads, _, columns = weights.shape
    tile = 2 * LANES
    return pl.pallas_call(
        merge_kernel,
        out_shape=jax.ShapeDtypeStruct((rows, dim), bf16),
        grid=(dim // tile,),
        in_specs=[
            pl.BlockSpec(grads.shape, lambda i: (0, 0, 0)),
            pl.BlockSpec((heads, tile, columns), lambda i: (0, i, 0)),
        ],
        out_specs=pl.BlockSpec((rows, tile), lambda i: (0, i)),
        scratch_shapes=[
            pltpu.VMEM((rows, 3 * LANES * heads), bf16),
            pltpu.VMEM((rows, (columns - 3 * LANES) * heads), bf16),
        ],
        compiler_params=params,
        cost_estimate=cost(2 * rows * dim * heads * columns, heads * dim * columns * 2),
        name="head_sum",
    )(grads, weights)


def per_device(ctx, tokens, feature_weight, window_weight, value_weight, log_decay, out_grad):
    rows, dim = tokens.shape
    nf2 = feature_weight.shape[1]
    nf = nf2 // 2
    dh = value_weight.shape[1]
    columns = 3 * dh + nf2
    chips, count, heads = lax.axis_size(ctx[:-1]), lax.axis_size(ctx), lax.axis_size("tp")
    fw_t = feature_weight.T
    tile = 2 * LANES
    spread = heads == 4 and count * tile == dim and count == 8
    packs = []
    if spread:
        packs = [jax.ShapeDtypeStruct((columns * tile // LANES, LANES), bf16)]
        packs += [jax.ShapeDtypeStruct((chips - 1, *packs[0].shape), bf16)]

    payload = 2 * rows + 2 * nf + 16
    block = jax.ShapeDtypeStruct((payload, LANES), bf16)
    outs = pl.pallas_call(
        partial(project_kernel, ctx, len(packs)),
        out_shape=packs
        + [block] * (chips + 2)
        + [
            jax.ShapeDtypeStruct((rows, nf2), bf16),
            jax.ShapeDtypeStruct((rows, 1), f32),
            jax.ShapeDtypeStruct((dim, 2 * dh), bf16),
            jax.ShapeDtypeStruct((dim, dh), bf16),
            jax.ShapeDtypeStruct((nf2, dim), bf16),
        ],
        in_specs=[HBM] * 6,
        out_specs=[VMEM] * (len(packs) + chips + 7),
        scratch_shapes=[
            pltpu.VMEM((rows, dim), bf16),
            pltpu.VMEM((1, rows), f32),
            pltpu.VMEM((rows, dh), bf16),
            pltpu.SemaphoreType.DMA((CHUNKS, 4)),
            pltpu.SemaphoreType.DMA((2,)),
        ],
        compiler_params=params,
        cost_estimate=cost(1, 1024),
        name="project",
    )(*in_hbm(tokens, fw_t, window_weight, value_weight, log_decay.T, out_grad))
    *sends, own, query, feat, cum, ww, vw, fw = outs[len(packs) :]

    swap = [(0, 1), (1, 0)]
    recv = {}
    for d in range(1, chips):
        recv[2 * d] = lax.ppermute(sends[d], ctx[:-1], [(i, i ^ d) for i in range(chips)])
    recv[1] = lax.ppermute(sends[0], "core", swap)
    if spread:
        across = lax.ppermute(outs[0], "tp", [(z, z ^ 2) for z in range(heads)])
    for d in range(1, chips):
        if spread and d == chips - 1:
            across, recv[2 * d] = lax.optimization_barrier((across, recv[2 * d]))
        recv[2 * d + 1] = lax.ppermute(recv[2 * d], "core", swap)
    recv = [recv[d] for d in range(1, count)]
    if count > 8:
        recv = [jnp.stack(recv)]

    if spread:
        early = lax.ppermute(outs[0], "tp", [(z, z ^ 1) for z in range(heads)])
        across, early, recv = lax.optimization_barrier((across, early, recv))
        near = [across, lax.ppermute(across, "tp", [(z, z ^ 1) for z in range(heads)])]

    attended, stat, sheet = pl.pallas_call(
        lambda *refs: query_kernel(ctx, count, len(recv), *refs),
        out_shape=[
            jax.ShapeDtypeStruct((rows, dh), bf16),
            jax.ShapeDtypeStruct((8, rows), f32),
            jax.ShapeDtypeStruct((rows, LANES), f32),
        ],
        in_specs=[VMEM] * (len(recv) + 4),
        out_specs=[VMEM] * 3,
        scratch_shapes=[
            pltpu.VMEM((count, 2 * rows, dh), bf16),
            pltpu.VMEM((WINDOW // rows + 1, rows, rows), f32),
            pltpu.VMEM((count, rows), f32),
        ],
        compiler_params=params,
        cost_estimate=cost(1, 1024),
        name="query_side",
    )(*recv, own, query, feat, cum)
    stats = [stat]
    for name in reversed(ctx):
        if spread and len(stats) == 2:
            near, sent, stats = lax.optimization_barrier((near, outs[1], stats))
        held = stats[0] if len(stats) == 1 else jnp.concatenate(stats, axis=0)
        stats.append(lax.ppermute(held, name, swap))
    if count > 8:
        stats = [jnp.concatenate(stats, axis=0)]

    if spread:
        first = [early, lax.ppermute(sent, "tp", [(z, z ^ 1) for z in range(heads)])]
        near, stats = lax.optimization_barrier((near, stats))
        pieces = [
            pl.pallas_call(
                stack_kernel,
                out_shape=jax.ShapeDtypeStruct((heads - 2, *packs[0].shape), bf16),
                in_specs=[VMEM] * (heads - 2),
                out_specs=VMEM,
                compiler_params=params,
                cost_estimate=cost(1, 1024),
                name="stack",
            )(*near)
        ]
        for d in range(1, chips):
            pieces.append(
                lax.ppermute(pieces[0], ctx[:-1], [(i, i ^ d) for i in range(chips)])
            )
        pieces[0], sheet = lax.optimization_barrier((pieces[0], sheet))

    grads = pl.pallas_call(
        lambda *refs: gradient_kernel(ctx, count, len(recv), len(stats), *refs),
        out_shape=jax.ShapeDtypeStruct((3 * rows + nf2 * rows // LANES, LANES), bf16),
        in_specs=[VMEM] * (len(recv) + len(stats) + 4),
        out_specs=VMEM,
        scratch_shapes=[pltpu.VMEM((count, LANES), f32)],
        compiler_params=params,
        cost_estimate=cost(1, 1024),
        name="gradients",
    )(*recv, *stats, own, query, feat, sheet)
    if not spread:
        weights = jnp.concatenate([window_weight, value_weight, feature_weight], axis=1)
        weights = lax.all_gather(weights, "tp")
        return (attended, merge(lax.all_gather(grads, "tp"), weights, rows, dim))

    first[1], grads = lax.optimization_barrier((first[1], grads))
    grads = lax.all_gather(grads, "tp")
    pieces, first, grads = lax.optimization_barrier((pieces, first, grads))
    sibling_grads = lax.ppermute(grads, "core", swap)

    def operands_of(grads):
        return pl.pallas_call(
            cat_kernel,
            out_shape=[
                jax.ShapeDtypeStruct((rows, 3 * LANES * heads), bf16),
                jax.ShapeDtypeStruct((rows, nf2 * heads), bf16),
            ],
            in_specs=[VMEM],
            out_specs=[VMEM] * 2,
            compiler_params=params,
            cost_estimate=cost(1, 1024),
            name="cat",
        )(grads)

    mine = operands_of(grads)

    def columns_of(distances, total):
        parts = [pieces[e // 2] for e in distances]
        args = [*mine, ww, vw, fw, *parts, *first, *total]
        return [
            pl.pallas_call(
                partial(columns_kernel, ctx, distances),
                out_shape=jax.ShapeDtypeStruct((rows, dim), bf16),
                in_specs=[VMEM] * (7 + len(parts)) + [ANY] * len(total),
                out_specs=ANY,
                scratch_shapes=[
                    pltpu.VMEM((len(parts), rows, tile), bf16),
                    pltpu.SemaphoreType.DMA((len(parts),)),
                ],
                input_output_aliases={len(args) - 1: 0} if total else {},
                compiler_params=params,
                cost_estimate=cost(1, 1024),
                name="columns",
            )(*args)
        ]

    total = columns_of((0, 2), [])
    sibling_grads, total = lax.optimization_barrier((sibling_grads, total))
    passed = pl.pallas_call(
        partial(passed_kernel, ctx, (0, 2, 4, 6)),
        out_shape=jax.ShapeDtypeStruct((chips, rows, tile), bf16),
        in_specs=[VMEM] * (7 + chips),
        out_specs=VMEM,
        compiler_params=params,
        cost_estimate=cost(1, 1024),
        name="passed",
    )(*operands_of(sibling_grads), ww, vw, fw, *pieces, *first)
    passed, total = lax.optimization_barrier((passed, total))
    received = lax.ppermute(passed, "core", swap)
    total = columns_of((4, 6), total)
    total = pl.pallas_call(
        partial(lay_kernel, ctx),
        out_shape=jax.ShapeDtypeStruct((rows, dim), bf16),
        in_specs=[VMEM, ANY],
        out_specs=ANY,
        scratch_shapes=[pltpu.SemaphoreType.DMA((chips,))],
        input_output_aliases={1: 0},
        compiler_params=params,
        cost_estimate=cost(1, 1024),
        name="lay",
    )(received, *total)
    return (attended, total)


def solution(mesh):
    blocks, tp = mesh.devices.shape
    bits = blocks.bit_length() - 1
    assert blocks == 2**bits
    ctx = tuple(f"half{i}" for i in range(bits - 1)) + ("core",)
    split = Mesh(mesh.devices.reshape((2,) * bits + (tp,)), (*ctx, "tp"))
    in_specs = (
        P(ctx, None),
        P(None, "tp"),
        P(None, "tp"),
        P(None, "tp"),
        P(ctx, "tp"),
        P(ctx, "tp"),
    )
    out_specs = (P(ctx, "tp"), P(ctx, None))
    return jax.shard_map(
        partial(per_device, ctx),
        mesh=split,
        in_specs=in_specs,
        out_specs=out_specs,
        check_vma=False,
    )
```

```python
from functools import partial

import jax
import jax.numpy as jnp
from jax import lax
from jax.experimental import pallas as pl
from jax.experimental.pallas import tpu as pltpu
from jax.sharding import Mesh
from jax.sharding import PartitionSpec as P

WINDOW = 1024
LANES = 128
MASKED = -1e30
CHUNKS = 4
f32 = jnp.float32
bf16 = jnp.bfloat16


def nn(a, b):
    return lax.dot_general(a, b, (((1,), (0,)), ((), ())), preferred_element_type=f32)


def nt(a, b):
    return lax.dot_general(a, b, (((1,), (1,)), ((), ())), preferred_element_type=f32)


def partner(me, d, count):
    assert count & (count - 1) == 0
    return jnp.bitwise_xor(me, d)


def wide(view, start, count):
    return jnp.concatenate(
        [view[start : start + count, :], view[start + count : start + 2 * count, :]], axis=1
    )


def put_wide(ref, start, value):
    count = value.shape[0]
    for half in range(value.shape[1] // LANES):
        ref[start + half * count : start + (half + 1) * count, :] = value[
            :, half * LANES : (half + 1) * LANES
        ]


def cum_row(view, start):
    tail = view[start : start + 16, :].astype(f32)
    first = tail[0:1] + tail[2:3] + tail[4:5]
    second = tail[1:2] + tail[3:4] + tail[5:6]
    return jnp.concatenate([first, second], axis=1)


def iotas(rows):
    return (
        lax.broadcasted_iota(jnp.int32, (rows, rows), 0),
        lax.broadcasted_iota(jnp.int32, (rows, rows), 1),
    )


def block_index(ctx):
    place = 0
    for name in ctx:
        place = place * lax.axis_size(name) + lax.axis_index(name)
    return place


def pack(me, ww_ref, vw_ref, fw_ref, out_ref):
    nf2 = fw_ref.shape[0]
    tile = 2 * LANES
    at = pl.multiple_of(me * tile, tile)
    rows = pl.ds(at, tile)
    out_ref[0:tile, :] = ww_ref[rows, 0:LANES]
    out_ref[tile : 2 * tile, :] = ww_ref[rows, LANES:]
    out_ref[2 * tile : 3 * tile, :] = vw_ref[rows, :]
    put_wide(out_ref, 3 * tile, fw_ref[:, rows])


def project_kernel(ctx, packs, tok_hbm, fw_hbm, ww_hbm, vw_hbm, ld_hbm, do_hbm, *rest):
    *sends, keys_ref, query_ref, feat_ref, cum_ref, ww_ref, vw_ref, fw_ref = rest[packs:-5]
    tok_ref, ld_ref, do_ref, sems, small = rest[-5:]
    me = block_index(ctx)
    rows, dim = tok_ref.shape
    dh = do_ref.shape[1]
    nf = fw_ref.shape[0] // 2
    span = dim // CHUNKS
    copies = []
    for c in range(CHUNKS):
        part = pl.ds(c * span, span)
        copies.append([
            pltpu.make_async_copy(tok_hbm.at[:, part], tok_ref.at[:, part], sems.at[c, 0]),
            pltpu.make_async_copy(ww_hbm.at[part, :], ww_ref.at[part, :], sems.at[c, 1]),
            pltpu.make_async_copy(vw_hbm.at[part, :], vw_ref.at[part, :], sems.at[c, 2]),
            pltpu.make_async_copy(fw_hbm.at[:, part], fw_ref.at[:, part], sems.at[c, 3]),
        ])
    others = [
        pltpu.make_async_copy(ld_hbm, ld_ref, small.at[0]),
        pltpu.make_async_copy(do_hbm, do_ref, small.at[1]),
    ]
    for copy in others:
        copy.start()
    for group in copies:
        for at, copy in enumerate(group):
            copy.start(priority=min(at, 1))
    for copy in others:
        copy.wait()
    at_row, at_col = iotas(rows)
    ld_r = ld_ref[...]
    ld_c = jnp.sum(jnp.where(at_row == at_col, ld_r, 0.0), axis=1, keepdims=True)
    cum_r = jnp.sum(jnp.where(at_row <= at_col, ld_c, 0.0), axis=0, keepdims=True)
    cum_ref[...] = jnp.sum(jnp.where(at_col <= at_row, ld_r, 0.0), axis=1, keepdims=True)
    high = cum_r.astype(bf16)
    left = cum_r - high.astype(f32)
    mid = left.astype(bf16)
    low = (left - mid.astype(f32)).astype(bf16)
    pieces = [t[:, h : h + LANES].astype(f32) for t in (high, mid, low) for h in range(0, rows, LANES)]
    tail = jnp.concatenate(pieces + [jnp.zeros((10, LANES), f32)], axis=0).astype(bf16)

    feat = jnp.zeros((rows, 2 * nf), f32)
    main = jnp.zeros((rows, 3 * dh), f32)
    for c in range(CHUNKS):
        for copy in copies[c]:
            copy.wait()
        part = slice(c * span, (c + 1) * span)
        tok = tok_ref[:, part]
        feat += nt(tok, fw_ref[:, part])
        main += nn(tok, jnp.concatenate([ww_ref[part, :], vw_ref[part, :]], axis=1))
    feat = feat.astype(bf16)
    window = main[:, : 2 * dh].astype(bf16)
    values = main[:, 2 * dh :].astype(bf16)
    feat_ref[...] = feat
    small_row, small_col = iotas(2 * nf)
    feat_t = nt((small_row == small_col).astype(bf16), feat).astype(bf16)
    feat_at = 2 * rows
    tail_at = feat_at + 2 * nf

    def put_keys(ref):
        ref[0:rows, :] = window[:, dh:]
        ref[rows : 2 * rows, :] = values
        put_wide(ref, feat_at, feat_t[nf:, :])
        ref[tail_at : tail_at + 16, :] = tail

    def put_query(ref):
        ref[0:rows, :] = window[:, :dh]
        ref[rows : 2 * rows, :] = do_ref[...]
        put_wide(ref, feat_at, feat_t[:nf, :])
        ref[tail_at : tail_at + 16, :] = tail

    put_keys(keys_ref)
    put_query(query_ref)
    for at, ref in enumerate(sends):
        later = jnp.bitwise_xor(me, max(2 * at, 1)) > me
        pl.when(later)(lambda ref=ref: put_keys(ref))
        pl.when(jnp.logical_not(later))(lambda ref=ref: put_query(ref))
    if packs:
        own_pack, other_pack = rest[:packs]
        pack(me, ww_ref, vw_ref, fw_ref, own_pack)
        for d in range(other_pack.shape[0]):
            piece = jnp.bitwise_xor(me, 2 * d + 2)
            pack(piece, ww_ref, vw_ref, fw_ref, other_pack.at[d])

def stack_kernel(*refs):
    *parts, out_ref = refs
    for t, ref in enumerate(parts):
        out_ref[t] = ref[...]


def between(totals, low, high):
    at = lax.broadcasted_iota(jnp.int32, totals.shape, 0)
    return jnp.sum(jnp.where((at > low) & (at < high), totals, 0.0), axis=0, keepdims=True)


def over_partners(count, body, carry):
    if count <= 8:
        for d in range(1, count):
            carry = body(d, carry)
        return carry
    return lax.fori_loop(1, count, body, carry)


def query_kernel(ctx, count, recvs, *rest):
    recvs, rest = rest[:recvs], rest[recvs:]
    own_ref, query_ref, feat_ref, cum_ref, *rest = rest
    near_ref, p_ref, cums_ref = rest[-3:]
    att_ref, stat_ref, sheet_ref = rest[:3]

    def recv(d):
        return recvs[d - 1] if len(recvs) > 1 else recvs[0].at[d - 1]

    me = block_index(ctx)
    rows, dh = att_ref.shape
    nf = feat_ref.shape[1] // 2
    back = WINDOW // rows
    feat_at = 2 * rows
    tail_at = feat_at + 2 * nf
    scale = dh ** (-0.5)
    feat_scale = nf ** (-0.5)
    wq = query_ref[0:rows, :]
    do = query_ref[rows : 2 * rows, :]
    q = feat_ref[:, :nf]
    at_row, at_col = iotas(rows)
    own_cum = cum_row(own_ref, tail_at)
    cums_ref[pl.ds(me, 1), :] = own_cum
    near_ref[me] = own_ref[0 : 2 * rows, :]

    def gather(d, carry):
        j = partner(me, d, count)
        view = recv(d)
        near_ref[j] = view[0 : 2 * rows, :]
        cums_ref[pl.ds(j, 1), :] = cum_row(view, tail_at)
        return carry

    over_partners(count, gather, 0)

    def near(w):
        return near_ref.at[jnp.maximum(me - back + w, 0)]

    top = jnp.full((rows, LANES), MASKED, f32)
    for w in range(back + 1):
        keys = own_ref[0:rows, :] if w == back else near(w)[0:rows, :]
        s = nt(wq, keys) * scale
        if w == back:
            s = jnp.where(at_col <= at_row, s, MASKED)
        elif w == 0:
            s = jnp.where((at_col > at_row) & (me >= back), s, MASKED)
        else:
            s = jnp.where(me >= back - w, s, MASKED)
        p_ref[w] = s
        for h in range(0, rows, LANES):
            top = jnp.maximum(top, s[:, h : h + LANES])
    top = jnp.max(top, axis=1, keepdims=True)
    total = jnp.zeros((rows, LANES), f32)
    out = jnp.zeros((rows, dh), f32)
    for w in range(back + 1):
        p = jnp.exp(p_ref[w] - top)
        for h in range(0, rows, LANES):
            total += p[:, h : h + LANES]
        vals = own_ref[rows : 2 * rows, :] if w == back else near(w)[rows : 2 * rows, :]
        out += nn(p.astype(bf16), vals)
    total = jnp.sum(total, axis=1, keepdims=True)
    windowed = out * (1.0 / total)

    cum_c = cum_ref[...]
    growth = jnp.exp(cum_c)
    totals = cums_ref[:, rows - 1 : rows]

    def forward(d, carry):
        num, den = carry
        j = partner(me, d, count)
        view = recv(d)
        gap = between(totals, j - 1, me)
        es = jnp.where(j < me, jnp.exp(jnp.minimum(gap - cums_ref[pl.ds(j, 1), :], 0.0)), 0.0)
        x = nn(q, wide(view, feat_at, nf)) * feat_scale
        weight = (1.0 + x + 0.5 * x * x) * es
        for h in range(0, rows, LANES):
            den += weight[:, h : h + LANES]
        num += nn(weight.astype(bf16), view[rows : 2 * rows, :])
        return num, den

    num, den = over_partners(
        count, forward, (jnp.zeros((rows, dh), f32), jnp.zeros((rows, LANES), f32))
    )
    x = nn(q, wide(own_ref, feat_at, nf)) * feat_scale
    e = jnp.where(at_col <= at_row, jnp.exp(jnp.minimum(cum_c - own_cum, 0.0)), 0.0)
    weight = (1.0 + x + 0.5 * x * x) * e
    num = num * growth + nn(weight.astype(bf16), own_ref[rows : 2 * rows, :])
    den = den * growth
    for h in range(0, rows, LANES):
        den += weight[:, h : h + LANES]
    rden = 1.0 / jnp.sum(den, axis=1, keepdims=True)
    linear = num * rden
    att_ref[...] = (linear + windowed).astype(bf16)
    do_f = do.astype(f32)
    delta_w = jnp.sum(do_f * windowed, axis=1, keepdims=True)
    delta_l = jnp.sum(do_f * linear, axis=1, keepdims=True)
    lse = top + jnp.log(total)
    lane = lax.broadcasted_iota(jnp.int32, (rows, LANES), 1)
    sheet = jnp.where(lane == 0, lse, 0.0)
    sheet = jnp.where(lane == 1, delta_w, sheet)
    sheet = jnp.where(lane == 2, rden, sheet)
    sheet = jnp.where(lane == 3, delta_l, sheet)
    sheet = jnp.where(lane == 4, cum_c, sheet)
    sheet_ref[...] = sheet
    stat_ref[...] = jnp.transpose(sheet)[0:8, :]


def gradient_kernel(ctx, count, recvs, stats, *rest):
    recvs, rest = rest[:recvs], rest[recvs:]
    stats, rest = rest[:stats], rest[stats:]
    own_ref, query_ref, feat_ref, sheet_ref, *rest, total_ref = rest

    def recv(d):
        return recvs[d - 1] if len(recvs) > 1 else recvs[0].at[d - 1]

    me = block_index(ctx)
    rows = feat_ref.shape[0]
    dh = LANES
    nf = feat_ref.shape[1] // 2
    feat_at = 2 * rows
    scale = dh ** (-0.5)
    feat_scale = nf ** (-0.5)
    at_row, at_col = iotas(rows)
    apart = at_row - at_col
    wq, wk = query_ref[0:rows, :], own_ref[0:rows, :]
    do, v = query_ref[rows : 2 * rows, :], own_ref[rows : 2 * rows, :]
    q, k = feat_ref[:, :nf], feat_ref[:, nf:]
    lse_c, dw_c = sheet_ref[:, 0:1], sheet_ref[:, 1:2]
    rden_c, dl_c, cum_c = sheet_ref[:, 2:3], sheet_ref[:, 3:4], sheet_ref[:, 4:5]
    def stat(d):
        if len(stats) == 1:
            return stats[0].at[pl.ds(pl.multiple_of(8 * d, 8), 8)]
        at = d.bit_length()
        return stats[at].at[pl.ds(8 * (d - (1 << at >> 1)), 8)]

    mine_ref = stat(0)
    own_cum = mine_ref[4:5, :]
    total_ref[pl.ds(me, 1), :] = own_cum[:, rows - LANES :]

    def place(d, carry):
        total_ref[pl.ds(partner(me, d, count), 1), :] = stat(d)[4:5, rows - LANES :]
        return carry

    over_partners(count, place, 0)
    totals = total_ref[:, LANES - 1 :]
    growth_c = jnp.exp(cum_c) * rden_c
    tail_c = jnp.exp(own_cum[:, rows - 1 : rows] - cum_c)

    def pick(flag, a, b):
        return jnp.where(flag, a, b)

    s = nt(wq, wk) * scale
    causal = at_col <= at_row
    p = jnp.where(causal, jnp.exp(s - lse_c), 0.0)
    dp = nt(do, v)
    dwq = nn((p * (dp - dw_c)).astype(bf16), wk)
    x = nn(q, wide(own_ref, feat_at, nf)) * feat_scale
    e = jnp.where(causal, jnp.exp(jnp.minimum(cum_c - own_cum, 0.0)), 0.0) * rden_c
    dx = (dp - dl_c) * e * (1.0 + x)
    dq_f = nt(dx.astype(bf16), wide(own_ref, feat_at, nf))

    s = nt(wk, wq) * scale
    causal = at_row <= at_col
    p = jnp.where(causal, jnp.exp(s - mine_ref[0:1, :]), 0.0)
    dp = nt(v, do)
    dwk = nn((p * (dp - mine_ref[1:2, :])).astype(bf16), wq)
    x = nn(k, wide(query_ref, feat_at, nf)) * feat_scale
    e = jnp.where(causal, jnp.exp(jnp.minimum(own_cum - cum_c, 0.0)), 0.0) * mine_ref[2:3, :]
    dx = (dp - mine_ref[3:4, :]) * e * (1.0 + x)
    dk_f = nt(dx.astype(bf16), wide(query_ref, feat_at, nf))
    dv = nn((p + (1.0 + x + 0.5 * x * x) * e).astype(bf16), do)

    def step(d, carry):
        dwq, dq_f, dwk, dk_f, dv = carry
        j = partner(me, d, count)
        view = recv(d)
        mine = j < me
        sign = pick(mine, 1, -1)
        limit = WINDOW - jnp.abs(me - j) * rows
        rows_w = pick(mine, wq, wk)
        rows_v = pick(mine, do, v)
        rows_f = pick(mine, q, k)
        other_w = view[0:rows, :]
        other_v = view[rows : 2 * rows, :]
        other_f = wide(view, feat_at, nf)
        st = stat(d)
        zero = jnp.zeros((1, rows), f32)
        cum = st[4:5, :]
        gap = between(totals, jnp.minimum(me, j), jnp.maximum(me, j))
        e_r = jnp.exp(jnp.minimum(gap + pick(mine, cum[:, rows - 1 : rows] - cum, cum), 0.0))
        e_r = e_r * pick(mine, 1.0, st[2:3, :])
        e_c = pick(mine, growth_c, tail_c)

        s = nt(rows_w, other_w) * scale
        p = jnp.exp(s - pick(mine, lse_c, 0.0) - pick(mine, zero, st[0:1, :]))
        p = jnp.where(apart * sign < limit, p, 0.0)
        dp = nt(rows_v, other_v)
        ds = p * (dp - pick(mine, dw_c, 0.0) - pick(mine, zero, st[1:2, :]))
        more_w = nn(ds.astype(bf16), other_w)
        x = nn(rows_f, other_f) * feat_scale
        e = e_r * e_c
        dx = (dp - pick(mine, dl_c, 0.0) - pick(mine, zero, st[3:4, :])) * e * (1.0 + x)
        more_f = nt(dx.astype(bf16), other_f)
        more_v = nn((p + (1.0 + x + 0.5 * x * x) * e).astype(bf16), other_v)
        dwq = dwq + pick(mine, more_w, 0.0)
        dwk = dwk + pick(mine, 0.0, more_w)
        dq_f = dq_f + pick(mine, more_f, 0.0)
        dk_f = dk_f + pick(mine, 0.0, more_f)
        dv = dv + pick(mine, 0.0, more_v)
        return dwq, dq_f, dwk, dk_f, dv

    dwq, dq_f, dwk, dk_f, dv = over_partners(count, step, (dwq, dq_f, dwk, dk_f, dv))
    dwq, dwk = (dwq * scale).astype(bf16), (dwk * scale).astype(bf16)
    dv = dv.astype(bf16)
    padded = jnp.concatenate([dq_f, dk_f, jnp.zeros((rows, LANES - 2 * nf), f32)], axis=1)
    dft = (jnp.transpose(padded)[: 2 * nf] * feat_scale).astype(bf16)
    (grad_ref,) = rest
    grad_ref[0:rows, :] = dwq
    grad_ref[rows : 2 * rows, :] = dwk
    grad_ref[2 * rows : 3 * rows, :] = dv
    put_wide(grad_ref, 3 * rows, dft)


def gather_rows(grad_ref, order, cat_ref, feat_ref):
    rows = cat_ref.shape[0]
    nf2 = feat_ref.shape[1] // len(order)
    for at, h in enumerate(order):
        for part in range(3):
            lane = (3 * at + part) * LANES
            cat_ref[:, lane : lane + LANES] = grad_ref[h, part * rows : (part + 1) * rows, :]
    dft = jnp.concatenate([wide(grad_ref.at[h], 3 * rows, nf2) for h in order], axis=0)
    feat_ref[...] = jnp.transpose(dft.astype(f32)).astype(bf16)


def cat_kernel(grad_ref, cat_ref, feat_ref):
    heads = grad_ref.shape[0]
    head = lax.axis_index("tp")
    order = [head] + [jnp.bitwise_xor(head, t) for t in range(1, heads)]
    gather_rows(grad_ref, order, cat_ref, feat_ref)


def column_sums(ctx, e, cat_ref, feat_ref, ww_ref, vw_ref, fw_ref, piece_ref, firsts):
    nf2 = fw_ref.shape[0]
    heads = feat_ref.shape[1] // nf2
    tile = 2 * LANES
    part = pl.ds(pl.multiple_of(jnp.bitwise_xor(block_index(ctx), e) * tile, tile), tile)
    views = [firsts[1].at[e // 2 - 1] if e > 1 else firsts[0]]
    views += [piece_ref.at[t] for t in range(heads - 2)]
    main = [ww_ref[part, :], vw_ref[part, :]]
    main += [v[m * tile : (m + 1) * tile, :] for v in views for m in range(3)]
    feats = [fw_ref[:, part]] + [wide(v, 3 * tile, nf2) for v in views]
    total = nt(cat_ref[...], jnp.concatenate(main, axis=1))
    total += nn(feat_ref[...], jnp.concatenate(feats, axis=0))
    return total.astype(bf16), part


def columns_kernel(ctx, distances, *rest):
    operands, rest = rest[:5], rest[5:]
    pieces, firsts = rest[: len(distances)], rest[len(distances) : len(distances) + 2]
    for n, (e, ref) in enumerate(zip(distances, pieces)):
        rest[-1][n], _ = column_sums(ctx, e, *operands, ref, firsts)


def lay_kernel(ctx, *refs):
    *tiles, received_ref, out_ref, sems = refs
    views = [(ref.at[n], 2 * (2 * m + n)) for m, ref in enumerate(tiles) for n in range(2)]
    views += [(received_ref.at[d], 2 * d + 1) for d in range(received_ref.shape[0])]
    copies = []
    for n, (view, e) in enumerate(views):
        tile = view.shape[1]
        at = jnp.bitwise_xor(block_index(ctx), e) * tile
        part = pl.ds(pl.multiple_of(at, tile), tile)
        copies.append(pltpu.make_async_copy(view, out_ref.at[:, part], sems.at[n]))
        copies[-1].start()
    for copy in copies:
        copy.wait()


def merge_kernel(grad_ref, weight_ref, out_ref, cat_ref, feat_ref):
    heads = grad_ref.shape[0]
    tile = out_ref.shape[1]
    lanes = 3 * LANES
    nf2 = feat_ref.shape[1] // heads

    @pl.when(pl.program_id(0) == 0)
    def _():
        gather_rows(grad_ref, range(heads), cat_ref, feat_ref)

    views = [weight_ref.at[h] for h in range(heads)]
    main = jnp.concatenate([v[:, 0:lanes] for v in views], axis=1)
    feats = jnp.concatenate([v[:, lanes:] for v in views], axis=1)
    out_ref[...] = (nt(cat_ref[...], main) + nt(feat_ref[...], feats)).astype(bf16)


VMEM = pl.BlockSpec(memory_space=pltpu.VMEM)
HBM = pl.BlockSpec(memory_space=pltpu.HBM)
ANY = pl.BlockSpec(memory_space=pl.ANY)
params = pltpu.CompilerParams(vmem_limit_bytes=32 * 1024 * 1024)


def in_hbm(*arrays):
    return [pltpu.with_memory_space_constraint(a, pltpu.HBM) for a in arrays]


def cost(flops, nbytes, exps=0):
    return pl.CostEstimate(flops=flops, bytes_accessed=nbytes, transcendentals=exps)


def merge(grads, weights, rows, dim):
    heads, _, columns = weights.shape
    tile = 2 * LANES
    return pl.pallas_call(
        merge_kernel,
        out_shape=jax.ShapeDtypeStruct((rows, dim), bf16),
        grid=(dim // tile,),
        in_specs=[
            pl.BlockSpec(grads.shape, lambda i: (0, 0, 0)),
            pl.BlockSpec((heads, tile, columns), lambda i: (0, i, 0)),
        ],
        out_specs=pl.BlockSpec((rows, tile), lambda i: (0, i)),
        scratch_shapes=[
            pltpu.VMEM((rows, 3 * LANES * heads), bf16),
            pltpu.VMEM((rows, (columns - 3 * LANES) * heads), bf16),
        ],
        compiler_params=params,
        cost_estimate=cost(2 * rows * dim * heads * columns, heads * dim * columns * 2),
        name="head_sum",
    )(grads, weights)


def per_device(ctx, tokens, feature_weight, window_weight, value_weight, log_decay, out_grad):
    rows, dim = tokens.shape
    nf2 = feature_weight.shape[1]
    nf = nf2 // 2
    dh = value_weight.shape[1]
    columns = 3 * dh + nf2
    chips, count, heads = lax.axis_size(ctx[:-1]), lax.axis_size(ctx), lax.axis_size("tp")
    fw_t = feature_weight.T
    tile = 2 * LANES
    spread = heads == 4 and count * tile == dim and count == 8
    packs = []
    if spread:
        packs = [jax.ShapeDtypeStruct((columns * tile // LANES, LANES), bf16)]
        packs += [jax.ShapeDtypeStruct((chips - 1, *packs[0].shape), bf16)]

    payload = 2 * rows + 2 * nf + 16
    block = jax.ShapeDtypeStruct((payload, LANES), bf16)
    outs = pl.pallas_call(
        partial(project_kernel, ctx, len(packs)),
        out_shape=packs
        + [block] * (chips + 2)
        + [
            jax.ShapeDtypeStruct((rows, nf2), bf16),
            jax.ShapeDtypeStruct((rows, 1), f32),
            jax.ShapeDtypeStruct((dim, 2 * dh), bf16),
            jax.ShapeDtypeStruct((dim, dh), bf16),
            jax.ShapeDtypeStruct((nf2, dim), bf16),
        ],
        in_specs=[HBM] * 6,
        out_specs=[VMEM] * (len(packs) + chips + 7),
        scratch_shapes=[
            pltpu.VMEM((rows, dim), bf16),
            pltpu.VMEM((1, rows), f32),
            pltpu.VMEM((rows, dh), bf16),
            pltpu.SemaphoreType.DMA((CHUNKS, 4)),
            pltpu.SemaphoreType.DMA((2,)),
        ],
        compiler_params=params,
        cost_estimate=cost(1, 1024),
        name="project",
    )(*in_hbm(tokens, fw_t, window_weight, value_weight, log_decay.T, out_grad))
    *sends, own, query, feat, cum, ww, vw, fw = outs[len(packs) :]

    swap = [(0, 1), (1, 0)]
    recv = {}
    for d in range(1, chips):
        recv[2 * d] = lax.ppermute(sends[d], ctx[:-1], [(i, i ^ d) for i in range(chips)])
    recv[1] = lax.ppermute(sends[0], "core", swap)
    if spread:
        across = lax.ppermute(outs[0], "tp", [(z, z ^ 2) for z in range(heads)])
    for d in range(1, chips):
        if spread and d == chips - 1:
            across, recv[2 * d] = lax.optimization_barrier((across, recv[2 * d]))
        recv[2 * d + 1] = lax.ppermute(recv[2 * d], "core", swap)
    recv = [recv[d] for d in range(1, count)]
    if count > 8:
        recv = [jnp.stack(recv)]

    if spread:
        early = lax.ppermute(outs[0], "tp", [(z, z ^ 1) for z in range(heads)])
        across, early, recv = lax.optimization_barrier((across, early, recv))
        near = [across, lax.ppermute(across, "tp", [(z, z ^ 1) for z in range(heads)])]

    attended, stat, sheet = pl.pallas_call(
        lambda *refs: query_kernel(ctx, count, len(recv), *refs),
        out_shape=[
            jax.ShapeDtypeStruct((rows, dh), bf16),
            jax.ShapeDtypeStruct((8, rows), f32),
            jax.ShapeDtypeStruct((rows, LANES), f32),
        ],
        in_specs=[VMEM] * (len(recv) + 4),
        out_specs=[VMEM] * 3,
        scratch_shapes=[
            pltpu.VMEM((count, 2 * rows, dh), bf16),
            pltpu.VMEM((WINDOW // rows + 1, rows, rows), f32),
            pltpu.VMEM((count, rows), f32),
        ],
        compiler_params=params,
        cost_estimate=cost(1, 1024),
        name="query_side",
    )(*recv, own, query, feat, cum)
    stats = [stat]
    for name in reversed(ctx):
        if spread and len(stats) == 2:
            near, sent, stats = lax.optimization_barrier((near, outs[1], stats))
        held = stats[0] if len(stats) == 1 else jnp.concatenate(stats, axis=0)
        stats.append(lax.ppermute(held, name, swap))
    if count > 8:
        stats = [jnp.concatenate(stats, axis=0)]

    if spread:
        first = [early, lax.ppermute(sent, "tp", [(z, z ^ 1) for z in range(heads)])]
        near, stats = lax.optimization_barrier((near, stats))
        pieces = [
            pl.pallas_call(
                stack_kernel,
                out_shape=jax.ShapeDtypeStruct((heads - 2, *packs[0].shape), bf16),
                in_specs=[VMEM] * (heads - 2),
                out_specs=VMEM,
                compiler_params=params,
                cost_estimate=cost(1, 1024),
                name="stack",
            )(*near)
        ]
        for d in (1, 2):
            pieces.append(
                lax.ppermute(pieces[0], ctx[:-1], [(i, i ^ d) for i in range(chips)])
            )
        pieces[0], sheet = lax.optimization_barrier((pieces[0], sheet))

    grads = pl.pallas_call(
        lambda *refs: gradient_kernel(ctx, count, len(recv), len(stats), *refs),
        out_shape=jax.ShapeDtypeStruct((3 * rows + nf2 * rows // LANES, LANES), bf16),
        in_specs=[VMEM] * (len(recv) + len(stats) + 4),
        out_specs=VMEM,
        scratch_shapes=[pltpu.VMEM((count, LANES), f32)],
        compiler_params=params,
        cost_estimate=cost(1, 1024),
        name="gradients",
    )(*recv, *stats, own, query, feat, sheet)
    if not spread:
        weights = jnp.concatenate([window_weight, value_weight, feature_weight], axis=1)
        weights = lax.all_gather(weights, "tp")
        return (attended, merge(lax.all_gather(grads, "tp"), weights, rows, dim))

    diagonal, grads = lax.optimization_barrier((pieces[0], grads))
    pieces.append(lax.ppermute(diagonal, ctx[:-1], [(i, i ^ 3) for i in range(chips)]))
    first[1], grads = lax.optimization_barrier((first[1], grads))
    grads = lax.all_gather(grads, "tp")
    pieces, first, grads = lax.optimization_barrier((pieces, first, grads))
    sibling_grads = lax.ppermute(grads, "core", swap)

    def operands_of(grads):
        return pl.pallas_call(
            cat_kernel,
            out_shape=[
                jax.ShapeDtypeStruct((rows, 3 * LANES * heads), bf16),
                jax.ShapeDtypeStruct((rows, nf2 * heads), bf16),
            ],
            in_specs=[VMEM],
            out_specs=[VMEM] * 2,
            compiler_params=params,
            cost_estimate=cost(1, 1024),
            name="cat",
        )(grads)

    mine = operands_of(grads)

    def columns_of(distances, operands):
        parts = [pieces[e // 2] for e in distances]
        return pl.pallas_call(
            partial(columns_kernel, ctx, distances),
            out_shape=jax.ShapeDtypeStruct((len(parts), rows, tile), bf16),
            in_specs=[VMEM] * (7 + len(parts)),
            out_specs=VMEM,
            compiler_params=params,
            cost_estimate=cost(1, 1024),
            name="columns",
        )(*operands, ww, vw, fw, *parts, *first)

    early_tiles = columns_of((0, 2), mine)
    sibling_grads, early_tiles = lax.optimization_barrier((sibling_grads, early_tiles))
    passed = columns_of((0, 2, 4, 6), operands_of(sibling_grads))
    passed, mine = lax.optimization_barrier((passed, mine))
    received = lax.ppermute(passed, "core", swap)
    late_tiles = columns_of((4, 6), mine)
    late_tiles, received = lax.optimization_barrier((late_tiles, received))
    total = pl.pallas_call(
        partial(lay_kernel, ctx),
        out_shape=jax.ShapeDtypeStruct((rows, dim), bf16),
        in_specs=[VMEM] * 3,
        out_specs=ANY,
        scratch_shapes=[pltpu.SemaphoreType.DMA((count,))],
        compiler_params=params,
        cost_estimate=cost(1, 1024),
        name="lay",
    )(early_tiles, late_tiles, received)
    return (attended, total)


def solution(mesh):
    blocks, tp = mesh.devices.shape
    bits = blocks.bit_length() - 1
    assert blocks == 2**bits
    ctx = tuple(f"half{i}" for i in range(bits - 1)) + ("core",)
    split = Mesh(mesh.devices.reshape((2,) * bits + (tp,)), (*ctx, "tp"))
    in_specs = (
        P(ctx, None),
        P(None, "tp"),
        P(None, "tp"),
        P(None, "tp"),
        P(ctx, "tp"),
        P(ctx, "tp"),
    )
    out_specs = (P(ctx, "tp"), P(ctx, None))
    return jax.shard_map(
        partial(per_device, ctx),
        mesh=split,
        in_specs=in_specs,
        out_specs=out_specs,
        check_vma=False,
    )
```

```python
from functools import partial

import jax
import jax.numpy as jnp
from jax import lax
from jax.experimental import pallas as pl
from jax.experimental.pallas import tpu as pltpu
from jax.sharding import Mesh
from jax.sharding import PartitionSpec as P

WINDOW = 1024
LANES = 128
MASKED = -1e30
CHUNKS = 4
f32 = jnp.float32
bf16 = jnp.bfloat16


def nn(a, b):
    return lax.dot_general(a, b, (((1,), (0,)), ((), ())), preferred_element_type=f32)


def nt(a, b):
    return lax.dot_general(a, b, (((1,), (1,)), ((), ())), preferred_element_type=f32)


def partner(me, d, count):
    assert count & (count - 1) == 0
    return jnp.bitwise_xor(me, d)


def wide(view, start, count):
    return jnp.concatenate(
        [view[start : start + count, :], view[start + count : start + 2 * count, :]], axis=1
    )


def put_wide(ref, start, value):
    count = value.shape[0]
    for half in range(value.shape[1] // LANES):
        ref[start + half * count : start + (half + 1) * count, :] = value[
            :, half * LANES : (half + 1) * LANES
        ]


def cum_row(view, start):
    tail = view[start : start + 16, :].astype(f32)
    first = tail[0:1] + tail[2:3] + tail[4:5]
    second = tail[1:2] + tail[3:4] + tail[5:6]
    return jnp.concatenate([first, second], axis=1)


def iotas(rows):
    return (
        lax.broadcasted_iota(jnp.int32, (rows, rows), 0),
        lax.broadcasted_iota(jnp.int32, (rows, rows), 1),
    )


def block_index(ctx):
    place = 0
    for name in ctx:
        place = place * lax.axis_size(name) + lax.axis_index(name)
    return place


def pack(me, ww_ref, vw_ref, fw_ref, out_ref):
    nf2 = fw_ref.shape[0]
    tile = 2 * LANES
    at = pl.multiple_of(me * tile, tile)
    rows = pl.ds(at, tile)
    out_ref[0:tile, :] = ww_ref[rows, 0:LANES]
    out_ref[tile : 2 * tile, :] = ww_ref[rows, LANES:]
    out_ref[2 * tile : 3 * tile, :] = vw_ref[rows, :]
    put_wide(out_ref, 3 * tile, fw_ref[:, rows])


def project_kernel(ctx, packs, tok_hbm, fw_hbm, ww_hbm, vw_hbm, ld_hbm, do_hbm, *rest):
    *sends, keys_ref, query_ref, feat_ref, cum_ref, ww_ref, vw_ref, fw_ref = rest[packs:-5]
    tok_ref, ld_ref, do_ref, sems, small = rest[-5:]
    me = block_index(ctx)
    rows, dim = tok_ref.shape
    dh = do_ref.shape[1]
    nf = fw_ref.shape[0] // 2
    span = dim // CHUNKS
    copies = []
    for c in range(CHUNKS):
        part = pl.ds(c * span, span)
        copies.append([
            pltpu.make_async_copy(tok_hbm.at[:, part], tok_ref.at[:, part], sems.at[c, 0]),
            pltpu.make_async_copy(ww_hbm.at[part, :], ww_ref.at[part, :], sems.at[c, 1]),
            pltpu.make_async_copy(vw_hbm.at[part, :], vw_ref.at[part, :], sems.at[c, 2]),
            pltpu.make_async_copy(fw_hbm.at[:, part], fw_ref.at[:, part], sems.at[c, 3]),
        ])
    others = [
        pltpu.make_async_copy(ld_hbm, ld_ref, small.at[0]),
        pltpu.make_async_copy(do_hbm, do_ref, small.at[1]),
    ]
    for copy in others:
        copy.start()
    for group in copies:
        for at, copy in enumerate(group):
            copy.start(priority=min(at, 1))
    for copy in others:
        copy.wait()
    at_row, at_col = iotas(rows)
    ld_r = ld_ref[...]
    ld_c = jnp.sum(jnp.where(at_row == at_col, ld_r, 0.0), axis=1, keepdims=True)
    cum_r = jnp.sum(jnp.where(at_row <= at_col, ld_c, 0.0), axis=0, keepdims=True)
    cum_ref[...] = jnp.sum(jnp.where(at_col <= at_row, ld_r, 0.0), axis=1, keepdims=True)
    high = cum_r.astype(bf16)
    left = cum_r - high.astype(f32)
    mid = left.astype(bf16)
    low = (left - mid.astype(f32)).astype(bf16)
    pieces = [t[:, h : h + LANES].astype(f32) for t in (high, mid, low) for h in range(0, rows, LANES)]
    tail = jnp.concatenate(pieces + [jnp.zeros((10, LANES), f32)], axis=0).astype(bf16)

    feat = jnp.zeros((rows, 2 * nf), f32)
    main = jnp.zeros((rows, 3 * dh), f32)
    for c in range(CHUNKS):
        for copy in copies[c]:
            copy.wait()
        part = slice(c * span, (c + 1) * span)
        tok = tok_ref[:, part]
        feat += nt(tok, fw_ref[:, part])
        main += nn(tok, jnp.concatenate([ww_ref[part, :], vw_ref[part, :]], axis=1))
    feat = feat.astype(bf16)
    window = main[:, : 2 * dh].astype(bf16)
    values = main[:, 2 * dh :].astype(bf16)
    feat_ref[...] = feat
    small_row, small_col = iotas(2 * nf)
    feat_t = nt((small_row == small_col).astype(bf16), feat).astype(bf16)
    feat_at = 2 * rows
    tail_at = feat_at + 2 * nf

    def put_keys(ref):
        ref[0:rows, :] = window[:, dh:]
        ref[rows : 2 * rows, :] = values
        put_wide(ref, feat_at, feat_t[nf:, :])
        ref[tail_at : tail_at + 16, :] = tail

    def put_query(ref):
        ref[0:rows, :] = window[:, :dh]
        ref[rows : 2 * rows, :] = do_ref[...]
        put_wide(ref, feat_at, feat_t[:nf, :])
        ref[tail_at : tail_at + 16, :] = tail

    put_keys(keys_ref)
    put_query(query_ref)
    for at, ref in enumerate(sends):
        later = jnp.bitwise_xor(me, max(2 * at, 1)) > me
        pl.when(later)(lambda ref=ref: put_keys(ref))
        pl.when(jnp.logical_not(later))(lambda ref=ref: put_query(ref))
    if packs:
        own_pack, other_pack = rest[:packs]
        pack(me, ww_ref, vw_ref, fw_ref, own_pack)
        for d in range(other_pack.shape[0]):
            piece = jnp.bitwise_xor(me, 2 * d + 2)
            pack(piece, ww_ref, vw_ref, fw_ref, other_pack.at[d])

def stack_kernel(*refs):
    *parts, out_ref = refs
    for t, ref in enumerate(parts):
        out_ref[t] = ref[...]


def between(totals, low, high):
    at = lax.broadcasted_iota(jnp.int32, totals.shape, 0)
    return jnp.sum(jnp.where((at > low) & (at < high), totals, 0.0), axis=0, keepdims=True)


def over_partners(count, body, carry):
    if count <= 8:
        for d in range(1, count):
            carry = body(d, carry)
        return carry
    return lax.fori_loop(1, count, body, carry)


def query_kernel(ctx, count, recvs, *rest):
    recvs, rest = rest[:recvs], rest[recvs:]
    own_ref, query_ref, feat_ref, cum_ref, *rest = rest
    near_ref, p_ref, cums_ref = rest[-3:]
    att_ref, stat_ref, sheet_ref = rest[:3]

    def recv(d):
        return recvs[d - 1] if len(recvs) > 1 else recvs[0].at[d - 1]

    me = block_index(ctx)
    rows, dh = att_ref.shape
    nf = feat_ref.shape[1] // 2
    back = WINDOW // rows
    feat_at = 2 * rows
    tail_at = feat_at + 2 * nf
    scale = dh ** (-0.5)
    feat_scale = nf ** (-0.5)
    wq = query_ref[0:rows, :]
    do = query_ref[rows : 2 * rows, :]
    q = feat_ref[:, :nf]
    at_row, at_col = iotas(rows)
    own_cum = cum_row(own_ref, tail_at)
    cums_ref[pl.ds(me, 1), :] = own_cum
    near_ref[me] = own_ref[0 : 2 * rows, :]

    def gather(d, carry):
        j = partner(me, d, count)
        view = recv(d)
        near_ref[j] = view[0 : 2 * rows, :]
        cums_ref[pl.ds(j, 1), :] = cum_row(view, tail_at)
        return carry

    over_partners(count, gather, 0)

    def near(w):
        return near_ref.at[jnp.maximum(me - back + w, 0)]

    top = jnp.full((rows, LANES), MASKED, f32)
    for w in range(back + 1):
        keys = own_ref[0:rows, :] if w == back else near(w)[0:rows, :]
        s = nt(wq, keys) * scale
        if w == back:
            s = jnp.where(at_col <= at_row, s, MASKED)
        elif w == 0:
            s = jnp.where((at_col > at_row) & (me >= back), s, MASKED)
        else:
            s = jnp.where(me >= back - w, s, MASKED)
        p_ref[w] = s
        for h in range(0, rows, LANES):
            top = jnp.maximum(top, s[:, h : h + LANES])
    top = jnp.max(top, axis=1, keepdims=True)
    total = jnp.zeros((rows, LANES), f32)
    out = jnp.zeros((rows, dh), f32)
    for w in range(back + 1):
        p = jnp.exp(p_ref[w] - top)
        for h in range(0, rows, LANES):
            total += p[:, h : h + LANES]
        vals = own_ref[rows : 2 * rows, :] if w == back else near(w)[rows : 2 * rows, :]
        out += nn(p.astype(bf16), vals)
    total = jnp.sum(total, axis=1, keepdims=True)
    windowed = out * (1.0 / total)

    cum_c = cum_ref[...]
    growth = jnp.exp(cum_c)
    totals = cums_ref[:, rows - 1 : rows]

    def forward(d, carry):
        num, den = carry
        j = partner(me, d, count)
        view = recv(d)
        gap = between(totals, j - 1, me)
        es = jnp.where(j < me, jnp.exp(jnp.minimum(gap - cums_ref[pl.ds(j, 1), :], 0.0)), 0.0)
        x = nn(q, wide(view, feat_at, nf)) * feat_scale
        weight = (1.0 + x + 0.5 * x * x) * es
        for h in range(0, rows, LANES):
            den += weight[:, h : h + LANES]
        num += nn(weight.astype(bf16), view[rows : 2 * rows, :])
        return num, den

    num, den = over_partners(
        count, forward, (jnp.zeros((rows, dh), f32), jnp.zeros((rows, LANES), f32))
    )
    x = nn(q, wide(own_ref, feat_at, nf)) * feat_scale
    e = jnp.where(at_col <= at_row, jnp.exp(jnp.minimum(cum_c - own_cum, 0.0)), 0.0)
    weight = (1.0 + x + 0.5 * x * x) * e
    num = num * growth + nn(weight.astype(bf16), own_ref[rows : 2 * rows, :])
    den = den * growth
    for h in range(0, rows, LANES):
        den += weight[:, h : h + LANES]
    rden = 1.0 / jnp.sum(den, axis=1, keepdims=True)
    linear = num * rden
    att_ref[...] = (linear + windowed).astype(bf16)
    do_f = do.astype(f32)
    delta_w = jnp.sum(do_f * windowed, axis=1, keepdims=True)
    delta_l = jnp.sum(do_f * linear, axis=1, keepdims=True)
    lse = top + jnp.log(total)
    lane = lax.broadcasted_iota(jnp.int32, (rows, LANES), 1)
    sheet = jnp.where(lane == 0, lse, 0.0)
    sheet = jnp.where(lane == 1, delta_w, sheet)
    sheet = jnp.where(lane == 2, rden, sheet)
    sheet = jnp.where(lane == 3, delta_l, sheet)
    sheet = jnp.where(lane == 4, cum_c, sheet)
    sheet_ref[...] = sheet
    stat_ref[...] = jnp.transpose(sheet)[0:8, :]


def gradient_kernel(ctx, count, recvs, stats, *rest):
    recvs, rest = rest[:recvs], rest[recvs:]
    stats, rest = rest[:stats], rest[stats:]
    own_ref, query_ref, feat_ref, sheet_ref, *rest, total_ref = rest

    def recv(d):
        return recvs[d - 1] if len(recvs) > 1 else recvs[0].at[d - 1]

    me = block_index(ctx)
    rows = feat_ref.shape[0]
    dh = LANES
    nf = feat_ref.shape[1] // 2
    feat_at = 2 * rows
    scale = dh ** (-0.5)
    feat_scale = nf ** (-0.5)
    at_row, at_col = iotas(rows)
    apart = at_row - at_col
    wq, wk = query_ref[0:rows, :], own_ref[0:rows, :]
    do, v = query_ref[rows : 2 * rows, :], own_ref[rows : 2 * rows, :]
    q, k = feat_ref[:, :nf], feat_ref[:, nf:]
    lse_c, dw_c = sheet_ref[:, 0:1], sheet_ref[:, 1:2]
    rden_c, dl_c, cum_c = sheet_ref[:, 2:3], sheet_ref[:, 3:4], sheet_ref[:, 4:5]
    def stat(d):
        if len(stats) == 1:
            return stats[0].at[pl.ds(pl.multiple_of(8 * d, 8), 8)]
        at = d.bit_length()
        return stats[at].at[pl.ds(8 * (d - (1 << at >> 1)), 8)]

    mine_ref = stat(0)
    own_cum = mine_ref[4:5, :]
    total_ref[pl.ds(me, 1), :] = own_cum[:, rows - LANES :]

    def place(d, carry):
        total_ref[pl.ds(partner(me, d, count), 1), :] = stat(d)[4:5, rows - LANES :]
        return carry

    over_partners(count, place, 0)
    totals = total_ref[:, LANES - 1 :]
    growth_c = jnp.exp(cum_c) * rden_c
    tail_c = jnp.exp(own_cum[:, rows - 1 : rows] - cum_c)

    def pick(flag, a, b):
        return jnp.where(flag, a, b)

    s = nt(wq, wk) * scale
    causal = at_col <= at_row
    p = jnp.where(causal, jnp.exp(s - lse_c), 0.0)
    dp = nt(do, v)
    dwq = nn((p * (dp - dw_c)).astype(bf16), wk)
    x = nn(q, wide(own_ref, feat_at, nf)) * feat_scale
    e = jnp.where(causal, jnp.exp(jnp.minimum(cum_c - own_cum, 0.0)), 0.0) * rden_c
    dx = (dp - dl_c) * e * (1.0 + x)
    dq_f = nt(dx.astype(bf16), wide(own_ref, feat_at, nf))

    s = nt(wk, wq) * scale
    causal = at_row <= at_col
    p = jnp.where(causal, jnp.exp(s - mine_ref[0:1, :]), 0.0)
    dp = nt(v, do)
    dwk = nn((p * (dp - mine_ref[1:2, :])).astype(bf16), wq)
    x = nn(k, wide(query_ref, feat_at, nf)) * feat_scale
    e = jnp.where(causal, jnp.exp(jnp.minimum(own_cum - cum_c, 0.0)), 0.0) * mine_ref[2:3, :]
    dx = (dp - mine_ref[3:4, :]) * e * (1.0 + x)
    dk_f = nt(dx.astype(bf16), wide(query_ref, feat_at, nf))
    dv = nn((p + (1.0 + x + 0.5 * x * x) * e).astype(bf16), do)

    def step(d, carry):
        dwq, dq_f, dwk, dk_f, dv = carry
        j = partner(me, d, count)
        view = recv(d)
        mine = j < me
        sign = pick(mine, 1, -1)
        limit = WINDOW - jnp.abs(me - j) * rows
        rows_w = pick(mine, wq, wk)
        rows_v = pick(mine, do, v)
        rows_f = pick(mine, q, k)
        other_w = view[0:rows, :]
        other_v = view[rows : 2 * rows, :]
        other_f = wide(view, feat_at, nf)
        st = stat(d)
        zero = jnp.zeros((1, rows), f32)
        cum = st[4:5, :]
        gap = between(totals, jnp.minimum(me, j), jnp.maximum(me, j))
        e_r = jnp.exp(jnp.minimum(gap + pick(mine, cum[:, rows - 1 : rows] - cum, cum), 0.0))
        e_r = e_r * pick(mine, 1.0, st[2:3, :])
        e_c = pick(mine, growth_c, tail_c)

        s = nt(rows_w, other_w) * scale
        p = jnp.exp(s - pick(mine, lse_c, 0.0) - pick(mine, zero, st[0:1, :]))
        p = jnp.where(apart * sign < limit, p, 0.0)
        dp = nt(rows_v, other_v)
        ds = p * (dp - pick(mine, dw_c, 0.0) - pick(mine, zero, st[1:2, :]))
        more_w = nn(ds.astype(bf16), other_w)
        x = nn(rows_f, other_f) * feat_scale
        e = e_r * e_c
        dx = (dp - pick(mine, dl_c, 0.0) - pick(mine, zero, st[3:4, :])) * e * (1.0 + x)
        more_f = nt(dx.astype(bf16), other_f)
        more_v = nn((p + (1.0 + x + 0.5 * x * x) * e).astype(bf16), other_v)
        dwq = dwq + pick(mine, more_w, 0.0)
        dwk = dwk + pick(mine, 0.0, more_w)
        dq_f = dq_f + pick(mine, more_f, 0.0)
        dk_f = dk_f + pick(mine, 0.0, more_f)
        dv = dv + pick(mine, 0.0, more_v)
        return dwq, dq_f, dwk, dk_f, dv

    dwq, dq_f, dwk, dk_f, dv = over_partners(count, step, (dwq, dq_f, dwk, dk_f, dv))
    dwq, dwk = (dwq * scale).astype(bf16), (dwk * scale).astype(bf16)
    dv = dv.astype(bf16)
    padded = jnp.concatenate([dq_f, dk_f, jnp.zeros((rows, LANES - 2 * nf), f32)], axis=1)
    dft = (jnp.transpose(padded)[: 2 * nf] * feat_scale).astype(bf16)
    (grad_ref,) = rest
    grad_ref[0:rows, :] = dwq
    grad_ref[rows : 2 * rows, :] = dwk
    grad_ref[2 * rows : 3 * rows, :] = dv
    put_wide(grad_ref, 3 * rows, dft)


def gather_rows(grad_ref, order, cat_ref, feat_ref):
    rows = cat_ref.shape[0]
    nf2 = feat_ref.shape[1] // len(order)
    for at, h in enumerate(order):
        for part in range(3):
            lane = (3 * at + part) * LANES
            cat_ref[:, lane : lane + LANES] = grad_ref[h, part * rows : (part + 1) * rows, :]
    dft = jnp.concatenate([wide(grad_ref.at[h], 3 * rows, nf2) for h in order], axis=0)
    feat_ref[...] = jnp.transpose(dft.astype(f32)).astype(bf16)


def cat_kernel(grad_ref, cat_ref, feat_ref):
    heads = grad_ref.shape[0]
    head = lax.axis_index("tp")
    order = [head] + [jnp.bitwise_xor(head, t) for t in range(1, heads)]
    gather_rows(grad_ref, order, cat_ref, feat_ref)


def column_sums(ctx, e, cat_ref, feat_ref, ww_ref, vw_ref, fw_ref, piece_ref, firsts):
    nf2 = fw_ref.shape[0]
    heads = feat_ref.shape[1] // nf2
    tile = 2 * LANES
    part = pl.ds(pl.multiple_of(jnp.bitwise_xor(block_index(ctx), e) * tile, tile), tile)
    views = [firsts[1].at[e // 2 - 1] if e > 1 else firsts[0]]
    views += [piece_ref.at[t] for t in range(heads - 2)]
    main = [ww_ref[part, :], vw_ref[part, :]]
    main += [v[m * tile : (m + 1) * tile, :] for v in views for m in range(3)]
    feats = [fw_ref[:, part]] + [wide(v, 3 * tile, nf2) for v in views]
    total = nt(cat_ref[...], jnp.concatenate(main, axis=1))
    total += nn(feat_ref[...], jnp.concatenate(feats, axis=0))
    return total.astype(bf16), part


def columns_kernel(ctx, distances, *rest):
    operands, rest = rest[:5], rest[5:]
    pieces, firsts = rest[: len(distances)], rest[len(distances) : len(distances) + 2]
    for n, (e, ref) in enumerate(zip(distances, pieces)):
        rest[-1][n], _ = column_sums(ctx, e, *operands, ref, firsts)


def lay_kernel(ctx, *refs):
    *tiles, received_ref, out_ref, sems = refs
    views = [(ref.at[n], 2 * (2 * m + n)) for m, ref in enumerate(tiles) for n in range(2)]
    views += [(received_ref.at[d], 2 * d + 1) for d in range(received_ref.shape[0])]
    copies = []
    for n, (view, e) in enumerate(views):
        tile = view.shape[1]
        at = jnp.bitwise_xor(block_index(ctx), e) * tile
        part = pl.ds(pl.multiple_of(at, tile), tile)
        copies.append(pltpu.make_async_copy(view, out_ref.at[:, part], sems.at[n]))
        copies[-1].start()
    for copy in copies:
        copy.wait()


def merge_kernel(grad_ref, weight_ref, out_ref, cat_ref, feat_ref):
    heads = grad_ref.shape[0]
    tile = out_ref.shape[1]
    lanes = 3 * LANES
    nf2 = feat_ref.shape[1] // heads

    @pl.when(pl.program_id(0) == 0)
    def _():
        gather_rows(grad_ref, range(heads), cat_ref, feat_ref)

    views = [weight_ref.at[h] for h in range(heads)]
    main = jnp.concatenate([v[:, 0:lanes] for v in views], axis=1)
    feats = jnp.concatenate([v[:, lanes:] for v in views], axis=1)
    out_ref[...] = (nt(cat_ref[...], main) + nt(feat_ref[...], feats)).astype(bf16)


VMEM = pl.BlockSpec(memory_space=pltpu.VMEM)
HBM = pl.BlockSpec(memory_space=pltpu.HBM)
ANY = pl.BlockSpec(memory_space=pl.ANY)
params = pltpu.CompilerParams(vmem_limit_bytes=32 * 1024 * 1024)


def in_hbm(*arrays):
    return [pltpu.with_memory_space_constraint(a, pltpu.HBM) for a in arrays]


def cost(flops, nbytes, exps=0):
    return pl.CostEstimate(flops=flops, bytes_accessed=nbytes, transcendentals=exps)


def merge(grads, weights, rows, dim):
    heads, _, columns = weights.shape
    tile = 2 * LANES
    return pl.pallas_call(
        merge_kernel,
        out_shape=jax.ShapeDtypeStruct((rows, dim), bf16),
        grid=(dim // tile,),
        in_specs=[
            pl.BlockSpec(grads.shape, lambda i: (0, 0, 0)),
            pl.BlockSpec((heads, tile, columns), lambda i: (0, i, 0)),
        ],
        out_specs=pl.BlockSpec((rows, tile), lambda i: (0, i)),
        scratch_shapes=[
            pltpu.VMEM((rows, 3 * LANES * heads), bf16),
            pltpu.VMEM((rows, (columns - 3 * LANES) * heads), bf16),
        ],
        compiler_params=params,
        cost_estimate=cost(2 * rows * dim * heads * columns, heads * dim * columns * 2),
        name="head_sum",
    )(grads, weights)


def per_device(ctx, tokens, feature_weight, window_weight, value_weight, log_decay, out_grad):
    rows, dim = tokens.shape
    nf2 = feature_weight.shape[1]
    nf = nf2 // 2
    dh = value_weight.shape[1]
    columns = 3 * dh + nf2
    chips, count, heads = lax.axis_size(ctx[:-1]), lax.axis_size(ctx), lax.axis_size("tp")
    fw_t = feature_weight.T
    tile = 2 * LANES
    spread = heads == 4 and count * tile == dim and count == 8
    packs = []
    if spread:
        packs = [jax.ShapeDtypeStruct((columns * tile // LANES, LANES), bf16)]
        packs += [jax.ShapeDtypeStruct((chips - 1, *packs[0].shape), bf16)]

    payload = 2 * rows + 2 * nf + 16
    block = jax.ShapeDtypeStruct((payload, LANES), bf16)
    outs = pl.pallas_call(
        partial(project_kernel, ctx, len(packs)),
        out_shape=packs
        + [block] * (chips + 2)
        + [
            jax.ShapeDtypeStruct((rows, nf2), bf16),
            jax.ShapeDtypeStruct((rows, 1), f32),
            jax.ShapeDtypeStruct((dim, 2 * dh), bf16),
            jax.ShapeDtypeStruct((dim, dh), bf16),
            jax.ShapeDtypeStruct((nf2, dim), bf16),
        ],
        in_specs=[HBM] * 6,
        out_specs=[VMEM] * (len(packs) + chips + 7),
        scratch_shapes=[
            pltpu.VMEM((rows, dim), bf16),
            pltpu.VMEM((1, rows), f32),
            pltpu.VMEM((rows, dh), bf16),
            pltpu.SemaphoreType.DMA((CHUNKS, 4)),
            pltpu.SemaphoreType.DMA((2,)),
        ],
        compiler_params=params,
        cost_estimate=cost(1, 1024),
        name="project",
    )(*in_hbm(tokens, fw_t, window_weight, value_weight, log_decay.T, out_grad))
    *sends, own, query, feat, cum, ww, vw, fw = outs[len(packs) :]

    swap = [(0, 1), (1, 0)]
    recv = {}
    for d in range(1, chips):
        recv[2 * d] = lax.ppermute(sends[d], ctx[:-1], [(i, i ^ d) for i in range(chips)])
    recv[1] = lax.ppermute(sends[0], "core", swap)
    if spread:
        across = lax.ppermute(outs[0], "tp", [(z, z ^ 2) for z in range(heads)])
    for d in range(1, chips):
        if spread and d == chips - 1:
            across, recv[2 * d] = lax.optimization_barrier((across, recv[2 * d]))
        recv[2 * d + 1] = lax.ppermute(recv[2 * d], "core", swap)
    recv = [recv[d] for d in range(1, count)]
    if count > 8:
        recv = [jnp.stack(recv)]

    if spread:
        early = lax.ppermute(outs[0], "tp", [(z, z ^ 1) for z in range(heads)])
        across, early, recv = lax.optimization_barrier((across, early, recv))
        near = [across, lax.ppermute(across, "tp", [(z, z ^ 1) for z in range(heads)])]

    attended, stat, sheet = pl.pallas_call(
        lambda *refs: query_kernel(ctx, count, len(recv), *refs),
        out_shape=[
            jax.ShapeDtypeStruct((rows, dh), bf16),
            jax.ShapeDtypeStruct((8, rows), f32),
            jax.ShapeDtypeStruct((rows, LANES), f32),
        ],
        in_specs=[VMEM] * (len(recv) + 4),
        out_specs=[VMEM] * 3,
        scratch_shapes=[
            pltpu.VMEM((count, 2 * rows, dh), bf16),
            pltpu.VMEM((WINDOW // rows + 1, rows, rows), f32),
            pltpu.VMEM((count, rows), f32),
        ],
        compiler_params=params,
        cost_estimate=cost(1, 1024),
        name="query_side",
    )(*recv, own, query, feat, cum)
    stats = [stat]
    for name in reversed(ctx):
        if spread and len(stats) == 2:
            near, sent, stats = lax.optimization_barrier((near, outs[1], stats))
        held = stats[0] if len(stats) == 1 else jnp.concatenate(stats, axis=0)
        stats.append(lax.ppermute(held, name, swap))
    if count > 8:
        stats = [jnp.concatenate(stats, axis=0)]

    if spread:
        first = [early, lax.ppermute(sent, "tp", [(z, z ^ 1) for z in range(heads)])]
        pieces = [
            pl.pallas_call(
                stack_kernel,
                out_shape=jax.ShapeDtypeStruct((heads - 2, *packs[0].shape), bf16),
                in_specs=[VMEM] * (heads - 2),
                out_specs=VMEM,
                compiler_params=params,
                cost_estimate=cost(1, 1024),
                name="stack",
            )(*near)
        ]
        for d in (1, 2):
            free, _ = lax.optimization_barrier((pieces[0], stats[d + 1]))
            pieces.append(lax.ppermute(free, ctx[:-1], [(i, i ^ d) for i in range(chips)]))
        pieces[0], sheet = lax.optimization_barrier((pieces[0], sheet))

    grads = pl.pallas_call(
        lambda *refs: gradient_kernel(ctx, count, len(recv), len(stats), *refs),
        out_shape=jax.ShapeDtypeStruct((3 * rows + nf2 * rows // LANES, LANES), bf16),
        in_specs=[VMEM] * (len(recv) + len(stats) + 4),
        out_specs=VMEM,
        scratch_shapes=[pltpu.VMEM((count, LANES), f32)],
        compiler_params=params,
        cost_estimate=cost(1, 1024),
        name="gradients",
    )(*recv, *stats, own, query, feat, sheet)
    if not spread:
        weights = jnp.concatenate([window_weight, value_weight, feature_weight], axis=1)
        weights = lax.all_gather(weights, "tp")
        return (attended, merge(lax.all_gather(grads, "tp"), weights, rows, dim))

    diagonal, grads = lax.optimization_barrier((pieces[0], grads))
    pieces.append(lax.ppermute(diagonal, ctx[:-1], [(i, i ^ 3) for i in range(chips)]))
    first[1], grads = lax.optimization_barrier((first[1], grads))
    grads = lax.all_gather(grads, "tp")
    pieces, first, grads = lax.optimization_barrier((pieces, first, grads))
    sibling_grads = lax.ppermute(grads, "core", swap)

    def operands_of(grads):
        return pl.pallas_call(
            cat_kernel,
            out_shape=[
                jax.ShapeDtypeStruct((rows, 3 * LANES * heads), bf16),
                jax.ShapeDtypeStruct((rows, nf2 * heads), bf16),
            ],
            in_specs=[VMEM],
            out_specs=[VMEM] * 2,
            compiler_params=params,
            cost_estimate=cost(1, 1024),
            name="cat",
        )(grads)

    mine = operands_of(grads)

    def columns_of(distances, operands):
        parts = [pieces[e // 2] for e in distances]
        return pl.pallas_call(
            partial(columns_kernel, ctx, distances),
            out_shape=jax.ShapeDtypeStruct((len(parts), rows, tile), bf16),
            in_specs=[VMEM] * (7 + len(parts)),
            out_specs=VMEM,
            compiler_params=params,
            cost_estimate=cost(1, 1024),
            name="columns",
        )(*operands, ww, vw, fw, *parts, *first)

    early_tiles = columns_of((0, 2), mine)
    sibling_grads, early_tiles = lax.optimization_barrier((sibling_grads, early_tiles))
    passed = columns_of((0, 2, 4, 6), operands_of(sibling_grads))
    passed, mine = lax.optimization_barrier((passed, mine))
    received = lax.ppermute(passed, "core", swap)
    late_tiles = columns_of((4, 6), mine)
    late_tiles, received = lax.optimization_barrier((late_tiles, received))
    total = pl.pallas_call(
        partial(lay_kernel, ctx),
        out_shape=jax.ShapeDtypeStruct((rows, dim), bf16),
        in_specs=[VMEM] * 3,
        out_specs=ANY,
        scratch_shapes=[pltpu.SemaphoreType.DMA((count,))],
        compiler_params=params,
        cost_estimate=cost(1, 1024),
        name="lay",
    )(early_tiles, late_tiles, received)
    return (attended, total)


def solution(mesh):
    blocks, tp = mesh.devices.shape
    bits = blocks.bit_length() - 1
    assert blocks == 2**bits
    ctx = tuple(f"half{i}" for i in range(bits - 1)) + ("core",)
    split = Mesh(mesh.devices.reshape((2,) * bits + (tp,)), (*ctx, "tp"))
    in_specs = (
        P(ctx, None),
        P(None, "tp"),
        P(None, "tp"),
        P(None, "tp"),
        P(ctx, "tp"),
        P(ctx, "tp"),
    )
    out_specs = (P(ctx, "tp"), P(ctx, None))
    return jax.shard_map(
        partial(per_device, ctx),
        mesh=split,
        in_specs=in_specs,
        out_specs=out_specs,
        check_vma=False,
    )
```

```python
from functools import partial

import jax
import jax.numpy as jnp
from jax import lax
from jax.experimental import pallas as pl
from jax.experimental.pallas import tpu as pltpu
from jax.sharding import Mesh
from jax.sharding import PartitionSpec as P

WINDOW = 1024
LANES = 128
MASKED = -1e30
CHUNKS = 4
f32 = jnp.float32
bf16 = jnp.bfloat16


def nn(a, b):
    return lax.dot_general(a, b, (((1,), (0,)), ((), ())), preferred_element_type=f32)


def nt(a, b):
    return lax.dot_general(a, b, (((1,), (1,)), ((), ())), preferred_element_type=f32)


def partner(me, d, count):
    assert count & (count - 1) == 0
    return jnp.bitwise_xor(me, d)


def wide(view, start, count):
    return jnp.concatenate(
        [view[start : start + count, :], view[start + count : start + 2 * count, :]], axis=1
    )


def put_wide(ref, start, value):
    count = value.shape[0]
    for half in range(value.shape[1] // LANES):
        ref[start + half * count : start + (half + 1) * count, :] = value[
            :, half * LANES : (half + 1) * LANES
        ]


def cum_row(view, start):
    tail = view[start : start + 16, :].astype(f32)
    first = tail[0:1] + tail[2:3] + tail[4:5]
    second = tail[1:2] + tail[3:4] + tail[5:6]
    return jnp.concatenate([first, second], axis=1)


def iotas(rows):
    return (
        lax.broadcasted_iota(jnp.int32, (rows, rows), 0),
        lax.broadcasted_iota(jnp.int32, (rows, rows), 1),
    )


def block_index(ctx):
    place = 0
    for name in ctx:
        place = place * lax.axis_size(name) + lax.axis_index(name)
    return place


def pack(me, ww_ref, vw_ref, fw_ref, out_ref):
    nf2 = fw_ref.shape[0]
    tile = 2 * LANES
    at = pl.multiple_of(me * tile, tile)
    rows = pl.ds(at, tile)
    out_ref[0:tile, :] = ww_ref[rows, 0:LANES]
    out_ref[tile : 2 * tile, :] = ww_ref[rows, LANES:]
    out_ref[2 * tile : 3 * tile, :] = vw_ref[rows, :]
    put_wide(out_ref, 3 * tile, fw_ref[:, rows])


def project_kernel(ctx, packs, tok_hbm, fw_hbm, ww_hbm, vw_hbm, ld_hbm, do_hbm, *rest):
    *sends, keys_ref, query_ref, feat_ref, cum_ref, ww_ref, vw_ref, fw_ref = rest[packs:-5]
    tok_ref, ld_ref, do_ref, sems, small = rest[-5:]
    me = block_index(ctx)
    rows, dim = tok_ref.shape
    dh = do_ref.shape[1]
    nf = fw_ref.shape[0] // 2
    span = dim // CHUNKS
    copies = []
    for c in range(CHUNKS):
        part = pl.ds(c * span, span)
        copies.append([
            pltpu.make_async_copy(tok_hbm.at[:, part], tok_ref.at[:, part], sems.at[c, 0]),
            pltpu.make_async_copy(ww_hbm.at[part, :], ww_ref.at[part, :], sems.at[c, 1]),
            pltpu.make_async_copy(vw_hbm.at[part, :], vw_ref.at[part, :], sems.at[c, 2]),
            pltpu.make_async_copy(fw_hbm.at[:, part], fw_ref.at[:, part], sems.at[c, 3]),
        ])
    others = [
        pltpu.make_async_copy(ld_hbm, ld_ref, small.at[0]),
        pltpu.make_async_copy(do_hbm, do_ref, small.at[1]),
    ]
    for copy in others:
        copy.start()
    for group in copies:
        for at, copy in enumerate(group):
            copy.start(priority=min(at, 1))
    for copy in others:
        copy.wait()
    at_row, at_col = iotas(rows)
    ld_r = ld_ref[...]
    ld_c = jnp.sum(jnp.where(at_row == at_col, ld_r, 0.0), axis=1, keepdims=True)
    cum_r = jnp.sum(jnp.where(at_row <= at_col, ld_c, 0.0), axis=0, keepdims=True)
    cum_ref[...] = jnp.sum(jnp.where(at_col <= at_row, ld_r, 0.0), axis=1, keepdims=True)
    high = cum_r.astype(bf16)
    left = cum_r - high.astype(f32)
    mid = left.astype(bf16)
    low = (left - mid.astype(f32)).astype(bf16)
    pieces = [t[:, h : h + LANES].astype(f32) for t in (high, mid, low) for h in range(0, rows, LANES)]
    tail = jnp.concatenate(pieces + [jnp.zeros((10, LANES), f32)], axis=0).astype(bf16)

    feat = jnp.zeros((rows, 2 * nf), f32)
    main = jnp.zeros((rows, 3 * dh), f32)
    for c in range(CHUNKS):
        for copy in copies[c]:
            copy.wait()
        part = slice(c * span, (c + 1) * span)
        tok = tok_ref[:, part]
        feat += nt(tok, fw_ref[:, part])
        main += nn(tok, jnp.concatenate([ww_ref[part, :], vw_ref[part, :]], axis=1))
    feat = feat.astype(bf16)
    window = main[:, : 2 * dh].astype(bf16)
    values = main[:, 2 * dh :].astype(bf16)
    feat_ref[...] = feat
    small_row, small_col = iotas(2 * nf)
    feat_t = nt((small_row == small_col).astype(bf16), feat).astype(bf16)
    feat_at = 2 * rows
    tail_at = feat_at + 2 * nf

    def put_keys(ref):
        ref[0:rows, :] = window[:, dh:]
        ref[rows : 2 * rows, :] = values
        put_wide(ref, feat_at, feat_t[nf:, :])
        ref[tail_at : tail_at + 16, :] = tail

    def put_query(ref):
        ref[0:rows, :] = window[:, :dh]
        ref[rows : 2 * rows, :] = do_ref[...]
        put_wide(ref, feat_at, feat_t[:nf, :])
        ref[tail_at : tail_at + 16, :] = tail

    put_keys(keys_ref)
    put_query(query_ref)
    for at, ref in enumerate(sends):
        later = jnp.bitwise_xor(me, max(2 * at, 1)) > me
        pl.when(later)(lambda ref=ref: put_keys(ref))
        pl.when(jnp.logical_not(later))(lambda ref=ref: put_query(ref))
    if packs:
        own_pack, other_pack = rest[:packs]
        pack(me, ww_ref, vw_ref, fw_ref, own_pack)
        for d in range(other_pack.shape[0]):
            piece = jnp.bitwise_xor(me, 2 * d + 4)
            pack(piece, ww_ref, vw_ref, fw_ref, other_pack.at[d])

def stack_kernel(*refs):
    *parts, out_ref = refs
    for t, ref in enumerate(parts):
        out_ref[t] = ref[...]


def between(totals, low, high):
    at = lax.broadcasted_iota(jnp.int32, totals.shape, 0)
    return jnp.sum(jnp.where((at > low) & (at < high), totals, 0.0), axis=0, keepdims=True)


def over_partners(count, body, carry):
    if count <= 8:
        for d in range(1, count):
            carry = body(d, carry)
        return carry
    return lax.fori_loop(1, count, body, carry)


def query_kernel(ctx, count, recvs, *rest):
    recvs, rest = rest[:recvs], rest[recvs:]
    own_ref, query_ref, feat_ref, cum_ref, *rest = rest
    near_ref, p_ref, cums_ref = rest[-3:]
    att_ref, stat_ref, sheet_ref = rest[:3]

    def recv(d):
        return recvs[d - 1] if len(recvs) > 1 else recvs[0].at[d - 1]

    me = block_index(ctx)
    rows, dh = att_ref.shape
    nf = feat_ref.shape[1] // 2
    back = WINDOW // rows
    feat_at = 2 * rows
    tail_at = feat_at + 2 * nf
    scale = dh ** (-0.5)
    feat_scale = nf ** (-0.5)
    wq = query_ref[0:rows, :]
    do = query_ref[rows : 2 * rows, :]
    q = feat_ref[:, :nf]
    at_row, at_col = iotas(rows)
    own_cum = cum_row(own_ref, tail_at)
    cums_ref[pl.ds(me, 1), :] = own_cum
    near_ref[me] = own_ref[0 : 2 * rows, :]

    def gather(d, carry):
        j = partner(me, d, count)
        view = recv(d)
        near_ref[j] = view[0 : 2 * rows, :]
        cums_ref[pl.ds(j, 1), :] = cum_row(view, tail_at)
        return carry

    over_partners(count, gather, 0)

    def near(w):
        return near_ref.at[jnp.maximum(me - back + w, 0)]

    top = jnp.full((rows, LANES), MASKED, f32)
    for w in range(back + 1):
        keys = own_ref[0:rows, :] if w == back else near(w)[0:rows, :]
        s = nt(wq, keys) * scale
        if w == back:
            s = jnp.where(at_col <= at_row, s, MASKED)
        elif w == 0:
            s = jnp.where((at_col > at_row) & (me >= back), s, MASKED)
        else:
            s = jnp.where(me >= back - w, s, MASKED)
        p_ref[w] = s
        for h in range(0, rows, LANES):
            top = jnp.maximum(top, s[:, h : h + LANES])
    top = jnp.max(top, axis=1, keepdims=True)
    total = jnp.zeros((rows, LANES), f32)
    out = jnp.zeros((rows, dh), f32)
    for w in range(back + 1):
        p = jnp.exp(p_ref[w] - top)
        for h in range(0, rows, LANES):
            total += p[:, h : h + LANES]
        vals = own_ref[rows : 2 * rows, :] if w == back else near(w)[rows : 2 * rows, :]
        out += nn(p.astype(bf16), vals)
    total = jnp.sum(total, axis=1, keepdims=True)
    windowed = out * (1.0 / total)

    cum_c = cum_ref[...]
    growth = jnp.exp(cum_c)
    totals = cums_ref[:, rows - 1 : rows]

    def forward(d, carry):
        num, den = carry
        j = partner(me, d, count)
        view = recv(d)
        gap = between(totals, j - 1, me)
        es = jnp.where(j < me, jnp.exp(jnp.minimum(gap - cums_ref[pl.ds(j, 1), :], 0.0)), 0.0)
        x = nn(q, wide(view, feat_at, nf)) * feat_scale
        weight = (1.0 + x + 0.5 * x * x) * es
        for h in range(0, rows, LANES):
            den += weight[:, h : h + LANES]
        num += nn(weight.astype(bf16), view[rows : 2 * rows, :])
        return num, den

    num, den = over_partners(
        count, forward, (jnp.zeros((rows, dh), f32), jnp.zeros((rows, LANES), f32))
    )
    x = nn(q, wide(own_ref, feat_at, nf)) * feat_scale
    e = jnp.where(at_col <= at_row, jnp.exp(jnp.minimum(cum_c - own_cum, 0.0)), 0.0)
    weight = (1.0 + x + 0.5 * x * x) * e
    num = num * growth + nn(weight.astype(bf16), own_ref[rows : 2 * rows, :])
    den = den * growth
    for h in range(0, rows, LANES):
        den += weight[:, h : h + LANES]
    rden = 1.0 / jnp.sum(den, axis=1, keepdims=True)
    linear = num * rden
    att_ref[...] = (linear + windowed).astype(bf16)
    do_f = do.astype(f32)
    delta_w = jnp.sum(do_f * windowed, axis=1, keepdims=True)
    delta_l = jnp.sum(do_f * linear, axis=1, keepdims=True)
    lse = top + jnp.log(total)
    lane = lax.broadcasted_iota(jnp.int32, (rows, LANES), 1)
    sheet = jnp.where(lane == 0, lse, 0.0)
    sheet = jnp.where(lane == 1, delta_w, sheet)
    sheet = jnp.where(lane == 2, rden, sheet)
    sheet = jnp.where(lane == 3, delta_l, sheet)
    sheet = jnp.where(lane == 4, cum_c, sheet)
    sheet_ref[...] = sheet
    stat_ref[...] = jnp.transpose(sheet)[0:8, :]


def gradient_kernel(ctx, count, recvs, stats, *rest):
    recvs, rest = rest[:recvs], rest[recvs:]
    stats, rest = rest[:stats], rest[stats:]
    own_ref, query_ref, feat_ref, sheet_ref, *rest, total_ref = rest

    def recv(d):
        return recvs[d - 1] if len(recvs) > 1 else recvs[0].at[d - 1]

    me = block_index(ctx)
    rows = feat_ref.shape[0]
    dh = LANES
    nf = feat_ref.shape[1] // 2
    feat_at = 2 * rows
    scale = dh ** (-0.5)
    feat_scale = nf ** (-0.5)
    at_row, at_col = iotas(rows)
    apart = at_row - at_col
    wq, wk = query_ref[0:rows, :], own_ref[0:rows, :]
    do, v = query_ref[rows : 2 * rows, :], own_ref[rows : 2 * rows, :]
    q, k = feat_ref[:, :nf], feat_ref[:, nf:]
    lse_c, dw_c = sheet_ref[:, 0:1], sheet_ref[:, 1:2]
    rden_c, dl_c, cum_c = sheet_ref[:, 2:3], sheet_ref[:, 3:4], sheet_ref[:, 4:5]
    def stat(d):
        if len(stats) == 1:
            return stats[0].at[pl.ds(pl.multiple_of(8 * d, 8), 8)]
        at = d.bit_length()
        return stats[at].at[pl.ds(8 * (d - (1 << at >> 1)), 8)]

    mine_ref = stat(0)
    own_cum = mine_ref[4:5, :]
    total_ref[pl.ds(me, 1), :] = own_cum[:, rows - LANES :]

    def place(d, carry):
        total_ref[pl.ds(partner(me, d, count), 1), :] = stat(d)[4:5, rows - LANES :]
        return carry

    over_partners(count, place, 0)
    totals = total_ref[:, LANES - 1 :]
    growth_c = jnp.exp(cum_c) * rden_c
    tail_c = jnp.exp(own_cum[:, rows - 1 : rows] - cum_c)

    def pick(flag, a, b):
        return jnp.where(flag, a, b)

    s = nt(wq, wk) * scale
    causal = at_col <= at_row
    p = jnp.where(causal, jnp.exp(s - lse_c), 0.0)
    dp = nt(do, v)
    dwq = nn((p * (dp - dw_c)).astype(bf16), wk)
    x = nn(q, wide(own_ref, feat_at, nf)) * feat_scale
    e = jnp.where(causal, jnp.exp(jnp.minimum(cum_c - own_cum, 0.0)), 0.0) * rden_c
    dx = (dp - dl_c) * e * (1.0 + x)
    dq_f = nt(dx.astype(bf16), wide(own_ref, feat_at, nf))

    s = nt(wk, wq) * scale
    causal = at_row <= at_col
    p = jnp.where(causal, jnp.exp(s - mine_ref[0:1, :]), 0.0)
    dp = nt(v, do)
    dwk = nn((p * (dp - mine_ref[1:2, :])).astype(bf16), wq)
    x = nn(k, wide(query_ref, feat_at, nf)) * feat_scale
    e = jnp.where(causal, jnp.exp(jnp.minimum(own_cum - cum_c, 0.0)), 0.0) * mine_ref[2:3, :]
    dx = (dp - mine_ref[3:4, :]) * e * (1.0 + x)
    dk_f = nt(dx.astype(bf16), wide(query_ref, feat_at, nf))
    dv = nn((p + (1.0 + x + 0.5 * x * x) * e).astype(bf16), do)

    def step(d, carry):
        dwq, dq_f, dwk, dk_f, dv = carry
        j = partner(me, d, count)
        view = recv(d)
        mine = j < me
        sign = pick(mine, 1, -1)
        limit = WINDOW - jnp.abs(me - j) * rows
        rows_w = pick(mine, wq, wk)
        rows_v = pick(mine, do, v)
        rows_f = pick(mine, q, k)
        other_w = view[0:rows, :]
        other_v = view[rows : 2 * rows, :]
        other_f = wide(view, feat_at, nf)
        st = stat(d)
        zero = jnp.zeros((1, rows), f32)
        cum = st[4:5, :]
        gap = between(totals, jnp.minimum(me, j), jnp.maximum(me, j))
        e_r = jnp.exp(jnp.minimum(gap + pick(mine, cum[:, rows - 1 : rows] - cum, cum), 0.0))
        e_r = e_r * pick(mine, 1.0, st[2:3, :])
        e_c = pick(mine, growth_c, tail_c)

        s = nt(rows_w, other_w) * scale
        p = jnp.exp(s - pick(mine, lse_c, 0.0) - pick(mine, zero, st[0:1, :]))
        p = jnp.where(apart * sign < limit, p, 0.0)
        dp = nt(rows_v, other_v)
        ds = p * (dp - pick(mine, dw_c, 0.0) - pick(mine, zero, st[1:2, :]))
        more_w = nn(ds.astype(bf16), other_w)
        x = nn(rows_f, other_f) * feat_scale
        e = e_r * e_c
        dx = (dp - pick(mine, dl_c, 0.0) - pick(mine, zero, st[3:4, :])) * e * (1.0 + x)
        more_f = nt(dx.astype(bf16), other_f)
        more_v = nn((p + (1.0 + x + 0.5 * x * x) * e).astype(bf16), other_v)
        dwq = dwq + pick(mine, more_w, 0.0)
        dwk = dwk + pick(mine, 0.0, more_w)
        dq_f = dq_f + pick(mine, more_f, 0.0)
        dk_f = dk_f + pick(mine, 0.0, more_f)
        dv = dv + pick(mine, 0.0, more_v)
        return dwq, dq_f, dwk, dk_f, dv

    dwq, dq_f, dwk, dk_f, dv = over_partners(count, step, (dwq, dq_f, dwk, dk_f, dv))
    dwq, dwk = (dwq * scale).astype(bf16), (dwk * scale).astype(bf16)
    dv = dv.astype(bf16)
    padded = jnp.concatenate([dq_f, dk_f, jnp.zeros((rows, LANES - 2 * nf), f32)], axis=1)
    dft = (jnp.transpose(padded)[: 2 * nf] * feat_scale).astype(bf16)
    (grad_ref,) = rest
    grad_ref[0:rows, :] = dwq
    grad_ref[rows : 2 * rows, :] = dwk
    grad_ref[2 * rows : 3 * rows, :] = dv
    put_wide(grad_ref, 3 * rows, dft)


def gather_rows(grad_ref, order, cat_ref, feat_ref):
    rows = cat_ref.shape[0]
    nf2 = feat_ref.shape[1] // len(order)
    for at, h in enumerate(order):
        for part in range(3):
            lane = (3 * at + part) * LANES
            cat_ref[:, lane : lane + LANES] = grad_ref[h, part * rows : (part + 1) * rows, :]
    dft = jnp.concatenate([wide(grad_ref.at[h], 3 * rows, nf2) for h in order], axis=0)
    feat_ref[...] = jnp.transpose(dft.astype(f32)).astype(bf16)


def cat_kernel(grad_ref, cat_ref, feat_ref):
    heads = grad_ref.shape[0]
    head = lax.axis_index("tp")
    order = [head] + [jnp.bitwise_xor(head, t) for t in range(1, heads)]
    gather_rows(grad_ref, order, cat_ref, feat_ref)


def column_sums(ctx, e, cat_ref, feat_ref, ww_ref, vw_ref, fw_ref, piece_ref, firsts):
    nf2 = fw_ref.shape[0]
    heads = feat_ref.shape[1] // nf2
    tile = 2 * LANES
    part = pl.ds(pl.multiple_of(jnp.bitwise_xor(block_index(ctx), e) * tile, tile), tile)
    if e // 2 == 1:
        views = [piece_ref.at[heads - 2]]
    else:
        views = [firsts[1].at[e // 2 - 2] if e > 1 else firsts[0]]
    views += [piece_ref.at[t] for t in range(heads - 2)]
    main = [ww_ref[part, :], vw_ref[part, :]]
    main += [v[m * tile : (m + 1) * tile, :] for v in views for m in range(3)]
    feats = [fw_ref[:, part]] + [wide(v, 3 * tile, nf2) for v in views]
    total = nt(cat_ref[...], jnp.concatenate(main, axis=1))
    total += nn(feat_ref[...], jnp.concatenate(feats, axis=0))
    return total.astype(bf16), part


def columns_kernel(ctx, distances, *rest):
    operands, rest = rest[:5], rest[5:]
    pieces, firsts = rest[: len(distances)], rest[len(distances) : len(distances) + 2]
    for n, (e, ref) in enumerate(zip(distances, pieces)):
        rest[-1][n], _ = column_sums(ctx, e, *operands, ref, firsts)


def lay_kernel(ctx, *refs):
    *tiles, received_ref, out_ref, sems = refs
    views = [(ref.at[n], 2 * (2 * m + n)) for m, ref in enumerate(tiles) for n in range(2)]
    views += [(received_ref.at[d], 2 * d + 1) for d in range(received_ref.shape[0])]
    copies = []
    for n, (view, e) in enumerate(views):
        tile = view.shape[1]
        at = jnp.bitwise_xor(block_index(ctx), e) * tile
        part = pl.ds(pl.multiple_of(at, tile), tile)
        copies.append(pltpu.make_async_copy(view, out_ref.at[:, part], sems.at[n]))
        copies[-1].start()
    for copy in copies:
        copy.wait()


def merge_kernel(grad_ref, weight_ref, out_ref, cat_ref, feat_ref):
    heads = grad_ref.shape[0]
    tile = out_ref.shape[1]
    lanes = 3 * LANES
    nf2 = feat_ref.shape[1] // heads

    @pl.when(pl.program_id(0) == 0)
    def _():
        gather_rows(grad_ref, range(heads), cat_ref, feat_ref)

    views = [weight_ref.at[h] for h in range(heads)]
    main = jnp.concatenate([v[:, 0:lanes] for v in views], axis=1)
    feats = jnp.concatenate([v[:, lanes:] for v in views], axis=1)
    out_ref[...] = (nt(cat_ref[...], main) + nt(feat_ref[...], feats)).astype(bf16)


VMEM = pl.BlockSpec(memory_space=pltpu.VMEM)
HBM = pl.BlockSpec(memory_space=pltpu.HBM)
ANY = pl.BlockSpec(memory_space=pl.ANY)
params = pltpu.CompilerParams(vmem_limit_bytes=32 * 1024 * 1024)


def in_hbm(*arrays):
    return [pltpu.with_memory_space_constraint(a, pltpu.HBM) for a in arrays]


def cost(flops, nbytes, exps=0):
    return pl.CostEstimate(flops=flops, bytes_accessed=nbytes, transcendentals=exps)


def merge(grads, weights, rows, dim):
    heads, _, columns = weights.shape
    tile = 2 * LANES
    return pl.pallas_call(
        merge_kernel,
        out_shape=jax.ShapeDtypeStruct((rows, dim), bf16),
        grid=(dim // tile,),
        in_specs=[
            pl.BlockSpec(grads.shape, lambda i: (0, 0, 0)),
            pl.BlockSpec((heads, tile, columns), lambda i: (0, i, 0)),
        ],
        out_specs=pl.BlockSpec((rows, tile), lambda i: (0, i)),
        scratch_shapes=[
            pltpu.VMEM((rows, 3 * LANES * heads), bf16),
            pltpu.VMEM((rows, (columns - 3 * LANES) * heads), bf16),
        ],
        compiler_params=params,
        cost_estimate=cost(2 * rows * dim * heads * columns, heads * dim * columns * 2),
        name="head_sum",
    )(grads, weights)


def per_device(ctx, tokens, feature_weight, window_weight, value_weight, log_decay, out_grad):
    rows, dim = tokens.shape
    nf2 = feature_weight.shape[1]
    nf = nf2 // 2
    dh = value_weight.shape[1]
    columns = 3 * dh + nf2
    chips, count, heads = lax.axis_size(ctx[:-1]), lax.axis_size(ctx), lax.axis_size("tp")
    fw_t = feature_weight.T
    tile = 2 * LANES
    spread = heads == 4 and count * tile == dim and count == 8
    packs = []
    if spread:
        packs = [jax.ShapeDtypeStruct((columns * tile // LANES, LANES), bf16)]
        packs += [jax.ShapeDtypeStruct((chips - 2, *packs[0].shape), bf16)]

    payload = 2 * rows + 2 * nf + 16
    block = jax.ShapeDtypeStruct((payload, LANES), bf16)
    outs = pl.pallas_call(
        partial(project_kernel, ctx, len(packs)),
        out_shape=packs
        + [block] * (chips + 2)
        + [
            jax.ShapeDtypeStruct((rows, nf2), bf16),
            jax.ShapeDtypeStruct((rows, 1), f32),
            jax.ShapeDtypeStruct((dim, 2 * dh), bf16),
            jax.ShapeDtypeStruct((dim, dh), bf16),
            jax.ShapeDtypeStruct((nf2, dim), bf16),
        ],
        in_specs=[HBM] * 6,
        out_specs=[VMEM] * (len(packs) + chips + 7),
        scratch_shapes=[
            pltpu.VMEM((rows, dim), bf16),
            pltpu.VMEM((1, rows), f32),
            pltpu.VMEM((rows, dh), bf16),
            pltpu.SemaphoreType.DMA((CHUNKS, 4)),
            pltpu.SemaphoreType.DMA((2,)),
        ],
        compiler_params=params,
        cost_estimate=cost(1, 1024),
        name="project",
    )(*in_hbm(tokens, fw_t, window_weight, value_weight, log_decay.T, out_grad))
    *sends, own, query, feat, cum, ww, vw, fw = outs[len(packs) :]

    swap = [(0, 1), (1, 0)]
    recv = {}
    for d in range(1, chips):
        recv[2 * d] = lax.ppermute(sends[d], ctx[:-1], [(i, i ^ d) for i in range(chips)])
    recv[1] = lax.ppermute(sends[0], "core", swap)
    if spread:
        across = lax.ppermute(outs[0], "tp", [(z, z ^ 2) for z in range(heads)])
    for d in range(1, chips):
        if spread and d == chips - 1:
            across, recv[2 * d] = lax.optimization_barrier((across, recv[2 * d]))
        recv[2 * d + 1] = lax.ppermute(recv[2 * d], "core", swap)
    recv = [recv[d] for d in range(1, count)]
    if count > 8:
        recv = [jnp.stack(recv)]

    if spread:
        early = lax.ppermute(outs[0], "tp", [(z, z ^ 1) for z in range(heads)])
        across, early, recv = lax.optimization_barrier((across, early, recv))
        near = [across, lax.ppermute(across, "tp", [(z, z ^ 1) for z in range(heads)])]

    attended, stat, sheet = pl.pallas_call(
        lambda *refs: query_kernel(ctx, count, len(recv), *refs),
        out_shape=[
            jax.ShapeDtypeStruct((rows, dh), bf16),
            jax.ShapeDtypeStruct((8, rows), f32),
            jax.ShapeDtypeStruct((rows, LANES), f32),
        ],
        in_specs=[VMEM] * (len(recv) + 4),
        out_specs=[VMEM] * 3,
        scratch_shapes=[
            pltpu.VMEM((count, 2 * rows, dh), bf16),
            pltpu.VMEM((WINDOW // rows + 1, rows, rows), f32),
            pltpu.VMEM((count, rows), f32),
        ],
        compiler_params=params,
        cost_estimate=cost(1, 1024),
        name="query_side",
    )(*recv, own, query, feat, cum)
    stats = [stat]
    for name in reversed(ctx):
        if spread and len(stats) == 2:
            near, sent, stats = lax.optimization_barrier((near, outs[1], stats))
        held = stats[0] if len(stats) == 1 else jnp.concatenate(stats, axis=0)
        stats.append(lax.ppermute(held, name, swap))
    if count > 8:
        stats = [jnp.concatenate(stats, axis=0)]

    if spread:
        first = [early, lax.ppermute(sent, "tp", [(z, z ^ 1) for z in range(heads)])]

        def stacked(parts):
            return pl.pallas_call(
                stack_kernel,
                out_shape=jax.ShapeDtypeStruct((len(parts), *packs[0].shape), bf16),
                in_specs=[VMEM] * len(parts),
                out_specs=VMEM,
                compiler_params=params,
                cost_estimate=cost(1, 1024),
                name="stack",
            )(*parts)

        pieces = [stacked(near)]
        for d in (1, 2):
            whole = stacked([*near, early]) if d == 1 else pieces[0]
            free, _ = lax.optimization_barrier((whole, stats[d + 1]))
            pieces.append(lax.ppermute(free, ctx[:-1], [(i, i ^ d) for i in range(chips)]))
        pieces[0], sheet = lax.optimization_barrier((pieces[0], sheet))

    grads = pl.pallas_call(
        lambda *refs: gradient_kernel(ctx, count, len(recv), len(stats), *refs),
        out_shape=jax.ShapeDtypeStruct((3 * rows + nf2 * rows // LANES, LANES), bf16),
        in_specs=[VMEM] * (len(recv) + len(stats) + 4),
        out_specs=VMEM,
        scratch_shapes=[pltpu.VMEM((count, LANES), f32)],
        compiler_params=params,
        cost_estimate=cost(1, 1024),
        name="gradients",
    )(*recv, *stats, own, query, feat, sheet)
    if not spread:
        weights = jnp.concatenate([window_weight, value_weight, feature_weight], axis=1)
        weights = lax.all_gather(weights, "tp")
        return (attended, merge(lax.all_gather(grads, "tp"), weights, rows, dim))

    diagonal, grads = lax.optimization_barrier((pieces[0], grads))
    pieces.append(lax.ppermute(diagonal, ctx[:-1], [(i, i ^ 3) for i in range(chips)]))
    first[1], grads = lax.optimization_barrier((first[1], grads))
    grads = lax.all_gather(grads, "tp")
    pieces, first, grads = lax.optimization_barrier((pieces, first, grads))
    sibling_grads = lax.ppermute(grads, "core", swap)

    def operands_of(grads):
        return pl.pallas_call(
            cat_kernel,
            out_shape=[
                jax.ShapeDtypeStruct((rows, 3 * LANES * heads), bf16),
                jax.ShapeDtypeStruct((rows, nf2 * heads), bf16),
            ],
            in_specs=[VMEM],
            out_specs=[VMEM] * 2,
            compiler_params=params,
            cost_estimate=cost(1, 1024),
            name="cat",
        )(grads)

    mine = operands_of(grads)

    def columns_of(distances, operands):
        parts = [pieces[e // 2] for e in distances]
        return pl.pallas_call(
            partial(columns_kernel, ctx, distances),
            out_shape=jax.ShapeDtypeStruct((len(parts), rows, tile), bf16),
            in_specs=[VMEM] * (7 + len(parts)),
            out_specs=VMEM,
            compiler_params=params,
            cost_estimate=cost(1, 1024),
            name="columns",
        )(*operands, ww, vw, fw, *parts, *first)

    early_tiles = columns_of((0, 2), mine)
    sibling_grads, early_tiles = lax.optimization_barrier((sibling_grads, early_tiles))
    passed = columns_of((0, 2, 4, 6), operands_of(sibling_grads))
    passed, mine = lax.optimization_barrier((passed, mine))
    received = lax.ppermute(passed, "core", swap)
    late_tiles = columns_of((4, 6), mine)
    late_tiles, received = lax.optimization_barrier((late_tiles, received))
    total = pl.pallas_call(
        partial(lay_kernel, ctx),
        out_shape=jax.ShapeDtypeStruct((rows, dim), bf16),
        in_specs=[VMEM] * 3,
        out_specs=ANY,
        scratch_shapes=[pltpu.SemaphoreType.DMA((count,))],
        compiler_params=params,
        cost_estimate=cost(1, 1024),
        name="lay",
    )(early_tiles, late_tiles, received)
    return (attended, total)


def solution(mesh):
    blocks, tp = mesh.devices.shape
    bits = blocks.bit_length() - 1
    assert blocks == 2**bits
    ctx = tuple(f"half{i}" for i in range(bits - 1)) + ("core",)
    split = Mesh(mesh.devices.reshape((2,) * bits + (tp,)), (*ctx, "tp"))
    in_specs = (
        P(ctx, None),
        P(None, "tp"),
        P(None, "tp"),
        P(None, "tp"),
        P(ctx, "tp"),
        P(ctx, "tp"),
    )
    out_specs = (P(ctx, "tp"), P(ctx, None))
    return jax.shard_map(
        partial(per_device, ctx),
        mesh=split,
        in_specs=in_specs,
        out_specs=out_specs,
        check_vma=False,
    )
```

```python
from functools import partial

import jax
import jax.numpy as jnp
from jax import lax
from jax.experimental import pallas as pl
from jax.experimental.pallas import tpu as pltpu
from jax.sharding import Mesh
from jax.sharding import PartitionSpec as P

WINDOW = 1024
LANES = 128
MASKED = -1e30
CHUNKS = 4
f32 = jnp.float32
bf16 = jnp.bfloat16


def nn(a, b):
    return lax.dot_general(a, b, (((1,), (0,)), ((), ())), preferred_element_type=f32)


def nt(a, b):
    return lax.dot_general(a, b, (((1,), (1,)), ((), ())), preferred_element_type=f32)


def partner(me, d, count):
    assert count & (count - 1) == 0
    return jnp.bitwise_xor(me, d)


def wide(view, start, count):
    return jnp.concatenate(
        [view[start : start + count, :], view[start + count : start + 2 * count, :]], axis=1
    )


def put_wide(ref, start, value):
    count = value.shape[0]
    for half in range(value.shape[1] // LANES):
        ref[start + half * count : start + (half + 1) * count, :] = value[
            :, half * LANES : (half + 1) * LANES
        ]


def cum_row(view, start):
    tail = view[start : start + 16, :].astype(f32)
    first = tail[0:1] + tail[2:3] + tail[4:5]
    second = tail[1:2] + tail[3:4] + tail[5:6]
    return jnp.concatenate([first, second], axis=1)


def iotas(rows):
    return (
        lax.broadcasted_iota(jnp.int32, (rows, rows), 0),
        lax.broadcasted_iota(jnp.int32, (rows, rows), 1),
    )


def block_index(ctx):
    place = 0
    for name in ctx:
        place = place * lax.axis_size(name) + lax.axis_index(name)
    return place


def pack(me, ww_ref, vw_ref, fw_ref, out_ref):
    nf2 = fw_ref.shape[0]
    tile = 2 * LANES
    at = pl.multiple_of(me * tile, tile)
    rows = pl.ds(at, tile)
    out_ref[0:tile, :] = ww_ref[rows, 0:LANES]
    out_ref[tile : 2 * tile, :] = ww_ref[rows, LANES:]
    out_ref[2 * tile : 3 * tile, :] = vw_ref[rows, :]
    put_wide(out_ref, 3 * tile, fw_ref[:, rows])


def project_kernel(ctx, packs, tok_hbm, fw_hbm, ww_hbm, vw_hbm, ld_hbm, do_hbm, *rest):
    *sends, keys_ref, query_ref, feat_ref, cum_ref, ww_ref, vw_ref, fw_ref = rest[packs:-5]
    tok_ref, ld_ref, do_ref, sems, small = rest[-5:]
    me = block_index(ctx)
    rows, dim = tok_ref.shape
    dh = do_ref.shape[1]
    nf = fw_ref.shape[0] // 2
    span = dim // CHUNKS
    copies = []
    for c in range(CHUNKS):
        part = pl.ds(c * span, span)
        copies.append([
            pltpu.make_async_copy(tok_hbm.at[:, part], tok_ref.at[:, part], sems.at[c, 0]),
            pltpu.make_async_copy(ww_hbm.at[part, :], ww_ref.at[part, :], sems.at[c, 1]),
            pltpu.make_async_copy(vw_hbm.at[part, :], vw_ref.at[part, :], sems.at[c, 2]),
            pltpu.make_async_copy(fw_hbm.at[:, part], fw_ref.at[:, part], sems.at[c, 3]),
        ])
    others = [
        pltpu.make_async_copy(ld_hbm, ld_ref, small.at[0]),
        pltpu.make_async_copy(do_hbm, do_ref, small.at[1]),
    ]
    for copy in others:
        copy.start()
    for group in copies:
        for at, copy in enumerate(group):
            copy.start(priority=min(at, 1))
    for copy in others:
        copy.wait()
    at_row, at_col = iotas(rows)
    ld_r = ld_ref[...]
    ld_c = jnp.sum(jnp.where(at_row == at_col, ld_r, 0.0), axis=1, keepdims=True)
    cum_r = jnp.sum(jnp.where(at_row <= at_col, ld_c, 0.0), axis=0, keepdims=True)
    cum_ref[...] = jnp.sum(jnp.where(at_col <= at_row, ld_r, 0.0), axis=1, keepdims=True)
    high = cum_r.astype(bf16)
    left = cum_r - high.astype(f32)
    mid = left.astype(bf16)
    low = (left - mid.astype(f32)).astype(bf16)
    pieces = [t[:, h : h + LANES].astype(f32) for t in (high, mid, low) for h in range(0, rows, LANES)]
    tail = jnp.concatenate(pieces + [jnp.zeros((10, LANES), f32)], axis=0).astype(bf16)

    feat = jnp.zeros((rows, 2 * nf), f32)
    main = jnp.zeros((rows, 3 * dh), f32)
    for c in range(CHUNKS):
        for copy in copies[c]:
            copy.wait()
        part = slice(c * span, (c + 1) * span)
        tok = tok_ref[:, part]
        feat += nt(tok, fw_ref[:, part])
        main += nn(tok, jnp.concatenate([ww_ref[part, :], vw_ref[part, :]], axis=1))
    feat = feat.astype(bf16)
    window = main[:, : 2 * dh].astype(bf16)
    values = main[:, 2 * dh :].astype(bf16)
    feat_ref[...] = feat
    small_row, small_col = iotas(2 * nf)
    feat_t = nt((small_row == small_col).astype(bf16), feat).astype(bf16)
    feat_at = 2 * rows
    tail_at = feat_at + 2 * nf

    def put_keys(ref):
        ref[0:rows, :] = window[:, dh:]
        ref[rows : 2 * rows, :] = values
        put_wide(ref, feat_at, feat_t[nf:, :])
        ref[tail_at : tail_at + 16, :] = tail

    def put_query(ref):
        ref[0:rows, :] = window[:, :dh]
        ref[rows : 2 * rows, :] = do_ref[...]
        put_wide(ref, feat_at, feat_t[:nf, :])
        ref[tail_at : tail_at + 16, :] = tail

    put_keys(keys_ref)
    put_query(query_ref)
    for at, ref in enumerate(sends):
        later = jnp.bitwise_xor(me, max(2 * at, 1)) > me
        pl.when(later)(lambda ref=ref: put_keys(ref))
        pl.when(jnp.logical_not(later))(lambda ref=ref: put_query(ref))
    if packs:
        own_pack, other_pack = rest[:packs]
        pack(me, ww_ref, vw_ref, fw_ref, own_pack)
        for d in range(other_pack.shape[0]):
            piece = jnp.bitwise_xor(me, 2 * d + 4)
            pack(piece, ww_ref, vw_ref, fw_ref, other_pack.at[d])

def stack_kernel(*refs):
    *parts, out_ref = refs
    for t, ref in enumerate(parts):
        out_ref[t] = ref[...]


def between(totals, low, high):
    at = lax.broadcasted_iota(jnp.int32, totals.shape, 0)
    return jnp.sum(jnp.where((at > low) & (at < high), totals, 0.0), axis=0, keepdims=True)


def over_partners(count, body, carry):
    if count <= 8:
        for d in range(1, count):
            carry = body(d, carry)
        return carry
    return lax.fori_loop(1, count, body, carry)


def query_kernel(ctx, count, recvs, *rest):
    recvs, rest = rest[:recvs], rest[recvs:]
    own_ref, query_ref, feat_ref, cum_ref, *rest = rest
    near_ref, p_ref, cums_ref = rest[-3:]
    att_ref, stat_ref, sheet_ref = rest[:3]

    def recv(d):
        return recvs[d - 1] if len(recvs) > 1 else recvs[0].at[d - 1]

    me = block_index(ctx)
    rows, dh = att_ref.shape
    nf = feat_ref.shape[1] // 2
    back = WINDOW // rows
    feat_at = 2 * rows
    tail_at = feat_at + 2 * nf
    scale = dh ** (-0.5)
    feat_scale = nf ** (-0.5)
    wq = query_ref[0:rows, :]
    do = query_ref[rows : 2 * rows, :]
    q = feat_ref[:, :nf]
    at_row, at_col = iotas(rows)
    own_cum = cum_row(own_ref, tail_at)
    cums_ref[pl.ds(me, 1), :] = own_cum
    near_ref[me] = own_ref[0 : 2 * rows, :]

    def gather(d, carry):
        j = partner(me, d, count)
        view = recv(d)
        near_ref[j] = view[0 : 2 * rows, :]
        cums_ref[pl.ds(j, 1), :] = cum_row(view, tail_at)
        return carry

    over_partners(count, gather, 0)

    def near(w):
        return near_ref.at[jnp.maximum(me - back + w, 0)]

    top = jnp.full((rows, LANES), MASKED, f32)
    for w in range(back + 1):
        keys = own_ref[0:rows, :] if w == back else near(w)[0:rows, :]
        s = nt(wq, keys) * scale
        if w == back:
            s = jnp.where(at_col <= at_row, s, MASKED)
        elif w == 0:
            s = jnp.where((at_col > at_row) & (me >= back), s, MASKED)
        else:
            s = jnp.where(me >= back - w, s, MASKED)
        p_ref[w] = s
        for h in range(0, rows, LANES):
            top = jnp.maximum(top, s[:, h : h + LANES])
    top = jnp.max(top, axis=1, keepdims=True)
    total = jnp.zeros((rows, LANES), f32)
    out = jnp.zeros((rows, dh), f32)
    for w in range(back + 1):
        p = jnp.exp(p_ref[w] - top)
        for h in range(0, rows, LANES):
            total += p[:, h : h + LANES]
        vals = own_ref[rows : 2 * rows, :] if w == back else near(w)[rows : 2 * rows, :]
        out += nn(p.astype(bf16), vals)
    total = jnp.sum(total, axis=1, keepdims=True)
    windowed = out * (1.0 / total)

    cum_c = cum_ref[...]
    growth = jnp.exp(cum_c)
    totals = cums_ref[:, rows - 1 : rows]

    def forward(d, carry):
        num, den = carry
        j = partner(me, d, count)
        view = recv(d)
        gap = between(totals, j - 1, me)
        es = jnp.where(j < me, jnp.exp(jnp.minimum(gap - cums_ref[pl.ds(j, 1), :], 0.0)), 0.0)
        x = nn(q, wide(view, feat_at, nf)) * feat_scale
        weight = (1.0 + x + 0.5 * x * x) * es
        for h in range(0, rows, LANES):
            den += weight[:, h : h + LANES]
        num += nn(weight.astype(bf16), view[rows : 2 * rows, :])
        return num, den

    num, den = over_partners(
        count, forward, (jnp.zeros((rows, dh), f32), jnp.zeros((rows, LANES), f32))
    )
    x = nn(q, wide(own_ref, feat_at, nf)) * feat_scale
    e = jnp.where(at_col <= at_row, jnp.exp(jnp.minimum(cum_c - own_cum, 0.0)), 0.0)
    weight = (1.0 + x + 0.5 * x * x) * e
    num = num * growth + nn(weight.astype(bf16), own_ref[rows : 2 * rows, :])
    den = den * growth
    for h in range(0, rows, LANES):
        den += weight[:, h : h + LANES]
    rden = 1.0 / jnp.sum(den, axis=1, keepdims=True)
    linear = num * rden
    att_ref[...] = (linear + windowed).astype(bf16)
    do_f = do.astype(f32)
    delta_w = jnp.sum(do_f * windowed, axis=1, keepdims=True)
    delta_l = jnp.sum(do_f * linear, axis=1, keepdims=True)
    lse = top + jnp.log(total)
    lane = lax.broadcasted_iota(jnp.int32, (rows, LANES), 1)
    sheet = jnp.where(lane == 0, lse, 0.0)
    sheet = jnp.where(lane == 1, delta_w, sheet)
    sheet = jnp.where(lane == 2, rden, sheet)
    sheet = jnp.where(lane == 3, delta_l, sheet)
    sheet = jnp.where(lane == 4, cum_c, sheet)
    sheet_ref[...] = sheet
    stat_ref[...] = jnp.transpose(sheet)[0:8, :]


def gradient_kernel(ctx, count, recvs, stats, *rest):
    recvs, rest = rest[:recvs], rest[recvs:]
    stats, rest = rest[:stats], rest[stats:]
    own_ref, query_ref, feat_ref, sheet_ref, *rest, total_ref = rest

    def recv(d):
        return recvs[d - 1] if len(recvs) > 1 else recvs[0].at[d - 1]

    me = block_index(ctx)
    rows = feat_ref.shape[0]
    dh = LANES
    nf = feat_ref.shape[1] // 2
    feat_at = 2 * rows
    scale = dh ** (-0.5)
    feat_scale = nf ** (-0.5)
    at_row, at_col = iotas(rows)
    apart = at_row - at_col
    wq, wk = query_ref[0:rows, :], own_ref[0:rows, :]
    do, v = query_ref[rows : 2 * rows, :], own_ref[rows : 2 * rows, :]
    q, k = feat_ref[:, :nf], feat_ref[:, nf:]
    lse_c, dw_c = sheet_ref[:, 0:1], sheet_ref[:, 1:2]
    rden_c, dl_c, cum_c = sheet_ref[:, 2:3], sheet_ref[:, 3:4], sheet_ref[:, 4:5]
    def stat(d):
        if len(stats) == 1:
            return stats[0].at[pl.ds(pl.multiple_of(8 * d, 8), 8)]
        at = d.bit_length()
        return stats[at].at[pl.ds(8 * (d - (1 << at >> 1)), 8)]

    mine_ref = stat(0)
    own_cum = mine_ref[4:5, :]
    total_ref[pl.ds(me, 1), :] = own_cum[:, rows - LANES :]

    def place(d, carry):
        total_ref[pl.ds(partner(me, d, count), 1), :] = stat(d)[4:5, rows - LANES :]
        return carry

    over_partners(count, place, 0)
    totals = total_ref[:, LANES - 1 :]
    growth_c = jnp.exp(cum_c) * rden_c
    tail_c = jnp.exp(own_cum[:, rows - 1 : rows] - cum_c)

    def pick(flag, a, b):
        return jnp.where(flag, a, b)

    s = nt(wq, wk) * scale
    causal = at_col <= at_row
    p = jnp.where(causal, jnp.exp(s - lse_c), 0.0)
    dp = nt(do, v)
    dwq = nn((p * (dp - dw_c)).astype(bf16), wk)
    x = nn(q, wide(own_ref, feat_at, nf)) * feat_scale
    e = jnp.where(causal, jnp.exp(jnp.minimum(cum_c - own_cum, 0.0)), 0.0) * rden_c
    dx = (dp - dl_c) * e * (1.0 + x)
    dq_f = nt(dx.astype(bf16), wide(own_ref, feat_at, nf))

    s = nt(wk, wq) * scale
    causal = at_row <= at_col
    p = jnp.where(causal, jnp.exp(s - mine_ref[0:1, :]), 0.0)
    dp = nt(v, do)
    dwk = nn((p * (dp - mine_ref[1:2, :])).astype(bf16), wq)
    x = nn(k, wide(query_ref, feat_at, nf)) * feat_scale
    e = jnp.where(causal, jnp.exp(jnp.minimum(own_cum - cum_c, 0.0)), 0.0) * mine_ref[2:3, :]
    dx = (dp - mine_ref[3:4, :]) * e * (1.0 + x)
    dk_f = nt(dx.astype(bf16), wide(query_ref, feat_at, nf))
    dv = nn((p + (1.0 + x + 0.5 * x * x) * e).astype(bf16), do)

    def step(d, carry):
        dwq, dq_f, dwk, dk_f, dv = carry
        j = partner(me, d, count)
        view = recv(d)
        mine = j < me
        sign = pick(mine, 1, -1)
        limit = WINDOW - jnp.abs(me - j) * rows
        rows_w = pick(mine, wq, wk)
        rows_v = pick(mine, do, v)
        rows_f = pick(mine, q, k)
        other_w = view[0:rows, :]
        other_v = view[rows : 2 * rows, :]
        other_f = wide(view, feat_at, nf)
        st = stat(d)
        zero = jnp.zeros((1, rows), f32)
        cum = st[4:5, :]
        gap = between(totals, jnp.minimum(me, j), jnp.maximum(me, j))
        e_r = jnp.exp(jnp.minimum(gap + pick(mine, cum[:, rows - 1 : rows] - cum, cum), 0.0))
        e_r = e_r * pick(mine, 1.0, st[2:3, :])
        e_c = pick(mine, growth_c, tail_c)

        s = nt(rows_w, other_w) * scale
        p = jnp.exp(s - pick(mine, lse_c, 0.0) - pick(mine, zero, st[0:1, :]))
        p = jnp.where(apart * sign < limit, p, 0.0)
        dp = nt(rows_v, other_v)
        ds = p * (dp - pick(mine, dw_c, 0.0) - pick(mine, zero, st[1:2, :]))
        more_w = nn(ds.astype(bf16), other_w)
        x = nn(rows_f, other_f) * feat_scale
        e = e_r * e_c
        dx = (dp - pick(mine, dl_c, 0.0) - pick(mine, zero, st[3:4, :])) * e * (1.0 + x)
        more_f = nt(dx.astype(bf16), other_f)
        more_v = nn((p + (1.0 + x + 0.5 * x * x) * e).astype(bf16), other_v)
        dwq = dwq + pick(mine, more_w, 0.0)
        dwk = dwk + pick(mine, 0.0, more_w)
        dq_f = dq_f + pick(mine, more_f, 0.0)
        dk_f = dk_f + pick(mine, 0.0, more_f)
        dv = dv + pick(mine, 0.0, more_v)
        return dwq, dq_f, dwk, dk_f, dv

    dwq, dq_f, dwk, dk_f, dv = over_partners(count, step, (dwq, dq_f, dwk, dk_f, dv))
    dwq, dwk = (dwq * scale).astype(bf16), (dwk * scale).astype(bf16)
    dv = dv.astype(bf16)
    padded = jnp.concatenate([dq_f, dk_f, jnp.zeros((rows, LANES - 2 * nf), f32)], axis=1)
    dft = (jnp.transpose(padded)[: 2 * nf] * feat_scale).astype(bf16)
    (grad_ref,) = rest
    grad_ref[0:rows, :] = dwq
    grad_ref[rows : 2 * rows, :] = dwk
    grad_ref[2 * rows : 3 * rows, :] = dv
    put_wide(grad_ref, 3 * rows, dft)


def gather_rows(grad_ref, order, cat_ref, feat_ref):
    rows = cat_ref.shape[0]
    nf2 = feat_ref.shape[1] // len(order)
    for at, h in enumerate(order):
        for part in range(3):
            lane = (3 * at + part) * LANES
            cat_ref[:, lane : lane + LANES] = grad_ref[h, part * rows : (part + 1) * rows, :]
    dft = jnp.concatenate([wide(grad_ref.at[h], 3 * rows, nf2) for h in order], axis=0)
    feat_ref[...] = jnp.transpose(dft.astype(f32)).astype(bf16)


def cat_kernel(grad_ref, cat_ref, feat_ref):
    heads = grad_ref.shape[0]
    head = lax.axis_index("tp")
    order = [head] + [jnp.bitwise_xor(head, t) for t in range(1, heads)]
    gather_rows(grad_ref, order, cat_ref, feat_ref)


def column_sums(ctx, e, cat_ref, feat_ref, ww_ref, vw_ref, fw_ref, piece_ref, firsts):
    nf2 = fw_ref.shape[0]
    heads = feat_ref.shape[1] // nf2
    tile = 2 * LANES
    part = pl.ds(pl.multiple_of(jnp.bitwise_xor(block_index(ctx), e) * tile, tile), tile)
    if e // 2 == 1:
        views = [piece_ref.at[heads - 2]]
    else:
        views = [firsts[1].at[e // 2 - 2] if e > 1 else firsts[0]]
    views += [piece_ref.at[t] for t in range(heads - 2)]
    main = [ww_ref[part, :], vw_ref[part, :]]
    main += [v[m * tile : (m + 1) * tile, :] for v in views for m in range(3)]
    feats = [fw_ref[:, part]] + [wide(v, 3 * tile, nf2) for v in views]
    total = nt(cat_ref[...], jnp.concatenate(main, axis=1))
    total += nn(feat_ref[...], jnp.concatenate(feats, axis=0))
    return total.astype(bf16), part


def columns_kernel(ctx, distances, *rest):
    operands, rest = rest[:5], rest[5:]
    pieces, firsts = rest[: len(distances)], rest[len(distances) : len(distances) + 2]
    for n, (e, ref) in enumerate(zip(distances, pieces)):
        rest[-1][n], _ = column_sums(ctx, e, *operands, ref, firsts)


def lay_kernel(ctx, *refs):
    own_ref, *received, out_ref, sems = refs
    views = [(own_ref.at[n], 2 * n) for n in range(own_ref.shape[0])]
    views += [(ref.at[n], 4 * m + 2 * n + 1) for m, ref in enumerate(received) for n in range(2)]
    copies = []
    for n, (view, e) in enumerate(views):
        tile = view.shape[1]
        at = jnp.bitwise_xor(block_index(ctx), e) * tile
        part = pl.ds(pl.multiple_of(at, tile), tile)
        copies.append(pltpu.make_async_copy(view, out_ref.at[:, part], sems.at[n]))
        copies[-1].start()
    for copy in copies:
        copy.wait()


def merge_kernel(grad_ref, weight_ref, out_ref, cat_ref, feat_ref):
    heads = grad_ref.shape[0]
    tile = out_ref.shape[1]
    lanes = 3 * LANES
    nf2 = feat_ref.shape[1] // heads

    @pl.when(pl.program_id(0) == 0)
    def _():
        gather_rows(grad_ref, range(heads), cat_ref, feat_ref)

    views = [weight_ref.at[h] for h in range(heads)]
    main = jnp.concatenate([v[:, 0:lanes] for v in views], axis=1)
    feats = jnp.concatenate([v[:, lanes:] for v in views], axis=1)
    out_ref[...] = (nt(cat_ref[...], main) + nt(feat_ref[...], feats)).astype(bf16)


VMEM = pl.BlockSpec(memory_space=pltpu.VMEM)
HBM = pl.BlockSpec(memory_space=pltpu.HBM)
ANY = pl.BlockSpec(memory_space=pl.ANY)
params = pltpu.CompilerParams(vmem_limit_bytes=32 * 1024 * 1024)


def in_hbm(*arrays):
    return [pltpu.with_memory_space_constraint(a, pltpu.HBM) for a in arrays]


def cost(flops, nbytes, exps=0):
    return pl.CostEstimate(flops=flops, bytes_accessed=nbytes, transcendentals=exps)


def merge(grads, weights, rows, dim):
    heads, _, columns = weights.shape
    tile = 2 * LANES
    return pl.pallas_call(
        merge_kernel,
        out_shape=jax.ShapeDtypeStruct((rows, dim), bf16),
        grid=(dim // tile,),
        in_specs=[
            pl.BlockSpec(grads.shape, lambda i: (0, 0, 0)),
            pl.BlockSpec((heads, tile, columns), lambda i: (0, i, 0)),
        ],
        out_specs=pl.BlockSpec((rows, tile), lambda i: (0, i)),
        scratch_shapes=[
            pltpu.VMEM((rows, 3 * LANES * heads), bf16),
            pltpu.VMEM((rows, (columns - 3 * LANES) * heads), bf16),
        ],
        compiler_params=params,
        cost_estimate=cost(2 * rows * dim * heads * columns, heads * dim * columns * 2),
        name="head_sum",
    )(grads, weights)


def per_device(ctx, tokens, feature_weight, window_weight, value_weight, log_decay, out_grad):
    rows, dim = tokens.shape
    nf2 = feature_weight.shape[1]
    nf = nf2 // 2
    dh = value_weight.shape[1]
    columns = 3 * dh + nf2
    chips, count, heads = lax.axis_size(ctx[:-1]), lax.axis_size(ctx), lax.axis_size("tp")
    fw_t = feature_weight.T
    tile = 2 * LANES
    spread = heads == 4 and count * tile == dim and count == 8
    packs = []
    if spread:
        packs = [jax.ShapeDtypeStruct((columns * tile // LANES, LANES), bf16)]
        packs += [jax.ShapeDtypeStruct((chips - 2, *packs[0].shape), bf16)]

    payload = 2 * rows + 2 * nf + 16
    block = jax.ShapeDtypeStruct((payload, LANES), bf16)
    outs = pl.pallas_call(
        partial(project_kernel, ctx, len(packs)),
        out_shape=packs
        + [block] * (chips + 2)
        + [
            jax.ShapeDtypeStruct((rows, nf2), bf16),
            jax.ShapeDtypeStruct((rows, 1), f32),
            jax.ShapeDtypeStruct((dim, 2 * dh), bf16),
            jax.ShapeDtypeStruct((dim, dh), bf16),
            jax.ShapeDtypeStruct((nf2, dim), bf16),
        ],
        in_specs=[HBM] * 6,
        out_specs=[VMEM] * (len(packs) + chips + 7),
        scratch_shapes=[
            pltpu.VMEM((rows, dim), bf16),
            pltpu.VMEM((1, rows), f32),
            pltpu.VMEM((rows, dh), bf16),
            pltpu.SemaphoreType.DMA((CHUNKS, 4)),
            pltpu.SemaphoreType.DMA((2,)),
        ],
        compiler_params=params,
        cost_estimate=cost(1, 1024),
        name="project",
    )(*in_hbm(tokens, fw_t, window_weight, value_weight, log_decay.T, out_grad))
    *sends, own, query, feat, cum, ww, vw, fw = outs[len(packs) :]

    swap = [(0, 1), (1, 0)]
    recv = {}
    for d in range(1, chips):
        recv[2 * d] = lax.ppermute(sends[d], ctx[:-1], [(i, i ^ d) for i in range(chips)])
    recv[1] = lax.ppermute(sends[0], "core", swap)
    if spread:
        across = lax.ppermute(outs[0], "tp", [(z, z ^ 2) for z in range(heads)])
    for d in range(1, chips):
        if spread and d == chips - 1:
            across, recv[2 * d] = lax.optimization_barrier((across, recv[2 * d]))
        recv[2 * d + 1] = lax.ppermute(recv[2 * d], "core", swap)
    recv = [recv[d] for d in range(1, count)]
    if count > 8:
        recv = [jnp.stack(recv)]

    if spread:
        early = lax.ppermute(outs[0], "tp", [(z, z ^ 1) for z in range(heads)])
        across, early, recv = lax.optimization_barrier((across, early, recv))
        near = [across, lax.ppermute(across, "tp", [(z, z ^ 1) for z in range(heads)])]

    attended, stat, sheet = pl.pallas_call(
        lambda *refs: query_kernel(ctx, count, len(recv), *refs),
        out_shape=[
            jax.ShapeDtypeStruct((rows, dh), bf16),
            jax.ShapeDtypeStruct((8, rows), f32),
            jax.ShapeDtypeStruct((rows, LANES), f32),
        ],
        in_specs=[VMEM] * (len(recv) + 4),
        out_specs=[VMEM] * 3,
        scratch_shapes=[
            pltpu.VMEM((count, 2 * rows, dh), bf16),
            pltpu.VMEM((WINDOW // rows + 1, rows, rows), f32),
            pltpu.VMEM((count, rows), f32),
        ],
        compiler_params=params,
        cost_estimate=cost(1, 1024),
        name="query_side",
    )(*recv, own, query, feat, cum)
    stats = [stat]
    for name in reversed(ctx):
        if spread and len(stats) == 2:
            near, sent, stats = lax.optimization_barrier((near, outs[1], stats))
        held = stats[0] if len(stats) == 1 else jnp.concatenate(stats, axis=0)
        stats.append(lax.ppermute(held, name, swap))
    if count > 8:
        stats = [jnp.concatenate(stats, axis=0)]

    if spread:
        first = [early, lax.ppermute(sent, "tp", [(z, z ^ 1) for z in range(heads)])]

        def stacked(parts):
            return pl.pallas_call(
                stack_kernel,
                out_shape=jax.ShapeDtypeStruct((len(parts), *packs[0].shape), bf16),
                in_specs=[VMEM] * len(parts),
                out_specs=VMEM,
                compiler_params=params,
                cost_estimate=cost(1, 1024),
                name="stack",
            )(*parts)

        pieces = [stacked(near)]
        for d in (1, 2):
            whole = stacked([*near, early]) if d == 1 else pieces[0]
            free, _ = lax.optimization_barrier((whole, stats[d + 1]))
            pieces.append(lax.ppermute(free, ctx[:-1], [(i, i ^ d) for i in range(chips)]))
        pieces[0], sheet = lax.optimization_barrier((pieces[0], sheet))

    grads = pl.pallas_call(
        lambda *refs: gradient_kernel(ctx, count, len(recv), len(stats), *refs),
        out_shape=jax.ShapeDtypeStruct((3 * rows + nf2 * rows // LANES, LANES), bf16),
        in_specs=[VMEM] * (len(recv) + len(stats) + 4),
        out_specs=VMEM,
        scratch_shapes=[pltpu.VMEM((count, LANES), f32)],
        compiler_params=params,
        cost_estimate=cost(1, 1024),
        name="gradients",
    )(*recv, *stats, own, query, feat, sheet)
    if not spread:
        weights = jnp.concatenate([window_weight, value_weight, feature_weight], axis=1)
        weights = lax.all_gather(weights, "tp")
        return (attended, merge(lax.all_gather(grads, "tp"), weights, rows, dim))

    diagonal, grads = lax.optimization_barrier((pieces[0], grads))
    pieces.append(lax.ppermute(diagonal, ctx[:-1], [(i, i ^ 3) for i in range(chips)]))
    first[1], grads = lax.optimization_barrier((first[1], grads))
    grads = lax.all_gather(grads, "tp")
    pieces, first, grads = lax.optimization_barrier((pieces, first, grads))
    sibling_grads = lax.ppermute(grads, "core", swap)

    def operands_of(grads):
        return pl.pallas_call(
            cat_kernel,
            out_shape=[
                jax.ShapeDtypeStruct((rows, 3 * LANES * heads), bf16),
                jax.ShapeDtypeStruct((rows, nf2 * heads), bf16),
            ],
            in_specs=[VMEM],
            out_specs=[VMEM] * 2,
            compiler_params=params,
            cost_estimate=cost(1, 1024),
            name="cat",
        )(grads)

    mine = operands_of(grads)

    def columns_of(distances, operands):
        parts = [pieces[e // 2] for e in distances]
        return pl.pallas_call(
            partial(columns_kernel, ctx, distances),
            out_shape=jax.ShapeDtypeStruct((len(parts), rows, tile), bf16),
            in_specs=[VMEM] * (7 + len(parts)),
            out_specs=VMEM,
            compiler_params=params,
            cost_estimate=cost(1, 1024),
            name="columns",
        )(*operands, ww, vw, fw, *parts, *first)

    own_tiles = columns_of((0, 2, 4, 6), mine)
    sibling_grads, own_tiles = lax.optimization_barrier((sibling_grads, own_tiles))
    sibling = operands_of(sibling_grads)
    received = []
    for distances in ((0, 2), (4, 6)):
        passed = columns_of(distances, sibling)
        passed, sibling = lax.optimization_barrier((passed, sibling))
        received.append(lax.ppermute(passed, "core", swap))
    total = pl.pallas_call(
        partial(lay_kernel, ctx),
        out_shape=jax.ShapeDtypeStruct((rows, dim), bf16),
        in_specs=[VMEM] * 3,
        out_specs=ANY,
        scratch_shapes=[pltpu.SemaphoreType.DMA((count,))],
        compiler_params=params,
        cost_estimate=cost(1, 1024),
        name="lay",
    )(own_tiles, *received)
    return (attended, total)


def solution(mesh):
    blocks, tp = mesh.devices.shape
    bits = blocks.bit_length() - 1
    assert blocks == 2**bits
    ctx = tuple(f"half{i}" for i in range(bits - 1)) + ("core",)
    split = Mesh(mesh.devices.reshape((2,) * bits + (tp,)), (*ctx, "tp"))
    in_specs = (
        P(ctx, None),
        P(None, "tp"),
        P(None, "tp"),
        P(None, "tp"),
        P(ctx, "tp"),
        P(ctx, "tp"),
    )
    out_specs = (P(ctx, "tp"), P(ctx, None))
    return jax.shard_map(
        partial(per_device, ctx),
        mesh=split,
        in_specs=in_specs,
        out_specs=out_specs,
        check_vma=False,
    )
```
